128 devices in a mesh: dp: 4 (over z_lo, core), fsdp: 32 (over y, x, z_hi).
Axes of the slice: x: 4, y: 4, z: 4 (z_hi: 2, z_lo: 2; z = z_hi * 2 + z_lo), core: 2. Of those that a mesh axis runs over, the one named last changes fastest.
Arguments:
- inputs: bfloat16 [32768, 1024], P(('dp', 'fsdp')), may hold values from -6 to 6
- cotangent: bfloat16 [32768, 1024], P(('dp', 'fsdp')), may hold values from -24 to 24
- lengths: int32 [128, 8], P(('dp', 'fsdp')), may hold values from 1 to 128, 256 in all within a row
- norm1_gain: bfloat16 [1024], P(('dp', 'fsdp')), may hold values from 0.25 to 1.75
- norm1_bias: bfloat16 [1024], P(('dp', 'fsdp')), may hold values from -1.75 to 1.75
- norm2_gain: bfloat16 [1024], P(('dp', 'fsdp')), may hold values from 0.25 to 1.75
- norm2_bias: bfloat16 [1024], P(('dp', 'fsdp')), may hold values from -1.75 to 1.75
- qkv_weight: bfloat16 [3145728], P(('dp', 'fsdp')), may hold values from -0.1875 to 0.1875
- qkv_bias: bfloat16 [3072], P(('dp', 'fsdp')), may hold values from -3 to 3
- dense_weight: bfloat16 [1048576], P(('dp', 'fsdp')), may hold values from -0.75 to 0.75
- dense_bias: bfloat16 [1024], P(('dp', 'fsdp')), may hold values from -3 to 3
- up_weight: bfloat16 [4194304], P(('dp', 'fsdp')), may hold values from -0.1875 to 0.1875
- up_bias: bfloat16 [4096], P(('dp', 'fsdp')), may hold values from -3 to 3
- down_weight: bfloat16 [4194304], P(('dp', 'fsdp')), may hold values from -0.09375 to 0.09375
- down_bias: bfloat16 [1024], P(('dp', 'fsdp')), may hold values from -3 to 3
Outputs:
- block_output: bfloat16 [32768, 1024], P(('dp', 'fsdp'))
- input_grad: float32 [32768, 1024], P(('dp', 'fsdp'))
- norm1_gain_grad: float32 [1024], P(('dp', 'fsdp'))
- norm1_bias_grad: float32 [1024], P(('dp', 'fsdp'))
- norm2_gain_grad: float32 [1024], P(('dp', 'fsdp'))
- norm2_bias_grad: float32 [1024], P(('dp', 'fsdp'))
- qkv_weight_grad: float32 [3145728], P(('dp', 'fsdp'))
- qkv_bias_grad: float32 [3072], P(('dp', 'fsdp'))
- dense_weight_grad: float32 [1048576], P(('dp', 'fsdp'))
- dense_bias_grad: float32 [1024], P(('dp', 'fsdp'))
- up_weight_grad: float32 [4194304], P(('dp', 'fsdp'))
- up_bias_grad: float32 [4096], P(('dp', 'fsdp'))
- down_weight_grad: float32 [4194304], P(('dp', 'fsdp'))
- down_bias_grad: float32 [1024], P(('dp', 'fsdp'))
The draws below stay inside these ranges and needn't reach their ends.
Inputs may be any that keep to these rules, and one draw needn't show every extreme that they name: Each row's entries sum to 256; the first 7 are document lengths, the last the padding at the row's end.
All inputs are finite; a program needn't handle non-finite values.
Results may differ from the reference program's by a relative error of at most 0.017.
Values may be sent and summed in bfloat16 or wider, within the bound.
No kernel may reach another device: no remote copies, remote signals or barrier semaphores. Data moves between devices by JAX's collectives and lax.ppermute only.
A program may use at most 256 MiB of HBM per device.

```python
import math
import jax
import jax.numpy as jnp
import numpy as np
from jax import lax

D = 1024
HEADS = 16
HEAD_DIM = 64
ROT = 16
FF = 4096
ROW = 256
SEGS = 8
SEQS = 128
TOKENS = 32768


def raised(values, own_key, source, target, parts, factor):
    def block_of(dim):
        return (jnp.arange(values.shape[dim]) // (values.shape[dim] // parts)).reshape((-1,) + (1,) * (values.ndim - 1 - dim))

    first = jax.random.permutation(own_key, parts)[block_of(target)]
    other_side = (block_of(target) + parts // 2) % parts
    return jnp.where((block_of(source) == first) | (block_of(source) == other_side), factor * values, values)


def block_scale(key, dims, split, low, largest):
    level, own = 1.0, jax.random.fold_in(key, 6)
    for position, blocks in split:
        heights = jnp.exp(jax.random.uniform(jax.random.fold_in(own, position), (blocks,), jnp.float32, low / len(split), largest / len(split)))
        level = level * jnp.repeat(heights, dims[position] // blocks).reshape([-1 if axis == position else 1 for axis in range(len(dims))])
    return level


def profile(number_of, total, most, slope):
    loads = [(1 << 20) // math.isqrt(grade ** slope) + 1 for grade in range(2, number_of + 1)]
    surplus, holding = total - most - (number_of - 1), [1] * (number_of - 1)
    while surplus > 0:
        candidates = [i for i in range(number_of - 1) if holding[i] < most]
        pool, budget = sum([loads[i] for i in candidates]), surplus
        for i in candidates:
            addition = min(most - holding[i], max(1, budget * loads[i] // pool), surplus)
            holding[i] = holding[i] + addition
            surplus = surplus - addition
    return np.array([most] + holding)


def uneven_parts(stream_key, amount, total, limit, lean):
    if amount == 2:
        one = jax.random.randint(stream_key, (), max(1, total - limit), min(limit, total - 1) + 1)
        return jnp.stack([one, total - one])
    sizes = jnp.asarray(profile(amount, total, limit, lean), jnp.int32)
    twos = (amount - 1) // 2
    giver, taker = sizes[1:1 + 2 * twos:2], sizes[2:2 + 2 * twos:2]
    margin = jnp.minimum(giver - 1, limit - taker)
    moved = jax.random.randint(jax.random.fold_in(stream_key, 1), (twos,), 0, 1 << 20) % (margin + 1)
    sizes = sizes.at[1:1 + 2 * twos:2].set(giver - moved).at[2:2 + 2 * twos:2].set(taker + moved)
    return sizes[jax.random.permutation(jax.random.fold_in(stream_key, 2), amount)]


def normal_values(key, dims, deviation, most, cuts=(), kind=jnp.bfloat16):
    array = jax.random.normal(key, dims, jnp.float32) * deviation
    if len(cuts) > 0:
        array = block_scale(key, dims, cuts, -0.22, 0.18) * array
    return jnp.clip(array, min=-most, max=most).astype(kind)


def heavy_noise(own_key, dims, deviation, reach, shards, heavy, kind=jnp.bfloat16):
    entries = deviation * jax.random.normal(own_key, dims, jnp.float32)
    if shards:
        entries = entries * block_scale(own_key, dims, shards, -0.22, 0.18)
    return jnp.clip(raised(entries, jax.random.fold_in(own_key, 3), *heavy), -reach, reach).astype(kind)


def setup_inputs(seed: int = 0) -> dict:
    key_list = jax.random.split(jax.random.key(seed), 16)
    inputs = normal_values(key_list[0], (TOKENS, D), 1.0, 6.0, ((0, 128),))
    cotangent = heavy_noise(key_list[1], (TOKENS, D), 1.0, 24.0, ((0, 128),), (0, 1, 128, 5.5))
    lengths = jax.vmap(lambda own: uneven_parts(own, SEGS, ROW, ROW // 2, 2))(jax.random.split(key_list[2], SEQS)).reshape((SEQS, SEGS)).astype(jnp.int32)
    norm1_gain = jnp.clip(1.0 + 0.15 * jax.random.normal(key_list[3], (D,), jnp.float32), 0.25, 1.75).astype(jnp.bfloat16)
    norm1_bias = normal_values(key_list[4], (D,), 0.3, 1.75, ((0, 128),))
    norm2_gain = jnp.clip(1.0 + 0.15 * jax.random.normal(key_list[5], (D,), jnp.float32), 0.25, 1.75).astype(jnp.bfloat16)
    norm2_bias = normal_values(key_list[6], (D,), 0.3, 1.75, ((0, 128),))
    qkv_weight = normal_values(key_list[7], (3 * D * D,), D ** -0.5, 0.1875, ((0, 128),))
    qkv_bias = normal_values(key_list[8], (3 * D,), 0.5, 3.0, ((0, 128),))
    dense_weight = normal_values(key_list[9], (D * D,), (D // 16) ** -0.5, 0.75, ((0, 128),))
    dense_bias = normal_values(key_list[10], (D,), 0.5, 3.0, ((0, 128),))
    up_weight = normal_values(key_list[11], (D * FF,), D ** -0.5, 0.1875, ((0, 128),))
    up_bias = normal_values(key_list[12], (FF,), 0.5, 3.0, ((0, 128),))
    down_weight = normal_values(key_list[13], (FF * D,), FF ** -0.5, 0.09375, ((0, 128),))
    down_bias = normal_values(key_list[14], (D,), 0.5, 3.0, ((0, 128),))
    return {"inputs": inputs, "cotangent": cotangent, "lengths": lengths, "norm1_gain": norm1_gain, "norm1_bias": norm1_bias, "norm2_gain": norm2_gain, "norm2_bias": norm2_bias, "qkv_weight": qkv_weight, "qkv_bias": qkv_bias, "dense_weight": dense_weight, "dense_bias": dense_bias, "up_weight": up_weight, "up_bias": up_bias, "down_weight": down_weight, "down_bias": down_bias}


@jax.custom_vjp
def low(v):
    return lax.optimization_barrier(v.astype(jnp.bfloat16)).astype(jnp.float32)

@jax.custom_vjp
def low_back(v):
    return v

def low_keep(v):
    return (low(v), None)

def low_pass(kept, grad):
    return (grad,)

def back_keep(v):
    return (v, None)

def back_low(kept, grad):
    return (low(grad),)
low.defvjp(low_keep, low_pass)
low_back.defvjp(back_keep, back_low)

def matmul(left, right):
    return jnp.dot(left, right, precision=lax.Precision.HIGHEST, preferred_element_type=jnp.float32)

def layer_norm(states, gain, offset):
    average = lax.optimization_barrier(jnp.mean(states, axis=-1, keepdims=True))
    centred = states - average
    spread = lax.optimization_barrier(jnp.mean(centred * centred, axis=-1, keepdims=True))
    return centred * lax.rsqrt(spread + 1e-05) * gain + offset

def documents(seg_lens):
    ends = jnp.cumsum(seg_lens).astype(jnp.int32)
    starts = (ends - seg_lens).astype(jnp.int32)
    places = jnp.arange(ROW, dtype=jnp.int32)
    doc_ids = lax.optimization_barrier(jnp.sum((places[:, None] >= ends[None, :]).astype(jnp.int32), axis=1)).astype(jnp.int32)
    matches = doc_ids[:, None] == jnp.arange(SEGS, dtype=jnp.int32)[None, :]
    firsts = lax.optimization_barrier(jnp.sum(jnp.where(matches, starts[None, :], 0), axis=1)).astype(jnp.int32)
    return (doc_ids, (places - firsts).astype(jnp.int32))

def rotary(doc_pos):
    half = ROT // 2
    freqs = 10000.0 ** (-(jnp.arange(half, dtype=jnp.float32) * 2.0) / ROT)
    angle = doc_pos.astype(jnp.float32)[:, None] * freqs[None, :]
    angle = jnp.concatenate([angle, angle], axis=-1)[:, None, :]
    return (jnp.cos(angle), jnp.sin(angle))

def rope(values, cosine, sine):
    half = ROT // 2
    leading = values[..., :ROT]
    turned = jnp.concatenate([-leading[..., half:], leading[..., :half]], axis=-1)
    return jnp.concatenate([leading * cosine + turned * sine, values[..., ROT:]], axis=-1)

def attend(item):
    queries, keys_rot, values, doc_ids = item
    places = jnp.arange(ROW, dtype=jnp.int32)
    allowed = (doc_ids[:, None] == doc_ids[None, :]) & (places[None, :] <= places[:, None])
    scores = jnp.einsum('qhd,khd->hqk', queries, keys_rot, precision=lax.Precision.HIGHEST) * HEAD_DIM ** (-0.5)
    scores = low_back(jnp.where(allowed[None], scores, -1000000000.0))
    probs = low(jax.nn.softmax(scores, axis=-1))
    return jnp.einsum('hqk,khd->qhd', probs, values, precision=lax.Precision.HIGHEST)

def layer(weights, states, doc_ids, doc_pos):
    gain_one, bias_one, gain_two, bias_two, w_qkv, b_qkv, w_dense, b_dense, w_up, b_up, w_down, b_down = weights
    count = doc_ids.shape[0]
    attn_in = low(layer_norm(states, gain_one, bias_one))
    mlp_in = low(layer_norm(states, gain_two, bias_two))
    projected = low_back(matmul(attn_in, w_qkv) + b_qkv).reshape(count, ROW, 3, HEADS, HEAD_DIM)
    cosine, sine = jax.vmap(rotary)(doc_pos)
    queries = low(rope(projected[:, :, 0], cosine, sine))
    keys_rot = low(rope(projected[:, :, 1], cosine, sine))
    values = low(projected[:, :, 2])
    context = lax.map(jax.checkpoint(attend), (queries, keys_rot, values, doc_ids))
    context = low_back(low(context)).reshape(count * ROW, D)
    attn_out = low_back(matmul(context, w_dense) + b_dense)
    hidden_pre = low_back(matmul(mlp_in, w_up) + b_up)
    hidden = low(jax.nn.gelu(hidden_pre, approximate=False))
    mlp_out = low_back(matmul(hidden, w_down) + b_down)
    return states + attn_out + mlp_out

def reference(inputs, cotangent, lengths, norm1_gain, norm1_bias, norm2_gain, norm2_bias, qkv_weight, qkv_bias, dense_weight, dense_bias, up_weight, up_bias, down_weight, down_bias):
    params = (norm1_gain.astype(jnp.float32), norm1_bias.astype(jnp.float32), norm2_gain.astype(jnp.float32), norm2_bias.astype(jnp.float32), qkv_weight.astype(jnp.float32).reshape(D, 3 * D), qkv_bias.astype(jnp.float32), dense_weight.astype(jnp.float32).reshape(D, D), dense_bias.astype(jnp.float32), up_weight.astype(jnp.float32).reshape(D, FF), up_bias.astype(jnp.float32), down_weight.astype(jnp.float32).reshape(FF, D), down_bias.astype(jnp.float32))
    span = math.gcd(SEQS, max(1, 4096 // ROW))
    groups = SEQS // span
    states = inputs.astype(jnp.float32).reshape(groups, span * ROW, D)
    upstream = cotangent.astype(jnp.float32).reshape(groups, span * ROW, D)
    seg_lens = lengths.reshape(groups, span, SEGS)

    def advance(totals, item):
        block_in, block_cot, block_lens = item
        doc_ids, doc_pos = jax.vmap(documents)(block_lens)
        keep = (doc_ids < SEGS - 1).astype(jnp.float32).reshape(-1)

        def forward(weights, states_in):
            return layer(weights, states_in, doc_ids, doc_pos)
        result, pullback = jax.vjp(forward, params, block_in)
        grad_params, grad_states = pullback(block_cot * keep[:, None])
        totals = jax.tree.map(jnp.add, totals, grad_params)
        return (totals, (result.astype(jnp.bfloat16), grad_states))
    zeros = jax.tree.map(jnp.zeros_like, params)
    totals, (outputs, grads) = lax.scan(advance, zeros, (states, upstream, seg_lens))
    return (outputs.reshape(TOKENS, D), grads.reshape(TOKENS, D), totals[0], totals[1], totals[2], totals[3], totals[4].reshape(-1), totals[5], totals[6].reshape(-1), totals[7], totals[8].reshape(-1), totals[9], totals[10].reshape(-1), totals[11])
```

```python
import jax
import jax.numpy as jnp
from jax import lax
from jax.experimental import pallas as pl
from jax.experimental.pallas import tpu as pltpu
from jax.sharding import PartitionSpec as P

D = 1024
HEADS = 16
HEAD_DIM = 64
ROT = 16
FF = 4096
ROW = 256
SEGS = 8
TP = 4
QC = 3 * D // TP
HC = FF // TP
LOCAL_HEADS = HEADS // TP
SMALL = 104
AXES = ("dp", "fsdp")
VMEM = 48 * 1024 * 1024

f32 = jnp.float32
bf16 = jnp.bfloat16


def dev(d, y, x, zh):
    return d * 32 + y * 8 + x * 2 + zh


def outer_groups():
    groups = []
    for d in range(4):
        for k in range(4):
            for zh in range(2):
                if d % 2 == 0:
                    groups.append([dev(d, i, k, zh) for i in range(4)])
                else:
                    groups.append([dev(d, k, i, zh) for i in range(4)])
    return groups


def inner_groups():
    groups = []
    for d in range(4):
        for k in range(4):
            if d % 2 == 0:
                groups.append([dev(d, k, i, zh) for i in range(4) for zh in range(2)])
            else:
                groups.append([dev(d, i, k, zh) for i in range(4) for zh in range(2)])
    return groups


def a2a(values, groups):
    return lax.all_to_all(values, AXES, 0, 0, tiled=True, axis_index_groups=groups)


def flip_core(values):
    return lax.ppermute(values, "dp", [(0, 1), (1, 0), (2, 3), (3, 2)])


def flip_chip(values):
    return lax.ppermute(values, "dp", [(0, 2), (2, 0), (1, 3), (3, 1)])


def dot(left, right):
    return jnp.dot(left, right, preferred_element_type=f32)


def dot_nt(left, right):
    return lax.dot_general(left, right, (((1,), (1,)), ((), ())), preferred_element_type=f32)


def dot_tn(left, right):
    return lax.dot_general(left, right, (((0,), (0,)), ((), ())), preferred_element_type=f32)


def params(flops, nbytes, trans=0):
    return dict(
        compiler_params=pltpu.CompilerParams(vmem_limit_bytes=VMEM),
        cost_estimate=pl.CostEstimate(
            flops=int(flops), bytes_accessed=int(nbytes), transcendentals=int(trans)
        ),
    )


def normalize(x):
    average = jnp.mean(x, axis=-1, keepdims=True)
    centred = x - average
    inv_std = lax.rsqrt(jnp.mean(centred * centred, axis=-1, keepdims=True) + 1e-05)
    return centred * inv_std, inv_std


def assemble_a_kernel(core_ref, buf_ref, wqkv_ref, wd_ref, small_ref):
    for d in range(4):
        for p in range(3):
            row = (d * 3 + p) * 16
            wqkv_ref[d, 0, 0, :, p * 256 : (p + 1) * 256] = buf_ref[0, 0, row : row + 16, :]
    for cg in range(4):
        row = 192 + cg * 16
        wd_ref[0, 0, :, cg * 256 : (cg + 1) * 256] = buf_ref[0, 0, row : row + 16, :]
    small_ref[0, 0] = buf_ref[0, 0, 256:272, :]


def swapped(y, x, core_ref):
    c = core_ref[0]
    return y + c * (x - y), x + c * (y - x)


def assemble_a(buf, core):
    grid_spec = pltpu.PrefetchScalarGridSpec(
        num_scalar_prefetch=1,
        grid=(4, 4),
        in_specs=[pl.BlockSpec((1, 1, 272, 256), lambda y, x, c: (*swapped(y, x, c), 0, 0))],
        out_specs=[
            pl.BlockSpec((4, 1, 1, 16, QC), lambda y, x, c: (0, y, x, 0, 0)),
            pl.BlockSpec((1, 1, 16, D), lambda y, x, c: (y, x, 0, 0)),
            pl.BlockSpec((1, 1, 16, 256), lambda y, x, c: (y, x, 0, 0)),
        ],
    )
    wqkv, wd, small = pl.pallas_call(
        assemble_a_kernel,
        grid_spec=grid_spec,
        out_shape=[
            jax.ShapeDtypeStruct((4, 4, 4, 16, QC), bf16),
            jax.ShapeDtypeStruct((4, 4, 16, D), bf16),
            jax.ShapeDtypeStruct((4, 4, 16, 256), bf16),
        ],
        **params(0, 5e6),
    )(core, buf)
    return wqkv.reshape(D, QC), wd.reshape(D // TP, D), small


def assemble_b_kernel(core_ref, buf_ref, wup_ref, wdown_ref):
    for d in range(4):
        for cg in range(4):
            row = (d * 4 + cg) * 16
            wup_ref[d, 0, 0, :, cg * 256 : (cg + 1) * 256] = buf_ref[0, 0, row : row + 16, :]
    for cg in range(4):
        row = 256 + cg * 64
        wdown_ref[0, 0, :, cg * 256 : (cg + 1) * 256] = buf_ref[0, 0, row : row + 64, :]


def assemble_b(buf, core):
    grid_spec = pltpu.PrefetchScalarGridSpec(
        num_scalar_prefetch=1,
        grid=(4, 4),
        in_specs=[pl.BlockSpec((1, 1, 512, 256), lambda y, x, c: (*swapped(y, x, c), 0, 0))],
        out_specs=[
            pl.BlockSpec((4, 1, 1, 16, HC), lambda y, x, c: (0, y, x, 0, 0)),
            pl.BlockSpec((1, 1, 64, D), lambda y, x, c: (y, x, 0, 0)),
        ],
    )
    wup, wdown = pl.pallas_call(
        assemble_b_kernel,
        grid_spec=grid_spec,
        out_shape=[
            jax.ShapeDtypeStruct((4, 4, 4, 16, HC), bf16),
            jax.ShapeDtypeStruct((4, 4, 64, D), bf16),
        ],
        **params(0, 8e6),
    )(core, buf)
    return wup.reshape(D, HC), wdown.reshape(HC, D)


def turn(u, cosine, sin_left, sin_right):
    return (
        u * cosine
        + pltpu.roll(u, u.shape[1] - ROT // 2, 1) * sin_left
        + pltpu.roll(u, ROT // 2, 1) * sin_right
    )


def attention_kernel(
    ends_ref,
    x_ref,
    cot_ref,
    wqkv_ref,
    wd_ref,
    vec_ref,
    qb_ref,
    cos_ref,
    sl_ref,
    sr_ref,
    ain_ref,
    min_ref,
    gb_ref,
    ctx_ref,
    dqkv_ref,
    sums_ref,
):
    r = pl.program_id(0)
    xhat, _ = normalize(x_ref[0].astype(f32))
    attn_in = (xhat * vec_ref[0:1] + vec_ref[1:2]).astype(bf16)
    ain_ref[...] = attn_in
    min_ref[...] = (xhat * vec_ref[2:3] + vec_ref[3:4]).astype(bf16)
    qkv = dot(attn_in, wqkv_ref[...]) + qb_ref[0:1]
    ends = [ends_ref[r * SEGS + j] for j in range(SEGS - 1)]
    rows = lax.broadcasted_iota(jnp.int32, (ROW, 1), 0)
    cols = lax.broadcasted_iota(jnp.int32, (1, ROW), 1)
    row_doc = sum([(rows >= e).astype(jnp.int32) for e in ends])
    col_doc = sum([(cols >= e).astype(jnp.int32) for e in ends])
    allowed = (row_doc == col_doc) & (cols <= rows)
    kept = jnp.where(rows < ends[-1], cot_ref[0].astype(f32), 0.0)
    gb = kept.astype(bf16)
    gb_ref[...] = gb
    dctx = dot_nt(gb, wd_ref[...]).astype(bf16)
    cosine, left, right = cos_ref[0], sl_ref[0], sr_ref[0]
    q = turn(qkv[:, 0:256], cosine, left, right).astype(bf16)
    k = turn(qkv[:, 256:512], cosine, left, right).astype(bf16)
    v = qkv[:, 512:768].astype(bf16)
    scale = HEAD_DIM**-0.5
    ctx, dq, dk, dv = [], [], [], []
    for h in range(LOCAL_HEADS):
        at = slice(h * HEAD_DIM, (h + 1) * HEAD_DIM)
        qh, kh, vh, dch = q[:, at], k[:, at], v[:, at], dctx[:, at]
        scores = jnp.where(allowed, dot_nt(qh, kh) * scale, -1000000000.0)
        shifted = jnp.exp(scores - jnp.max(scores, axis=-1, keepdims=True))
        probs = shifted * (1.0 / jnp.sum(shifted, axis=-1, keepdims=True))
        low = probs.astype(bf16)
        ctx.append(dot(low, vh))
        dv.append(dot_tn(low, dch))
        dprobs = dot_nt(dch, vh)
        inner = jnp.sum(dprobs * probs, axis=-1, keepdims=True)
        ds = (probs * (dprobs - inner)).astype(bf16)
        dq.append(dot(ds, kh) * scale)
        dk.append(dot_tn(ds, qh) * scale)
    ctx_ref[...] = jnp.concatenate(ctx, axis=1).astype(bf16)
    dqs = turn(jnp.concatenate(dq, axis=1), cosine, -left, -right)
    dks = turn(jnp.concatenate(dk, axis=1), cosine, -left, -right)
    dqkv = jnp.concatenate([dqs, dks] + dv, axis=1).astype(bf16)
    dqkv_ref[...] = dqkv

    @pl.when(r == 0)
    def _():
        sums_ref[...] = jnp.zeros_like(sums_ref)
        sums_ref[0:1, :] = jnp.sum(kept, axis=0, keepdims=True)

    sums_ref[1:2, 0:QC] += jnp.sum(dqkv.astype(f32), axis=0, keepdims=True)


def attention(ends, x4, cot4, wqkv, wd, vec, qb, cosine, left, right):
    row = lambda r, e: (r, 0)
    row3 = lambda r, e: (r, 0, 0)
    fixed = lambda r, e: (0, 0)
    grid_spec = pltpu.PrefetchScalarGridSpec(
        num_scalar_prefetch=1,
        grid=(TP,),
        in_specs=[
            pl.BlockSpec((1, ROW, D), row3),
            pl.BlockSpec((1, ROW, D), row3),
            pl.BlockSpec((D, QC), fixed),
            pl.BlockSpec((D // TP, D), fixed),
            pl.BlockSpec((8, D), fixed),
            pl.BlockSpec((8, QC), fixed),
            pl.BlockSpec((1, ROW, 256), row3),
            pl.BlockSpec((1, ROW, 256), row3),
            pl.BlockSpec((1, ROW, 256), row3),
        ],
        out_specs=[
            pl.BlockSpec((ROW, D), row),
            pl.BlockSpec((ROW, D), row),
            pl.BlockSpec((ROW, D), row),
            pl.BlockSpec((ROW, 256), row),
            pl.BlockSpec((ROW, QC), row),
            pl.BlockSpec((8, D), fixed),
        ],
    )
    tokens = TP * ROW
    return pl.pallas_call(
        attention_kernel,
        grid_spec=grid_spec,
        out_shape=[
            jax.ShapeDtypeStruct((tokens, D), bf16),
            jax.ShapeDtypeStruct((tokens, D), bf16),
            jax.ShapeDtypeStruct((tokens, D), bf16),
            jax.ShapeDtypeStruct((tokens, 256), bf16),
            jax.ShapeDtypeStruct((tokens, QC), bf16),
            jax.ShapeDtypeStruct((8, D), f32),
        ],
        **params(4e9, 2e7, 1e6),
    )(ends, x4, cot4, wqkv, wd, vec, qb, cosine, left, right)


def grads_a_kernel(core_ref, ain_ref, dqkv_ref, ctx_ref, gb_ref, out_ref):
    d = pl.program_id(0)
    c = core_ref[0]
    dqkv_grad = dot_tn(ain_ref[...], dqkv_ref[...]).astype(bf16)
    dense_grad = dot_tn(ctx_ref[...], gb_ref[...]).astype(bf16)
    base = pl.multiple_of(d * 48, 16)
    dense_base = pl.multiple_of(192 + d * 16, 16)
    for y in range(4):
        for x in range(4):
            b, a = y + c * (x - y), x + c * (y - x)
            at = slice((y * 4 + x) * 16, (y * 4 + x + 1) * 16)
            for p in range(3):
                out_ref[b, a, pl.ds(base + p * 16, 16), :] = dqkv_grad[at, p * 256 : (p + 1) * 256]
            out_ref[b, a, pl.ds(dense_base, 16), :] = dense_grad[at]


def grads_a(core, attn_in, dqkv, ctx, gb):
    tokens = TP * ROW
    grid_spec = pltpu.PrefetchScalarGridSpec(
        num_scalar_prefetch=1,
        grid=(4,),
        in_specs=[
            pl.BlockSpec((tokens, 256), lambda d, c: (0, d)),
            pl.BlockSpec((tokens, QC), lambda d, c: (0, 0)),
            pl.BlockSpec((tokens, 256), lambda d, c: (0, 0)),
            pl.BlockSpec((tokens, 256), lambda d, c: (0, d)),
        ],
        out_specs=pl.BlockSpec((4, 4, 256, 256), lambda d, c: (0, 0, 0, 0)),
    )
    return pl.pallas_call(
        grads_a_kernel,
        grid_spec=grid_spec,
        out_shape=jax.ShapeDtypeStruct((4, 4, 256, 256), bf16),
        **params(2.2e9, 1e7),
    )(core, attn_in, dqkv, ctx, gb)


def grads_down_kernel(core_ref, hidden_ref, gb_ref, out_ref):
    y = pl.program_id(0)
    c = core_ref[0]
    grad = dot_tn(hidden_ref[...], gb_ref[...]).astype(bf16)
    for x in range(4):
        b, a = y + c * (x - y), x + c * (y - x)
        for cg in range(4):
            out_ref[b, a, cg * 64 : (cg + 1) * 64, :] = grad[
                x * 64 : (x + 1) * 64, cg * 256 : (cg + 1) * 256
            ]


def grads_down(core, hidden, gb):
    tokens = TP * ROW
    grid_spec = pltpu.PrefetchScalarGridSpec(
        num_scalar_prefetch=1,
        grid=(4,),
        in_specs=[
            pl.BlockSpec((tokens, 256), lambda y, c: (0, y)),
            pl.BlockSpec((tokens, D), lambda y, c: (0, 0)),
        ],
        out_specs=pl.BlockSpec((4, 4, 256, 256), lambda y, c: (0, 0, 0, 0)),
    )
    return pl.pallas_call(
        grads_down_kernel,
        grid_spec=grid_spec,
        out_shape=jax.ShapeDtypeStruct((4, 4, 256, 256), bf16),
        **params(2.2e9, 6e6),
    )(core, hidden, gb)


def grads_up_kernel(core_ref, min_ref, dpre_ref, small_ref, out_ref):
    d = pl.program_id(0)
    c = core_ref[0]
    grad = dot_tn(min_ref[...], dpre_ref[...]).astype(bf16)
    base = pl.multiple_of(d * 64, 16)
    for y in range(4):
        for x in range(4):
            b, a = y + c * (x - y), x + c * (y - x)
            at = slice((y * 4 + x) * 16, (y * 4 + x + 1) * 16)
            for cg in range(4):
                out_ref[b, a, pl.ds(base + cg * 16, 16), :] = grad[at, cg * 256 : (cg + 1) * 256]

    @pl.when(d == 0)
    def _():
        for y in range(4):
            for x in range(4):
                b, a = y + c * (x - y), x + c * (y - x)
                out_ref[b, a, 256:272, :] = small_ref[y, x]


def grads_up(core, mlp_in, dpre, small):
    tokens = TP * ROW
    grid_spec = pltpu.PrefetchScalarGridSpec(
        num_scalar_prefetch=1,
        grid=(4,),
        in_specs=[
            pl.BlockSpec((tokens, 256), lambda d, c: (0, d)),
            pl.BlockSpec((tokens, HC), lambda d, c: (0, 0)),
            pl.BlockSpec((4, 4, 16, 256), lambda d, c: (0, 0, 0, 0)),
        ],
        out_specs=pl.BlockSpec((4, 4, 272, 256), lambda d, c: (0, 0, 0, 0)),
    )
    return pl.pallas_call(
        grads_up_kernel,
        grid_spec=grid_spec,
        out_shape=jax.ShapeDtypeStruct((4, 4, 272, 256), bf16),
        **params(2.2e9, 6e6),
    )(core, mlp_in, dpre, small)


def hidden_kernel(min_ref, gb_ref, wup_ref, wdown_ref, ub_ref, hidden_ref, dpre_ref, sums_ref):
    t = pl.program_id(1)
    pre = dot(min_ref[...], wup_ref[...]) + ub_ref[0:1]
    back = dot_nt(gb_ref[...], wdown_ref[...])
    size = jnp.abs(pre) * 0.7071067811865476
    bell = jnp.exp(-0.5 * pre * pre)
    s = 1.0 / (1.0 + 0.3275911 * size)
    poly = s * (
        0.127414796
        + s * (-0.142248368 + s * (0.7107068705 + s * (-0.7265760135 + s * 0.5307027145)))
    )
    tail = poly * bell
    cumul = jnp.where(pre >= 0.0, 1.0 - tail, tail)
    hidden_ref[...] = (pre * cumul).astype(bf16)
    dpre = (back * (cumul + pre * (bell * 0.3989422804014327))).astype(bf16)
    dpre_ref[...] = dpre

    @pl.when(t == 0)
    def _():
        sums_ref[...] = jnp.zeros_like(sums_ref)

    sums_ref[0:1, :] += jnp.sum(dpre.astype(f32), axis=0, keepdims=True)


def hidden_units(mlp_in, gb, wup, wdown, ub):
    tokens = TP * ROW
    return pl.pallas_call(
        hidden_kernel,
        grid=(4, 4),
        in_specs=[
            pl.BlockSpec((256, D), lambda j, t: (t, 0)),
            pl.BlockSpec((256, D), lambda j, t: (t, 0)),
            pl.BlockSpec((D, 256), lambda j, t: (0, j)),
            pl.BlockSpec((256, D), lambda j, t: (j, 0)),
            pl.BlockSpec((8, 256), lambda j, t: (0, j)),
        ],
        out_specs=[
            pl.BlockSpec((256, 256), lambda j, t: (t, j)),
            pl.BlockSpec((256, 256), lambda j, t: (t, j)),
            pl.BlockSpec((8, 256), lambda j, t: (0, j)),
        ],
        out_shape=[
            jax.ShapeDtypeStruct((tokens, HC), bf16),
            jax.ShapeDtypeStruct((tokens, HC), bf16),
            jax.ShapeDtypeStruct((8, HC), f32),
        ],
        **params(8e9, 2e7, 2e6),
    )(mlp_in, gb, wup, wdown, ub)


def outputs_kernel(
    x_ref,
    ctx_ref,
    hidden_ref,
    dqkv_ref,
    dpre_ref,
    wd_ref,
    wdown_ref,
    wqkv_ref,
    wup_ref,
    vec_ref,
    out_ref,
    sums_ref,
):
    t = pl.program_id(0)
    forward = dot(ctx_ref[...], wd_ref[...]) + dot(hidden_ref[...], wdown_ref[...])
    out_ref[0, 0] = forward.astype(bf16)
    dattn = dot_nt(dqkv_ref[...], wqkv_ref[...])
    dmlp = dot_nt(dpre_ref[...], wup_ref[...])
    xhat, _ = normalize(x_ref[0].astype(f32))

    @pl.when(t == 0)
    def _():
        sums_ref[...] = jnp.zeros_like(sums_ref)

    sums_ref[0:1, :] += jnp.sum(dattn * xhat, axis=0, keepdims=True)
    sums_ref[1:2, :] += jnp.sum(dattn, axis=0, keepdims=True)
    sums_ref[2:3, :] += jnp.sum(dmlp * xhat, axis=0, keepdims=True)
    sums_ref[3:4, :] += jnp.sum(dmlp, axis=0, keepdims=True)
    out_ref[0, 1] = (dattn * vec_ref[0:1] + dmlp * vec_ref[2:3]).astype(bf16)


def outputs(x4, ctx, hidden, dqkv, dpre, wd, wdown, wqkv, wup, vec):
    row = lambda t: (t, 0)
    fixed = lambda t: (0, 0)
    return pl.pallas_call(
        outputs_kernel,
        grid=(TP,),
        in_specs=[
            pl.BlockSpec((1, ROW, D), lambda t: (t, 0, 0)),
            pl.BlockSpec((ROW, 256), row),
            pl.BlockSpec((ROW, HC), row),
            pl.BlockSpec((ROW, QC), row),
            pl.BlockSpec((ROW, HC), row),
            pl.BlockSpec((D // TP, D), fixed),
            pl.BlockSpec((HC, D), fixed),
            pl.BlockSpec((D, QC), fixed),
            pl.BlockSpec((D, HC), fixed),
            pl.BlockSpec((8, D), fixed),
        ],
        out_specs=[
            pl.BlockSpec((1, 2, ROW, D), lambda t: (t, 0, 0, 0)),
            pl.BlockSpec((8, D), fixed),
        ],
        out_shape=[
            jax.ShapeDtypeStruct((TP, 2, ROW, D), bf16),
            jax.ShapeDtypeStruct((8, D), f32),
        ],
        **params(6.5e9, 2e7),
    )(x4, ctx, hidden, dqkv, dpre, wd, wdown, wqkv, wup, vec)


def rotary_tables(ends, starts_len):
    places = jnp.arange(ROW, dtype=jnp.int32)
    passed = places[None, :, None] >= ends[:, None, : SEGS - 1]
    first = jnp.max(jnp.where(passed, ends[:, None, : SEGS - 1], 0), axis=-1)
    place = (places[None, :] - first).astype(f32)
    half = ROT // 2
    freqs = 10000.0 ** (-(jnp.arange(half, dtype=f32) * 2.0) / ROT)
    angle = place[:, :, None] * freqs
    cosine, sine = jnp.cos(angle), jnp.sin(angle)
    zeros = jnp.zeros_like(sine)
    rest = jnp.zeros((TP, ROW, HEAD_DIM - ROT), f32)
    wide = lambda parts: jnp.tile(jnp.concatenate(parts, axis=-1), (1, 1, LOCAL_HEADS))
    return (
        wide([cosine, cosine, rest + 1.0]),
        wide([-sine, zeros, rest]),
        wide([zeros, sine, rest]),
    )


def widen(vector, rows=8):
    return jnp.pad(vector[None, :], ((0, rows - 1), (0, 0)))


def body(
    inputs,
    cotangent,
    lengths,
    norm1_gain,
    norm1_bias,
    norm2_gain,
    norm2_bias,
    qkv_weight,
    qkv_bias,
    dense_weight,
    dense_bias,
    up_weight,
    up_bias,
    down_weight,
    down_bias,
):
    me = lax.axis_index("dp")
    core = (me % 2).astype(jnp.int32)
    core1 = core[None]
    outer, inner = outer_groups(), inner_groups()

    x_pair = jnp.stack([inputs, flip_chip(inputs)])
    x4 = jnp.concatenate([x_pair, flip_core(x_pair)])
    cot_pair = jnp.stack([cotangent, flip_chip(cotangent)])
    cot4 = jnp.concatenate([cot_pair, flip_core(cot_pair)])

    qkv_piece = qkv_weight.reshape(8, 3, 4, 256).transpose(2, 1, 0, 3).reshape(4, 24, 256)
    up_piece = up_weight.reshape(8, 4, 4, 256).transpose(1, 2, 0, 3).reshape(4, 32, 256)
    vector = jnp.concatenate(
        [
            norm1_gain,
            norm1_bias,
            norm2_gain,
            norm2_bias,
            qkv_bias,
            dense_bias,
            up_bias,
            down_bias,
            lengths[0].astype(bf16),
        ]
    )
    vector = jnp.pad(vector, (0, 256 - SMALL - SEGS))
    small_piece = jnp.broadcast_to(widen(vector)[None], (4, 8, 256))
    first = lax.all_to_all(
        jnp.concatenate([qkv_piece, up_piece, small_piece], axis=1), "dp", 0, 0, tiled=True
    )
    dense_piece = dense_weight.reshape(8, 4, 256).transpose(1, 0, 2).reshape(32, 256)
    down_piece = down_weight.reshape(32, 4, 256).transpose(1, 0, 2).reshape(128, 256)
    vectors = first[:, 56, :]
    block = jnp.concatenate(
        [
            first[:, :24].reshape(96, 256),
            dense_piece,
            jnp.pad(vectors, ((0, 4), (0, 0))),
            first[:, 24:56].reshape(128, 256),
            down_piece,
        ]
    )
    second = a2a(jnp.broadcast_to(block[None], (8, 392, 256)).reshape(8 * 392, 256), inner)
    second = second.reshape(4, 2, 392, 256)
    units = lambda v, n: v.reshape(4, 2, n, 8, 256).transpose(0, 2, 1, 3, 4).reshape(4, n * 16, 256)
    block_a = units(second[:, :, :136], 17)
    block_up = units(second[:, :, 136:264], 16)
    block_down = second[:, :, 264:].reshape(4, 2, 4, 32, 256).transpose(0, 2, 1, 3, 4)
    block_b = jnp.concatenate([block_up, block_down.reshape(4, 256, 256)], axis=1)
    third_a = a2a(jnp.broadcast_to(block_a[None], (4, 4, 272, 256)), outer)
    third_b = a2a(jnp.broadcast_to(block_b[None], (4, 4, 512, 256)), outer)

    lens = vectors[:, SMALL : SMALL + SEGS].astype(f32)
    order = jnp.array([0, 2, 1, 3], jnp.int32) ^ me
    pick = (order[:, None] == jnp.arange(4, dtype=jnp.int32)[None, :]).astype(f32)
    lens4 = jnp.sum(pick[:, :, None] * lens[None], axis=1)
    ends = jnp.cumsum(lens4, axis=1).astype(jnp.int32)
    cosine, left, right = rotary_tables(ends, None)

    wqkv, wd, small = assemble_a(third_a, core1)
    small = small.reshape(4, 4, 2, 8, 256)[:, :, :, :4, :SMALL]
    small = small.transpose(3, 0, 1, 2, 4).reshape(128, SMALL).astype(f32)
    vec = jnp.pad(small[:, :32].reshape(128, 4, 8).transpose(1, 0, 2).reshape(4, D), ((0, 4), (0, 0)))
    qkv_b = small[:, 32:56].reshape(3, 4, 256)
    up_b = small[:, 64:96].reshape(4, HC)
    own = (jnp.arange(4, dtype=jnp.int32) == me).astype(f32)
    qkv_b = jnp.sum(qkv_b * own[None, :, None], axis=1).reshape(QC)
    up_b = jnp.sum(up_b * own[:, None], axis=0)
    out_b = small[:, 56:64].reshape(D) + small[:, 96:104].reshape(D)

    attn_in, mlp_in, gb, ctx, dqkv, sums_a = attention(
        ends.reshape(-1), x4, cot4, wqkv, wd, vec, widen(qkv_b), cosine, left, right
    )
    sent_a = a2a(grads_a(core1, attn_in, dqkv, ctx, gb), outer)

    wup, wdown = assemble_b(third_b, core1)
    hidden, dpre, sums_b = hidden_units(mlp_in, gb, wup, wdown, widen(up_b))
    sent_down = a2a(grads_down(core1, hidden, gb), outer)
    both, sums_c = outputs(x4, ctx, hidden, dqkv, dpre, wd, wdown, wqkv, wup, vec)

    halves = both[:2].astype(f32) + flip_core(both[2:]).astype(f32)
    mine, theirs = halves[0], halves[1].astype(bf16)
    total = mine + flip_chip(theirs).astype(f32)
    states = inputs.astype(f32)
    block_output = (states + total[0] + out_b[None, :]).astype(bf16)
    normed, inv_std = normalize(states)
    scaled = total[1]
    mean_e = jnp.mean(scaled, axis=-1, keepdims=True)
    mean_ex = jnp.mean(scaled * normed, axis=-1, keepdims=True)
    rows = jnp.arange(ROW, dtype=jnp.int32)
    keep = rows < ends[0, SEGS - 2]
    upstream = jnp.where(keep[:, None], cotangent.astype(f32), 0.0)
    input_grad = upstream + inv_std * (scaled - mean_e - normed * mean_ex)

    cut = lambda v, n: v.reshape(128, n)
    qkv_bg = (sums_a[1, :QC].reshape(3, 1, 256) * own[None, :, None]).reshape(-1)
    up_bg = (sums_b[0][None, :] * own[:, None]).reshape(-1)
    table = jnp.concatenate(
        [
            cut(sums_c[0], 8),
            cut(sums_c[1], 8),
            cut(sums_c[2], 8),
            cut(sums_c[3], 8),
            cut(qkv_bg, 24),
            cut(sums_a[0], 8),
            cut(up_bg, 32),
            cut(sums_a[0], 8),
        ],
        axis=1,
    )
    table = jnp.pad(table, ((0, 0), (0, 128 - SMALL)))

    def split(values):
        high = lax.reduce_precision(values, 8, 7)
        return jnp.concatenate([high, values - high], axis=-1).astype(bf16)

    rows_small = split(table).reshape(4, 4, 4, 2, 256).transpose(1, 2, 3, 0, 4)
    rows_small = jnp.pad(rows_small, ((0, 0), (0, 0), (0, 0), (0, 4), (0, 0))).reshape(4, 4, 16, 256)
    sent_up = a2a(grads_up(core1, mlp_in, dpre, rows_small), outer)

    def add(values):
        return jnp.sum(values.astype(f32), axis=0)

    def halve(values, n, size):
        return values.reshape(4, n, 2, size, 256).transpose(0, 2, 1, 3, 4).reshape(8, n * size, 256)

    def rejoin(values):
        return values[..., :128] + values[..., 128:]

    sum_a = halve(add(sent_a), 16, 8).astype(bf16)
    sum_down = halve(add(sent_down), 4, 32).astype(bf16)
    sum_up = add(sent_up)
    sum_small = split(rejoin(sum_up[:, 256:272]).reshape(8, 8, 128))
    sum_up = halve(sum_up[:, :256], 16, 8).astype(bf16)
    fourth = a2a(jnp.concatenate([sum_a, sum_up, sum_small, sum_down], axis=1), inner)
    final = add(fourth.reshape(8, 392, 256))
    dense_grad = final[96:128].reshape(4, 8, 256).transpose(1, 0, 2).reshape(-1)
    down_grad = final[264:392].reshape(4, 32, 256).transpose(1, 0, 2).reshape(-1)
    small_sum = jnp.pad(rejoin(final[256:264])[:4], ((0, 0), (0, 128)))
    last = jnp.concatenate(
        [
            final[0:96].reshape(4, 24, 256),
            final[128:256].reshape(4, 32, 256),
            jnp.pad(small_sum[:, None, :], ((0, 0), (0, 7), (0, 0))),
        ],
        axis=1,
    )
    last = lax.all_to_all(last, "dp", 0, 0, tiled=True)
    qkv_grad = last[:, :24].reshape(4, 3, 8, 256).transpose(2, 1, 0, 3).reshape(-1)
    up_grad = last[:, 24:56].reshape(4, 4, 8, 256).transpose(2, 0, 1, 3).reshape(-1)
    tiny = jnp.sum(last[:, 56, :SMALL], axis=0)
    return (
        block_output,
        input_grad,
        tiny[0:8],
        tiny[8:16],
        tiny[16:24],
        tiny[24:32],
        qkv_grad,
        tiny[32:56],
        dense_grad,
        tiny[56:64],
        up_grad,
        tiny[64:96],
        down_grad,
        tiny[96:104],
    )


def solution(mesh):
    flat = P(("dp", "fsdp"))
    rows = P(("dp", "fsdp"), None)
    return jax.shard_map(
        body,
        mesh=mesh,
        in_specs=(rows,) * 3 + (flat,) * 12,
        out_specs=(rows,) * 2 + (flat,) * 12,
        check_vma=False,
    )
```

```python
import jax
import jax.numpy as jnp
import ml_dtypes
import numpy as np
from jax import lax
from jax.experimental import pallas as pl
from jax.experimental.pallas import tpu as pltpu
from jax.sharding import PartitionSpec as P

D = 1024
HEADS = 16
HEAD_DIM = 64
ROT = 16
FF = 4096
ROW = 256
SEGS = 8
TP = 4
QC = 3 * D // TP
HC = FF // TP
LOCAL_HEADS = HEADS // TP
AXES = ("dp", "fsdp")
VMEM = 36 * 1024 * 1024

f32 = jnp.float32
bf16 = jnp.bfloat16


def dev(d, y, x, zh):
    return d * 32 + y * 8 + x * 2 + zh


def outer_groups(flip=0):
    groups = []
    for d in range(4):
        for k in range(4):
            for zh in range(2):
                if d % 2 == flip:
                    groups.append([dev(d, i, k, zh) for i in range(4)])
                else:
                    groups.append([dev(d, k, i, zh) for i in range(4)])
    return groups


def inner_groups():
    return outer_groups(flip=1)


def stack_groups():
    return [
        [dev(d, y, x, zh) for d in range(4) for zh in range(2)] for y in range(4) for x in range(4)
    ]


def plane_groups():
    return [
        [dev(d, y, x, zh) for y in range(4) for x in range(4)] for d in range(4) for zh in range(2)
    ]


def outer_flip(values, step):
    pairs = [(g[i], g[i ^ step]) for g in outer_groups() for i in range(4)]
    return lax.ppermute(values, AXES, pairs)


def a2a(values, groups):
    return lax.all_to_all(values, AXES, 0, 0, tiled=True, axis_index_groups=groups)


def flip_core(values):
    return lax.ppermute(values, "dp", [(0, 1), (1, 0), (2, 3), (3, 2)])


def flip_chip(values):
    return lax.ppermute(values, "dp", [(0, 2), (2, 0), (1, 3), (3, 1)])


def flip_far(values):
    return lax.ppermute(values, "fsdp", [(i, i ^ 1) for i in range(32)])


def dot(left, right):
    return jnp.dot(left, right, preferred_element_type=f32)


def dot_nt(left, right):
    return lax.dot_general(left, right, (((1,), (1,)), ((), ())), preferred_element_type=f32)


def dot_tn(left, right):
    return lax.dot_general(left, right, (((0,), (0,)), ((), ())), preferred_element_type=f32)


def in_hbm(values):
    return pltpu.with_memory_space_constraint(values, pltpu.HBM)


VMEM_SPEC = pl.BlockSpec(memory_space=pltpu.VMEM)
SMEM_SPEC = pl.BlockSpec(memory_space=pltpu.SMEM)
HBM_SPEC = pl.BlockSpec(memory_space=pltpu.HBM)
SPECS = {"s": SMEM_SPEC, "v": VMEM_SPEC, "h": HBM_SPEC}


def call(kernel, out_shape, *args, places=None, outs=None, scratch=(), flops=0, nbytes=0, trans=0):
    places = places or "s" + "v" * (len(args) - 1)
    out_specs = jax.tree.map(lambda _: VMEM_SPEC, out_shape)
    if outs is not None:
        out_specs = [SPECS[o] for o in outs]
        out_shape = [
            pltpu.HBM(v.shape, v.dtype) if o == "h" else v for o, v in zip(outs, out_shape)
        ]
    args = [in_hbm(v) if p == "h" else v for p, v in zip(places, args)]
    return pl.pallas_call(
        kernel,
        in_specs=[SPECS[p] for p in places],
        out_specs=out_specs,
        out_shape=out_shape,
        scratch_shapes=list(scratch),
        compiler_params=pltpu.CompilerParams(vmem_limit_bytes=VMEM),
        cost_estimate=pl.CostEstimate(
            flops=int(flops), bytes_accessed=int(nbytes), transcendentals=int(trans)
        ),
    )(*args)


def shaped(*shape, dtype=bf16):
    return jax.ShapeDtypeStruct(shape, dtype)


def normalize(x):
    average = jnp.mean(x, axis=-1, keepdims=True)
    centred = x - average
    inv_std = lax.rsqrt(jnp.mean(centred * centred, axis=-1, keepdims=True) + 1e-05)
    return centred * inv_std, inv_std


STARTS = (0, 4, 8, 12, 16, 28, 32, 48)
SIZES = (8, 8, 8, 8, 24, 8, 32, 8)
IMAGE = 64
LENS = 52
SLOT = QC + HC + IMAGE // 8 * 256


def tile(n):
    return pl.ds(pl.multiple_of(n * 256, 256), 256)


def swapped(y, x, c):
    return y + c * (x - y), x + c * (y - x)


def prepare_kernel(
    place_ref, qkv_ref, up_ref, dense_in, down_in, len_in, n1g, n1b, n2g, n2b, qb, db, ub, dnb,
    out_ref, pieces_ref, image_ref, *rest
):
    sources = (len_in, n1g, n1b, n2g, n2b, qb, db, ub, dnb)
    holders, sem = rest[:9], rest[9]
    copies = [
        pltpu.make_async_copy(src, dst, sem.at[i])
        for i, (src, dst) in enumerate(zip(sources, holders))
    ]
    for copy in copies:
        copy.start()
    for d in range(4):
        for zh in range(2):
            s = d * 2 + zh
            for p in range(3):
                at = p * D + d * 256
                out_ref[s, :, p * 256 : (p + 1) * 256] = qkv_ref[:, at : at + 256]
            out_ref[s, :, QC : QC + HC] = up_ref[:, d * HC : (d + 1) * HC]
    pieces_ref[0:32, :] = down_in[...]
    pieces_ref[32:40, :] = dense_in[...]
    image_ref[...] = jnp.zeros_like(image_ref)
    for copy in copies:
        copy.wait()
    p = place_ref[0]
    for start, size, ref in zip(STARTS, SIZES, holders[1:]):
        first = p * size
        row, lane = start + first // 256, first % 256
        wide = 512 if size == 24 else 256
        values = jnp.concatenate(
            [ref[...].astype(f32), jnp.zeros((1, wide - size), f32)], axis=1
        )
        values = pltpu.roll(values, lane, 1)
        image_ref[pl.ds(row, 1), :] = values[:, :256]
        if wide == 512:
            image_ref[pl.ds(row + 1, 1), :] = values[:, 256:]
    lens = jnp.concatenate(
        [holders[0][...].astype(f32), jnp.zeros((1, 256 - SEGS), f32)], axis=1
    )
    image_ref[LENS : LENS + 1, :] = pltpu.roll(lens, place_ref[1] * SEGS, 1)
    for g in range(IMAGE // 8):
        block = image_ref[g * 8 : (g + 1) * 8, :].astype(bf16)
        at = QC + HC + g * 256
        for s in range(8):
            out_ref[s, :, at : at + 256] = block


def prepare(place, qkv, up, dense, down, lengths, vectors):
    vectors = [v[None, :] for v in vectors]
    return call(
        prepare_kernel,
        [shaped(8, 8, SLOT), shaped(40, D)],
        place,
        qkv,
        up,
        dense,
        down,
        lengths,
        *vectors,
        places="svvvv" + "h" * 9,
        scratch=[pltpu.VMEM((IMAGE, 256), f32), pltpu.VMEM((1, SEGS), jnp.int32)]
        + [pltpu.VMEM(v.shape, bf16) for v in vectors]
        + [pltpu.SemaphoreType.DMA((9,))],
        nbytes=1e6,
    )


def spread_kernel(far_ref, first_ref, mine_ref, theirs_ref, out_ref, lens_ref):
    far = far_ref[0] == 1
    mine, theirs = mine_ref[...].astype(f32), theirs_ref[...].astype(f32)
    low, high = jnp.where(far, theirs, mine), jnp.where(far, mine, theirs)
    down = jnp.concatenate([low[:32], high[:32]], axis=0).astype(bf16)
    dense = jnp.concatenate([low[32:], high[32:]], axis=0).astype(bf16)
    images = []
    for g in range(IMAGE // 8):
        at = QC + HC + g * 256
        parts = [first_ref[d, :, at : at + 256].astype(f32) for d in range(4)]
        total = sum(parts)
        images.append(total[:8] + total[8:])
    image = jnp.concatenate(images, axis=0)
    lens_ref[...] = image[LENS : LENS + 1, :].astype(jnp.int32)
    image = image.astype(bf16)
    for i in range(4):
        for d in range(4):
            for p in range(3):
                row = (d * 3 + p) * 16
                out_ref[i, row : row + 16, :] = first_ref[d, :, p * 256 : (p + 1) * 256]
            for cg in range(4):
                row = 256 + (d * 4 + cg) * 16
                at = QC + cg * 256
                out_ref[i, row : row + 16, :] = first_ref[d, :, at : at + 256]
        for cg in range(4):
            at = slice(cg * 256, (cg + 1) * 256)
            out_ref[i, 192 + cg * 16 : 208 + cg * 16, :] = dense[:, at]
            out_ref[i, 512 + cg * 64 : 576 + cg * 64, :] = down[:, at]
        out_ref[i, 768 : 768 + IMAGE, :] = image


def spread(far, first, mine, theirs):
    return call(
        spread_kernel,
        [shaped(4, 768 + IMAGE, 256), shaped(1, 256, dtype=jnp.int32)],
        far,
        first,
        mine,
        theirs,
        nbytes=2e6,
    )


def widen_kernel(in_ref, a_ref, b_ref):
    image = sum([in_ref[a, 768 : 768 + IMAGE, :].astype(f32) for a in range(4)]).astype(bf16)

    @pl.loop(0, 4)
    def _(i):
        for a in range(4):
            a_ref[i, a * 256 : (a + 1) * 256, :] = in_ref[a, 0:256, :]
            b_ref[i, a * 512 : (a + 1) * 512, :] = in_ref[a, 256:768, :]
        a_ref[i, 1024 : 1024 + IMAGE, :] = image


def widen(second):
    return call(
        widen_kernel,
        [shaped(4, 1024 + IMAGE, 256), shaped(4, 2048, 256)],
        second,
        places="v",
        nbytes=8e6,
    )


def assemble_a(me, buf_ref, wqkv_ref, wd_ref):
    c = me % 2
    for y in range(4):
        for x in range(4):
            b, a = swapped(y, x, c)
            yx = y * 4 + x
            base = a * 256
            for d in range(4):
                for p in range(3):
                    row = pl.multiple_of(base + (d * 3 + p) * 16, 16)
                    wqkv_ref[d * 256 + yx * 16 : d * 256 + yx * 16 + 16, p * 256 : (p + 1) * 256] = (
                        buf_ref[b, pl.ds(row, 16), :]
                    )
            for cg in range(4):
                row = pl.multiple_of(base + 192 + cg * 16, 16)
                wd_ref[yx * 16 : yx * 16 + 16, cg * 256 : (cg + 1) * 256] = buf_ref[
                    b, pl.ds(row, 16), :
                ]


def read_vectors(me, buf_ref, vec_ref, qb_ref, ub_ref):
    image = sum([buf_ref[b, 1024 : 1024 + IMAGE, :].astype(f32) for b in range(4)])

    def long(start):
        return jnp.concatenate([image[start + i : start + i + 1, :] for i in range(4)], axis=1)

    vec_ref[...] = jnp.zeros_like(vec_ref)
    for i in range(4):
        vec_ref[i : i + 1, :] = long(4 * i)
    vec_ref[4:5, :] = long(28) + long(48)
    own = [jnp.where(me == d, 1.0, 0.0) for d in range(4)]
    rows = [sum([image[16 + p * 4 + d : 17 + p * 4 + d] * own[d] for d in range(4)]) for p in range(3)]
    qb_ref[...] = jnp.concatenate(rows, axis=1)
    ub_ref[...] = sum([long(32 + 4 * d) * own[d] for d in range(4)])


def assemble_b(me, buf_ref, wup_ref, wdown_ref):
    c = me % 2
    for y in range(4):
        for x in range(4):
            b, a = swapped(y, x, c)
            yx = y * 4 + x
            base = a * 512
            for d in range(4):
                for cg in range(4):
                    row = pl.multiple_of(base + (d * 4 + cg) * 16, 16)
                    wup_ref[d * 256 + yx * 16 : d * 256 + yx * 16 + 16, cg * 256 : (cg + 1) * 256] = (
                        buf_ref[b, pl.ds(row, 16), :]
                    )
            for cg in range(4):
                row = pl.multiple_of(base + 256 + cg * 64, 16)
                wdown_ref[yx * 64 : yx * 64 + 64, cg * 256 : (cg + 1) * 256] = buf_ref[
                    b, pl.ds(row, 64), :
                ]


def turn(u, cosine, sin_left, sin_right):
    return (
        u * cosine
        + pltpu.roll(u, u.shape[1] - ROT // 2, 1) * sin_left
        + pltpu.roll(u, ROT // 2, 1) * sin_right
    )


def rotary_tables():
    places = np.arange(ROW, dtype=np.float32)
    freqs = (10000.0 ** (-(np.arange(ROT // 2, dtype=np.float32) * 2.0) / ROT)).astype(np.float32)
    angle = (places[:, None] * freqs[None, :]).astype(np.float32)
    cosine, sine = np.cos(angle), np.sin(angle)
    zeros = np.zeros_like(sine)
    rest = np.zeros((ROW, HEAD_DIM - ROT), np.float32)
    parts = [[cosine, cosine, rest + 1.0], [-sine, zeros, rest], [zeros, sine, rest]]
    columns = []
    for part in parts:
        whole = np.tile(np.concatenate(part, axis=1), (1, 2)).astype(np.float32)
        high = whole.astype(ml_dtypes.bfloat16)
        columns += [high, (whole - high.astype(np.float32)).astype(ml_dtypes.bfloat16)]
    return np.concatenate(columns, axis=1)


def attention_kernel(
    info_ref,
    x0,
    x1,
    x2,
    x3,
    c0,
    c1,
    c2,
    c3,
    buf_ref,
    rot_ref,
    sent_out,
    min_out,
    gb_out,
    ctx_out,
    dqkv_out,
    wqkv_out,
    wd_out,
    vec_ref,
    ub_ref,
    sums_ref,
    x_ref,
    cot_ref,
    wqkv_ref,
    wd_ref,
    qb_ref,
    ain_ref,
    min_ref,
    gb_ref,
    ctx_ref,
    dqkv_ref,
    sent_ref,
    in_sem,
    out_sem,
    weight_sem,
    sent_sem,
):
    me = info_ref[64]
    loads = []
    for i, (one, other) in enumerate(zip((x0, x1, x2, x3), (c0, c1, c2, c3))):
        loads.append(pltpu.make_async_copy(one, x_ref.at[i], in_sem.at[i, 0]))
        loads.append(pltpu.make_async_copy(other, cot_ref.at[i], in_sem.at[i, 1]))
    for load in loads:
        load.start()
    assemble_a(me, buf_ref, wqkv_ref, wd_ref)
    read_vectors(me, buf_ref, vec_ref, qb_ref, ub_ref)
    weights = [
        pltpu.make_async_copy(wqkv_ref, wqkv_out, weight_sem.at[0]),
        pltpu.make_async_copy(wd_ref, wd_out, weight_sem.at[1]),
    ]
    for copy in weights:
        copy.start()
    stores = ((min_ref, min_out), (gb_ref, gb_out), (ctx_ref, ctx_out), (dqkv_ref, dqkv_out))

    def store(n, r):
        rows = pl.ds(pl.multiple_of(r * ROW, ROW), ROW)
        src, dst = stores[n]
        return pltpu.make_async_copy(src.at[rows, :], dst.at[rows, :], out_sem.at[n, r])

    sums_ref[...] = jnp.zeros_like(sums_ref)

    @pl.loop(0, TP)
    def _(r):
        pltpu.make_async_copy(x0, x_ref.at[r], in_sem.at[r, 0]).wait()
        pltpu.make_async_copy(c0, cot_ref.at[r], in_sem.at[r, 1]).wait()
        here = pl.ds(pl.multiple_of(r * ROW, ROW), ROW)
        xhat, _ = normalize(x_ref[r].astype(f32))
        attn_in = (xhat * vec_ref[0:1] + vec_ref[1:2]).astype(bf16)
        ain_ref[here, :] = attn_in
        min_ref[here, :] = (xhat * vec_ref[2:3] + vec_ref[3:4]).astype(bf16)
        qkv = dot(attn_in, wqkv_ref[...]) + qb_ref[...]
        d = me ^ ((r & 1) * 2 + r // 2)
        base = (d * 2 + info_ref[65]) * SEGS
        ends, end = [], 0
        for j in range(SEGS - 1):
            end = end + info_ref[base + j]
            ends.append(end)
        rows = lax.broadcasted_iota(jnp.int32, (ROW, 1), 0)
        cols = lax.broadcasted_iota(jnp.int32, (1, ROW), 1)
        row_doc = sum([(rows >= e).astype(jnp.int32) for e in ends])
        col_doc = sum([(cols >= e).astype(jnp.int32) for e in ends])
        allowed = (row_doc == col_doc) & (cols <= rows)
        start = jnp.zeros_like(rows)
        for e in ends:
            start = jnp.maximum(start, jnp.where(rows >= e, e, 0))
        kept = jnp.where(rows < ends[-1], cot_ref[r].astype(f32), 0.0)
        gb = kept.astype(bf16)
        gb_ref[here, :] = gb
        dctx = dot_nt(gb, wd_ref[...]).astype(bf16)
        chosen = ((rows - start) == cols).astype(f32).astype(bf16)
        table = dot(chosen, rot_ref[...])
        pair = lambda n: table[:, n * 256 : n * 256 + 128] + table[:, n * 256 + 128 : n * 256 + 256]
        cosine, left, right = [jnp.concatenate([pair(n)] * 2, axis=1) for n in range(3)]
        q = turn(qkv[:, 0:256], cosine, left, right).astype(bf16)
        k = turn(qkv[:, 256:512], cosine, left, right).astype(bf16)
        v = qkv[:, 512:768].astype(bf16)
        scale = HEAD_DIM**-0.5
        ctx, dq, dk, dv = [], [], [], []
        for h in range(LOCAL_HEADS):
            at = slice(h * HEAD_DIM, (h + 1) * HEAD_DIM)
            qh, kh, vh, dch = q[:, at], k[:, at], v[:, at], dctx[:, at]
            scores = jnp.where(allowed, dot_nt(qh, kh) * scale, -1000000000.0)
            shifted = jnp.exp(scores - jnp.max(scores, axis=-1, keepdims=True))
            probs = shifted * (1.0 / jnp.sum(shifted, axis=-1, keepdims=True))
            low = probs.astype(bf16)
            ctx.append(dot(low, vh))
            dv.append(dot_tn(low, dch))
            dprobs = dot_nt(dch, vh)
            inner = jnp.sum(dprobs * probs, axis=-1, keepdims=True)
            ds = (probs * (dprobs - inner)).astype(bf16)
            dq.append(dot(ds, kh) * scale)
            dk.append(dot_tn(ds, qh) * scale)
        ctx_ref[here, :] = jnp.concatenate(ctx, axis=1).astype(bf16)
        dqs = turn(jnp.concatenate(dq, axis=1), cosine, -left, -right)
        dks = turn(jnp.concatenate(dk, axis=1), cosine, -left, -right)
        dqkv = jnp.concatenate([dqs, dks] + dv, axis=1).astype(bf16)
        dqkv_ref[here, :] = dqkv

        @pl.when(r == 0)
        def _():
            sums_ref[0:1, :] = jnp.sum(kept, axis=0, keepdims=True)

        sums_ref[1:2, 0:QC] += jnp.sum(dqkv.astype(f32), axis=0, keepdims=True)
        for n in range(4):
            store(n, r).start()

    c = me % 2

    def sent(d, n):
        rows = pl.ds(pl.multiple_of(d * 48, 16), 48)
        if n == 1:
            rows = pl.ds(pl.multiple_of(192 + d * 16, 16), 16)
        return pltpu.make_async_copy(
            sent_ref.at[:, :, rows, :], sent_out.at[:, :, rows, :], sent_sem.at[d, n]
        )

    @pl.loop(0, 4)
    def _(d):
        qkv_grad = dot_tn(ain_ref[:, tile(d)], dqkv_ref[...]).astype(bf16)
        dense_grad = dot_tn(ctx_ref[...], gb_ref[:, tile(d)]).astype(bf16)
        base = pl.multiple_of(d * 48, 16)
        dense_base = pl.multiple_of(192 + d * 16, 16)
        for y in range(4):
            for x in range(4):
                b, a = swapped(y, x, c)
                at = slice((y * 4 + x) * 16, (y * 4 + x + 1) * 16)
                for p in range(3):
                    sent_ref[b, a, pl.ds(base + p * 16, 16), :] = qkv_grad[
                        at, p * 256 : (p + 1) * 256
                    ]
                sent_ref[b, a, pl.ds(dense_base, 16), :] = dense_grad[at]
        sent(d, 0).start()
        sent(d, 1).start()

    for copy in weights:
        copy.wait()

    @pl.loop(0, 4)
    def _(i):
        for n in range(4):
            store(n, i).wait()
        sent(i, 0).wait()
        sent(i, 1).wait()


def attention(info, xs, cots, buf):
    tokens = TP * ROW
    dma = pltpu.SemaphoreType.DMA
    return call(
        attention_kernel,
        [
            shaped(4, 4, 256, 256),
            shaped(tokens, D),
            shaped(tokens, D),
            shaped(tokens, 256),
            shaped(tokens, QC),
            shaped(D, QC),
            shaped(D // TP, D),
            shaped(8, D, dtype=f32),
            shaped(1, HC, dtype=f32),
            shaped(8, D, dtype=f32),
        ],
        info,
        *xs,
        *cots,
        buf,
        jnp.asarray(rotary_tables()),
        places="s" + "h" * 8 + "vv",
        outs="hhhhhhhvvv",
        scratch=[
            pltpu.VMEM((TP, ROW, D), bf16),
            pltpu.VMEM((TP, ROW, D), bf16),
            pltpu.VMEM((D, QC), bf16),
            pltpu.VMEM((D // TP, D), bf16),
            pltpu.VMEM((1, QC), f32),
            pltpu.VMEM((tokens, D), bf16),
            pltpu.VMEM((tokens, D), bf16),
            pltpu.VMEM((tokens, D), bf16),
            pltpu.VMEM((tokens, 256), bf16),
            pltpu.VMEM((tokens, QC), bf16),
            pltpu.VMEM((4, 4, 256, 256), bf16),
            dma((4, 2)),
            dma((4, 4)),
            dma((2,)),
            dma((4, 2)),
        ],
        flops=6e9,
        nbytes=2e7,
        trans=1e6,
    )


def mlp_kernel(
    me_ref,
    buf_in,
    min_in,
    gb_in,
    ub_ref,
    sent_out,
    hidden_out,
    dpre_out,
    wup_out,
    wdown_out,
    sums_ref,
    buf_ref,
    min_ref,
    gb_ref,
    wup_ref,
    wdown_ref,
    hidden_ref,
    dpre_ref,
    sent_ref,
    buf_sem,
    in_sem,
    out_sem,
    weight_sem,
    sent_sem,
):
    me = me_ref[0]
    c = me % 2
    parts = [pltpu.make_async_copy(buf_in.at[b], buf_ref.at[b], buf_sem.at[b]) for b in range(4)]

    def load(t, n):
        src, dst = ((min_in, min_ref), (gb_in, gb_ref))[n]
        return pltpu.make_async_copy(src.at[tile(t), :], dst.at[tile(t), :], in_sem.at[t, n])

    for part in parts:
        part.start()
    for t in range(4):
        for n in range(2):
            load(t, n).start()
    for part in parts:
        part.wait()
    assemble_b(me, buf_ref, wup_ref, wdown_ref)
    weights = [
        pltpu.make_async_copy(wup_ref, wup_out, weight_sem.at[0]),
        pltpu.make_async_copy(wdown_ref, wdown_out, weight_sem.at[1]),
    ]
    for copy in weights:
        copy.start()
    sums_ref[...] = jnp.zeros_like(sums_ref)

    def store(j, n):
        src, dst = ((hidden_ref, hidden_out), (dpre_ref, dpre_out))[n]
        return pltpu.make_async_copy(src.at[:, tile(j)], dst.at[:, tile(j)], out_sem.at[j, n])

    @pl.loop(0, 16)
    def _(i):
        jn, tn = i // 4, i % 4
        j, t = tile(jn), tile(tn)

        @pl.when(i < 4)
        def _():
            load(tn, 0).wait()
            load(tn, 1).wait()

        pre = dot(min_ref[t, :], wup_ref[:, j]) + ub_ref[:, j]
        back = dot_nt(gb_ref[t, :], wdown_ref[j, :])
        size = jnp.abs(pre) * 0.7071067811865476
        bell = jnp.exp(-0.5 * pre * pre)
        s = 1.0 / (1.0 + 0.3275911 * size)
        poly = s * (
            0.127414796
            + s * (-0.142248368 + s * (0.7107068705 + s * (-0.7265760135 + s * 0.5307027145)))
        )
        tail = poly * bell
        cumul = jnp.where(pre >= 0.0, 1.0 - tail, tail)
        hidden_ref[t, j] = (pre * cumul).astype(bf16)
        dpre = (back * (cumul + pre * (bell * 0.3989422804014327))).astype(bf16)
        dpre_ref[t, j] = dpre
        sums_ref[0:1, j] += jnp.sum(dpre.astype(f32), axis=0, keepdims=True)

        @pl.when(tn == 3)
        def _():
            store(jn, 0).start()
            store(jn, 1).start()

    @pl.loop(0, 4)
    def _(y):
        grad = dot_tn(hidden_ref[:, tile(y)], gb_ref[...]).astype(bf16)
        for x in range(4):
            b, a = swapped(y, x, c)
            for cg in range(4):
                sent_ref[b, a, 256 + cg * 64 : 256 + (cg + 1) * 64, :] = grad[
                    x * 64 : (x + 1) * 64, cg * 256 : (cg + 1) * 256
                ]

    def sent(rows, n):
        return pltpu.make_async_copy(
            sent_ref.at[:, :, rows, :], sent_out.at[:, :, rows, :], sent_sem.at[n]
        )

    below = sent(pl.ds(256, 256), 4)
    below.start()

    def above(d):
        return sent(pl.ds(pl.multiple_of(d * 64, 64), 64), d)

    @pl.loop(0, 4)
    def _(d):
        grad = dot_tn(min_ref[:, tile(d)], dpre_ref[...]).astype(bf16)
        for y in range(4):
            for x in range(4):
                b, a = swapped(y, x, c)
                at = slice((y * 4 + x) * 16, (y * 4 + x + 1) * 16)
                for cg in range(4):
                    row = pl.multiple_of(d * 64 + cg * 16, 16)
                    sent_ref[b, a, pl.ds(row, 16), :] = grad[at, cg * 256 : (cg + 1) * 256]
        above(d).start()

    for copy in weights:
        copy.wait()

    @pl.loop(0, 4)
    def _(i):
        store(i, 0).wait()
        store(i, 1).wait()
        above(i).wait()

    below.wait()


def mlp(me, buf, mlp_in, gb, ub):
    tokens = TP * ROW
    dma = pltpu.SemaphoreType.DMA
    return call(
        mlp_kernel,
        [
            shaped(4, 4, 512, 256),
            shaped(tokens, HC),
            shaped(tokens, HC),
            shaped(D, HC),
            shaped(HC, D),
            shaped(8, HC, dtype=f32),
        ],
        me,
        buf,
        mlp_in,
        gb,
        ub,
        places="shhhv",
        outs="hhhhhv",
        scratch=[
            pltpu.VMEM((4, 2048, 256), bf16),
            pltpu.VMEM((tokens, D), bf16),
            pltpu.VMEM((tokens, D), bf16),
            pltpu.VMEM((D, HC), bf16),
            pltpu.VMEM((HC, D), bf16),
            pltpu.VMEM((tokens, HC), bf16),
            pltpu.VMEM((tokens, HC), bf16),
            pltpu.VMEM((4, 4, 512, 256), bf16),
            dma((4,)),
            dma((4, 2)),
            dma((4, 2)),
            dma((2,)),
            dma((5,)),
        ],
        flops=1.3e10,
        nbytes=2e7,
        trans=2e6,
    )


def outputs_kernel(
    me_ref,
    x0,
    x1,
    x2,
    x3,
    ctx_in,
    hidden_in,
    dqkv_in,
    dpre_in,
    wd_in,
    wdown_in,
    wqkv_in,
    wup_in,
    vec_ref,
    sums_a_ref,
    sums_b_ref,
    theirs_out,
    mine_out,
    image_ref,
    x_ref,
    ctx_ref,
    hidden_ref,
    dqkv_ref,
    dpre_ref,
    wd_ref,
    wdown_ref,
    wqkv_ref,
    wup_ref,
    both_ref,
    sums_ref,
    weight_sem,
    in_sem,
    out_sem,
):
    pairs = ((wqkv_in, wqkv_ref), (wup_in, wup_ref), (wdown_in, wdown_ref), (wd_in, wd_ref))
    weights = [
        pltpu.make_async_copy(src, dst, weight_sem.at[i]) for i, (src, dst) in enumerate(pairs)
    ]
    inputs = (
        (dqkv_in, dqkv_ref),
        (dpre_in, dpre_ref),
        (hidden_in, hidden_ref),
        (ctx_in, ctx_ref),
    )

    def load(t, n):
        src, dst = inputs[n]
        return pltpu.make_async_copy(src.at[tile(t), :], dst.at[tile(t), :], in_sem.at[t, n])

    rows = [
        pltpu.make_async_copy(src, x_ref.at[i], in_sem.at[i, 4])
        for i, src in enumerate((x0, x1, x2, x3))
    ]
    order = (2, 3, 0, 1)
    for n in range(4):
        load(order[0], n).start()
        weights[n].start()
    rows[order[0]].start()
    for t in order[1:]:
        for n in range(4):
            load(t, n).start()
        rows[t].start()
    sums_ref[...] = jnp.zeros_like(sums_ref)

    def store(i):
        return pltpu.make_async_copy(both_ref.at[i], theirs_out.at[i], out_sem.at[i])

    def store_mine(i):
        return pltpu.make_async_copy(both_ref.at[i + 2], mine_out.at[i], out_sem.at[i + 2])

    for weight in weights:
        weight.wait()

    @pl.loop(0, TP)
    def _(i):
        t = (i + 2) % 4
        pltpu.make_async_copy(x0, x_ref.at[t], in_sem.at[t, 4]).wait()
        for n in range(4):
            load(t, n).wait()
        here = tile(t)
        dattn = dot_nt(dqkv_ref[here, :], wqkv_ref[...])
        dmlp = dot_nt(dpre_ref[here, :], wup_ref[...])
        xhat, _ = normalize(x_ref[t].astype(f32))
        sums_ref[0:1, :] += jnp.sum(dattn * xhat, axis=0, keepdims=True)
        sums_ref[1:2, :] += jnp.sum(dattn, axis=0, keepdims=True)
        sums_ref[2:3, :] += jnp.sum(dmlp * xhat, axis=0, keepdims=True)
        sums_ref[3:4, :] += jnp.sum(dmlp, axis=0, keepdims=True)
        both_ref[i, 1] = (dattn * vec_ref[0:1] + dmlp * vec_ref[2:3]).astype(bf16)
        forward = dot(ctx_ref[here, :], wd_ref[...]) + dot(hidden_ref[here, :], wdown_ref[...])
        both_ref[i, 0] = forward.astype(bf16)

        @pl.when(i < 2)
        def _():
            store(i).start()

        @pl.when(i >= 2)
        def _():
            store_mine(i - 2).start()

    me = me_ref[0]
    image_ref[...] = jnp.zeros_like(image_ref)

    def put(row, ref, line, count):
        for i in range(count):
            image_ref[pl.ds(row + i, 1), :] = ref[line : line + 1, i * 256 : (i + 1) * 256]

    for i in range(4):
        put(4 * i, sums_ref, i, 4)
    for p in range(3):
        image_ref[pl.ds(16 + p * 4 + me, 1), :] = sums_a_ref[1:2, p * 256 : (p + 1) * 256]
    put(28, sums_a_ref, 0, 4)
    put(32 + 4 * me, sums_b_ref, 0, 4)
    put(48, sums_a_ref, 0, 4)
    for i in range(2):
        store(i).wait()
        store_mine(i).wait()


def outputs(me, xs, ctx, hidden, dqkv, dpre, wd, wdown, wqkv, wup, vec, sums_a, sums_b):
    tokens = TP * ROW
    dma = pltpu.SemaphoreType.DMA
    half = shaped(2, 2, ROW, D)
    return call(
        outputs_kernel,
        [half, half, shaped(IMAGE, 256, dtype=f32)],
        me,
        *xs,
        ctx,
        hidden,
        dqkv,
        dpre,
        wd,
        wdown,
        wqkv,
        wup,
        vec,
        sums_a,
        sums_b,
        places="s" + "h" * 12 + "vvv",
        outs="hhv",
        scratch=[
            pltpu.VMEM((TP, ROW, D), bf16),
            pltpu.VMEM((tokens, 256), bf16),
            pltpu.VMEM((tokens, HC), bf16),
            pltpu.VMEM((tokens, QC), bf16),
            pltpu.VMEM((tokens, HC), bf16),
            pltpu.VMEM((D // TP, D), bf16),
            pltpu.VMEM((HC, D), bf16),
            pltpu.VMEM((D, QC), bf16),
            pltpu.VMEM((D, HC), bf16),
            pltpu.VMEM((TP, 2, ROW, D), bf16),
            pltpu.VMEM((8, D), f32),
            dma((4,)),
            dma((4, 5)),
            dma((4,)),
        ],
        flops=6.5e9,
        nbytes=2e7,
    )


def half_kernel(mine0_ref, got0_ref, mine1_ref, got1_ref, kept_ref, send_ref):
    kept_ref[...] = mine0_ref[0].astype(f32) + got0_ref[0].astype(f32)
    send_ref[...] = (mine1_ref[0].astype(f32) + got1_ref[0].astype(f32)).astype(bf16)


def half_sum(mine, got):
    mine, got = in_hbm(mine), in_hbm(got)
    first = pl.BlockSpec((1, 1, ROW, D // 2), lambda i, k: (0, i, 0, k))
    second = pl.BlockSpec((1, 1, ROW, D // 2), lambda i, k: (1, i, 0, k))
    out = pl.BlockSpec((1, ROW, D // 2), lambda i, k: (i, 0, k))
    return pl.pallas_call(
        half_kernel,
        grid=(2, 2),
        in_specs=[first, first, second, second],
        out_specs=[out, out],
        out_shape=[pltpu.HBM((2, ROW, D), f32), pltpu.HBM((2, ROW, D), bf16)],
        compiler_params=pltpu.CompilerParams(vmem_limit_bytes=VMEM),
        cost_estimate=pl.CostEstimate(flops=0, bytes_accessed=8000000, transcendentals=0),
    )(mine, got, mine, got)


def close_kernel(len_ref, x_ref, cot_ref, kept_ref, got_ref, vec_ref, out_ref, grad_ref):
    x = x_ref[...].astype(f32)
    out_ref[...] = (x + kept_ref[0] + got_ref[0].astype(f32) + vec_ref[4:5]).astype(bf16)
    e = kept_ref[1] + got_ref[1].astype(f32)
    xhat, inv_std = normalize(x)
    mean_e = jnp.mean(e, axis=-1, keepdims=True)
    mean_ex = jnp.mean(e * xhat, axis=-1, keepdims=True)
    used = sum([len_ref[0, j] for j in range(SEGS - 1)])
    rows = lax.broadcasted_iota(jnp.int32, (ROW, 1), 0)
    kept = jnp.where(rows < used, cot_ref[...].astype(f32), 0.0)
    grad_ref[...] = kept + inv_std * (e - mean_e - xhat * mean_ex)


def close(lengths, x, cot, kept, got, vec):
    return call(
        close_kernel,
        [shaped(ROW, D), shaped(ROW, D, dtype=f32)],
        lengths,
        x,
        cot,
        kept,
        got,
        vec,
        nbytes=6e6,
    )


def add_kernel(a_ref, b_ref, image_ref, out_ref):
    total = sum([a_ref[i, 0].astype(f32) for i in range(4)])
    out_ref[0, 0:256, :] = total.astype(bf16)
    total = sum([b_ref[i, 0].astype(f32) for i in range(4)])
    out_ref[0, 256:768, :] = total.astype(bf16)
    image = image_ref[...]
    high = image.astype(bf16)
    out_ref[0, 768 : 768 + IMAGE, :] = high
    out_ref[0, 768 + IMAGE : 768 + 2 * IMAGE, :] = (image - high.astype(f32)).astype(bf16)


def add(sent_a, sent_b, image):
    rows = 768 + 2 * IMAGE
    return pl.pallas_call(
        add_kernel,
        grid=(4,),
        in_specs=[
            pl.BlockSpec((4, 1, 256, 256), lambda a: (0, a, 0, 0)),
            pl.BlockSpec((4, 1, 512, 256), lambda a: (0, a, 0, 0)),
            pl.BlockSpec((IMAGE, 256), lambda a: (0, 0)),
        ],
        out_specs=pl.BlockSpec((1, rows, 256), lambda a: (a, 0, 0)),
        out_shape=pltpu.HBM((4, rows, 256), bf16),
        compiler_params=pltpu.CompilerParams(vmem_limit_bytes=VMEM),
        cost_estimate=pl.CostEstimate(flops=0, bytes_accessed=8000000, transcendentals=0),
    )(in_hbm(sent_a), in_hbm(sent_b), image)


def part_kernel(far_ref, in_ref, slots_ref, keep_ref, send_ref, total_ref):
    far = far_ref[0]
    total_ref[...] = sum([in_ref[i].astype(f32) for i in range(4)])
    image = total_ref[768 : 768 + IMAGE, :] + total_ref[768 + IMAGE : 768 + 2 * IMAGE, :]
    for d in range(4):
        for zh in range(2):
            s = d * 2 + zh
            for p in range(3):
                row = (d * 3 + p) * 16 + zh * 8
                slots_ref[s, p * 8 : p * 8 + 8, :] = total_ref[row : row + 8, :]
            for cg in range(4):
                row = 256 + (d * 4 + cg) * 16 + zh * 8
                slots_ref[s, 24 + cg * 8 : 32 + cg * 8, :] = total_ref[row : row + 8, :]
            slots_ref[s, 56 : 56 + IMAGE, :] = image
    for ref, half in ((keep_ref, far), (send_ref, 1 - far)):
        for cg in range(4):
            row = pl.multiple_of(192 + cg * 16 + half * 8, 8)
            ref[cg * 8 : cg * 8 + 8, :] = total_ref[pl.ds(row, 8), :]
            row = pl.multiple_of(512 + cg * 64 + half * 32, 8)
            ref[32 + cg * 32 : 64 + cg * 32, :] = total_ref[pl.ds(row, 32), :]


def part(far, received):
    return call(
        part_kernel,
        [shaped(8, 56 + IMAGE, 256, dtype=f32), shaped(160, 256, dtype=f32), shaped(160, 256, dtype=f32)],
        far,
        received,
        scratch=[pltpu.VMEM((768 + 2 * IMAGE, 256), f32)],
        nbytes=4e6,
    )


def finish_kernel(place_ref, slots_ref, keep_ref, got_ref, qkv_ref, up_ref, dense_ref, down_ref, *rest):
    tiny_refs, image_ref = rest[:8], rest[8]
    image_ref[...] = sum([slots_ref[s, 56 : 56 + IMAGE, :] for s in range(8)])
    for d in range(4):
        for p in range(3):
            at = p * D + d * 256
            rows = slice(p * 8, p * 8 + 8)
            qkv_ref[:, at : at + 256] = slots_ref[2 * d, rows, :] + slots_ref[2 * d + 1, rows, :]
        for cg in range(4):
            at = d * HC + cg * 256
            rows = slice(24 + cg * 8, 32 + cg * 8)
            up_ref[:, at : at + 256] = slots_ref[2 * d, rows, :] + slots_ref[2 * d + 1, rows, :]
    for cg in range(4):
        at = slice(cg * 256, (cg + 1) * 256)
        rows = slice(cg * 8, cg * 8 + 8)
        dense_ref[:, at] = keep_ref[rows, :] + got_ref[rows, :]
        rows = slice(32 + cg * 32, 64 + cg * 32)
        down_ref[:, at] = keep_ref[rows, :] + got_ref[rows, :]
    p = place_ref[0]
    for start, size, ref in zip(STARTS, SIZES, tiny_refs):
        first = p * size
        row, lane = start + first // 256, first % 256
        values = image_ref[pl.ds(row, 1), :]
        if size == 24:
            values = jnp.concatenate([values, image_ref[pl.ds(row + 1, 1), :]], axis=1)
        ref[...] = pltpu.roll(values, values.shape[1] - lane, 1)[:, :size]


def finish(place, slots, keep, got):
    return call(
        finish_kernel,
        [
            shaped(8, 3 * D, dtype=f32),
            shaped(8, FF, dtype=f32),
            shaped(8, D, dtype=f32),
            shaped(32, D, dtype=f32),
        ]
        + [shaped(1, size, dtype=f32) for size in SIZES],
        place,
        slots,
        keep,
        got,
        scratch=[pltpu.VMEM((IMAGE, 256), f32)],
        nbytes=2e6,
    )


def body(
    inputs,
    cotangent,
    lengths,
    norm1_gain,
    norm1_bias,
    norm2_gain,
    norm2_bias,
    qkv_weight,
    qkv_bias,
    dense_weight,
    dense_bias,
    up_weight,
    up_bias,
    down_weight,
    down_bias,
):
    me = lax.axis_index("dp").astype(jnp.int32)
    index = lax.axis_index("fsdp").astype(jnp.int32)
    half = index % 2
    far = half[None]
    me1 = me[None]
    place = jnp.stack([me * 32 + index, me * 2 + half])
    outer, inner = outer_groups(), inner_groups()

    vectors = (
        norm1_gain,
        norm1_bias,
        norm2_gain,
        norm2_bias,
        qkv_bias,
        dense_bias,
        up_bias,
        down_bias,
    )
    slots, pieces = prepare(
        place,
        qkv_weight.reshape(8, 3 * D),
        up_weight.reshape(8, FF),
        dense_weight.reshape(8, D),
        down_weight.reshape(32, D),
        lengths,
        vectors,
    )
    far_pieces = flip_far(pieces)
    first = a2a(slots, stack_groups())
    block, lens = spread(far, first.reshape(4, 16, SLOT), pieces, far_pieces)
    info = jnp.concatenate([lens[0, :64], me1, far])

    block, x0, c0 = lax.optimization_barrier((block, inputs, cotangent))
    x1, c1 = flip_chip(x0), flip_chip(c0)
    second = a2a(block, inner)
    second, x1, c1 = lax.optimization_barrier((second, x1, c1))
    x2, x3 = flip_core(x0), flip_core(x1)
    c2, c3 = flip_core(c0), flip_core(c1)
    xs, cots = (x0, x1, x2, x3), (c0, c1, c2, c3)
    wide_a, wide_b = widen(second)
    third_a = a2a(wide_a, outer)
    third_b = a2a(wide_b, outer)

    sent_a, mlp_in, gb, ctx, dqkv, wqkv, wd, vec, up_b, sums_a = attention(info, xs, cots, third_a)
    sent_a = a2a(sent_a, outer)
    sent_b, hidden, dpre, wup, wdown, sums_b = mlp(me1, third_b, mlp_in, gb, up_b)
    sent_b = a2a(sent_b, outer)
    theirs, mine, image = outputs(
        me1, xs, ctx, hidden, dqkv, dpre, wd, wdown, wqkv, wup, vec, sums_a, sums_b
    )

    kept, send = half_sum(mine, flip_core(theirs))
    other = flip_chip(send)

    image = image + outer_flip(image, 1)
    image = image + outer_flip(image, 2)
    fourth = a2a(add(sent_a, sent_b, image), inner)
    slots, keep, send = part(far, fourth)
    block_output, input_grad = close(lengths, inputs, cotangent, kept, other, vec)
    results = finish(place, a2a(slots, stack_groups()), keep, flip_far(send))
    flat = [r.reshape(-1) for r in results]
    return (
        block_output,
        input_grad,
        flat[4],
        flat[5],
        flat[6],
        flat[7],
        flat[0],
        flat[8],
        flat[2],
        flat[9],
        flat[1],
        flat[10],
        flat[3],
        flat[11],
    )


def solution(mesh):
    flat = P(("dp", "fsdp"))
    rows = P(("dp", "fsdp"), None)
    return jax.shard_map(
        body,
        mesh=mesh,
        in_specs=(rows,) * 3 + (flat,) * 12,
        out_specs=(rows,) * 2 + (flat,) * 12,
        check_vma=False,
    )
```

```python
import jax
import jax.numpy as jnp
import ml_dtypes
import numpy as np
from jax import lax
from jax.experimental import pallas as pl
from jax.experimental.pallas import tpu as pltpu
from jax.sharding import PartitionSpec as P

D = 1024
HEADS = 16
HEAD_DIM = 64
ROT = 16
FF = 4096
ROW = 256
SEGS = 8
TP = 4
QC = 3 * D // TP
HC = FF // TP
LOCAL_HEADS = HEADS // TP
AXES = ("dp", "fsdp")
VMEM = 44 * 1024 * 1024

f32 = jnp.float32
bf16 = jnp.bfloat16


def dev(d, y, x, zh):
    return d * 32 + y * 8 + x * 2 + zh


def outer_groups(flip=0):
    groups = []
    for d in range(4):
        for k in range(4):
            for zh in range(2):
                if d % 2 == flip:
                    groups.append([dev(d, i, k, zh) for i in range(4)])
                else:
                    groups.append([dev(d, k, i, zh) for i in range(4)])
    return groups


def inner_groups():
    return outer_groups(flip=1)


def stack_groups():
    return [
        [dev(d, y, x, zh) for d in range(4) for zh in range(2)] for y in range(4) for x in range(4)
    ]


def plane_groups():
    return [
        [dev(d, y, x, zh) for y in range(4) for x in range(4)] for d in range(4) for zh in range(2)
    ]


def a2a(values, groups):
    return lax.all_to_all(values, AXES, 0, 0, tiled=True, axis_index_groups=groups)


def flip_core(values):
    return lax.ppermute(values, "dp", [(0, 1), (1, 0), (2, 3), (3, 2)])


def flip_chip(values):
    return lax.ppermute(values, "dp", [(0, 2), (2, 0), (1, 3), (3, 1)])


def flip_far(values):
    return lax.ppermute(values, "fsdp", [(i, i ^ 1) for i in range(32)])


def dot(left, right):
    return jnp.dot(left, right, preferred_element_type=f32)


def dot_nt(left, right):
    return lax.dot_general(left, right, (((1,), (1,)), ((), ())), preferred_element_type=f32)


def dot_tn(left, right):
    return lax.dot_general(left, right, (((0,), (0,)), ((), ())), preferred_element_type=f32)


def in_hbm(values):
    return pltpu.with_memory_space_constraint(values, pltpu.HBM)


VMEM_SPEC = pl.BlockSpec(memory_space=pltpu.VMEM)
SMEM_SPEC = pl.BlockSpec(memory_space=pltpu.SMEM)
HBM_SPEC = pl.BlockSpec(memory_space=pltpu.HBM)
SPECS = {"s": SMEM_SPEC, "v": VMEM_SPEC, "u": VMEM_SPEC, "h": HBM_SPEC}


def call(kernel, out_shape, *args, places=None, outs=None, scratch=(), flops=0, nbytes=0, trans=0):
    places = places or "s" + "v" * (len(args) - 1)
    out_specs = jax.tree.map(lambda _: VMEM_SPEC, out_shape)
    if outs is not None:
        out_specs = [SPECS[o] for o in outs]
        out_shape = [
            v if o == "v" else pltpu.HBM(v.shape, v.dtype) for o, v in zip(outs, out_shape)
        ]
    args = [in_hbm(v) if p == "h" else v for p, v in zip(places, args)]
    return pl.pallas_call(
        kernel,
        in_specs=[SPECS[p] for p in places],
        out_specs=out_specs,
        out_shape=out_shape,
        scratch_shapes=list(scratch),
        compiler_params=pltpu.CompilerParams(vmem_limit_bytes=VMEM),
        cost_estimate=pl.CostEstimate(
            flops=int(flops), bytes_accessed=int(nbytes), transcendentals=int(trans)
        ),
    )(*args)


def shaped(*shape, dtype=bf16):
    return jax.ShapeDtypeStruct(shape, dtype)


def normalize(x):
    average = jnp.mean(x, axis=-1, keepdims=True)
    centred = x - average
    inv_std = lax.rsqrt(jnp.mean(centred * centred, axis=-1, keepdims=True) + 1e-05)
    return centred * inv_std, inv_std


STARTS = (0, 4, 8, 12, 16, 28, 32, 48)
SIZES = (8, 8, 8, 8, 24, 8, 32, 8)
IMAGE = 64
LENS = 64
SLOT = QC + HC + 128


def tile(n):
    return pl.ds(pl.multiple_of(n * 256, 256), 256)


def swapped(y, x, c):
    return y + c * (x - y), x + c * (y - x)


def prepare_kernel(
    qkv_ref, up_ref, dense_in, down_in, len_in, n1g, n1b, n2g, n2b, qb, db, ub, dnb,
    out_ref, pieces_ref, tile_ref, *rest
):
    sources = (len_in, n1g, n1b, n2g, n2b, qb, db, ub, dnb)
    holders, sem = rest[:9], rest[9]
    copies = [
        pltpu.make_async_copy(src, dst, sem.at[i])
        for i, (src, dst) in enumerate(zip(sources, holders))
    ]
    for copy in copies:
        copy.start()
    for d in range(4):
        for zh in range(2):
            s = d * 2 + zh
            for p in range(3):
                at = p * D + d * 256
                out_ref[s, :, p * 256 : (p + 1) * 256] = qkv_ref[:, at : at + 256]
            out_ref[s, :, QC : QC + HC] = up_ref[:, d * HC : (d + 1) * HC]
    pieces_ref[0:32, :] = down_in[...]
    pieces_ref[32:40, :] = dense_in[...]
    tile_ref[...] = jnp.zeros_like(tile_ref)
    for copy in copies:
        copy.wait()
    for i, (size, ref) in enumerate(zip(SIZES, holders[1:])):
        tile_ref[i : i + 1, 0:size] = ref[...].astype(f32)
    tile_ref[0:1, LENS : LENS + SEGS] = holders[0][...].astype(f32)
    block = tile_ref[...].astype(bf16)
    for s in range(8):
        out_ref[s, :, QC + HC : SLOT] = block


def prepare(qkv, up, dense, down, lengths, vectors):
    vectors = [v[None, :] for v in vectors]
    return call(
        prepare_kernel,
        [shaped(8, 8, SLOT), shaped(40, D)],
        qkv,
        up,
        dense,
        down,
        lengths,
        *vectors,
        places="vvvv" + "h" * 9,
        scratch=[pltpu.VMEM((8, 128), f32), pltpu.VMEM((1, SEGS), jnp.int32)]
        + [pltpu.VMEM(v.shape, bf16) for v in vectors]
        + [pltpu.SemaphoreType.DMA((9,))],
        nbytes=1e6,
    )


def locate(p, start, size):
    first = p * size
    return start + first // 256, first % 256


def spread_kernel(index_ref, first_ref, mine_ref, theirs_ref, out_ref, lens_ref, image_ref):
    index = index_ref[0]
    far = index % 2 == 1
    mine, theirs = mine_ref[...].astype(f32), theirs_ref[...].astype(f32)
    low, high = jnp.where(far, theirs, mine), jnp.where(far, mine, theirs)
    down = jnp.concatenate([low[:32], high[:32]], axis=0).astype(bf16)
    dense = jnp.concatenate([low[32:], high[32:]], axis=0).astype(bf16)
    image_ref[...] = jnp.zeros_like(image_ref)
    lens = []
    for d in range(4):
        both = first_ref[d, :, QC + HC : SLOT].astype(f32)
        for zh in range(2):
            p = d * 32 + index // 2 * 2 + zh
            tile = both[zh * 8 : zh * 8 + 8]
            lens.append(tile[0:1, LENS : LENS + SEGS])
            for i, (start, size) in enumerate(zip(STARTS, SIZES)):
                row, lane = locate(p, start, size)
                wide = 512 if size == 24 else 256
                blank = jnp.zeros((1, wide - size), f32)
                values = jnp.concatenate([tile[i : i + 1, :size], blank], axis=1)
                values = pltpu.roll(values, lane, 1)
                image_ref[pl.ds(row, 1), :] += values[:, :256]
                if wide == 512:
                    image_ref[pl.ds(row + 1, 1), :] += values[:, 256:]
    lens_ref[...] = jnp.concatenate(lens, axis=1).astype(jnp.int32)
    image = image_ref[...].astype(bf16)
    for i in range(4):
        for d in range(4):
            for p in range(3):
                row = (d * 3 + p) * 16
                out_ref[i, row : row + 16, :] = first_ref[d, :, p * 256 : (p + 1) * 256]
            for cg in range(4):
                row = 256 + (d * 4 + cg) * 16
                at = QC + cg * 256
                out_ref[i, row : row + 16, :] = first_ref[d, :, at : at + 256]
        for cg in range(4):
            at = slice(cg * 256, (cg + 1) * 256)
            out_ref[i, 192 + cg * 16 : 208 + cg * 16, :] = dense[:, at]
            out_ref[i, 512 + cg * 64 : 576 + cg * 64, :] = down[:, at]
        out_ref[i, 768 : 768 + IMAGE, :] = image


def spread(index, first, mine, theirs):
    return call(
        spread_kernel,
        [shaped(4, 768 + IMAGE, 256), shaped(1, 64, dtype=jnp.int32)],
        index,
        first,
        mine,
        theirs,
        scratch=[pltpu.VMEM((IMAGE, 256), f32)],
        nbytes=2e6,
    )


def widen_a_kernel(in_ref, out_ref):
    image = sum([in_ref[a, 768 : 768 + IMAGE, :].astype(f32) for a in range(4)]).astype(bf16)
    for i in range(4):
        for a in range(4):
            out_ref[i, a * 256 : (a + 1) * 256, :] = in_ref[a, 0:256, :]
        out_ref[i, 1024 : 1024 + IMAGE, :] = image


def widen_a(second):
    return call(
        widen_a_kernel, [shaped(4, 1024 + IMAGE, 256)], second, places="v", outs="u", nbytes=4e6
    )[0]


def widen_b_kernel(in_ref, out_ref):
    @pl.loop(0, 4)
    def _(i):
        for a in range(4):
            out_ref[i, a * 512 : (a + 1) * 512, :] = in_ref[a, 256:768, :]


def widen_b(second):
    return call(
        widen_b_kernel, [shaped(4, 2048, 256)], second, places="v", outs="u", nbytes=6e6
    )[0]


def assemble_a(me, buf_ref, wqkv_ref, wd_ref):
    c = me % 2
    for y in range(4):
        for x in range(4):
            b, a = swapped(y, x, c)
            yx = y * 4 + x
            base = a * 256
            for d in range(4):
                for p in range(3):
                    row = pl.multiple_of(base + (d * 3 + p) * 16, 16)
                    wqkv_ref[d * 256 + yx * 16 : d * 256 + yx * 16 + 16, p * 256 : (p + 1) * 256] = (
                        buf_ref[b, pl.ds(row, 16), :]
                    )
            for cg in range(4):
                row = pl.multiple_of(base + 192 + cg * 16, 16)
                wd_ref[yx * 16 : yx * 16 + 16, cg * 256 : (cg + 1) * 256] = buf_ref[
                    b, pl.ds(row, 16), :
                ]


def read_vectors(me, buf_ref, vec_ref, qb_ref, ub_ref):
    image = sum([buf_ref[b, 1024 : 1024 + IMAGE, :].astype(f32) for b in range(4)])

    def long(start):
        return jnp.concatenate([image[start + i : start + i + 1, :] for i in range(4)], axis=1)

    vec_ref[...] = jnp.zeros_like(vec_ref)
    for i in range(4):
        vec_ref[i : i + 1, :] = long(4 * i)
    vec_ref[4:5, :] = long(28) + long(48)
    own = [jnp.where(me == d, 1.0, 0.0) for d in range(4)]
    rows = [sum([image[16 + p * 4 + d : 17 + p * 4 + d] * own[d] for d in range(4)]) for p in range(3)]
    qb_ref[...] = jnp.concatenate(rows, axis=1)
    ub_ref[...] = sum([long(32 + 4 * d) * own[d] for d in range(4)])


def assemble_b(me, buf_ref, wup_ref, wdown_ref):
    c = me % 2
    for y in range(4):
        for x in range(4):
            b, a = swapped(y, x, c)
            yx = y * 4 + x
            base = a * 512
            for d in range(4):
                for cg in range(4):
                    row = pl.multiple_of(base + (d * 4 + cg) * 16, 16)
                    wup_ref[d * 256 + yx * 16 : d * 256 + yx * 16 + 16, cg * 256 : (cg + 1) * 256] = (
                        buf_ref[b, pl.ds(row, 16), :]
                    )
            for cg in range(4):
                row = pl.multiple_of(base + 256 + cg * 64, 16)
                wdown_ref[yx * 64 : yx * 64 + 64, cg * 256 : (cg + 1) * 256] = buf_ref[
                    b, pl.ds(row, 64), :
                ]


def turn(u, cosine, sin_left, sin_right):
    return (
        u * cosine
        + pltpu.roll(u, u.shape[1] - ROT // 2, 1) * sin_left
        + pltpu.roll(u, ROT // 2, 1) * sin_right
    )


def rotary_tables():
    places = np.arange(ROW, dtype=np.float32)
    freqs = (10000.0 ** (-(np.arange(ROT // 2, dtype=np.float32) * 2.0) / ROT)).astype(np.float32)
    angle = (places[:, None] * freqs[None, :]).astype(np.float32)
    cosine, sine = np.cos(angle), np.sin(angle)
    zeros = np.zeros_like(sine)
    rest = np.zeros((ROW, HEAD_DIM - ROT), np.float32)
    parts = [[cosine, cosine, rest + 1.0], [-sine, zeros, rest], [zeros, sine, rest]]
    columns = []
    for part in parts:
        whole = np.tile(np.concatenate(part, axis=1), (1, 2)).astype(np.float32)
        high = whole.astype(ml_dtypes.bfloat16)
        columns += [high, (whole - high.astype(np.float32)).astype(ml_dtypes.bfloat16)]
    return np.concatenate(columns, axis=1)


def row_sums(values):
    total = jnp.sum(values, axis=1, keepdims=True)
    return jnp.transpose(jnp.broadcast_to(total, (256, 128)))[0:1, :]


def through(sums, matrix):
    high = sums.astype(bf16)
    low = (sums - high.astype(f32)).astype(bf16)
    both = jnp.concatenate([high.astype(f32), low.astype(f32)] + [jnp.zeros_like(sums)] * 6, axis=0)
    out = dot_nt(both.astype(bf16), matrix)
    return out[0:1] + out[1:2]


def attention_kernel(
    info_ref,
    x0,
    x1,
    x2,
    x3,
    c0,
    c1,
    c2,
    c3,
    buf_ref,
    rot_ref,
    sent_out,
    min_out,
    gb_out,
    ctx_out,
    dqkv_out,
    wd_out,
    wqkv_out,
    xhat_out,
    vec_ref,
    ub_ref,
    sums_ref,
    x_ref,
    cot_ref,
    wqkv_ref,
    wd_ref,
    qb_ref,
    min_ref,
    gb_ref,
    ctx_ref,
    dqkv_ref,
    xhat_ref,
    sent_ref,
    in_sem,
    out_sem,
    weight_sem,
    sent_sem,
    vec_col_ref,
):
    me = info_ref[64]
    loads = []
    for i, (one, other) in enumerate(zip((x0, x1, x2, x3), (c0, c1, c2, c3))):
        loads.append(pltpu.make_async_copy(one, x_ref.at[i], in_sem.at[i, 0]))
        loads.append(pltpu.make_async_copy(other, cot_ref.at[i], in_sem.at[i, 1]))
    for load in loads[:2]:
        load.start()
    assemble_a(me, buf_ref, wqkv_ref, wd_ref)
    for load in loads[2:]:
        load.start()
    read_vectors(me, buf_ref, vec_ref, qb_ref, ub_ref)
    weights = [
        pltpu.make_async_copy(wd_ref, wd_out, weight_sem.at[0]),
        pltpu.make_async_copy(wqkv_ref, wqkv_out, weight_sem.at[1]),
    ]
    for copy in weights:
        copy.start()
    stores = (
        (min_ref, min_out),
        (gb_ref, gb_out),
        (ctx_ref, ctx_out),
        (xhat_ref, xhat_out),
        (dqkv_ref, dqkv_out),
    )

    def store(n, r):
        rows = pl.ds(pl.multiple_of(r * ROW, ROW), ROW)
        src, dst = stores[n]
        return pltpu.make_async_copy(src.at[rows, :], dst.at[rows, :], out_sem.at[n, r])

    sums_ref[...] = jnp.zeros_like(sums_ref)

    @pl.loop(0, TP)
    def _(r):
        pltpu.make_async_copy(x0, x_ref.at[r], in_sem.at[r, 0]).wait()
        pltpu.make_async_copy(c0, cot_ref.at[r], in_sem.at[r, 1]).wait()
        here = pl.ds(pl.multiple_of(r * ROW, ROW), ROW)
        xhat, _ = normalize(x_ref[r].astype(f32))
        xhat_ref[here, :] = xhat.astype(bf16)
        attn_in = (xhat * vec_ref[0:1] + vec_ref[1:2]).astype(bf16)
        min_ref[here, :] = (xhat * vec_ref[2:3] + vec_ref[3:4]).astype(bf16)
        qkv = dot(attn_in, wqkv_ref[...]) + qb_ref[...]
        d = me ^ ((r & 1) * 2 + r // 2)
        base = (d * 2 + info_ref[65]) * SEGS
        ends, end = [], 0
        for j in range(SEGS - 1):
            end = end + info_ref[base + j]
            ends.append(end)
        rows = lax.broadcasted_iota(jnp.int32, (ROW, 1), 0)
        cols = lax.broadcasted_iota(jnp.int32, (1, ROW), 1)
        row_doc = sum([(rows >= e).astype(jnp.int32) for e in ends])
        col_doc = sum([(cols >= e).astype(jnp.int32) for e in ends])
        allowed = (row_doc == col_doc) & (rows <= cols)
        start = jnp.zeros_like(rows)
        for e in ends:
            start = jnp.maximum(start, jnp.where(rows >= e, e, 0))
        kept = jnp.where(rows < ends[-1], cot_ref[r].astype(f32), 0.0)
        gb = kept.astype(bf16)
        gb_ref[here, :] = gb
        dctx = dot_nt(gb, wd_ref[...]).astype(bf16)
        chosen = ((rows - start) == cols).astype(f32).astype(bf16)
        table = dot(chosen, rot_ref[...])
        pair = lambda n: table[:, n * 256 : n * 256 + 128] + table[:, n * 256 + 128 : n * 256 + 256]
        cosine, left, right = [jnp.concatenate([pair(n)] * 2, axis=1) for n in range(3)]
        scale = HEAD_DIM**-0.5
        q = (turn(qkv[:, 0:256], cosine, left, right).astype(bf16).astype(f32) * scale).astype(bf16)
        k = turn(qkv[:, 256:512], cosine, left, right).astype(bf16)
        v = qkv[:, 512:768].astype(bf16)
        lanes = lax.broadcasted_iota(jnp.int32, (1, 256), 1) // HEAD_DIM
        ctx, dq, dk, dv = [jnp.zeros((ROW, 256), f32)] * 4
        heads = range(LOCAL_HEADS)
        only = [(lanes == h).astype(f32).astype(bf16) for h in heads]
        qs, dcs = [q * m for m in only], [dctx * m for m in only]
        s_all = dot_nt(k, jnp.concatenate(qs, axis=0))
        dp_all = dot_nt(v, jnp.concatenate(dcs, axis=0))
        cut = [slice(h * ROW, (h + 1) * ROW) for h in heads]
        scores = [jnp.where(allowed, s_all[:, c], -1000000000.0) for c in cut]
        dprobs = [dp_all[:, c] for c in cut]
        probs = []
        for h in heads:
            shifted = jnp.exp(scores[h] - jnp.max(scores[h], axis=0, keepdims=True))
            probs.append(shifted * (1.0 / jnp.sum(shifted, axis=0, keepdims=True)))
        lows = [p.astype(bf16) for p in probs]
        ds = []
        for h in heads:
            inner = jnp.sum(dprobs[h] * probs[h], axis=0, keepdims=True)
            ds.append((probs[h] * (dprobs[h] - inner)).astype(bf16))
        p_all = jnp.concatenate(lows, axis=0)
        ds_all = jnp.concatenate(ds, axis=0)
        ctx = dot_tn(p_all, jnp.concatenate([v * m for m in only], axis=0))
        dq = dot_tn(ds_all, jnp.concatenate([k * m for m in only], axis=0))
        dv = dot(jnp.concatenate(lows, axis=1), jnp.concatenate(dcs, axis=0))
        dk = dot(jnp.concatenate(ds, axis=1), jnp.concatenate(qs, axis=0))
        ctx_ref[here, :] = ctx.astype(bf16)
        dqs = turn(dq * scale, cosine, -left, -right)
        dks = turn(dk, cosine, -left, -right)
        dqkv = jnp.concatenate([dqs, dks, dv], axis=1).astype(bf16)
        dqkv_ref[here, :] = dqkv

        @pl.when(r == 0)
        def _():
            sums_ref[0:1, :] = jnp.sum(kept, axis=0, keepdims=True)

        sums_ref[1:2, 0:QC] += jnp.sum(dqkv.astype(f32), axis=0, keepdims=True)
        for n in range(5):
            store(n, r).start()

    c = me % 2
    sums_ref[3:4, :] = through(sums_ref[1:2, 0:QC], wqkv_ref[...])
    columns = jnp.transpose(vec_ref[...])
    vec_col_ref[...] = columns

    def sent(d, n):
        rows = pl.ds(pl.multiple_of(d * 48, 16), 48)
        if n == 1:
            rows = pl.ds(pl.multiple_of(192 + d * 16, 16), 16)
        return pltpu.make_async_copy(
            sent_ref.at[:, :, rows, :], sent_out.at[:, :, rows, :], sent_sem.at[d, n]
        )

    @pl.loop(0, 4)
    def _(d):
        raw = dot_tn(xhat_ref[:, tile(d)], dqkv_ref[...])
        gain, bias = vec_col_ref[tile(d), 0:1], vec_col_ref[tile(d), 1:2]
        qkv_grad = (raw * gain + bias * sums_ref[1:2, 0:QC]).astype(bf16)
        sums_ref[2:3, tile(d)] = row_sums(raw * wqkv_ref[tile(d), :].astype(f32))
        dense_grad = dot_tn(ctx_ref[...], gb_ref[:, tile(d)]).astype(bf16)
        base = pl.multiple_of(d * 48, 16)
        dense_base = pl.multiple_of(192 + d * 16, 16)
        for y in range(4):
            for x in range(4):
                b, a = swapped(y, x, c)
                at = slice((y * 4 + x) * 16, (y * 4 + x + 1) * 16)
                for p in range(3):
                    sent_ref[b, a, pl.ds(base + p * 16, 16), :] = qkv_grad[
                        at, p * 256 : (p + 1) * 256
                    ]
                sent_ref[b, a, pl.ds(dense_base, 16), :] = dense_grad[at]
        sent(d, 0).start()
        sent(d, 1).start()

    for copy in weights:
        copy.wait()

    @pl.loop(0, 4)
    def _(i):
        for n in range(5):
            store(n, i).wait()
        sent(i, 0).wait()
        sent(i, 1).wait()


def attention(info, xs, cots, buf):
    tokens = TP * ROW
    dma = pltpu.SemaphoreType.DMA
    return call(
        attention_kernel,
        [
            shaped(4, 4, 256, 256),
            shaped(tokens, D),
            shaped(tokens, D),
            shaped(tokens, 256),
            shaped(tokens, QC),
            shaped(D // TP, D),
            shaped(D, QC),
            shaped(tokens, D),
            shaped(8, D, dtype=f32),
            shaped(1, HC, dtype=f32),
            shaped(8, D, dtype=f32),
        ],
        info,
        *xs,
        *cots,
        buf,
        jnp.asarray(rotary_tables()),
        places="s" + "h" * 8 + "vv",
        outs="hhhhhhhhvvv",
        scratch=[
            pltpu.VMEM((TP, ROW, D), bf16),
            pltpu.VMEM((TP, ROW, D), bf16),
            pltpu.VMEM((D, QC), bf16),
            pltpu.VMEM((D // TP, D), bf16),
            pltpu.VMEM((1, QC), f32),
            pltpu.VMEM((tokens, D), bf16),
            pltpu.VMEM((tokens, D), bf16),
            pltpu.VMEM((tokens, 256), bf16),
            pltpu.VMEM((tokens, QC), bf16),
            pltpu.VMEM((tokens, D), bf16),
            pltpu.VMEM((4, 4, 256, 256), bf16),
            dma((4, 2)),
            dma((5, 4)),
            dma((2,)),
            dma((4, 2)),
            pltpu.VMEM((D, 8), f32),
        ],
        flops=6e9,
        nbytes=2e7,
        trans=1e6,
    )


def mlp_kernel(
    me_ref,
    buf_in,
    min_in,
    gb_in,
    xhat_in,
    ub_ref,
    vec_ref,
    sums_a_ref,
    sent_out,
    hidden_out,
    dpre_out,
    wup_out,
    wdown_out,
    buf_ref,
    min_ref,
    gb_ref,
    wup_ref,
    wdown_ref,
    hidden_ref,
    dpre_ref,
    sent_ref,
    xhat_ref,
    sums_ref,
    image_ref,
    parts_ref,
    vec_col_ref,
    buf_sem,
    in_sem,
    out_sem,
    weight_sem,
    sent_sem,
    image_sem,
):
    me = me_ref[0]
    c = me % 2
    parts = [pltpu.make_async_copy(buf_in.at[b], buf_ref.at[b], buf_sem.at[b]) for b in range(4)]

    def load(t, n):
        src, dst = ((min_in, min_ref), (gb_in, gb_ref), (xhat_in, xhat_ref))[n]
        return pltpu.make_async_copy(src.at[tile(t), :], dst.at[tile(t), :], in_sem.at[t, n])

    for part in parts:
        part.start()
    for t in range(4):
        for n in range(2):
            load(t, n).start()
    for part in parts:
        part.wait()
    for t in range(4):
        load(t, 2).start()
    assemble_b(me, buf_ref, wup_ref, wdown_ref)
    weights = [
        pltpu.make_async_copy(wup_ref, wup_out, weight_sem.at[0]),
        pltpu.make_async_copy(wdown_ref, wdown_out, weight_sem.at[1]),
    ]
    for copy in weights:
        copy.start()
    sums_ref[...] = jnp.zeros_like(sums_ref)

    def store(t, n):
        src, dst = ((hidden_ref, hidden_out), (dpre_ref, dpre_out))[n]
        return pltpu.make_async_copy(src.at[tile(t), :], dst.at[tile(t), :], out_sem.at[t, n])

    @pl.loop(0, TP)
    def _(tn):
        t = tile(tn)
        load(tn, 0).wait()
        load(tn, 1).wait()

        def products(n):
            at = slice(n * 256, (n + 1) * 256)
            pre = dot(min_ref[t, :], wup_ref[:, at]) + ub_ref[:, at]
            return pre, dot_nt(gb_ref[t, :], wdown_ref[at, :])

        ahead = products(0)
        for n in range(4):
            at = slice(n * 256, (n + 1) * 256)
            pre, back = ahead
            if n < 3:
                ahead = products(n + 1)
            size = jnp.abs(pre) * 0.7071067811865476
            bell = jnp.exp(-0.5 * pre * pre)
            s = 1.0 / (1.0 + 0.3275911 * size)
            poly = s * (
                0.127414796
                + s * (-0.142248368 + s * (0.7107068705 + s * (-0.7265760135 + s * 0.5307027145)))
            )
            tail = poly * bell
            cumul = jnp.where(pre >= 0.0, 1.0 - tail, tail)
            hidden_ref[t, at] = (pre * cumul).astype(bf16)
            dpre = (back * (cumul + pre * (bell * 0.3989422804014327))).astype(bf16)
            dpre_ref[t, at] = dpre
            sums_ref[0:1, at] += jnp.sum(dpre.astype(f32), axis=0, keepdims=True)
        store(tn, 0).start()
        store(tn, 1).start()

    @pl.loop(0, 4)
    def _(y):
        grad = dot_tn(hidden_ref[:, tile(y)], gb_ref[...]).astype(bf16)
        for x in range(4):
            b, a = swapped(y, x, c)
            for cg in range(4):
                sent_ref[b, a, 256 + cg * 64 : 256 + (cg + 1) * 64, :] = grad[
                    x * 64 : (x + 1) * 64, cg * 256 : (cg + 1) * 256
                ]

    def sent(a, rows, n):
        base = a * 512 + rows.start
        return pltpu.make_async_copy(
            sent_ref.at[:, a, rows, :],
            sent_out.at[:, pl.ds(pl.multiple_of(base, 16), rows.size), :],
            sent_sem.at[a, n],
        )

    for a in range(4):
        sent(a, pl.ds(256, 256), 4).start()

    sums_ref[2:3, :] = through(sums_ref[0:1, :], wup_ref[...])
    vec_col_ref[...] = jnp.transpose(vec_ref[...])
    for t in range(4):
        load(t, 2).wait()

    def above(a, d):
        return sent(a, pl.ds(pl.multiple_of(d * 64, 64), 64), d)

    @pl.loop(0, 4)
    def _(d):
        raw = dot_tn(xhat_ref[:, tile(d)], dpre_ref[...])
        gain, bias = vec_col_ref[tile(d), 2:3], vec_col_ref[tile(d), 3:4]
        grad = (raw * gain + bias * sums_ref[0:1, :]).astype(bf16)
        sums_ref[1:2, tile(d)] = row_sums(raw * wup_ref[tile(d), :].astype(f32))
        for y in range(4):
            for x in range(4):
                b, a = swapped(y, x, c)
                at = slice((y * 4 + x) * 16, (y * 4 + x + 1) * 16)
                for cg in range(4):
                    row = pl.multiple_of(d * 64 + cg * 16, 16)
                    sent_ref[b, a, pl.ds(row, 16), :] = grad[at, cg * 256 : (cg + 1) * 256]
        for a in range(4):
            above(a, d).start()

    image_ref[...] = jnp.zeros_like(image_ref)

    def put(row, ref, line, count):
        for i in range(count):
            image_ref[pl.ds(row + i, 1), :] = ref[line : line + 1, i * 256 : (i + 1) * 256]

    put(0, sums_a_ref, 2, 4)
    put(4, sums_a_ref, 3, 4)
    put(8, sums_ref, 1, 4)
    put(12, sums_ref, 2, 4)
    for p in range(3):
        image_ref[pl.ds(16 + p * 4 + me, 1), :] = sums_a_ref[1:2, p * 256 : (p + 1) * 256]
    put(28, sums_a_ref, 0, 4)
    put(32 + 4 * me, sums_ref, 0, 4)
    put(48, sums_a_ref, 0, 4)
    image = image_ref[...]
    high = image.astype(bf16)
    parts_ref[0:IMAGE, :] = high
    parts_ref[IMAGE : 2 * IMAGE, :] = (image - high.astype(f32)).astype(bf16)
    images = [
        pltpu.make_async_copy(parts_ref, sent_out.at[b, pl.ds(2048, 2 * IMAGE), :], image_sem.at[b])
        for b in range(4)
    ]
    for copy in images:
        copy.start()
    for copy in weights:
        copy.wait()
    for i in range(TP):
        store(i, 0).wait()
        store(i, 1).wait()
        for n in range(4):
            above(i, n).wait()
        sent(i, pl.ds(256, 256), 4).wait()
    for copy in images:
        copy.wait()


def mlp(me, buf, mlp_in, gb, xhat, ub, vec, sums):
    tokens = TP * ROW
    dma = pltpu.SemaphoreType.DMA
    return call(
        mlp_kernel,
        [
            shaped(4, 2048 + 2 * IMAGE, 256),
            shaped(tokens, HC),
            shaped(tokens, HC),
            shaped(D, HC),
            shaped(HC, D),
        ],
        me,
        buf,
        mlp_in,
        gb,
        xhat,
        ub,
        vec,
        sums,
        places="s" + "h" * 4 + "vvv",
        outs="hhhhh",
        scratch=[
            pltpu.VMEM((4, 2048, 256), bf16),
            pltpu.VMEM((tokens, D), bf16),
            pltpu.VMEM((tokens, D), bf16),
            pltpu.VMEM((D, HC), bf16),
            pltpu.VMEM((HC, D), bf16),
            pltpu.VMEM((tokens, HC), bf16),
            pltpu.VMEM((tokens, HC), bf16),
            pltpu.VMEM((4, 4, 512, 256), bf16),
            pltpu.VMEM((tokens, D), bf16),
            pltpu.VMEM((8, D), f32),
            pltpu.VMEM((IMAGE, 256), f32),
            pltpu.VMEM((2 * IMAGE, 256), bf16),
            pltpu.VMEM((D, 8), f32),
            dma((4,)),
            dma((4, 3)),
            dma((4, 2)),
            dma((2,)),
            dma((4, 5)),
            dma((4,)),
        ],
        flops=9e9,
        nbytes=2e7,
        trans=2e6,
    )


def outputs_kernel(
    ctx_in,
    hidden_in,
    dqkv_in,
    dpre_in,
    wd_in,
    wdown_in,
    wqkv_in,
    wup_in,
    vec_ref,
    theirs_out,
    mine_out,
    ctx_ref,
    hidden_ref,
    dqkv_ref,
    dpre_ref,
    wd_ref,
    wdown_ref,
    wqkv_ref,
    wup_ref,
    both_ref,
    weight_sem,
    in_sem,
    out_sem,
):
    pairs = ((wqkv_in, wqkv_ref), (wup_in, wup_ref), (wd_in, wd_ref), (wdown_in, wdown_ref))
    weights = [
        pltpu.make_async_copy(src, dst, weight_sem.at[i]) for i, (src, dst) in enumerate(pairs)
    ]
    inputs = (
        (dqkv_in, dqkv_ref),
        (dpre_in, dpre_ref),
        (ctx_in, ctx_ref),
        (hidden_in, hidden_ref),
    )

    def load(t, n):
        src, dst = inputs[n]
        return pltpu.make_async_copy(src.at[tile(t), :], dst.at[tile(t), :], in_sem.at[t, n])

    def finished(i, n):
        dst = (theirs_out, mine_out)[n]
        return pltpu.make_async_copy(both_ref.at[i], dst.at[i - 2 * n], out_sem.at[i])

    for i in range(TP):
        for n in range(4):
            load((i + 2) % 4, n).start()
            if i == 0:
                weights[n].start()
    for weight in weights:
        weight.wait()

    @pl.loop(0, TP)
    def _(i):
        t = (i + 2) % 4
        for n in range(4):
            load(t, n).wait()
        here = tile(t)
        dattn = dot_nt(dqkv_ref[here, :], wqkv_ref[...])
        dmlp = dot_nt(dpre_ref[here, :], wup_ref[...])
        both_ref[i, 1] = (dattn * vec_ref[0:1] + dmlp * vec_ref[2:3]).astype(bf16)
        forward = dot(ctx_ref[here, :], wd_ref[...]) + dot(hidden_ref[here, :], wdown_ref[...])
        both_ref[i, 0] = forward.astype(bf16)

        @pl.when(i < 2)
        def _():
            finished(i, 0).start()

        @pl.when(i >= 2)
        def _():
            finished(i, 1).start()

    for i in range(TP):
        finished(i, i // 2).wait()


def outputs(ctx, hidden, dqkv, dpre, wd, wdown, wqkv, wup, vec):
    tokens = TP * ROW
    dma = pltpu.SemaphoreType.DMA
    return call(
        outputs_kernel,
        [shaped(2, 2, ROW, D), shaped(2, 2, ROW, D)],
        ctx,
        hidden,
        dqkv,
        dpre,
        wd,
        wdown,
        wqkv,
        wup,
        vec,
        places="h" * 8 + "v",
        outs="hh",
        scratch=[
            pltpu.VMEM((tokens, 256), bf16),
            pltpu.VMEM((tokens, HC), bf16),
            pltpu.VMEM((tokens, QC), bf16),
            pltpu.VMEM((tokens, HC), bf16),
            pltpu.VMEM((D // TP, D), bf16),
            pltpu.VMEM((HC, D), bf16),
            pltpu.VMEM((D, QC), bf16),
            pltpu.VMEM((D, HC), bf16),
            pltpu.VMEM((TP, 2, ROW, D), bf16),
            dma((4,)),
            dma((4, 4)),
            dma((4,)),
        ],
        flops=6.5e9,
        nbytes=1.6e7,
    )


def half_kernel(a0_ref, b0_ref, a1_ref, b1_ref, kept_ref, send_ref):
    kept_ref[...] = a0_ref[...].astype(f32) + b0_ref[...].astype(f32)
    send_ref[...] = (a1_ref[...].astype(f32) + b1_ref[...].astype(f32)).astype(bf16)


def half_sum(mine, got):
    mine, got = in_hbm(mine), in_hbm(got)
    first = pl.BlockSpec((1, 1, ROW // 2, D), lambda n, k: (0, n, k, 0))
    second = pl.BlockSpec((1, 1, ROW // 2, D), lambda n, k: (1, n, k, 0))
    out = pl.BlockSpec((1, 1, ROW // 2, D), lambda n, k: (0, n, k, 0))
    return pl.pallas_call(
        half_kernel,
        grid=(2, 2),
        in_specs=[first, first, second, second],
        out_specs=[out, out],
        out_shape=[pltpu.HBM((1, 2, ROW, D), f32), pltpu.HBM((1, 2, ROW, D), bf16)],
        compiler_params=pltpu.CompilerParams(vmem_limit_bytes=VMEM),
        cost_estimate=pl.CostEstimate(flops=0, bytes_accessed=8000000, transcendentals=0),
    )(mine, got, mine, got)


def close_kernel(len_ref, x_ref, cot_ref, kept_ref, got_ref, vec_ref, out_ref, grad_ref):
    x = x_ref[...].astype(f32)
    out_ref[...] = (x + kept_ref[0, 0] + got_ref[0, 0].astype(f32) + vec_ref[4:5]).astype(bf16)
    e = kept_ref[0, 1] + got_ref[0, 1].astype(f32)
    xhat, inv_std = normalize(x)
    mean_e = jnp.mean(e, axis=-1, keepdims=True)
    mean_ex = jnp.mean(e * xhat, axis=-1, keepdims=True)
    used = sum([len_ref[0, j] for j in range(SEGS - 1)])
    rows = pl.program_id(0) * x.shape[0] + lax.broadcasted_iota(jnp.int32, (x.shape[0], 1), 0)
    kept = jnp.where(rows < used, cot_ref[...].astype(f32), 0.0)
    grad_ref[...] = kept + inv_std * (e - mean_e - xhat * mean_ex)


def close(lengths, x, cot, kept, got, vec):
    row = pl.BlockSpec((ROW // 4, D), lambda k: (k, 0))
    both = pl.BlockSpec((1, 2, ROW // 4, D), lambda k: (0, 0, k, 0))
    return pl.pallas_call(
        close_kernel,
        grid=(4,),
        in_specs=[SMEM_SPEC, row, row, both, both, pl.BlockSpec((8, D), lambda k: (0, 0))],
        out_specs=[row, row],
        out_shape=[pltpu.HBM((ROW, D), bf16), pltpu.HBM((ROW, D), f32)],
        compiler_params=pltpu.CompilerParams(vmem_limit_bytes=VMEM),
        cost_estimate=pl.CostEstimate(flops=0, bytes_accessed=6000000, transcendentals=0),
    )(lengths, *[in_hbm(v) for v in (x, cot, kept, got)], vec)


def add_early_kernel(a_ref, out_ref):
    out_ref[0] = sum([a_ref[i, 0].astype(f32) for i in range(4)]).astype(bf16)


def add_early(sent_a):
    return pl.pallas_call(
        add_early_kernel,
        grid=(4,),
        in_specs=[pl.BlockSpec((4, 1, 256, 256), lambda a: (0, a, 0, 0))],
        out_specs=pl.BlockSpec((1, 256, 256), lambda a: (a, 0, 0)),
        out_shape=pltpu.HBM((4, 256, 256), bf16),
        compiler_params=pltpu.CompilerParams(vmem_limit_bytes=VMEM),
        cost_estimate=pl.CostEstimate(flops=0, bytes_accessed=3000000, transcendentals=0),
    )(in_hbm(sent_a))


def add(early, sent_b):
    rows = 768 + 2 * IMAGE

    def kernel(early_ref, b_ref, image_ref, out_ref, sums_ref):
        out_ref[0, 0:256, :] = early_ref[0]
        total = sum([b_ref[i].astype(f32) for i in range(4)])
        out_ref[0, 256:768, :] = total.astype(bf16)

        @pl.when(pl.program_id(0) == 0)
        def _():
            image = sum([image_ref[i].astype(f32) for i in range(4)])
            image = image[:IMAGE] + image[IMAGE:]
            high = image.astype(bf16)
            sums_ref[0:IMAGE, :] = high
            sums_ref[IMAGE : 2 * IMAGE, :] = (image - high.astype(f32)).astype(bf16)

        out_ref[0, 768:rows, :] = sums_ref[...]

    return pl.pallas_call(
        kernel,
        grid=(4,),
        in_specs=[
            pl.BlockSpec((1, 256, 256), lambda a: (a, 0, 0)),
            pl.BlockSpec((4, 512, 256), lambda a: (0, a, 0)),
            pl.BlockSpec((4, 2 * IMAGE, 256), lambda a: (0, 2048 // (2 * IMAGE), 0)),
        ],
        out_specs=pl.BlockSpec((1, rows, 256), lambda a: (a, 0, 0)),
        out_shape=pltpu.HBM((4, rows, 256), bf16),
        scratch_shapes=[pltpu.VMEM((2 * IMAGE, 256), bf16)],
        compiler_params=pltpu.CompilerParams(vmem_limit_bytes=VMEM),
        cost_estimate=pl.CostEstimate(flops=0, bytes_accessed=6000000, transcendentals=0),
    )(in_hbm(early), in_hbm(sent_b), in_hbm(sent_b))


LAST = QC + HC + 4 * 256


def image_rows(d):
    return [start + d for start in STARTS[:4]] + [28 + d, 48 + d] + [
        32 + 4 * d + i for i in range(4)
    ] + [16 + 3 * d + i for i in range(3)]


def part_kernel(far_ref, in_ref, slots_ref, keep_ref, send_ref, total_ref, rows_ref):
    far = far_ref[0]
    total_ref[...] = sum([in_ref[i].astype(f32) for i in range(4)])
    rows_ref[...] = jnp.zeros_like(rows_ref)
    for d in range(4):
        for i, row in enumerate(image_rows(d)):
            high = total_ref[768 + row : 769 + row, :]
            low = total_ref[768 + IMAGE + row : 769 + IMAGE + row, :]
            rows_ref[d, i : i + 1, :] = high + low
        image = rows_ref[d]
        high = image.astype(bf16)
        low = (image - high.astype(f32)).astype(bf16)
        for zh in range(2):
            s = d * 2 + zh
            for p in range(3):
                row = (d * 3 + p) * 16 + zh * 8
                slots_ref[s, :, p * 256 : (p + 1) * 256] = total_ref[row : row + 8, :].astype(bf16)
            for cg in range(4):
                row = 256 + (d * 4 + cg) * 16 + zh * 8
                at = QC + cg * 256
                slots_ref[s, :, at : at + 256] = total_ref[row : row + 8, :].astype(bf16)
            for n, block in enumerate((high[:8], high[8:], low[:8], low[8:])):
                at = QC + HC + n * 256
                slots_ref[s, :, at : at + 256] = block
    for ref, half in ((keep_ref, far), (send_ref, 1 - far)):
        for cg in range(4):
            at = slice(cg * 256, (cg + 1) * 256)
            row = pl.multiple_of(192 + cg * 16 + half * 8, 8)
            ref[32:40, at] = total_ref[pl.ds(row, 8), :].astype(ref.dtype)
            row = pl.multiple_of(512 + cg * 64 + half * 32, 8)
            ref[0:32, at] = total_ref[pl.ds(row, 32), :].astype(ref.dtype)


def part(far, received):
    return call(
        part_kernel,
        [shaped(8, 8, LAST), shaped(40, D, dtype=f32), shaped(40, D)],
        far,
        received,
        outs="uuu",
        scratch=[pltpu.VMEM((768 + 2 * IMAGE, 256), f32), pltpu.VMEM((4, 16, 256), f32)],
        nbytes=4e6,
    )


def finish_kernel(place_ref, slots_ref, keep_ref, got_ref, qkv_ref, up_ref, dense_ref, down_ref, *rest):
    tiny_refs, image_ref = rest[:8], rest[8]
    image = [jnp.zeros((8, 256), f32)] * 2
    for s in range(8):
        for n in range(4):
            at = QC + HC + n * 256
            image[n % 2] = image[n % 2] + slots_ref[s, :, at : at + 256].astype(f32)
    image_ref[0:8, :] = image[0]
    image_ref[8:16, :] = image[1]
    for d in range(4):
        both = slots_ref[2 * d, :, 0 : QC + HC].astype(f32) + slots_ref[
            2 * d + 1, :, 0 : QC + HC
        ].astype(f32)
        for p in range(3):
            at = p * D + d * 256
            qkv_ref[:, at : at + 256] = both[:, p * 256 : (p + 1) * 256]
        up_ref[:, d * HC : (d + 1) * HC] = both[:, QC:]
    total = keep_ref[...] + got_ref[...].astype(f32)
    dense_ref[...] = total[32:40]
    down_ref[...] = total[0:32]
    p = place_ref[0]
    f = p % 32
    lines = (0, 1, 2, 3, 10 + f * 24 // 256, 4, 6 + f // 8, 5)
    for line, size, ref in zip(lines, SIZES, tiny_refs):
        lane = (p * size) % 256
        values = image_ref[pl.ds(line, 1), :]
        if size == 24:
            values = jnp.concatenate([values, image_ref[pl.ds(line + 1, 1), :]], axis=1)
        ref[...] = pltpu.roll(values, values.shape[1] - lane, 1)[:, :size]


def finish(place, slots, keep, got):
    return call(
        finish_kernel,
        [
            shaped(8, 3 * D, dtype=f32),
            shaped(8, FF, dtype=f32),
            shaped(8, D, dtype=f32),
            shaped(32, D, dtype=f32),
        ]
        + [shaped(1, size, dtype=f32) for size in SIZES],
        place,
        slots,
        keep,
        got,
        scratch=[pltpu.VMEM((16, 256), f32)],
        nbytes=2e6,
    )


def body(
    inputs,
    cotangent,
    lengths,
    norm1_gain,
    norm1_bias,
    norm2_gain,
    norm2_bias,
    qkv_weight,
    qkv_bias,
    dense_weight,
    dense_bias,
    up_weight,
    up_bias,
    down_weight,
    down_bias,
):
    me = lax.axis_index("dp").astype(jnp.int32)
    index = lax.axis_index("fsdp").astype(jnp.int32)
    far = (index % 2)[None]
    me1 = me[None]
    outer, inner = outer_groups(), inner_groups()

    vectors = (
        norm1_gain,
        norm1_bias,
        norm2_gain,
        norm2_bias,
        qkv_bias,
        dense_bias,
        up_bias,
        down_bias,
    )
    slots, pieces = prepare(
        qkv_weight.reshape(8, 3 * D),
        up_weight.reshape(8, FF),
        dense_weight.reshape(8, D),
        down_weight.reshape(32, D),
        lengths,
        vectors,
    )
    far_pieces = flip_far(pieces)
    first = a2a(slots, stack_groups())
    block, lens = spread(index[None], first.reshape(4, 16, SLOT), pieces, far_pieces)
    info = jnp.concatenate([lens[0], me1, far])

    block, x0 = lax.optimization_barrier((block, inputs))
    x1 = flip_chip(x0)
    second = a2a(block, inner)
    second, x1, c0 = lax.optimization_barrier((second, x1, cotangent))
    c1 = flip_chip(c0)
    third_a = a2a(widen_a(second), outer)
    x2, x3 = flip_core(x0), flip_core(x1)
    c2, c3 = flip_core(c0), flip_core(c1)
    xs, cots = (x0, x1, x2, x3), (c0, c1, c2, c3)
    wide_b, xs, cots = lax.optimization_barrier((widen_b(second), xs, cots))
    third_b = a2a(wide_b, outer)

    sent_a, mlp_in, gb, ctx, dqkv, wd, wqkv, xhat, vec, up_b, sums = attention(
        info, xs, cots, third_a
    )
    sent_a = a2a(sent_a, outer)
    sent_b, hidden, dpre, wup, wdown = mlp(me1, third_b, mlp_in, gb, xhat, up_b, vec, sums)
    sent_b = a2a(sent_b, outer)

    theirs, mine = outputs(ctx, hidden, dqkv, dpre, wd, wdown, wqkv, wup, vec)
    kept, send = half_sum(mine, flip_core(theirs))

    early, send, sent_b = lax.optimization_barrier((add_early(sent_a), send, sent_b))
    got = flip_chip(send)
    fourth = a2a(add(early, sent_b), inner)
    slots, keep, rest = part(far, fourth)
    block_output, input_grad = close(lengths, inputs, cotangent, kept, got, vec)
    place = (me * 32 + index)[None]
    results = finish(place, a2a(slots, stack_groups()), keep, flip_far(rest))
    flat = [r.reshape(-1) for r in results]
    return (
        block_output,
        input_grad,
        flat[4],
        flat[5],
        flat[6],
        flat[7],
        flat[0],
        flat[8],
        flat[2],
        flat[9],
        flat[1],
        flat[10],
        flat[3],
        flat[11],
    )


def solution(mesh):
    flat = P(("dp", "fsdp"))
    rows = P(("dp", "fsdp"), None)
    return jax.shard_map(
        body,
        mesh=mesh,
        in_specs=(rows,) * 3 + (flat,) * 12,
        out_specs=(rows,) * 2 + (flat,) * 12,
        check_vma=False,
    )
```

```python
import jax
import jax.numpy as jnp
import ml_dtypes
import numpy as np
from jax import lax
from jax.experimental import pallas as pl
from jax.experimental.pallas import tpu as pltpu
from jax.sharding import PartitionSpec as P

D = 1024
HEADS = 16
HEAD_DIM = 64
ROT = 16
FF = 4096
ROW = 256
SEGS = 8
TP = 4
QC = 3 * D // TP
HC = FF // TP
LOCAL_HEADS = HEADS // TP
AXES = ("dp", "fsdp")
VMEM = 44 * 1024 * 1024

f32 = jnp.float32
bf16 = jnp.bfloat16


def dev(d, y, x, zh):
    return d * 32 + y * 8 + x * 2 + zh


def outer_groups(flip=0):
    groups = []
    for d in range(4):
        for k in range(4):
            for zh in range(2):
                if d % 2 == flip:
                    groups.append([dev(d, i, k, zh) for i in range(4)])
                else:
                    groups.append([dev(d, k, i, zh) for i in range(4)])
    return groups


def inner_groups():
    return outer_groups(flip=1)


def stack_groups():
    return [
        [dev(d, y, x, zh) for d in range(4) for zh in range(2)] for y in range(4) for x in range(4)
    ]


def plane_groups():
    return [
        [dev(d, y, x, zh) for y in range(4) for x in range(4)] for d in range(4) for zh in range(2)
    ]


def ring(values, groups, step):
    pairs = [(g[i], g[(i + step) % 4]) for g in groups for i in range(4)]
    return lax.ppermute(values, AXES, pairs)


STEPS = (0, 1, 3, 2)


def gather(values, groups):
    return [values] + [ring(values, groups, k) for k in STEPS[1:]]


def scatter(values, groups):
    return [values[0]] + [ring(v, groups, k) for v, k in zip(values[1:], STEPS[1:])]


def a2a(values, groups):
    return lax.all_to_all(values, AXES, 0, 0, tiled=True, axis_index_groups=groups)


def flip_core(values):
    return lax.ppermute(values, "dp", [(0, 1), (1, 0), (2, 3), (3, 2)])


def flip_chip(values):
    return lax.ppermute(values, "dp", [(0, 2), (2, 0), (1, 3), (3, 1)])


def flip_far(values):
    return lax.ppermute(values, "fsdp", [(i, i ^ 1) for i in range(32)])


def dot(left, right):
    return jnp.dot(left, right, preferred_element_type=f32)


def dot_nt(left, right):
    return lax.dot_general(left, right, (((1,), (1,)), ((), ())), preferred_element_type=f32)


def dot_tn(left, right):
    return lax.dot_general(left, right, (((0,), (0,)), ((), ())), preferred_element_type=f32)


def in_hbm(values):
    return pltpu.with_memory_space_constraint(values, pltpu.HBM)


VMEM_SPEC = pl.BlockSpec(memory_space=pltpu.VMEM)
SMEM_SPEC = pl.BlockSpec(memory_space=pltpu.SMEM)
HBM_SPEC = pl.BlockSpec(memory_space=pltpu.HBM)
SPECS = {"s": SMEM_SPEC, "v": VMEM_SPEC, "u": VMEM_SPEC, "h": HBM_SPEC}


def call(kernel, out_shape, *args, places=None, outs=None, scratch=(), flops=0, nbytes=0, trans=0):
    places = places or "s" + "v" * (len(args) - 1)
    out_specs = jax.tree.map(lambda _: VMEM_SPEC, out_shape)
    if outs is not None:
        out_specs = [SPECS[o] for o in outs]
        out_shape = [
            v if o == "v" else pltpu.HBM(v.shape, v.dtype) for o, v in zip(outs, out_shape)
        ]
    args = [in_hbm(v) if p == "h" else v for p, v in zip(places, args)]
    return pl.pallas_call(
        kernel,
        in_specs=[SPECS[p] for p in places],
        out_specs=out_specs,
        out_shape=out_shape,
        scratch_shapes=list(scratch),
        compiler_params=pltpu.CompilerParams(vmem_limit_bytes=VMEM),
        cost_estimate=pl.CostEstimate(
            flops=int(flops), bytes_accessed=int(nbytes), transcendentals=int(trans)
        ),
    )(*args)


def shaped(*shape, dtype=bf16):
    return jax.ShapeDtypeStruct(shape, dtype)


def normalize(x):
    average = jnp.mean(x, axis=-1, keepdims=True)
    centred = x - average
    inv_std = lax.rsqrt(jnp.mean(centred * centred, axis=-1, keepdims=True) + 1e-05)
    return centred * inv_std, inv_std


STARTS = (0, 4, 8, 12, 16, 28, 32, 48)
SIZES = (8, 8, 8, 8, 24, 8, 32, 8)
IMAGE = 64
LENS = 64
SLOT = QC + HC + 128


def tile(n):
    return pl.ds(pl.multiple_of(n * 256, 256), 256)


def swapped(y, x, c):
    return y + c * (x - y), x + c * (y - x)


def prepare_kernel(
    qkv_ref, up_ref, dense_in, down_in, len_in, n1g, n1b, n2g, n2b, qb, db, ub, dnb,
    out_ref, pieces_ref, tile_ref, *rest
):
    sources = (len_in, n1g, n1b, n2g, n2b, qb, db, ub, dnb)
    holders, sem = rest[:9], rest[9]
    copies = [
        pltpu.make_async_copy(src, dst, sem.at[i])
        for i, (src, dst) in enumerate(zip(sources, holders))
    ]
    for copy in copies:
        copy.start()
    for d in range(4):
        for zh in range(2):
            s = d * 2 + zh
            for p in range(3):
                at = p * D + d * 256
                out_ref[s, :, p * 256 : (p + 1) * 256] = qkv_ref[:, at : at + 256]
            out_ref[s, :, QC : QC + HC] = up_ref[:, d * HC : (d + 1) * HC]
    pieces_ref[0:32, :] = down_in[...]
    pieces_ref[32:40, :] = dense_in[...]
    tile_ref[...] = jnp.zeros_like(tile_ref)
    for copy in copies:
        copy.wait()
    for i, (size, ref) in enumerate(zip(SIZES, holders[1:])):
        tile_ref[i : i + 1, 0:size] = ref[...].astype(f32)
    tile_ref[0:1, LENS : LENS + SEGS] = holders[0][...].astype(f32)
    block = tile_ref[...].astype(bf16)
    for s in range(8):
        out_ref[s, :, QC + HC : SLOT] = block


def prepare(qkv, up, dense, down, lengths, vectors):
    vectors = [v[None, :] for v in vectors]
    return call(
        prepare_kernel,
        [shaped(8, 8, SLOT), shaped(40, D)],
        qkv,
        up,
        dense,
        down,
        lengths,
        *vectors,
        places="vvvv" + "h" * 9,
        scratch=[pltpu.VMEM((8, 128), f32), pltpu.VMEM((1, SEGS), jnp.int32)]
        + [pltpu.VMEM(v.shape, bf16) for v in vectors]
        + [pltpu.SemaphoreType.DMA((9,))],
        nbytes=1e6,
    )


def locate(p, start, size):
    first = p * size
    return start + first // 256, first % 256


def spread_kernel(index_ref, first_ref, mine_ref, theirs_ref, out_ref, lens_ref, image_ref):
    index = index_ref[0]
    far = index % 2 == 1
    mine, theirs = mine_ref[...].astype(f32), theirs_ref[...].astype(f32)
    low, high = jnp.where(far, theirs, mine), jnp.where(far, mine, theirs)
    down = jnp.concatenate([low[:32], high[:32]], axis=0).astype(bf16)
    dense = jnp.concatenate([low[32:], high[32:]], axis=0).astype(bf16)
    image_ref[...] = jnp.zeros_like(image_ref)
    lens = []
    for d in range(4):
        both = first_ref[d, :, QC + HC : SLOT].astype(f32)
        for zh in range(2):
            p = d * 32 + index // 2 * 2 + zh
            tile = both[zh * 8 : zh * 8 + 8]
            lens.append(tile[0:1, LENS : LENS + SEGS])
            for i, (start, size) in enumerate(zip(STARTS, SIZES)):
                row, lane = locate(p, start, size)
                wide = 512 if size == 24 else 256
                blank = jnp.zeros((1, wide - size), f32)
                values = jnp.concatenate([tile[i : i + 1, :size], blank], axis=1)
                values = pltpu.roll(values, lane, 1)
                image_ref[pl.ds(row, 1), :] += values[:, :256]
                if wide == 512:
                    image_ref[pl.ds(row + 1, 1), :] += values[:, 256:]
    lens_ref[...] = jnp.concatenate(lens, axis=1).astype(jnp.int32)
    image = image_ref[...].astype(bf16)
    for d in range(4):
        for p in range(3):
            row = (d * 3 + p) * 16
            out_ref[row : row + 16, :] = first_ref[d, :, p * 256 : (p + 1) * 256]
        for cg in range(4):
            row = 256 + (d * 4 + cg) * 16
            at = QC + cg * 256
            out_ref[row : row + 16, :] = first_ref[d, :, at : at + 256]
    for cg in range(4):
        at = slice(cg * 256, (cg + 1) * 256)
        out_ref[192 + cg * 16 : 208 + cg * 16, :] = dense[:, at]
        out_ref[512 + cg * 64 : 576 + cg * 64, :] = down[:, at]
    out_ref[768 : 768 + IMAGE, :] = image


def spread(index, first, mine, theirs):
    return call(
        spread_kernel,
        [shaped(768 + IMAGE, 256), shaped(1, 64, dtype=jnp.int32)],
        index,
        first,
        mine,
        theirs,
        scratch=[pltpu.VMEM((IMAGE, 256), f32)],
        nbytes=2e6,
    )


def merge_a_kernel(place_ref, b0, b1, b2, b3, out_ref):
    blocks = (b0, b1, b2, b3)
    for block, step in zip(blocks, STEPS):
        a = (place_ref[0] + 4 - step) % 4
        out_ref[tile(a), :] = block[0:256, :]
    total = sum([block[768 : 768 + IMAGE, :].astype(f32) for block in blocks])
    out_ref[1024 : 1024 + IMAGE, :] = total.astype(bf16)


def merge_a(place, blocks):
    return call(
        merge_a_kernel, [shaped(1024 + IMAGE, 256)], place, *blocks, outs="u", nbytes=1e6
    )[0]


def merge_b_kernel(place_ref, b0, b1, b2, b3, out_ref):
    for block, step in zip((b0, b1, b2, b3), STEPS):
        a = (place_ref[0] + 4 - step) % 4
        out_ref[pl.ds(pl.multiple_of(a * 512, 512), 512), :] = block[256:768, :]


def merge_b(place, blocks):
    return call(merge_b_kernel, [shaped(2048, 256)], place, *blocks, outs="u", nbytes=2e6)[0]


def assemble_a(me, buf_ref, wqkv_ref, wd_ref):
    c = me % 2
    for y in range(4):
        for x in range(4):
            b, a = swapped(y, x, c)
            yx = y * 4 + x
            base = a * 256
            for d in range(4):
                for p in range(3):
                    row = pl.multiple_of(base + (d * 3 + p) * 16, 16)
                    wqkv_ref[d * 256 + yx * 16 : d * 256 + yx * 16 + 16, p * 256 : (p + 1) * 256] = (
                        buf_ref[b, pl.ds(row, 16), :]
                    )
            for cg in range(4):
                row = pl.multiple_of(base + 192 + cg * 16, 16)
                wd_ref[yx * 16 : yx * 16 + 16, cg * 256 : (cg + 1) * 256] = buf_ref[
                    b, pl.ds(row, 16), :
                ]


def read_vectors(me, buf_ref, vec_ref, qb_ref, ub_ref):
    image = sum([buf_ref[b, 1024 : 1024 + IMAGE, :].astype(f32) for b in range(4)])

    def long(start):
        return jnp.concatenate([image[start + i : start + i + 1, :] for i in range(4)], axis=1)

    vec_ref[...] = jnp.zeros_like(vec_ref)
    for i in range(4):
        vec_ref[i : i + 1, :] = long(4 * i)
    vec_ref[4:5, :] = long(28) + long(48)
    own = [jnp.where(me == d, 1.0, 0.0) for d in range(4)]
    rows = [sum([image[16 + p * 4 + d : 17 + p * 4 + d] * own[d] for d in range(4)]) for p in range(3)]
    qb_ref[...] = jnp.concatenate(rows, axis=1)
    ub_ref[...] = sum([long(32 + 4 * d) * own[d] for d in range(4)])


def assemble_b(me, buf_ref, wup_ref, wdown_ref):
    c = me % 2
    for y in range(4):
        for x in range(4):
            b, a = swapped(y, x, c)
            yx = y * 4 + x
            base = a * 512
            for d in range(4):
                for cg in range(4):
                    row = pl.multiple_of(base + (d * 4 + cg) * 16, 16)
                    wup_ref[d * 256 + yx * 16 : d * 256 + yx * 16 + 16, cg * 256 : (cg + 1) * 256] = (
                        buf_ref[b, pl.ds(row, 16), :]
                    )
            for cg in range(4):
                row = pl.multiple_of(base + 256 + cg * 64, 16)
                wdown_ref[yx * 64 : yx * 64 + 64, cg * 256 : (cg + 1) * 256] = buf_ref[
                    b, pl.ds(row, 64), :
                ]


def turn(u, cosine, sin_left, sin_right):
    return (
        u * cosine
        + pltpu.roll(u, u.shape[1] - ROT // 2, 1) * sin_left
        + pltpu.roll(u, ROT // 2, 1) * sin_right
    )


def rotary_tables():
    places = np.arange(ROW, dtype=np.float32)
    freqs = (10000.0 ** (-(np.arange(ROT // 2, dtype=np.float32) * 2.0) / ROT)).astype(np.float32)
    angle = (places[:, None] * freqs[None, :]).astype(np.float32)
    cosine, sine = np.cos(angle), np.sin(angle)
    zeros = np.zeros_like(sine)
    rest = np.zeros((ROW, HEAD_DIM - ROT), np.float32)
    parts = [[cosine, cosine, rest + 1.0], [-sine, zeros, rest], [zeros, sine, rest]]
    columns = []
    for part in parts:
        whole = np.tile(np.concatenate(part, axis=1), (1, 2)).astype(np.float32)
        high = whole.astype(ml_dtypes.bfloat16)
        columns += [high, (whole - high.astype(np.float32)).astype(ml_dtypes.bfloat16)]
    return np.concatenate(columns, axis=1)


def row_sums(values):
    total = jnp.sum(values, axis=1, keepdims=True)
    return jnp.transpose(jnp.broadcast_to(total, (256, 128)))[0:1, :]


def through(sums, matrix):
    high = sums.astype(bf16)
    low = (sums - high.astype(f32)).astype(bf16)
    both = jnp.concatenate([high.astype(f32), low.astype(f32)] + [jnp.zeros_like(sums)] * 6, axis=0)
    out = dot_nt(both.astype(bf16), matrix)
    return out[0:1] + out[1:2]


def attention_kernel(
    info_ref,
    x0,
    x1,
    x2,
    x3,
    c0,
    c1,
    c2,
    c3,
    w0,
    w1,
    w2,
    w3,
    rot_ref,
    sent_out,
    min_out,
    gb_out,
    ctx_out,
    dqkv_out,
    wd_out,
    wqkv_out,
    xhat_out,
    vec_ref,
    ub_ref,
    sums_ref,
    x_ref,
    cot_ref,
    wqkv_ref,
    wd_ref,
    qb_ref,
    min_ref,
    gb_ref,
    ctx_ref,
    dqkv_ref,
    xhat_ref,
    sent_ref,
    in_sem,
    out_sem,
    weight_sem,
    sent_sem,
    vec_col_ref,
    buf_ref,
    buf_sem,
):
    me = info_ref[64]
    place = info_ref[66]
    parts = []
    for n, (src, step) in enumerate(zip((w0, w1, w2, w3), STEPS)):
        b = (place + 4 - step) % 4
        parts.append(pltpu.make_async_copy(src, buf_ref.at[b], buf_sem.at[n]))
    for copy in parts:
        copy.start()
    loads = []
    for i, (one, other) in enumerate(zip((x0, x1, x2, x3), (c0, c1, c2, c3))):
        loads.append(pltpu.make_async_copy(one, x_ref.at[i], in_sem.at[i, 0]))
        loads.append(pltpu.make_async_copy(other, cot_ref.at[i], in_sem.at[i, 1]))
    for load in loads[:2]:
        load.start()
    for copy in parts:
        copy.wait()
    assemble_a(me, buf_ref, wqkv_ref, wd_ref)
    for load in loads[2:]:
        load.start()
    read_vectors(me, buf_ref, vec_ref, qb_ref, ub_ref)
    weights = [
        pltpu.make_async_copy(wd_ref, wd_out, weight_sem.at[0]),
        pltpu.make_async_copy(wqkv_ref, wqkv_out, weight_sem.at[1]),
    ]
    for copy in weights:
        copy.start()
    stores = (
        (min_ref, min_out),
        (gb_ref, gb_out),
        (ctx_ref, ctx_out),
        (xhat_ref, xhat_out),
        (dqkv_ref, dqkv_out),
    )

    def store(n, r):
        rows = pl.ds(pl.multiple_of(r * ROW, ROW), ROW)
        src, dst = stores[n]
        return pltpu.make_async_copy(src.at[rows, :], dst.at[rows, :], out_sem.at[n, r])

    sums_ref[...] = jnp.zeros_like(sums_ref)

    @pl.loop(0, TP)
    def _(r):
        pltpu.make_async_copy(x0, x_ref.at[r], in_sem.at[r, 0]).wait()
        pltpu.make_async_copy(c0, cot_ref.at[r], in_sem.at[r, 1]).wait()
        here = pl.ds(pl.multiple_of(r * ROW, ROW), ROW)
        xhat, _ = normalize(x_ref[r].astype(f32))
        xhat_ref[here, :] = xhat.astype(bf16)
        attn_in = (xhat * vec_ref[0:1] + vec_ref[1:2]).astype(bf16)
        min_ref[here, :] = (xhat * vec_ref[2:3] + vec_ref[3:4]).astype(bf16)
        qkv = dot(attn_in, wqkv_ref[...]) + qb_ref[...]
        d = me ^ ((r & 1) * 2 + r // 2)
        base = (d * 2 + info_ref[65]) * SEGS
        ends, end = [], 0
        for j in range(SEGS - 1):
            end = end + info_ref[base + j]
            ends.append(end)
        rows = lax.broadcasted_iota(jnp.int32, (ROW, 1), 0)
        cols = lax.broadcasted_iota(jnp.int32, (1, ROW), 1)
        row_doc = sum([(rows >= e).astype(jnp.int32) for e in ends])
        col_doc = sum([(cols >= e).astype(jnp.int32) for e in ends])
        allowed = (row_doc == col_doc) & (rows <= cols)
        start = jnp.zeros_like(rows)
        for e in ends:
            start = jnp.maximum(start, jnp.where(rows >= e, e, 0))
        kept = jnp.where(rows < ends[-1], cot_ref[r].astype(f32), 0.0)
        gb = kept.astype(bf16)
        gb_ref[here, :] = gb
        dctx = dot_nt(gb, wd_ref[...]).astype(bf16)
        chosen = ((rows - start) == cols).astype(f32).astype(bf16)
        table = dot(chosen, rot_ref[...])
        pair = lambda n: table[:, n * 256 : n * 256 + 128] + table[:, n * 256 + 128 : n * 256 + 256]
        cosine, left, right = [jnp.concatenate([pair(n)] * 2, axis=1) for n in range(3)]
        scale = HEAD_DIM**-0.5
        q = (turn(qkv[:, 0:256], cosine, left, right).astype(bf16).astype(f32) * scale).astype(bf16)
        k = turn(qkv[:, 256:512], cosine, left, right).astype(bf16)
        v = qkv[:, 512:768].astype(bf16)
        lanes = lax.broadcasted_iota(jnp.int32, (1, 256), 1) // HEAD_DIM
        ctx, dq, dk, dv = [jnp.zeros((ROW, 256), f32)] * 4
        heads = range(LOCAL_HEADS)
        only = [(lanes == h).astype(f32).astype(bf16) for h in heads]
        qs, dcs = [q * m for m in only], [dctx * m for m in only]
        s_all = dot_nt(k, jnp.concatenate(qs, axis=0))
        dp_all = dot_nt(v, jnp.concatenate(dcs, axis=0))
        cut = [slice(h * ROW, (h + 1) * ROW) for h in heads]
        scores = [jnp.where(allowed, s_all[:, c], -1000000000.0) for c in cut]
        dprobs = [dp_all[:, c] for c in cut]
        probs = []
        for h in heads:
            shifted = jnp.exp(scores[h] - jnp.max(scores[h], axis=0, keepdims=True))
            probs.append(shifted * (1.0 / jnp.sum(shifted, axis=0, keepdims=True)))
        lows = [p.astype(bf16) for p in probs]
        ds = []
        for h in heads:
            inner = jnp.sum(dprobs[h] * probs[h], axis=0, keepdims=True)
            ds.append((probs[h] * (dprobs[h] - inner)).astype(bf16))
        p_all = jnp.concatenate(lows, axis=0)
        ds_all = jnp.concatenate(ds, axis=0)
        ctx = dot_tn(p_all, jnp.concatenate([v * m for m in only], axis=0))
        dq = dot_tn(ds_all, jnp.concatenate([k * m for m in only], axis=0))
        dv = dot(jnp.concatenate(lows, axis=1), jnp.concatenate(dcs, axis=0))
        dk = dot(jnp.concatenate(ds, axis=1), jnp.concatenate(qs, axis=0))
        ctx_ref[here, :] = ctx.astype(bf16)
        dqs = turn(dq * scale, cosine, -left, -right)
        dks = turn(dk, cosine, -left, -right)
        dqkv = jnp.concatenate([dqs, dks, dv], axis=1).astype(bf16)
        dqkv_ref[here, :] = dqkv

        @pl.when(r == 0)
        def _():
            sums_ref[0:1, :] = jnp.sum(kept, axis=0, keepdims=True)

        sums_ref[1:2, 0:QC] += jnp.sum(dqkv.astype(f32), axis=0, keepdims=True)
        for n in range(5):
            store(n, r).start()

    c = me % 2
    sums_ref[3:4, :] = through(sums_ref[1:2, 0:QC], wqkv_ref[...])
    columns = jnp.transpose(vec_ref[...])
    vec_col_ref[...] = columns

    def sent(d, n):
        rows = pl.ds(pl.multiple_of(d * 48, 16), 48)
        if n == 1:
            rows = pl.ds(pl.multiple_of(192 + d * 16, 16), 16)
        return pltpu.make_async_copy(
            sent_ref.at[:, :, rows, :], sent_out.at[:, :, rows, :], sent_sem.at[d, n]
        )

    @pl.loop(0, 4)
    def _(d):
        raw = dot_tn(xhat_ref[:, tile(d)], dqkv_ref[...])
        gain, bias = vec_col_ref[tile(d), 0:1], vec_col_ref[tile(d), 1:2]
        qkv_grad = (raw * gain + bias * sums_ref[1:2, 0:QC]).astype(bf16)
        sums_ref[2:3, tile(d)] = row_sums(raw * wqkv_ref[tile(d), :].astype(f32))
        dense_grad = dot_tn(ctx_ref[...], gb_ref[:, tile(d)]).astype(bf16)
        base = pl.multiple_of(d * 48, 16)
        dense_base = pl.multiple_of(192 + d * 16, 16)
        for y in range(4):
            for x in range(4):
                b, a = swapped(y, x, c)
                at = slice((y * 4 + x) * 16, (y * 4 + x + 1) * 16)
                for p in range(3):
                    sent_ref[b, a, pl.ds(base + p * 16, 16), :] = qkv_grad[
                        at, p * 256 : (p + 1) * 256
                    ]
                sent_ref[b, a, pl.ds(dense_base, 16), :] = dense_grad[at]
        sent(d, 0).start()
        sent(d, 1).start()

    for copy in weights:
        copy.wait()

    @pl.loop(0, 4)
    def _(i):
        for n in range(5):
            store(n, i).wait()
        sent(i, 0).wait()
        sent(i, 1).wait()


def attention(info, xs, cots, blocks):
    tokens = TP * ROW
    dma = pltpu.SemaphoreType.DMA
    return call(
        attention_kernel,
        [
            shaped(4, 4, 256, 256),
            shaped(tokens, D),
            shaped(tokens, D),
            shaped(tokens, 256),
            shaped(tokens, QC),
            shaped(D // TP, D),
            shaped(D, QC),
            shaped(tokens, D),
            shaped(8, D, dtype=f32),
            shaped(1, HC, dtype=f32),
            shaped(8, D, dtype=f32),
        ],
        info,
        *xs,
        *cots,
        *blocks,
        jnp.asarray(rotary_tables()),
        places="s" + "h" * 12 + "v",
        outs="h" * 8 + "vvv",
        scratch=[
            pltpu.VMEM((TP, ROW, D), bf16),
            pltpu.VMEM((TP, ROW, D), bf16),
            pltpu.VMEM((D, QC), bf16),
            pltpu.VMEM((D // TP, D), bf16),
            pltpu.VMEM((1, QC), f32),
            pltpu.VMEM((tokens, D), bf16),
            pltpu.VMEM((tokens, D), bf16),
            pltpu.VMEM((tokens, 256), bf16),
            pltpu.VMEM((tokens, QC), bf16),
            pltpu.VMEM((tokens, D), bf16),
            pltpu.VMEM((4, 4, 256, 256), bf16),
            dma((4, 2)),
            dma((5, 4)),
            dma((2,)),
            dma((4, 2)),
            pltpu.VMEM((D, 8), f32),
            pltpu.VMEM((4, 1024 + IMAGE, 256), bf16),
            dma((4,)),
        ],
        flops=6e9,
        nbytes=2e7,
        trans=1e6,
    )


def mlp_kernel(
    info_ref,
    w0,
    w1,
    w2,
    w3,
    min_in,
    gb_in,
    xhat_in,
    ub_ref,
    vec_ref,
    sums_a_ref,
    sent_out,
    hidden_out,
    dpre_out,
    wup_out,
    wdown_out,
    buf_ref,
    min_ref,
    gb_ref,
    wup_ref,
    wdown_ref,
    hidden_ref,
    dpre_ref,
    sent_ref,
    xhat_ref,
    sums_ref,
    image_ref,
    parts_ref,
    vec_col_ref,
    buf_sem,
    in_sem,
    out_sem,
    weight_sem,
    sent_sem,
    image_sem,
):
    me, place = info_ref[64], info_ref[66]
    c = me % 2
    parts = []
    for n, (src, step) in enumerate(zip((w0, w1, w2, w3), STEPS)):
        b = (place + 4 - step) % 4
        parts.append(pltpu.make_async_copy(src, buf_ref.at[b], buf_sem.at[n]))

    def load(t, n):
        src, dst = ((min_in, min_ref), (gb_in, gb_ref), (xhat_in, xhat_ref))[n]
        return pltpu.make_async_copy(src.at[tile(t), :], dst.at[tile(t), :], in_sem.at[t, n])

    for part in parts:
        part.start()
    for t in range(4):
        for n in range(2):
            load(t, n).start()
    for part in parts:
        part.wait()
    for t in range(4):
        load(t, 2).start()
    assemble_b(me, buf_ref, wup_ref, wdown_ref)
    weights = [
        pltpu.make_async_copy(wup_ref, wup_out, weight_sem.at[0]),
        pltpu.make_async_copy(wdown_ref, wdown_out, weight_sem.at[1]),
    ]
    for copy in weights:
        copy.start()
    sums_ref[...] = jnp.zeros_like(sums_ref)

    def store(t, n):
        src, dst = ((hidden_ref, hidden_out), (dpre_ref, dpre_out))[n]
        return pltpu.make_async_copy(src.at[tile(t), :], dst.at[tile(t), :], out_sem.at[t, n])

    @pl.loop(0, TP)
    def _(tn):
        t = tile(tn)
        load(tn, 0).wait()
        load(tn, 1).wait()

        def products(n):
            at = slice(n * 256, (n + 1) * 256)
            pre = dot(min_ref[t, :], wup_ref[:, at]) + ub_ref[:, at]
            return pre, dot_nt(gb_ref[t, :], wdown_ref[at, :])

        ahead = products(0)
        for n in range(4):
            at = slice(n * 256, (n + 1) * 256)
            pre, back = ahead
            if n < 3:
                ahead = products(n + 1)
            size = jnp.abs(pre) * 0.7071067811865476
            bell = jnp.exp(-0.5 * pre * pre)
            s = 1.0 / (1.0 + 0.3275911 * size)
            poly = s * (
                0.127414796
                + s * (-0.142248368 + s * (0.7107068705 + s * (-0.7265760135 + s * 0.5307027145)))
            )
            tail = poly * bell
            cumul = jnp.where(pre >= 0.0, 1.0 - tail, tail)
            hidden_ref[t, at] = (pre * cumul).astype(bf16)
            dpre = (back * (cumul + pre * (bell * 0.3989422804014327))).astype(bf16)
            dpre_ref[t, at] = dpre
            sums_ref[0:1, at] += jnp.sum(dpre.astype(f32), axis=0, keepdims=True)
        store(tn, 0).start()
        store(tn, 1).start()

    @pl.loop(0, 4)
    def _(y):
        grad = dot_tn(hidden_ref[:, tile(y)], gb_ref[...]).astype(bf16)
        for x in range(4):
            b, a = swapped(y, x, c)
            for cg in range(4):
                sent_ref[b, a, 256 + cg * 64 : 256 + (cg + 1) * 64, :] = grad[
                    x * 64 : (x + 1) * 64, cg * 256 : (cg + 1) * 256
                ]

    def sent(a, rows, n):
        base = a * 512 + rows.start
        return pltpu.make_async_copy(
            sent_ref.at[:, a, rows, :],
            sent_out.at[:, pl.ds(pl.multiple_of(base, 16), rows.size), :],
            sent_sem.at[a, n],
        )

    for a in range(4):
        sent(a, pl.ds(256, 256), 4).start()

    sums_ref[2:3, :] = through(sums_ref[0:1, :], wup_ref[...])
    vec_col_ref[...] = jnp.transpose(vec_ref[...])
    for t in range(4):
        load(t, 2).wait()

    def above(a, d):
        return sent(a, pl.ds(pl.multiple_of(d * 64, 64), 64), d)

    @pl.loop(0, 4)
    def _(d):
        raw = dot_tn(xhat_ref[:, tile(d)], dpre_ref[...])
        gain, bias = vec_col_ref[tile(d), 2:3], vec_col_ref[tile(d), 3:4]
        grad = (raw * gain + bias * sums_ref[0:1, :]).astype(bf16)
        sums_ref[1:2, tile(d)] = row_sums(raw * wup_ref[tile(d), :].astype(f32))
        for y in range(4):
            for x in range(4):
                b, a = swapped(y, x, c)
                at = slice((y * 4 + x) * 16, (y * 4 + x + 1) * 16)
                for cg in range(4):
                    row = pl.multiple_of(d * 64 + cg * 16, 16)
                    sent_ref[b, a, pl.ds(row, 16), :] = grad[at, cg * 256 : (cg + 1) * 256]
        for a in range(4):
            above(a, d).start()

    image_ref[...] = jnp.zeros_like(image_ref)

    def put(row, ref, line, count):
        for i in range(count):
            image_ref[pl.ds(row + i, 1), :] = ref[line : line + 1, i * 256 : (i + 1) * 256]

    put(0, sums_a_ref, 2, 4)
    put(4, sums_a_ref, 3, 4)
    put(8, sums_ref, 1, 4)
    put(12, sums_ref, 2, 4)
    for p in range(3):
        image_ref[pl.ds(16 + p * 4 + me, 1), :] = sums_a_ref[1:2, p * 256 : (p + 1) * 256]
    put(28, sums_a_ref, 0, 4)
    put(32 + 4 * me, sums_ref, 0, 4)
    put(48, sums_a_ref, 0, 4)
    image = image_ref[...]
    high = image.astype(bf16)
    parts_ref[0:IMAGE, :] = high
    parts_ref[IMAGE : 2 * IMAGE, :] = (image - high.astype(f32)).astype(bf16)
    images = [
        pltpu.make_async_copy(parts_ref, sent_out.at[b, pl.ds(2048, 2 * IMAGE), :], image_sem.at[b])
        for b in range(4)
    ]
    for copy in images:
        copy.start()
    for copy in weights:
        copy.wait()
    for i in range(TP):
        store(i, 0).wait()
        store(i, 1).wait()
        for n in range(4):
            above(i, n).wait()
        sent(i, pl.ds(256, 256), 4).wait()
    for copy in images:
        copy.wait()


def mlp(info, blocks, mlp_in, gb, xhat, ub, vec, sums):
    tokens = TP * ROW
    dma = pltpu.SemaphoreType.DMA
    return call(
        mlp_kernel,
        [
            shaped(4, 2048 + 2 * IMAGE, 256),
            shaped(tokens, HC),
            shaped(tokens, HC),
            shaped(D, HC),
            shaped(HC, D),
        ],
        info,
        *blocks,
        mlp_in,
        gb,
        xhat,
        ub,
        vec,
        sums,
        places="s" + "h" * 7 + "vvv",
        outs="h" * 5,
        scratch=[
            pltpu.VMEM((4, 2048, 256), bf16),
            pltpu.VMEM((tokens, D), bf16),
            pltpu.VMEM((tokens, D), bf16),
            pltpu.VMEM((D, HC), bf16),
            pltpu.VMEM((HC, D), bf16),
            pltpu.VMEM((tokens, HC), bf16),
            pltpu.VMEM((tokens, HC), bf16),
            pltpu.VMEM((4, 4, 512, 256), bf16),
            pltpu.VMEM((tokens, D), bf16),
            pltpu.VMEM((8, D), f32),
            pltpu.VMEM((IMAGE, 256), f32),
            pltpu.VMEM((2 * IMAGE, 256), bf16),
            pltpu.VMEM((D, 8), f32),
            dma((4,)),
            dma((4, 3)),
            dma((4, 2)),
            dma((2,)),
            dma((4, 5)),
            dma((4,)),
        ],
        flops=9e9,
        nbytes=2e7,
        trans=2e6,
    )


def outputs_kernel(
    ctx_in,
    hidden_in,
    dqkv_in,
    dpre_in,
    wd_in,
    wdown_in,
    wqkv_in,
    wup_in,
    vec_ref,
    theirs_out,
    mine_out,
    ctx_ref,
    hidden_ref,
    dqkv_ref,
    dpre_ref,
    wd_ref,
    wdown_ref,
    wqkv_ref,
    wup_ref,
    both_ref,
    weight_sem,
    in_sem,
    out_sem,
):
    pairs = ((wqkv_in, wqkv_ref), (wup_in, wup_ref), (wd_in, wd_ref), (wdown_in, wdown_ref))
    weights = [
        pltpu.make_async_copy(src, dst, weight_sem.at[i]) for i, (src, dst) in enumerate(pairs)
    ]
    inputs = (
        (dqkv_in, dqkv_ref),
        (dpre_in, dpre_ref),
        (ctx_in, ctx_ref),
        (hidden_in, hidden_ref),
    )

    def load(t, n):
        src, dst = inputs[n]
        return pltpu.make_async_copy(src.at[tile(t), :], dst.at[tile(t), :], in_sem.at[t, n])

    def finished(i, n):
        dst = (theirs_out, mine_out)[n]
        return pltpu.make_async_copy(both_ref.at[i], dst.at[i - 2 * n], out_sem.at[i])

    for i in range(TP):
        for n in range(4):
            load((i + 2) % 4, n).start()
            if i == 0:
                weights[n].start()
    for weight in weights:
        weight.wait()

    @pl.loop(0, TP)
    def _(i):
        t = (i + 2) % 4
        for n in range(4):
            load(t, n).wait()
        here = tile(t)
        dattn = dot_nt(dqkv_ref[here, :], wqkv_ref[...])
        dmlp = dot_nt(dpre_ref[here, :], wup_ref[...])
        both_ref[i, 1] = (dattn * vec_ref[0:1] + dmlp * vec_ref[2:3]).astype(bf16)
        forward = dot(ctx_ref[here, :], wd_ref[...]) + dot(hidden_ref[here, :], wdown_ref[...])
        both_ref[i, 0] = forward.astype(bf16)

        @pl.when(i < 2)
        def _():
            finished(i, 0).start()

        @pl.when(i >= 2)
        def _():
            finished(i, 1).start()

    for i in range(TP):
        finished(i, i // 2).wait()


def outputs(ctx, hidden, dqkv, dpre, wd, wdown, wqkv, wup, vec):
    tokens = TP * ROW
    dma = pltpu.SemaphoreType.DMA
    return call(
        outputs_kernel,
        [shaped(2, 2, ROW, D), shaped(2, 2, ROW, D)],
        ctx,
        hidden,
        dqkv,
        dpre,
        wd,
        wdown,
        wqkv,
        wup,
        vec,
        places="h" * 8 + "v",
        outs="hh",
        scratch=[
            pltpu.VMEM((tokens, 256), bf16),
            pltpu.VMEM((tokens, HC), bf16),
            pltpu.VMEM((tokens, QC), bf16),
            pltpu.VMEM((tokens, HC), bf16),
            pltpu.VMEM((D // TP, D), bf16),
            pltpu.VMEM((HC, D), bf16),
            pltpu.VMEM((D, QC), bf16),
            pltpu.VMEM((D, HC), bf16),
            pltpu.VMEM((TP, 2, ROW, D), bf16),
            dma((4,)),
            dma((4, 4)),
            dma((4,)),
        ],
        flops=6.5e9,
        nbytes=1.6e7,
    )


def half_kernel(a0_ref, b0_ref, a1_ref, b1_ref, kept_ref, send_ref):
    kept_ref[...] = a0_ref[...].astype(f32) + b0_ref[...].astype(f32)
    send_ref[...] = (a1_ref[...].astype(f32) + b1_ref[...].astype(f32)).astype(bf16)


def half_sum(mine, got):
    mine, got = in_hbm(mine), in_hbm(got)
    first = pl.BlockSpec((1, 1, ROW // 2, D), lambda n, k: (0, n, k, 0))
    second = pl.BlockSpec((1, 1, ROW // 2, D), lambda n, k: (1, n, k, 0))
    out = pl.BlockSpec((1, 1, ROW // 2, D), lambda n, k: (0, n, k, 0))
    return pl.pallas_call(
        half_kernel,
        grid=(2, 2),
        in_specs=[first, first, second, second],
        out_specs=[out, out],
        out_shape=[pltpu.HBM((1, 2, ROW, D), f32), pltpu.HBM((1, 2, ROW, D), bf16)],
        compiler_params=pltpu.CompilerParams(vmem_limit_bytes=VMEM),
        cost_estimate=pl.CostEstimate(flops=0, bytes_accessed=8000000, transcendentals=0),
    )(mine, got, mine, got)


def close_kernel(len_ref, x_ref, cot_ref, kept_ref, got_ref, vec_ref, out_ref, grad_ref):
    x = x_ref[...].astype(f32)
    out_ref[...] = (x + kept_ref[0, 0] + got_ref[0, 0].astype(f32) + vec_ref[4:5]).astype(bf16)
    e = kept_ref[0, 1] + got_ref[0, 1].astype(f32)
    xhat, inv_std = normalize(x)
    mean_e = jnp.mean(e, axis=-1, keepdims=True)
    mean_ex = jnp.mean(e * xhat, axis=-1, keepdims=True)
    used = sum([len_ref[0, j] for j in range(SEGS - 1)])
    rows = pl.program_id(0) * x.shape[0] + lax.broadcasted_iota(jnp.int32, (x.shape[0], 1), 0)
    kept = jnp.where(rows < used, cot_ref[...].astype(f32), 0.0)
    grad_ref[...] = kept + inv_std * (e - mean_e - xhat * mean_ex)


def close(lengths, x, cot, kept, got, vec):
    row = pl.BlockSpec((ROW // 4, D), lambda k: (k, 0))
    both = pl.BlockSpec((1, 2, ROW // 4, D), lambda k: (0, 0, k, 0))
    return pl.pallas_call(
        close_kernel,
        grid=(4,),
        in_specs=[SMEM_SPEC, row, row, both, both, pl.BlockSpec((8, D), lambda k: (0, 0))],
        out_specs=[row, row],
        out_shape=[pltpu.HBM((ROW, D), bf16), pltpu.HBM((ROW, D), f32)],
        compiler_params=pltpu.CompilerParams(vmem_limit_bytes=VMEM),
        cost_estimate=pl.CostEstimate(flops=0, bytes_accessed=6000000, transcendentals=0),
    )(lengths, *[in_hbm(v) for v in (x, cot, kept, got)], vec)


def add_early_kernel(a_ref, out_ref):
    out_ref[0] = sum([a_ref[i, 0].astype(f32) for i in range(4)]).astype(bf16)


def add_early(sent_a):
    return pl.pallas_call(
        add_early_kernel,
        grid=(4,),
        in_specs=[pl.BlockSpec((4, 1, 256, 256), lambda a: (0, a, 0, 0))],
        out_specs=pl.BlockSpec((1, 256, 256), lambda a: (a, 0, 0)),
        out_shape=pltpu.HBM((4, 256, 256), bf16),
        compiler_params=pltpu.CompilerParams(vmem_limit_bytes=VMEM),
        cost_estimate=pl.CostEstimate(flops=0, bytes_accessed=3000000, transcendentals=0),
    )(in_hbm(sent_a))


def add_kernel(place_ref, early_ref, b_ref, image_ref, o0, o1, o2, o3, sums_ref, both_ref, sem):
    n = pl.program_id(0)
    total = sum([b_ref[i].astype(f32) for i in range(4)]).astype(bf16)

    @pl.when(n == 0)
    def _():
        image = sum([image_ref[i].astype(f32) for i in range(4)])
        image = image[:IMAGE] + image[IMAGE:]
        high = image.astype(bf16)
        sums_ref[0:IMAGE, :] = high
        sums_ref[IMAGE : 2 * IMAGE, :] = (image - high.astype(f32)).astype(bf16)

    both_ref[n, 0:256, :] = early_ref[0]
    both_ref[n, 256:768, :] = total
    both_ref[n, 768 : 768 + 2 * IMAGE, :] = sums_ref[...]
    copies = [
        pltpu.make_async_copy(both_ref.at[k], out, sem.at[k]) for k, out in enumerate((o0, o1, o2, o3))
    ]
    for k, copy in enumerate(copies):
        pl.when(n == k)(copy.start)

    @pl.when(n == 3)
    def _():
        for copy in copies:
            copy.wait()


def step_of(n):
    return jnp.where(n < 2, n, 5 - n)


def add(place, early, sent_b):
    rows = 768 + 2 * IMAGE
    sent_b = in_hbm(sent_b)
    return pl.pallas_call(
        add_kernel,
        grid_spec=pltpu.PrefetchScalarGridSpec(
            num_scalar_prefetch=1,
            grid=(4,),
            in_specs=[
                pl.BlockSpec((1, 256, 256), lambda n, p: ((p[0] + step_of(n)) % 4, 0, 0)),
                pl.BlockSpec((4, 512, 256), lambda n, p: (0, (p[0] + step_of(n)) % 4, 0)),
                pl.BlockSpec((4, 2 * IMAGE, 256), lambda n, p: (0, 2048 // (2 * IMAGE), 0)),
            ],
            out_specs=[HBM_SPEC] * 4,
            scratch_shapes=[
                pltpu.VMEM((2 * IMAGE, 256), bf16),
                pltpu.VMEM((4, rows, 256), bf16),
                pltpu.SemaphoreType.DMA((4,)),
            ],
        ),
        out_shape=[pltpu.HBM((rows, 256), bf16)] * 4,
        compiler_params=pltpu.CompilerParams(vmem_limit_bytes=VMEM),
        cost_estimate=pl.CostEstimate(flops=0, bytes_accessed=6000000, transcendentals=0),
    )(place, in_hbm(early), sent_b, sent_b)


LAST = QC + HC + 4 * 256


def image_rows(d):
    return [start + d for start in STARTS[:4]] + [28 + d, 48 + d] + [
        32 + 4 * d + i for i in range(4)
    ] + [16 + 3 * d + i for i in range(3)]


def part_kernel(far_ref, r0, r1, r2, r3, slots_ref, keep_ref, send_ref, total_ref, rows_ref):
    far = far_ref[0]
    total_ref[...] = sum([ref[...].astype(f32) for ref in (r0, r1, r2, r3)])
    rows_ref[...] = jnp.zeros_like(rows_ref)
    for d in range(4):
        for i, row in enumerate(image_rows(d)):
            high = total_ref[768 + row : 769 + row, :]
            low = total_ref[768 + IMAGE + row : 769 + IMAGE + row, :]
            rows_ref[d, i : i + 1, :] = high + low
        image = rows_ref[d]
        high = image.astype(bf16)
        low = (image - high.astype(f32)).astype(bf16)
        for zh in range(2):
            s = d * 2 + zh
            for p in range(3):
                row = (d * 3 + p) * 16 + zh * 8
                slots_ref[s, :, p * 256 : (p + 1) * 256] = total_ref[row : row + 8, :].astype(bf16)
            for cg in range(4):
                row = 256 + (d * 4 + cg) * 16 + zh * 8
                at = QC + cg * 256
                slots_ref[s, :, at : at + 256] = total_ref[row : row + 8, :].astype(bf16)
            for n, block in enumerate((high[:8], high[8:], low[:8], low[8:])):
                at = QC + HC + n * 256
                slots_ref[s, :, at : at + 256] = block
    for ref, half in ((keep_ref, far), (send_ref, 1 - far)):
        for cg in range(4):
            at = slice(cg * 256, (cg + 1) * 256)
            row = pl.multiple_of(192 + cg * 16 + half * 8, 8)
            ref[32:40, at] = total_ref[pl.ds(row, 8), :].astype(ref.dtype)
            row = pl.multiple_of(512 + cg * 64 + half * 32, 8)
            ref[0:32, at] = total_ref[pl.ds(row, 32), :].astype(ref.dtype)


def part(far, received):
    return call(
        part_kernel,
        [shaped(8, 8, LAST), shaped(40, D, dtype=f32), shaped(40, D)],
        far,
        *received,
        outs="uuu",
        scratch=[pltpu.VMEM((768 + 2 * IMAGE, 256), f32), pltpu.VMEM((4, 16, 256), f32)],
        nbytes=4e6,
    )


def finish_kernel(place_ref, slots_ref, keep_ref, got_ref, qkv_ref, up_ref, dense_ref, down_ref, *rest):
    tiny_refs, image_ref = rest[:8], rest[8]
    image = [jnp.zeros((8, 256), f32)] * 2
    for s in range(8):
        for n in range(4):
            at = QC + HC + n * 256
            image[n % 2] = image[n % 2] + slots_ref[s, :, at : at + 256].astype(f32)
    image_ref[0:8, :] = image[0]
    image_ref[8:16, :] = image[1]
    for d in range(4):
        both = slots_ref[2 * d, :, 0 : QC + HC].astype(f32) + slots_ref[
            2 * d + 1, :, 0 : QC + HC
        ].astype(f32)
        for p in range(3):
            at = p * D + d * 256
            qkv_ref[:, at : at + 256] = both[:, p * 256 : (p + 1) * 256]
        up_ref[:, d * HC : (d + 1) * HC] = both[:, QC:]
    total = keep_ref[...] + got_ref[...].astype(f32)
    dense_ref[...] = total[32:40]
    down_ref[...] = total[0:32]
    p = place_ref[0]
    f = p % 32
    lines = (0, 1, 2, 3, 10 + f * 24 // 256, 4, 6 + f // 8, 5)
    for line, size, ref in zip(lines, SIZES, tiny_refs):
        lane = (p * size) % 256
        values = image_ref[pl.ds(line, 1), :]
        if size == 24:
            values = jnp.concatenate([values, image_ref[pl.ds(line + 1, 1), :]], axis=1)
        ref[...] = pltpu.roll(values, values.shape[1] - lane, 1)[:, :size]


def finish(place, slots, keep, got):
    return call(
        finish_kernel,
        [
            shaped(8, 3 * D, dtype=f32),
            shaped(8, FF, dtype=f32),
            shaped(8, D, dtype=f32),
            shaped(32, D, dtype=f32),
        ]
        + [shaped(1, size, dtype=f32) for size in SIZES],
        place,
        slots,
        keep,
        got,
        scratch=[pltpu.VMEM((16, 256), f32)],
        nbytes=2e6,
    )


def body(
    inputs,
    cotangent,
    lengths,
    norm1_gain,
    norm1_bias,
    norm2_gain,
    norm2_bias,
    qkv_weight,
    qkv_bias,
    dense_weight,
    dense_bias,
    up_weight,
    up_bias,
    down_weight,
    down_bias,
):
    me = lax.axis_index("dp").astype(jnp.int32)
    index = lax.axis_index("fsdp").astype(jnp.int32)
    far = (index % 2)[None]
    me1 = me[None]
    outer, inner = outer_groups(), inner_groups()

    vectors = (
        norm1_gain,
        norm1_bias,
        norm2_gain,
        norm2_bias,
        qkv_bias,
        dense_bias,
        up_bias,
        down_bias,
    )
    slots, pieces = prepare(
        qkv_weight.reshape(8, 3 * D),
        up_weight.reshape(8, FF),
        dense_weight.reshape(8, D),
        down_weight.reshape(32, D),
        lengths,
        vectors,
    )
    far_pieces = flip_far(pieces)
    first = a2a(slots, stack_groups())
    block, lens = spread(index[None], first.reshape(4, 16, SLOT), pieces, far_pieces)
    along_x, along_y = index // 2 % 4, index // 8
    core = me % 2 == 1
    near = jnp.where(core, along_x, along_y)[None]
    deep = jnp.where(core, along_y, along_x)[None]
    info = jnp.concatenate([lens[0], me1, far, near])

    block, x0, c0 = lax.optimization_barrier((block, inputs, cotangent))
    x1, c1 = flip_chip(x0), flip_chip(c0)
    second = gather(block, inner)
    second, x0, c0 = lax.optimization_barrier((second, x0, c0))
    third_a = gather(merge_a(deep, second), outer)
    x2, x3 = flip_core(x0), flip_core(x1)
    c2, c3 = flip_core(c0), flip_core(c1)
    xs, cots = (x0, x1, x2, x3), (c0, c1, c2, c3)
    wide_b, third_a, xs, cots = lax.optimization_barrier(
        (merge_b(deep, second), third_a, xs, cots)
    )
    third_b = gather(wide_b, outer)

    sent_a, mlp_in, gb, ctx, dqkv, wd, wqkv, xhat, vec, up_b, sums = attention(
        info, xs, cots, third_a
    )
    sent_a = a2a(sent_a, outer)
    sent_b, hidden, dpre, wup, wdown = mlp(info, third_b, mlp_in, gb, xhat, up_b, vec, sums)
    sent_b = a2a(sent_b, outer)

    theirs, mine = outputs(ctx, hidden, dqkv, dpre, wd, wdown, wqkv, wup, vec)
    kept, send = half_sum(mine, flip_core(theirs))

    got = flip_chip(send)
    early, send = lax.optimization_barrier((add_early(sent_a), send))
    fourth = scatter(add(deep, early, sent_b), inner)
    fourth, got = lax.optimization_barrier((fourth, got))
    slots, keep, rest = part(far, fourth)
    block_output, input_grad = close(lengths, inputs, cotangent, kept, got, vec)
    place = (me * 32 + index)[None]
    slots, rest, block_output, input_grad = lax.optimization_barrier(
        (a2a(slots, stack_groups()), flip_far(rest), block_output, input_grad)
    )
    results = finish(place, slots, keep, rest)
    flat = [r.reshape(-1) for r in results]
    return (
        block_output,
        input_grad,
        flat[4],
        flat[5],
        flat[6],
        flat[7],
        flat[0],
        flat[8],
        flat[2],
        flat[9],
        flat[1],
        flat[10],
        flat[3],
        flat[11],
    )


def solution(mesh):
    flat = P(("dp", "fsdp"))
    rows = P(("dp", "fsdp"), None)
    return jax.shard_map(
        body,
        mesh=mesh,
        in_specs=(rows,) * 3 + (flat,) * 12,
        out_specs=(rows,) * 2 + (flat,) * 12,
        check_vma=False,
    )
```

```python
import jax
import jax.numpy as jnp
import ml_dtypes
import numpy as np
from jax import lax
from jax.experimental import pallas as pl
from jax.experimental.pallas import tpu as pltpu
from jax.sharding import PartitionSpec as P

D = 1024
HEADS = 16
HEAD_DIM = 64
ROT = 16
FF = 4096
ROW = 256
SEGS = 8
TP = 4
QC = 3 * D // TP
HC = FF // TP
LOCAL_HEADS = HEADS // TP
STRIP = 32
AXES = ("dp", "fsdp")
VMEM = 44 * 1024 * 1024

f32 = jnp.float32
bf16 = jnp.bfloat16


def dev(d, y, x, zh):
    return d * 32 + y * 8 + x * 2 + zh


def outer_groups(flip=0):
    groups = []
    for d in range(4):
        for k in range(4):
            for zh in range(2):
                if d % 2 == flip:
                    groups.append([dev(d, i, k, zh) for i in range(4)])
                else:
                    groups.append([dev(d, k, i, zh) for i in range(4)])
    return groups


def inner_groups():
    return outer_groups(flip=1)


def stack_groups():
    return [
        [dev(d, y, x, zh) for d in range(4) for zh in range(2)] for y in range(4) for x in range(4)
    ]


def plane_groups():
    return [
        [dev(d, y, x, zh) for y in range(4) for x in range(4)] for d in range(4) for zh in range(2)
    ]


def ring(values, groups, step):
    pairs = [(g[i], g[(i + step) % 4]) for g in groups for i in range(4)]
    return lax.ppermute(values, AXES, pairs)


STEPS = (0, 1, 3, 2)


def gather(values, groups):
    return [values] + [ring(values, groups, k) for k in STEPS[1:]]


def scatter(values, groups):
    return [values[0]] + [ring(v, groups, k) for v, k in zip(values[1:], STEPS[1:])]


def a2a(values, groups):
    return lax.all_to_all(values, AXES, 0, 0, tiled=True, axis_index_groups=groups)


def flip_core(values):
    return lax.ppermute(values, "dp", [(0, 1), (1, 0), (2, 3), (3, 2)])


def flip_chip(values):
    return lax.ppermute(values, "dp", [(0, 2), (2, 0), (1, 3), (3, 1)])


def flip_far(values):
    return lax.ppermute(values, "fsdp", [(i, i ^ 1) for i in range(32)])


def dot(left, right):
    return jnp.dot(left, right, preferred_element_type=f32)


def dot_nt(left, right):
    return lax.dot_general(left, right, (((1,), (1,)), ((), ())), preferred_element_type=f32)


def dot_tn(left, right):
    return lax.dot_general(left, right, (((0,), (0,)), ((), ())), preferred_element_type=f32)


def in_hbm(values):
    return pltpu.with_memory_space_constraint(values, pltpu.HBM)


VMEM_SPEC = pl.BlockSpec(memory_space=pltpu.VMEM)
SMEM_SPEC = pl.BlockSpec(memory_space=pltpu.SMEM)
HBM_SPEC = pl.BlockSpec(memory_space=pltpu.HBM)
SPECS = {"a": pl.BlockSpec(memory_space=pl.ANY), "s": SMEM_SPEC, "v": VMEM_SPEC, "u": VMEM_SPEC, "h": HBM_SPEC}


def call(kernel, out_shape, *args, places=None, outs=None, scratch=(), flops=0, nbytes=0, trans=0):
    places = places or "s" + "v" * (len(args) - 1)
    out_specs = jax.tree.map(lambda _: VMEM_SPEC, out_shape)
    if outs is not None:
        out_specs = [SPECS[o] for o in outs]
        out_shape = [
            v if o == "v" else pltpu.HBM(v.shape, v.dtype) for o, v in zip(outs, out_shape)
        ]
    args = [in_hbm(v) if p == "h" else v for p, v in zip(places, args)]
    return pl.pallas_call(
        kernel,
        in_specs=[SPECS[p] for p in places],
        out_specs=out_specs,
        out_shape=out_shape,
        scratch_shapes=list(scratch),
        compiler_params=pltpu.CompilerParams(vmem_limit_bytes=VMEM),
        cost_estimate=pl.CostEstimate(
            flops=int(flops), bytes_accessed=int(nbytes), transcendentals=int(trans)
        ),
    )(*args)


def shaped(*shape, dtype=bf16):
    return jax.ShapeDtypeStruct(shape, dtype)


def normalize(x):
    average = jnp.mean(x, axis=-1, keepdims=True)
    centred = x - average
    inv_std = lax.rsqrt(jnp.mean(centred * centred, axis=-1, keepdims=True) + 1e-05)
    return centred * inv_std, inv_std


STARTS = (0, 4, 8, 12, 16, 28, 32, 48)
SIZES = (8, 8, 8, 8, 24, 8, 32, 8)
IMAGE = 64
LENS = 64
SLOT = QC + HC + 128


def tile(n):
    return pl.ds(pl.multiple_of(n * 256, 256), 256)


def swapped(y, x, c):
    return y + c * (x - y), x + c * (y - x)


def prepare_kernel(
    qkv_ref, up_ref, dense_in, down_in, len_in, n1g, n1b, n2g, n2b, qb, db, ub, dnb,
    out_ref, pieces_ref, tile_ref, *rest
):
    sources = (len_in, n1g, n1b, n2g, n2b, qb, db, ub, dnb)
    holders, sem = rest[:9], rest[9]
    copies = [
        pltpu.make_async_copy(src, dst, sem.at[i])
        for i, (src, dst) in enumerate(zip(sources, holders))
    ]
    for copy in copies:
        copy.start()
    for d in range(4):
        for zh in range(2):
            s = d * 2 + zh
            for p in range(3):
                at = p * D + d * 256
                out_ref[s, :, p * 256 : (p + 1) * 256] = qkv_ref[:, at : at + 256]
            out_ref[s, :, QC : QC + HC] = up_ref[:, d * HC : (d + 1) * HC]
    pieces_ref[0:32, :] = down_in[...]
    pieces_ref[32:40, :] = dense_in[...]
    tile_ref[...] = jnp.zeros_like(tile_ref)
    for copy in copies:
        copy.wait()
    for i, (size, ref) in enumerate(zip(SIZES, holders[1:])):
        tile_ref[i : i + 1, 0:size] = ref[...].astype(f32)
    tile_ref[0:1, LENS : LENS + SEGS] = holders[0][...].astype(f32)
    block = tile_ref[...].astype(bf16)
    for s in range(8):
        out_ref[s, :, QC + HC : SLOT] = block


def prepare(qkv, up, dense, down, lengths, vectors):
    vectors = [v[None, :] for v in vectors]
    return call(
        prepare_kernel,
        [shaped(8, 8, SLOT), shaped(40, D)],
        qkv,
        up,
        dense,
        down,
        lengths,
        *vectors,
        places="vvvv" + "h" * 9,
        scratch=[pltpu.VMEM((8, 128), f32), pltpu.VMEM((1, SEGS), jnp.int32)]
        + [pltpu.VMEM(v.shape, bf16) for v in vectors]
        + [pltpu.SemaphoreType.DMA((9,))],
        nbytes=1e6,
    )


def locate(p, start, size):
    first = p * size
    return start + first // 256, first % 256


def spread_kernel(index_ref, first_ref, mine_ref, theirs_ref, out_ref, lens_ref, image_ref):
    index = index_ref[0]
    far = index % 2 == 1
    mine, theirs = mine_ref[...].astype(f32), theirs_ref[...].astype(f32)
    low, high = jnp.where(far, theirs, mine), jnp.where(far, mine, theirs)
    down = jnp.concatenate([low[:32], high[:32]], axis=0).astype(bf16)
    dense = jnp.concatenate([low[32:], high[32:]], axis=0).astype(bf16)
    image_ref[...] = jnp.zeros_like(image_ref)
    lens = []
    for d in range(4):
        both = first_ref[d, :, QC + HC : SLOT].astype(f32)
        for zh in range(2):
            p = d * 32 + index // 2 * 2 + zh
            tile = both[zh * 8 : zh * 8 + 8]
            lens.append(tile[0:1, LENS : LENS + SEGS])
            for i, (start, size) in enumerate(zip(STARTS, SIZES)):
                row, lane = locate(p, start, size)
                wide = 512 if size == 24 else 256
                blank = jnp.zeros((1, wide - size), f32)
                values = jnp.concatenate([tile[i : i + 1, :size], blank], axis=1)
                values = pltpu.roll(values, lane, 1)
                image_ref[pl.ds(row, 1), :] += values[:, :256]
                if wide == 512:
                    image_ref[pl.ds(row + 1, 1), :] += values[:, 256:]
    lens_ref[...] = jnp.concatenate(lens, axis=1).astype(jnp.int32)
    image = image_ref[...].astype(bf16)
    for d in range(4):
        for p in range(3):
            row = (d * 3 + p) * 16
            out_ref[row : row + 16, :] = first_ref[d, :, p * 256 : (p + 1) * 256]
        for cg in range(4):
            row = 256 + (d * 4 + cg) * 16
            at = QC + cg * 256
            out_ref[row : row + 16, :] = first_ref[d, :, at : at + 256]
    for cg in range(4):
        at = slice(cg * 256, (cg + 1) * 256)
        out_ref[192 + cg * 16 : 208 + cg * 16, :] = dense[:, at]
        out_ref[512 + cg * 64 : 576 + cg * 64, :] = down[:, at]
    out_ref[768 : 768 + IMAGE, :] = image


def spread(index, first, mine, theirs):
    return call(
        spread_kernel,
        [shaped(768 + IMAGE, 256), shaped(1, 64, dtype=jnp.int32)],
        index,
        first,
        mine,
        theirs,
        scratch=[pltpu.VMEM((IMAGE, 256), f32)],
        nbytes=2e6,
    )


def merge_a_kernel(place_ref, b0, b1, b2, b3, out_ref):
    blocks = (b0, b1, b2, b3)
    for block, step in zip(blocks, STEPS):
        a = (place_ref[0] + 4 - step) % 4
        out_ref[tile(a), :] = block[0:256, :]
    total = sum([block[768 : 768 + IMAGE, :].astype(f32) for block in blocks])
    out_ref[1024 : 1024 + IMAGE, :] = total.astype(bf16)


def merge_a(place, blocks):
    return call(
        merge_a_kernel, [shaped(1024 + IMAGE, 256)], place, *blocks, outs="u", nbytes=1e6
    )[0]


def merge_b_kernel(place_ref, b0, b1, b2, b3, out_ref):
    for block, step in zip((b0, b1, b2, b3), STEPS):
        a = (place_ref[0] + 4 - step) % 4
        out_ref[pl.ds(pl.multiple_of(a * 512, 512), 512), :] = block[256:768, :]


def merge_b(place, blocks):
    return call(merge_b_kernel, [shaped(2048, 256)], place, *blocks, outs="u", nbytes=2e6)[0]


def assemble_a(me, buf_ref, wqkv_ref, wd_ref):
    c = me % 2
    for y in range(4):
        for x in range(4):
            b, a = swapped(y, x, c)
            yx = y * 4 + x
            base = a * 256
            for d in range(4):
                for p in range(3):
                    row = pl.multiple_of(base + (d * 3 + p) * 16, 16)
                    wqkv_ref[d * 256 + yx * 16 : d * 256 + yx * 16 + 16, p * 256 : (p + 1) * 256] = (
                        buf_ref[b, pl.ds(row, 16), :]
                    )
            for cg in range(4):
                row = pl.multiple_of(base + 192 + cg * 16, 16)
                wd_ref[yx * 16 : yx * 16 + 16, cg * 256 : (cg + 1) * 256] = buf_ref[
                    b, pl.ds(row, 16), :
                ]


def read_vectors(me, buf_ref, vec_ref, qb_ref, ub_ref):
    image = sum([buf_ref[b, 1024 : 1024 + IMAGE, :].astype(f32) for b in range(4)])

    def long(start):
        return jnp.concatenate([image[start + i : start + i + 1, :] for i in range(4)], axis=1)

    vec_ref[...] = jnp.zeros_like(vec_ref)
    for i in range(4):
        vec_ref[i : i + 1, :] = long(4 * i)
    vec_ref[4:5, :] = long(28) + long(48)
    own = [jnp.where(me == d, 1.0, 0.0) for d in range(4)]
    rows = [sum([image[16 + p * 4 + d : 17 + p * 4 + d] * own[d] for d in range(4)]) for p in range(3)]
    qb_ref[...] = jnp.concatenate(rows, axis=1)
    ub_ref[...] = sum([long(32 + 4 * d) * own[d] for d in range(4)])


def assemble_b(me, buf_ref, wup_ref, wdown_ref):
    c = me % 2
    for y in range(4):
        for x in range(4):
            b, a = swapped(y, x, c)
            yx = y * 4 + x
            base = a * 512
            for d in range(4):
                for cg in range(4):
                    row = pl.multiple_of(base + (d * 4 + cg) * 16, 16)
                    wup_ref[d * 256 + yx * 16 : d * 256 + yx * 16 + 16, cg * 256 : (cg + 1) * 256] = (
                        buf_ref[b, pl.ds(row, 16), :]
                    )
            for cg in range(4):
                row = pl.multiple_of(base + 256 + cg * 64, 16)
                wdown_ref[yx * 64 : yx * 64 + 64, cg * 256 : (cg + 1) * 256] = buf_ref[
                    b, pl.ds(row, 64), :
                ]


def turn(u, cosine, sin_left, sin_right):
    return (
        u * cosine
        + pltpu.roll(u, u.shape[1] - ROT // 2, 1) * sin_left
        + pltpu.roll(u, ROT // 2, 1) * sin_right
    )


def rotary_tables():
    places = np.arange(ROW, dtype=np.float32)
    freqs = (10000.0 ** (-(np.arange(ROT // 2, dtype=np.float32) * 2.0) / ROT)).astype(np.float32)
    angle = (places[:, None] * freqs[None, :]).astype(np.float32)
    cosine, sine = np.cos(angle), np.sin(angle)
    zeros = np.zeros_like(sine)
    rest = np.zeros((ROW, HEAD_DIM - ROT), np.float32)
    parts = [[cosine, cosine, rest + 1.0], [-sine, zeros, rest], [zeros, sine, rest]]
    columns = []
    for part in parts:
        whole = np.tile(np.concatenate(part, axis=1), (1, 2)).astype(np.float32)
        high = whole.astype(ml_dtypes.bfloat16)
        columns += [high, (whole - high.astype(np.float32)).astype(ml_dtypes.bfloat16)]
    return np.concatenate(columns, axis=1)


def row_sums(values):
    total = jnp.sum(values, axis=1, keepdims=True)
    return jnp.transpose(jnp.broadcast_to(total, (256, 128)))[0:1, :]


def through(sums, matrix):
    high = sums.astype(bf16)
    low = (sums - high.astype(f32)).astype(bf16)
    both = jnp.concatenate([high.astype(f32), low.astype(f32)] + [jnp.zeros_like(sums)] * 6, axis=0)
    out = dot_nt(both.astype(bf16), matrix)
    return out[0:1] + out[1:2]


def attention_kernel(
    info_ref,
    x0,
    x1,
    x2,
    x3,
    c0,
    c1,
    c2,
    c3,
    w0,
    w1,
    w2,
    w3,
    rot_in,
    sent_out,
    gb_out,
    ctx_out,
    dqkv_out,
    xhat_out,
    vec_ref,
    ub_ref,
    sums_ref,
    x_ref,
    cot_ref,
    wqkv_ref,
    wd_ref,
    qb_ref,
    gb_ref,
    ctx_ref,
    dqkv_ref,
    xhat_ref,
    sent_ref,
    in_sem,
    out_sem,
    sent_sem,
    vec_col_ref,
    buf_ref,
    buf_sem,
    rot_ref,
    rot_sem,
):
    me = info_ref[64]
    place = info_ref[66]
    parts = []
    for n, (src, step) in enumerate(zip((w0, w1, w2, w3), STEPS)):
        b = (place + 4 - step) % 4
        parts.append(pltpu.make_async_copy(src, buf_ref.at[b], buf_sem.at[n]))
    for copy in parts:
        copy.start()
    loads = []
    for i, (one, other) in enumerate(zip((x0, x1, x2, x3), (c0, c1, c2, c3))):
        loads.append(pltpu.make_async_copy(one, x_ref.at[i], in_sem.at[i, 0]))
        loads.append(pltpu.make_async_copy(other, cot_ref.at[i], in_sem.at[i, 1]))
    for load in loads[:2]:
        load.start()
    for copy in parts:
        copy.wait()
    assemble_a(me, buf_ref, wqkv_ref, wd_ref)
    rotary = pltpu.make_async_copy(rot_in, rot_ref, rot_sem)
    rotary.start()
    for load in loads[2:]:
        load.start()
    read_vectors(me, buf_ref, vec_ref, qb_ref, ub_ref)
    rotary.wait()
    stores = (
        (gb_ref, gb_out),
        (ctx_ref, ctx_out),
        (xhat_ref, xhat_out),
        (dqkv_ref, dqkv_out),
    )

    def store(n, r):
        rows = pl.ds(pl.multiple_of(r * ROW, ROW), ROW)
        src, dst = stores[n]
        return pltpu.make_async_copy(src.at[rows, :], dst.at[rows, :], out_sem.at[n, r])

    sums_ref[...] = jnp.zeros_like(sums_ref)

    @pl.loop(0, TP)
    def _(r):
        pltpu.make_async_copy(x0, x_ref.at[r], in_sem.at[r, 0]).wait()
        pltpu.make_async_copy(c0, cot_ref.at[r], in_sem.at[r, 1]).wait()
        here = pl.ds(pl.multiple_of(r * ROW, ROW), ROW)
        xhat, _ = normalize(x_ref[r].astype(f32))
        xhat_ref[here, :] = xhat.astype(bf16)
        attn_in = (xhat * vec_ref[0:1] + vec_ref[1:2]).astype(bf16)
        qkv = dot(attn_in, wqkv_ref[...]) + qb_ref[...]
        d = me ^ ((r & 1) * 2 + r // 2)
        base = (d * 2 + info_ref[65]) * SEGS
        ends, end = [], 0
        for j in range(SEGS - 1):
            end = end + info_ref[base + j]
            ends.append(end)
        rows = lax.broadcasted_iota(jnp.int32, (ROW, 1), 0)
        cols = lax.broadcasted_iota(jnp.int32, (1, ROW), 1)
        row_doc = sum([(rows >= e).astype(jnp.int32) for e in ends])
        col_doc = sum([(cols >= e).astype(jnp.int32) for e in ends])
        allowed = (row_doc == col_doc) & (rows <= cols)
        start = jnp.zeros_like(rows)
        for e in ends:
            start = jnp.maximum(start, jnp.where(rows >= e, e, 0))
        kept = jnp.where(rows < ends[-1], cot_ref[r].astype(f32), 0.0)
        gb = kept.astype(bf16)
        gb_ref[here, :] = gb
        dctx = dot_nt(gb, wd_ref[...]).astype(bf16)
        chosen = ((rows - start) == cols).astype(f32).astype(bf16)
        table = dot(chosen, rot_ref[...])
        pair = lambda n: table[:, n * 256 : n * 256 + 128] + table[:, n * 256 + 128 : n * 256 + 256]
        cosine, left, right = [jnp.concatenate([pair(n)] * 2, axis=1) for n in range(3)]
        scale = HEAD_DIM**-0.5
        q = (turn(qkv[:, 0:256], cosine, left, right).astype(bf16).astype(f32) * scale).astype(bf16)
        k = turn(qkv[:, 256:512], cosine, left, right).astype(bf16)
        v = qkv[:, 512:768].astype(bf16)
        lanes = lax.broadcasted_iota(jnp.int32, (1, 256), 1) // HEAD_DIM
        ctx, dq, dk, dv = [jnp.zeros((ROW, 256), f32)] * 4
        heads = range(LOCAL_HEADS)
        only = [(lanes == h).astype(f32).astype(bf16) for h in heads]
        qs, dcs = [q * m for m in only], [dctx * m for m in only]
        s_all = dot_nt(k, jnp.concatenate(qs, axis=0))
        dp_all = dot_nt(v, jnp.concatenate(dcs, axis=0))
        cut = [slice(h * ROW, (h + 1) * ROW) for h in heads]
        scores = [jnp.where(allowed, s_all[:, c], -1000000000.0) for c in cut]
        dprobs = [dp_all[:, c] for c in cut]
        probs = []
        for h in heads:
            shifted = jnp.exp(scores[h] - jnp.max(scores[h], axis=0, keepdims=True))
            probs.append(shifted * (1.0 / jnp.sum(shifted, axis=0, keepdims=True)))
        lows = [p.astype(bf16) for p in probs]
        ds = []
        for h in heads:
            inner = jnp.sum(dprobs[h] * probs[h], axis=0, keepdims=True)
            ds.append((probs[h] * (dprobs[h] - inner)).astype(bf16))
        p_all = jnp.concatenate(lows, axis=0)
        ds_all = jnp.concatenate(ds, axis=0)
        ctx = dot_tn(p_all, jnp.concatenate([v * m for m in only], axis=0))
        dq = dot_tn(ds_all, jnp.concatenate([k * m for m in only], axis=0))
        dv = dot(jnp.concatenate(lows, axis=1), jnp.concatenate(dcs, axis=0))
        dk = dot(jnp.concatenate(ds, axis=1), jnp.concatenate(qs, axis=0))
        ctx_ref[here, :] = ctx.astype(bf16)
        dqs = turn(dq * scale, cosine, -left, -right)
        dks = turn(dk, cosine, -left, -right)
        dqkv = jnp.concatenate([dqs, dks, dv], axis=1).astype(bf16)
        dqkv_ref[here, :] = dqkv

        @pl.when(r == 0)
        def _():
            sums_ref[0:1, :] = jnp.sum(kept, axis=0, keepdims=True)

        sums_ref[1:2, 0:QC] += jnp.sum(dqkv.astype(f32), axis=0, keepdims=True)
        for n in range(4):
            store(n, r).start()

    c = me % 2
    sums_ref[3:4, :] = through(sums_ref[1:2, 0:QC], wqkv_ref[...])
    columns = jnp.transpose(vec_ref[...])
    vec_col_ref[...] = columns

    def sent(d, n):
        rows = pl.ds(pl.multiple_of(d * 48, 16), 48)
        if n == 1:
            rows = pl.ds(pl.multiple_of(192 + d * 16, 16), 16)
        return pltpu.make_async_copy(
            sent_ref.at[:, :, rows, :], sent_out.at[:, :, rows, :], sent_sem.at[d, n]
        )

    @pl.loop(0, 4)
    def _(d):
        raw = dot_tn(xhat_ref[:, tile(d)], dqkv_ref[...])
        gain, bias = vec_col_ref[tile(d), 0:1], vec_col_ref[tile(d), 1:2]
        qkv_grad = (raw * gain + bias * sums_ref[1:2, 0:QC]).astype(bf16)
        sums_ref[2:3, tile(d)] = row_sums(raw * wqkv_ref[tile(d), :].astype(f32))
        dense_grad = dot_tn(ctx_ref[...], gb_ref[:, tile(d)]).astype(bf16)
        base = pl.multiple_of(d * 48, 16)
        dense_base = pl.multiple_of(192 + d * 16, 16)
        for y in range(4):
            for x in range(4):
                b, a = swapped(y, x, c)
                at = slice((y * 4 + x) * 16, (y * 4 + x + 1) * 16)
                for p in range(3):
                    sent_ref[b, a, pl.ds(base + p * 16, 16), :] = qkv_grad[
                        at, p * 256 : (p + 1) * 256
                    ]
                sent_ref[b, a, pl.ds(dense_base, 16), :] = dense_grad[at]
        sent(d, 0).start()
        sent(d, 1).start()

    @pl.loop(0, 4)
    def _(i):
        for n in range(4):
            store(n, i).wait()
        sent(i, 0).wait()
        sent(i, 1).wait()


def attention(info, xs, cots, blocks):
    tokens = TP * ROW
    dma = pltpu.SemaphoreType.DMA
    return call(
        attention_kernel,
        [
            shaped(4, 4, 256, 256),
            shaped(tokens, D),
            shaped(tokens, 256),
            shaped(tokens, QC),
            shaped(tokens, D),
            shaped(8, D, dtype=f32),
            shaped(1, HC, dtype=f32),
            shaped(8, D, dtype=f32),
        ],
        info,
        *xs,
        *cots,
        *blocks,
        jnp.asarray(rotary_tables()),
        places="s" + "a" * 12 + "h",
        outs="h" * 5 + "vvv",
        scratch=[
            pltpu.VMEM((TP, ROW, D), bf16),
            pltpu.VMEM((TP, ROW, D), bf16),
            pltpu.VMEM((D, QC), bf16),
            pltpu.VMEM((D // TP, D), bf16),
            pltpu.VMEM((1, QC), f32),
            pltpu.VMEM((tokens, D), bf16),
            pltpu.VMEM((tokens, 256), bf16),
            pltpu.VMEM((tokens, QC), bf16),
            pltpu.VMEM((tokens, D), bf16),
            pltpu.VMEM((4, 4, 256, 256), bf16),
            dma((4, 2)),
            dma((4, 4)),
            dma((4, 2)),
            pltpu.VMEM((D, 8), f32),
            pltpu.VMEM((4, 1024 + IMAGE, 256), bf16),
            dma((4,)),
            pltpu.VMEM((ROW, 768), bf16),
            dma,
        ],
        flops=6e9,
        nbytes=2e7,
        trans=1e6,
    )


def mlp_kernel(
    info_ref,
    w0,
    w1,
    w2,
    w3,
    gb_in,
    xhat_in,
    ub_ref,
    vec_ref,
    sums_a_ref,
    sent_out,
    hidden_out,
    dpre_out,
    buf_ref,
    gb_ref,
    wup_ref,
    wdown_ref,
    hidden_ref,
    dpre_ref,
    sent_ref,
    xhat_ref,
    sums_ref,
    image_ref,
    vec_col_ref,
    min_ref,
    rows_ref,
    turned_ref,
    buf_sem,
    in_sem,
    out_sem,
    sent_sem,
    image_sem,
):
    me, place = info_ref[64], info_ref[66]
    c = me % 2
    parts = []
    for n, (src, step) in enumerate(zip((w0, w1, w2, w3), STEPS)):
        b = (place + 4 - step) % 4
        parts.append(pltpu.make_async_copy(src, buf_ref.at[b], buf_sem.at[n]))

    def load(t, n):
        src, dst = ((gb_in, gb_ref), (xhat_in, xhat_ref))[n]
        return pltpu.make_async_copy(src.at[tile(t), :], dst.at[tile(t), :], in_sem.at[t, n])

    for part in parts:
        part.start()
    for t in range(4):
        for n in range(2):
            load(t, n).start()
    for part in parts:
        part.wait()
    assemble_b(me, buf_ref, wup_ref, wdown_ref)
    sums_ref[...] = jnp.zeros_like(sums_ref)

    vec_col_ref[...] = jnp.transpose(vec_ref[...])
    rows_ref[...] = jnp.zeros_like(rows_ref)

    def store(j, n):
        src, dst = ((hidden_ref, hidden_out), (dpre_ref, dpre_out))[n]
        return pltpu.make_async_copy(src.at[:, tile(j)], dst.at[:, tile(j)], out_sem.at[j, n])

    def sent_up(j):
        rows = pl.ds(pl.multiple_of(j * 64, 64), 64)
        return pltpu.make_async_copy(
            sent_ref.at[:, :, rows, :], sent_out.at[:, :, rows, :], sent_sem.at[j, 4]
        )

    def sent_down(j, x):
        b, a = swapped(j, x, c)
        rows = pl.ds(256, 256)
        return pltpu.make_async_copy(
            sent_ref.at[b, a, rows, :], sent_out.at[b, a, rows, :], sent_sem.at[j, x]
        )

    def hidden_tile(j, t):
        at = pl.ds(t * ROW, ROW)
        pre = dot(min_ref[at, :], wup_ref[:, tile(j)]) + ub_ref[:, tile(j)]
        return pre, dot_nt(gb_ref[at, :], wdown_ref[tile(j), :])

    def activate(j, t, pre, back):
        total = jnp.zeros((8, 256), f32)
        for i in range(0, ROW, STRIP):
            at = pl.ds(t * ROW + i, STRIP)
            a, b = pre[i : i + STRIP], back[i : i + STRIP]
            size = jnp.abs(a) * 0.7071067811865476
            bell = jnp.exp(-0.5 * a * a)
            s = 1.0 / (1.0 + 0.3275911 * size)
            poly = s * (
                0.127414796
                + s * (-0.142248368 + s * (0.7107068705 + s * (-0.7265760135 + s * 0.5307027145)))
            )
            tail = poly * bell
            cumul = jnp.where(a >= 0.0, 1.0 - tail, tail)
            hidden_ref[at, tile(j)] = (a * cumul).astype(bf16)
            dpre = (b * (cumul + a * (bell * 0.3989422804014327))).astype(bf16)
            dpre_ref[at, tile(j)] = dpre
            total += jnp.sum(dpre.astype(f32).reshape(STRIP // 8, 8, 256), axis=0)
        return jnp.sum(total, axis=0, keepdims=True)

    def put_down(j):
        down = dot_tn(hidden_ref[:, tile(j)], gb_ref[...]).astype(bf16)
        for x in range(4):
            b, a = swapped(j, x, c)
            for cg in range(4):
                sent_ref[b, a, 256 + cg * 64 : 256 + (cg + 1) * 64, :] = down[
                    x * 64 : (x + 1) * 64, cg * 256 : (cg + 1) * 256
                ]

    def put_up(j, t, raw):
        row = pl.multiple_of(j * 64 + t * 16, 16)
        sums = sums_ref[0:1, tile(j)]
        for y in range(4):
            for x in range(4):
                b, a = swapped(y, x, c)
                i = (y * 4 + x) * 16
                at = slice(t * 256 + i, t * 256 + i + 16)
                part = raw[i : i + 16]
                product = part * wup_ref[at, tile(j)].astype(f32)
                rows_ref[at, :] += product[:, :128] + product[:, 128:]
                gain, bias = vec_col_ref[at, 2:3], vec_col_ref[at, 3:4]
                sent_ref[b, a, pl.ds(row, 16), :] = (part * gain + bias * sums).astype(bf16)

    def step(j, last=False, first=False):
        if not last:
            total = jnp.zeros((1, 256), f32)
        for t in range(TP):
            if first:
                at = pl.ds(t * ROW, ROW)
                load(t, 0).wait()
                load(t, 1).wait()
                for i in range(0, ROW, 16):
                    strip = pl.ds(t * ROW + i, 16)
                    values = xhat_ref[strip, :].astype(f32)
                    min_ref[strip, :] = (values * vec_ref[2:3] + vec_ref[3:4]).astype(bf16)
                turned_ref[:, at] = jnp.transpose(xhat_ref[at, :])
            if not last:
                pre, back = hidden_tile(j, t)
            if not first:
                if t == 0:
                    put_down(j - 1)
                raw = dot(turned_ref[t * 256 : (t + 1) * 256, :], dpre_ref[:, tile(j - 1)])
            if not last:
                total += activate(j, t, pre, back)
            if not first:
                put_up(j - 1, t, raw)
        if not last:
            sums_ref[0:1, tile(j)] = total
            store(j, 0).start()
            store(j, 1).start()
        if not first:
            sent_up(j - 1).start()
            for x in range(4):
                sent_down(j - 1, x).start()

    step(0, first=True)

    @pl.loop(1, 4)
    def _(j):
        step(j)

    step(4, last=True)
    total = jnp.sum(rows_ref[...], axis=1, keepdims=True)
    sums_ref[1:2, :] = jnp.transpose(jnp.broadcast_to(total, (D, 128)))[0:1, :]
    sums_ref[2:3, :] = through(sums_ref[0:1, :], wup_ref[...])

    image_ref[...] = jnp.zeros_like(image_ref)

    def put(row, ref, line, count):
        for i in range(count):
            image_ref[pl.ds(row + i, 1), :] = ref[line : line + 1, i * 256 : (i + 1) * 256]

    put(0, sums_a_ref, 2, 4)
    put(4, sums_a_ref, 3, 4)
    put(8, sums_ref, 1, 4)
    put(12, sums_ref, 2, 4)
    for p in range(3):
        image_ref[pl.ds(16 + p * 4 + me, 1), :] = sums_a_ref[1:2, p * 256 : (p + 1) * 256]
    put(28, sums_a_ref, 0, 4)
    put(32 + 4 * me, sums_ref, 0, 4)
    put(48, sums_a_ref, 0, 4)
    image = image_ref[...]
    high = image.astype(bf16)
    low = (image - high.astype(f32)).astype(bf16)
    for b in range(4):
        for a in range(4):
            half = (high, low)[a // 2]
            sent_ref[b, a, 512 : 512 + IMAGE // 2, :] = half[a % 2 * 32 : a % 2 * 32 + 32]
    rows = pl.ds(512, IMAGE // 2)
    images = pltpu.make_async_copy(
        sent_ref.at[:, :, rows, :], sent_out.at[:, :, rows, :], image_sem
    )
    images.start()
    for i in range(TP):
        store(i, 0).wait()
        store(i, 1).wait()
        sent_up(i).wait()
        for x in range(4):
            sent_down(i, x).wait()
    images.wait()


def mlp(info, blocks, gb, xhat, ub, vec, sums):
    tokens = TP * ROW
    dma = pltpu.SemaphoreType.DMA
    return call(
        mlp_kernel,
        [
            shaped(4, 4, 512 + IMAGE // 2, 256),
            shaped(tokens, HC),
            shaped(tokens, HC),
        ],
        info,
        *blocks,
        gb,
        xhat,
        ub,
        vec,
        sums,
        places="s" + "a" * 4 + "hhvvv",
        outs="hhh",
        scratch=[
            pltpu.VMEM((4, 2048, 256), bf16),
            pltpu.VMEM((tokens, D), bf16),
            pltpu.VMEM((D, HC), bf16),
            pltpu.VMEM((HC, D), bf16),
            pltpu.VMEM((tokens, HC), bf16),
            pltpu.VMEM((tokens, HC), bf16),
            pltpu.VMEM((4, 4, 512 + IMAGE // 2, 256), bf16),
            pltpu.VMEM((tokens, D), bf16),
            pltpu.VMEM((8, D), f32),
            pltpu.VMEM((IMAGE, 256), f32),
            pltpu.VMEM((D, 8), f32),
            pltpu.VMEM((tokens, D), bf16),
            pltpu.VMEM((D, 128), f32),
            pltpu.VMEM((D, tokens), bf16),
            dma((4,)),
            dma((4, 2)),
            dma((4, 2)),
            dma((4, 5)),
            dma,
        ],
        flops=9e9,
        nbytes=2e7,
        trans=2e6,
    )


def outputs_kernel(
    info_ref,
    ctx_in,
    hidden_in,
    dqkv_in,
    dpre_in,
    a0,
    a1,
    a2,
    a3,
    b0,
    b1,
    b2,
    b3,
    vec_ref,
    theirs_out,
    mine_out,
    ctx_ref,
    hidden_ref,
    dqkv_ref,
    dpre_ref,
    wd_ref,
    wdown_ref,
    wqkv_ref,
    wup_ref,
    both_ref,
    buf_a_ref,
    buf_b_ref,
    weight_sem,
    in_sem,
    out_sem,
):
    me, place = info_ref[64], info_ref[66]
    weights = []
    for n, step in enumerate(STEPS):
        b = (place + 4 - step) % 4
        pairs = (((a0, a1, a2, a3)[n], buf_a_ref), ((b0, b1, b2, b3)[n], buf_b_ref))
        for i, (src, dst) in enumerate(pairs):
            weights.append(pltpu.make_async_copy(src, dst.at[b], weight_sem.at[n, i]))
    inputs = (
        (dqkv_in, dqkv_ref),
        (dpre_in, dpre_ref),
        (ctx_in, ctx_ref),
        (hidden_in, hidden_ref),
    )

    def load(t, n):
        src, dst = inputs[n]
        return pltpu.make_async_copy(src.at[tile(t), :], dst.at[tile(t), :], in_sem.at[t, n])

    def finished(i, n):
        dst = (theirs_out, mine_out)[n]
        return pltpu.make_async_copy(both_ref.at[i], dst.at[i - 2 * n], out_sem.at[i])

    for weight in weights:
        weight.start()
    for i in range(TP):
        for n in range(4):
            load((i + 2) % 4, n).start()
    for weight in weights:
        weight.wait()
    assemble_a(me, buf_a_ref, wqkv_ref, wd_ref)
    assemble_b(me, buf_b_ref, wup_ref, wdown_ref)

    @pl.loop(0, TP)
    def _(i):
        t = (i + 2) % 4
        for n in range(4):
            load(t, n).wait()
        here = tile(t)
        dattn = dot_nt(dqkv_ref[here, :], wqkv_ref[...])
        dmlp = dot_nt(dpre_ref[here, :], wup_ref[...])
        both_ref[i, 1] = (dattn * vec_ref[0:1] + dmlp * vec_ref[2:3]).astype(bf16)
        forward = dot(ctx_ref[here, :], wd_ref[...]) + dot(hidden_ref[here, :], wdown_ref[...])
        both_ref[i, 0] = forward.astype(bf16)

        @pl.when(i < 2)
        def _():
            finished(i, 0).start()

        @pl.when(i >= 2)
        def _():
            finished(i, 1).start()

    for i in range(TP):
        finished(i, i // 2).wait()


def outputs(info, ctx, hidden, dqkv, dpre, blocks_a, blocks_b, vec):
    tokens = TP * ROW
    dma = pltpu.SemaphoreType.DMA
    return call(
        outputs_kernel,
        [shaped(2, 2, ROW, D), shaped(2, 2, ROW, D)],
        info,
        ctx,
        hidden,
        dqkv,
        dpre,
        *blocks_a,
        *blocks_b,
        vec,
        places="s" + "a" * 12 + "v",
        outs="hh",
        scratch=[
            pltpu.VMEM((tokens, 256), bf16),
            pltpu.VMEM((tokens, HC), bf16),
            pltpu.VMEM((tokens, QC), bf16),
            pltpu.VMEM((tokens, HC), bf16),
            pltpu.VMEM((D // TP, D), bf16),
            pltpu.VMEM((HC, D), bf16),
            pltpu.VMEM((D, QC), bf16),
            pltpu.VMEM((D, HC), bf16),
            pltpu.VMEM((TP, 2, ROW, D), bf16),
            pltpu.VMEM((4, 1024 + IMAGE, 256), bf16),
            pltpu.VMEM((4, 2048, 256), bf16),
            dma((4, 2)),
            dma((4, 4)),
            dma((4,)),
        ],
        flops=6.5e9,
        nbytes=1.6e7,
    )


def half_kernel(mine_in, got_in, kept_out, send_out, mine_ref, got_ref, kept_ref, send_ref, in_sem, out_sem):
    loads = []
    for i in (1, 0):
        for n in range(2):
            pair = (
                pltpu.make_async_copy(mine_in.at[i, n], mine_ref.at[i, n], in_sem.at[i, n, 0]),
                pltpu.make_async_copy(got_in.at[i, n], got_ref.at[i, n], in_sem.at[i, n, 1]),
            )
            loads.append((i, n, pair))
            for copy in pair:
                copy.start()
    stores = []
    for i, n, pair in loads:
        for copy in pair:
            copy.wait()
        total = mine_ref[i, n].astype(f32) + got_ref[i, n].astype(f32)
        ref, out = ((kept_ref, kept_out), (send_ref, send_out))[i]
        ref[n] = total.astype(ref.dtype)
        stores.append(pltpu.make_async_copy(ref.at[n], out.at[0, n], out_sem.at[i, n]))
        stores[-1].start()
    for store in stores:
        store.wait()


def half_sum(mine, got):
    dma = pltpu.SemaphoreType.DMA
    return call(
        half_kernel,
        [shaped(1, 2, ROW, D, dtype=f32), shaped(1, 2, ROW, D)],
        mine,
        got,
        places="ha",
        outs="hh",
        scratch=[
            pltpu.VMEM((2, 2, ROW, D), bf16),
            pltpu.VMEM((2, 2, ROW, D), bf16),
            pltpu.VMEM((2, ROW, D), f32),
            pltpu.VMEM((2, ROW, D), bf16),
            dma((2, 2, 2)),
            dma((2, 2)),
        ],
        nbytes=8e6,
    )


def close_kernel(len_ref, x_ref, cot_ref, kept_ref, got_ref, vec_ref, out_ref, grad_ref):
    x = x_ref[...].astype(f32)
    out_ref[...] = (x + kept_ref[0, 0] + got_ref[0, 0].astype(f32) + vec_ref[4:5]).astype(bf16)
    e = kept_ref[0, 1] + got_ref[0, 1].astype(f32)
    xhat, inv_std = normalize(x)
    mean_e = jnp.mean(e, axis=-1, keepdims=True)
    mean_ex = jnp.mean(e * xhat, axis=-1, keepdims=True)
    used = sum([len_ref[0, j] for j in range(SEGS - 1)])
    rows = pl.program_id(0) * x.shape[0] + lax.broadcasted_iota(jnp.int32, (x.shape[0], 1), 0)
    kept = jnp.where(rows < used, cot_ref[...].astype(f32), 0.0)
    grad_ref[...] = kept + inv_std * (e - mean_e - xhat * mean_ex)


def close(lengths, x, cot, kept, got, vec):
    row = pl.BlockSpec((ROW // 4, D), lambda k: (k, 0))
    both = pl.BlockSpec((1, 2, ROW // 4, D), lambda k: (0, 0, k, 0))
    return pl.pallas_call(
        close_kernel,
        grid=(4,),
        in_specs=[SMEM_SPEC, row, row, both, both, pl.BlockSpec((8, D), lambda k: (0, 0))],
        out_specs=[row, row],
        out_shape=[pltpu.HBM((ROW, D), bf16), pltpu.HBM((ROW, D), f32)],
        compiler_params=pltpu.CompilerParams(vmem_limit_bytes=VMEM),
        cost_estimate=pl.CostEstimate(flops=0, bytes_accessed=6000000, transcendentals=0),
    )(lengths, *[in_hbm(v) for v in (x, cot, kept, got)], vec)


def add_early_kernel(a_ref, out_ref):
    out_ref[0] = sum([a_ref[i, 0].astype(f32) for i in range(4)]).astype(bf16)


def add_early(sent_a):
    return pl.pallas_call(
        add_early_kernel,
        grid=(4,),
        in_specs=[pl.BlockSpec((4, 1, 256, 256), lambda a: (0, a, 0, 0))],
        out_specs=pl.BlockSpec((1, 256, 256), lambda a: (a, 0, 0)),
        out_shape=pltpu.HBM((4, 256, 256), bf16),
        compiler_params=pltpu.CompilerParams(vmem_limit_bytes=VMEM),
        cost_estimate=pl.CostEstimate(flops=0, bytes_accessed=3000000, transcendentals=0),
    )(sent_a)


def add_kernel(
    place_ref, early_in, b_in, o0, o1, o2, o3, early_ref, b_ref, image_ref, both_ref, early_sem, b_sem, image_sem, sem
):
    place = place_ref[0]

    def load(n, i):
        a = (place + STEPS[n]) % 4
        return pltpu.make_async_copy(
            b_in.at[i, a, pl.ds(0, 512), :], b_ref.at[n, i], b_sem.at[n, i]
        )

    images = [
        pltpu.make_async_copy(
            b_in.at[i, :, pl.ds(512, IMAGE // 2), :], image_ref.at[i], image_sem.at[i]
        )
        for i in range(4)
    ]
    early = [
        pltpu.make_async_copy(
            early_in.at[(place + step) % 4], early_ref.at[n], early_sem.at[n]
        )
        for n, step in enumerate(STEPS)
    ]
    for copy in images:
        copy.start()
    for n in range(4):
        early[n].start()
        for i in range(4):
            load(n, i).start()
    for copy in images:
        copy.wait()
    image = sum([image_ref[i].astype(f32) for i in range(4)]).reshape(2, IMAGE, 256)
    image = image[0] + image[1]
    high = image.astype(bf16)
    low = (image - high.astype(f32)).astype(bf16)
    stores = [
        pltpu.make_async_copy(both_ref.at[n], out, sem.at[n]) for n, out in enumerate((o0, o1, o2, o3))
    ]
    for n in range(4):
        both_ref[n, 768 : 768 + IMAGE, :] = high
        both_ref[n, 768 + IMAGE : 768 + 2 * IMAGE, :] = low
        early[n].wait()
        both_ref[n, 0:256, :] = early_ref[n]
        for i in range(4):
            load(n, i).wait()
        total = sum([b_ref[n, i].astype(f32) for i in range(4)])
        both_ref[n, 256:768, :] = total.astype(bf16)
        stores[n].start()
    for store in stores:
        store.wait()


def add(place, early, sent_b):
    rows = 768 + 2 * IMAGE
    dma = pltpu.SemaphoreType.DMA
    return call(
        add_kernel,
        [shaped(rows, 256)] * 4,
        place,
        early,
        sent_b,
        places="shh",
        outs="hhhh",
        scratch=[
            pltpu.VMEM((4, 256, 256), bf16),
            pltpu.VMEM((4, 4, 512, 256), bf16),
            pltpu.VMEM((4, 4, IMAGE // 2, 256), bf16),
            pltpu.VMEM((4, rows, 256), bf16),
            dma((4,)),
            dma((4, 4)),
            dma((4,)),
            dma((4,)),
        ],
        nbytes=6e6,
    )


LAST = QC + HC + 4 * 256


def image_rows(d):
    return [start + d for start in STARTS[:4]] + [28 + d, 48 + d] + [
        32 + 4 * d + i for i in range(4)
    ] + [16 + 3 * d + i for i in range(3)]


def part_kernel(
    far_ref, r0, r1, r2, r3, slots_ref, keep_ref, send_ref, total_ref, rows_ref, in_ref, sem
):
    far = far_ref[0]
    loads = [
        pltpu.make_async_copy(r, in_ref.at[i], sem.at[i]) for i, r in enumerate((r0, r1, r2, r3))
    ]
    for load in loads:
        load.start()
    for load in loads:
        load.wait()
    total_ref[...] = sum([in_ref[i].astype(f32) for i in range(4)])
    rows_ref[...] = jnp.zeros_like(rows_ref)
    for d in range(4):
        for i, row in enumerate(image_rows(d)):
            high = total_ref[768 + row : 769 + row, :]
            low = total_ref[768 + IMAGE + row : 769 + IMAGE + row, :]
            rows_ref[d, i : i + 1, :] = high + low
        image = rows_ref[d]
        high = image.astype(bf16)
        low = (image - high.astype(f32)).astype(bf16)
        for zh in range(2):
            s = d * 2 + zh
            for p in range(3):
                row = (d * 3 + p) * 16 + zh * 8
                slots_ref[s, :, p * 256 : (p + 1) * 256] = total_ref[row : row + 8, :].astype(bf16)
            for cg in range(4):
                row = 256 + (cg * 4 + d) * 16 + zh * 8
                at = QC + cg * 256
                slots_ref[s, :, at : at + 256] = total_ref[row : row + 8, :].astype(bf16)
            for n, block in enumerate((high[:8], high[8:], low[:8], low[8:])):
                at = QC + HC + n * 256
                slots_ref[s, :, at : at + 256] = block
    for ref, half in ((keep_ref, far), (send_ref, 1 - far)):
        for cg in range(4):
            at = slice(cg * 256, (cg + 1) * 256)
            row = pl.multiple_of(192 + cg * 16 + half * 8, 8)
            ref[32:40, at] = total_ref[pl.ds(row, 8), :].astype(ref.dtype)
            row = pl.multiple_of(512 + cg * 64 + half * 32, 8)
            ref[0:32, at] = total_ref[pl.ds(row, 32), :].astype(ref.dtype)


def part(far, received):
    return call(
        part_kernel,
        [shaped(8, 8, LAST), shaped(40, D, dtype=f32), shaped(40, D)],
        far,
        *received,
        places="saaaa",
        outs="uuu",
        scratch=[
            pltpu.VMEM((768 + 2 * IMAGE, 256), f32),
            pltpu.VMEM((4, 16, 256), f32),
            pltpu.VMEM((4, 768 + 2 * IMAGE, 256), bf16),
            pltpu.SemaphoreType.DMA((4,)),
        ],
        nbytes=4e6,
    )


def finish_kernel(place_ref, slots_ref, keep_ref, got_ref, qkv_ref, up_ref, dense_ref, down_ref, *rest):
    tiny_refs, image_ref = rest[:8], rest[8]
    image = [jnp.zeros((8, 256), f32)] * 2
    for s in range(8):
        for n in range(4):
            at = QC + HC + n * 256
            image[n % 2] = image[n % 2] + slots_ref[s, :, at : at + 256].astype(f32)
    image_ref[0:8, :] = image[0]
    image_ref[8:16, :] = image[1]
    for d in range(4):
        both = slots_ref[2 * d, :, 0 : QC + HC].astype(f32) + slots_ref[
            2 * d + 1, :, 0 : QC + HC
        ].astype(f32)
        for p in range(3):
            at = p * D + d * 256
            qkv_ref[:, at : at + 256] = both[:, p * 256 : (p + 1) * 256]
        up_ref[:, d * HC : (d + 1) * HC] = both[:, QC:]
    total = keep_ref[...] + got_ref[...].astype(f32)
    dense_ref[...] = total[32:40]
    down_ref[...] = total[0:32]
    p = place_ref[0]
    f = p % 32
    lines = (0, 1, 2, 3, 10 + f * 24 // 256, 4, 6 + f // 8, 5)
    for line, size, ref in zip(lines, SIZES, tiny_refs):
        lane = (p * size) % 256
        values = image_ref[pl.ds(line, 1), :]
        if size == 24:
            values = jnp.concatenate([values, image_ref[pl.ds(line + 1, 1), :]], axis=1)
        ref[...] = pltpu.roll(values, values.shape[1] - lane, 1)[:, :size]


def finish(place, slots, keep, got):
    return call(
        finish_kernel,
        [
            shaped(8, 3 * D, dtype=f32),
            shaped(8, FF, dtype=f32),
            shaped(8, D, dtype=f32),
            shaped(32, D, dtype=f32),
        ]
        + [shaped(1, size, dtype=f32) for size in SIZES],
        place,
        slots,
        keep,
        got,
        scratch=[pltpu.VMEM((16, 256), f32)],
        nbytes=2e6,
    )


def body(
    inputs,
    cotangent,
    lengths,
    norm1_gain,
    norm1_bias,
    norm2_gain,
    norm2_bias,
    qkv_weight,
    qkv_bias,
    dense_weight,
    dense_bias,
    up_weight,
    up_bias,
    down_weight,
    down_bias,
):
    me = lax.axis_index("dp").astype(jnp.int32)
    index = lax.axis_index("fsdp").astype(jnp.int32)
    far = (index % 2)[None]
    me1 = me[None]
    outer, inner = outer_groups(), inner_groups()

    vectors = (
        norm1_gain,
        norm1_bias,
        norm2_gain,
        norm2_bias,
        qkv_bias,
        dense_bias,
        up_bias,
        down_bias,
    )
    x2, c2 = flip_core(inputs), flip_core(cotangent)
    slots, pieces = prepare(
        qkv_weight.reshape(8, 3 * D),
        up_weight.reshape(8, FF),
        dense_weight.reshape(8, D),
        down_weight.reshape(32, D),
        lengths,
        vectors,
    )
    slots, x2, c2 = lax.optimization_barrier((slots, x2, c2))
    far_pieces = flip_far(pieces)
    first = a2a(slots, stack_groups())
    block, lens = spread(index[None], first.reshape(4, 16, SLOT), pieces, far_pieces)
    along_x, along_y = index // 2 % 4, index // 8
    core = me % 2 == 1
    near = jnp.where(core, along_x, along_y)[None]
    deep = jnp.where(core, along_y, along_x)[None]
    info = jnp.concatenate([lens[0], me1, far, near])

    block, x0, c0 = lax.optimization_barrier((block, inputs, cotangent))
    x1, c1 = flip_chip(x0), flip_chip(c0)
    second = gather(block, inner)
    second, x1 = lax.optimization_barrier((second, x1))
    third_a = gather(merge_a(deep, second), outer)
    x3, c3 = flip_core(x1), flip_core(c1)
    xs, cots = (x0, x1, x2, x3), (c0, c1, c2, c3)
    wide_b, xs, cots = lax.optimization_barrier((merge_b(deep, second), xs, cots))
    third_b = gather(wide_b, outer)

    sent_a, gb, ctx, dqkv, xhat, vec, up_b, sums = attention(info, xs, cots, third_a)
    sent_a = a2a(sent_a, outer)
    sent_b, hidden, dpre = mlp(info, third_b, gb, xhat, up_b, vec, sums)
    sent_b = a2a(sent_b, outer)

    theirs, mine = outputs(info, ctx, hidden, dqkv, dpre, third_a, third_b, vec)
    kept, send = half_sum(mine, flip_core(theirs))

    got = flip_chip(send)
    early, send = lax.optimization_barrier((add_early(sent_a), send))
    fourth = scatter(add(deep, early, sent_b), inner)
    slots, keep, rest = part(far, fourth)
    block_output, input_grad = close(lengths, inputs, cotangent, kept, got, vec)
    place = (me * 32 + index)[None]
    slots, rest, block_output, input_grad = lax.optimization_barrier(
        (a2a(slots, stack_groups()), flip_far(rest), block_output, input_grad)
    )
    results = finish(place, slots, keep, rest)
    flat = [r.reshape(-1) for r in results]
    return (
        block_output,
        input_grad,
        flat[4],
        flat[5],
        flat[6],
        flat[7],
        flat[0],
        flat[8],
        flat[2],
        flat[9],
        flat[1],
        flat[10],
        flat[3],
        flat[11],
    )


def solution(mesh):
    flat = P(("dp", "fsdp"))
    rows = P(("dp", "fsdp"), None)
    return jax.shard_map(
        body,
        mesh=mesh,
        in_specs=(rows,) * 3 + (flat,) * 12,
        out_specs=(rows,) * 2 + (flat,) * 12,
        check_vma=False,
    )
```

```python
import jax
import jax.numpy as jnp
import ml_dtypes
import numpy as np
from jax import lax
from jax.experimental import pallas as pl
from jax.experimental.pallas import tpu as pltpu
from jax.sharding import PartitionSpec as P

D = 1024
HEADS = 16
HEAD_DIM = 64
ROT = 16
FF = 4096
ROW = 256
SEGS = 8
TP = 4
QC = 3 * D // TP
HC = FF // TP
LOCAL_HEADS = HEADS // TP
STRIP = 32
AXES = ("dp", "fsdp")
VMEM = 44 * 1024 * 1024

f32 = jnp.float32
bf16 = jnp.bfloat16


def dev(d, y, x, zh):
    return d * 32 + y * 8 + x * 2 + zh


def outer_groups(flip=0):
    groups = []
    for d in range(4):
        for k in range(4):
            for zh in range(2):
                if d % 2 == flip:
                    groups.append([dev(d, i, k, zh) for i in range(4)])
                else:
                    groups.append([dev(d, k, i, zh) for i in range(4)])
    return groups


def inner_groups():
    return outer_groups(flip=1)


def stack_groups():
    return [
        [dev(d, y, x, zh) for d in range(4) for zh in range(2)] for y in range(4) for x in range(4)
    ]


def plane_groups():
    return [
        [dev(d, y, x, zh) for y in range(4) for x in range(4)] for d in range(4) for zh in range(2)
    ]


def ring(values, groups, step):
    pairs = [(g[i], g[(i + step) % 4]) for g in groups for i in range(4)]
    return lax.ppermute(values, AXES, pairs)


STEPS = (0, 1, 3, 2)


def gather(values, groups):
    return [values] + [ring(values, groups, k) for k in STEPS[1:]]


def scatter(values, groups):
    return [values[0]] + [ring(v, groups, k) for v, k in zip(values[1:], STEPS[1:])]


def a2a(values, groups):
    return lax.all_to_all(values, AXES, 0, 0, tiled=True, axis_index_groups=groups)


def flip_core(values):
    return lax.ppermute(values, "dp", [(0, 1), (1, 0), (2, 3), (3, 2)])


def flip_chip(values):
    return lax.ppermute(values, "dp", [(0, 2), (2, 0), (1, 3), (3, 1)])


def flip_far(values):
    return lax.ppermute(values, "fsdp", [(i, i ^ 1) for i in range(32)])


def dot(left, right):
    return jnp.dot(left, right, preferred_element_type=f32)


def dot_nt(left, right):
    return lax.dot_general(left, right, (((1,), (1,)), ((), ())), preferred_element_type=f32)


def dot_tn(left, right):
    return lax.dot_general(left, right, (((0,), (0,)), ((), ())), preferred_element_type=f32)


def in_hbm(values):
    return pltpu.with_memory_space_constraint(values, pltpu.HBM)


VMEM_SPEC = pl.BlockSpec(memory_space=pltpu.VMEM)
SMEM_SPEC = pl.BlockSpec(memory_space=pltpu.SMEM)
HBM_SPEC = pl.BlockSpec(memory_space=pltpu.HBM)
SPECS = {"a": pl.BlockSpec(memory_space=pl.ANY), "s": SMEM_SPEC, "v": VMEM_SPEC, "u": VMEM_SPEC, "h": HBM_SPEC}


def call(kernel, out_shape, *args, places=None, outs=None, scratch=(), flops=0, nbytes=0, trans=0):
    places = places or "s" + "v" * (len(args) - 1)
    out_specs = jax.tree.map(lambda _: VMEM_SPEC, out_shape)
    if outs is not None:
        out_specs = [SPECS[o] for o in outs]
        out_shape = [
            v if o == "v" else pltpu.HBM(v.shape, v.dtype) for o, v in zip(outs, out_shape)
        ]
    args = [in_hbm(v) if p == "h" else v for p, v in zip(places, args)]
    return pl.pallas_call(
        kernel,
        in_specs=[SPECS[p] for p in places],
        out_specs=out_specs,
        out_shape=out_shape,
        scratch_shapes=list(scratch),
        compiler_params=pltpu.CompilerParams(vmem_limit_bytes=VMEM),
        cost_estimate=pl.CostEstimate(
            flops=int(flops), bytes_accessed=int(nbytes), transcendentals=int(trans)
        ),
    )(*args)


def shaped(*shape, dtype=bf16):
    return jax.ShapeDtypeStruct(shape, dtype)


def normalize(x):
    average = jnp.mean(x, axis=-1, keepdims=True)
    centred = x - average
    inv_std = lax.rsqrt(jnp.mean(centred * centred, axis=-1, keepdims=True) + 1e-05)
    return centred * inv_std, inv_std


STARTS = (0, 4, 8, 12, 16, 28, 32, 48)
SIZES = (8, 8, 8, 8, 24, 8, 32, 8)
IMAGE = 64
LENS = 64
SLOT = QC + HC + 128


def tile(n):
    return pl.ds(pl.multiple_of(n * 256, 256), 256)


def swapped(y, x, c):
    return y + c * (x - y), x + c * (y - x)


def prepare_kernel(
    qkv_ref, up_ref, dense_in, down_in, len_in, n1g, n1b, n2g, n2b, qb, db, ub, dnb,
    out_ref, pieces_ref, tile_ref, *rest
):
    sources = (len_in, n1g, n1b, n2g, n2b, qb, db, ub, dnb)
    holders, sem = rest[:9], rest[9]
    copies = [
        pltpu.make_async_copy(src, dst, sem.at[i])
        for i, (src, dst) in enumerate(zip(sources, holders))
    ]
    for copy in copies:
        copy.start()
    for d in range(4):
        for zh in range(2):
            s = d * 2 + zh
            for p in range(3):
                at = p * D + d * 256
                out_ref[s, :, p * 256 : (p + 1) * 256] = qkv_ref[:, at : at + 256]
            out_ref[s, :, QC : QC + HC] = up_ref[:, d * HC : (d + 1) * HC]
    pieces_ref[0:32, :] = down_in[...]
    pieces_ref[32:40, :] = dense_in[...]
    tile_ref[...] = jnp.zeros_like(tile_ref)
    for copy in copies:
        copy.wait()
    for i, (size, ref) in enumerate(zip(SIZES, holders[1:])):
        tile_ref[i : i + 1, 0:size] = ref[...].astype(f32)
    tile_ref[0:1, LENS : LENS + SEGS] = holders[0][...].astype(f32)
    block = tile_ref[...].astype(bf16)
    for s in range(8):
        out_ref[s, :, QC + HC : SLOT] = block


def prepare(qkv, up, dense, down, lengths, vectors):
    vectors = [v[None, :] for v in vectors]
    return call(
        prepare_kernel,
        [shaped(8, 8, SLOT), shaped(40, D)],
        qkv,
        up,
        dense,
        down,
        lengths,
        *vectors,
        places="vvvv" + "h" * 9,
        scratch=[pltpu.VMEM((8, 128), f32), pltpu.VMEM((1, SEGS), jnp.int32)]
        + [pltpu.VMEM(v.shape, bf16) for v in vectors]
        + [pltpu.SemaphoreType.DMA((9,))],
        nbytes=1e6,
    )


def locate(p, start, size):
    first = p * size
    return start + first // 256, first % 256


def spread_kernel(index_ref, first_ref, mine_ref, theirs_ref, out_ref, lens_ref, image_ref):
    index = index_ref[0]
    far = index % 2 == 1
    mine, theirs = mine_ref[...].astype(f32), theirs_ref[...].astype(f32)
    low, high = jnp.where(far, theirs, mine), jnp.where(far, mine, theirs)
    down = jnp.concatenate([low[:32], high[:32]], axis=0).astype(bf16)
    dense = jnp.concatenate([low[32:], high[32:]], axis=0).astype(bf16)
    image_ref[...] = jnp.zeros_like(image_ref)
    lens = []
    for d in range(4):
        both = first_ref[d, :, QC + HC : SLOT].astype(f32)
        for zh in range(2):
            p = d * 32 + index // 2 * 2 + zh
            tile = both[zh * 8 : zh * 8 + 8]
            lens.append(tile[0:1, LENS : LENS + SEGS])
            for i, (start, size) in enumerate(zip(STARTS, SIZES)):
                row, lane = locate(p, start, size)
                wide = 512 if size == 24 else 256
                blank = jnp.zeros((1, wide - size), f32)
                values = jnp.concatenate([tile[i : i + 1, :size], blank], axis=1)
                values = pltpu.roll(values, lane, 1)
                image_ref[pl.ds(row, 1), :] += values[:, :256]
                if wide == 512:
                    image_ref[pl.ds(row + 1, 1), :] += values[:, 256:]
    lens_ref[...] = jnp.concatenate(lens, axis=1).astype(jnp.int32)
    image = image_ref[...].astype(bf16)
    for d in range(4):
        for p in range(3):
            row = (d * 3 + p) * 16
            out_ref[row : row + 16, :] = first_ref[d, :, p * 256 : (p + 1) * 256]
        for cg in range(4):
            row = 256 + (d * 4 + cg) * 16
            at = QC + cg * 256
            out_ref[row : row + 16, :] = first_ref[d, :, at : at + 256]
    for cg in range(4):
        at = slice(cg * 256, (cg + 1) * 256)
        out_ref[192 + cg * 16 : 208 + cg * 16, :] = dense[:, at]
        out_ref[512 + cg * 64 : 576 + cg * 64, :] = down[:, at]
    out_ref[768 : 768 + IMAGE, :] = image


def spread(index, first, mine, theirs):
    return call(
        spread_kernel,
        [shaped(768 + IMAGE, 256), shaped(1, 64, dtype=jnp.int32)],
        index,
        first,
        mine,
        theirs,
        scratch=[pltpu.VMEM((IMAGE, 256), f32)],
        nbytes=2e6,
    )


def merge_a_kernel(place_ref, b0, b1, b2, b3, out_ref):
    blocks = (b0, b1, b2, b3)
    for block, step in zip(blocks, STEPS):
        a = (place_ref[0] + 4 - step) % 4
        out_ref[tile(a), :] = block[0:256, :]
    total = sum([block[768 : 768 + IMAGE, :].astype(f32) for block in blocks])
    out_ref[1024 : 1024 + IMAGE, :] = total.astype(bf16)


def merge_a(place, blocks):
    return call(
        merge_a_kernel, [shaped(1024 + IMAGE, 256)], place, *blocks, outs="u", nbytes=1e6
    )[0]


def merge_b_kernel(place_ref, b0, b1, b2, b3, out_ref):
    for block, step in zip((b0, b1, b2, b3), STEPS):
        a = (place_ref[0] + 4 - step) % 4
        out_ref[pl.ds(pl.multiple_of(a * 512, 512), 512), :] = block[256:768, :]


def merge_b(place, blocks):
    return call(merge_b_kernel, [shaped(2048, 256)], place, *blocks, outs="u", nbytes=2e6)[0]


def assemble_a(me, buf_ref, wqkv_ref, wd_ref):
    c = me % 2
    for y in range(4):
        for x in range(4):
            b, a = swapped(y, x, c)
            yx = y * 4 + x
            base = a * 256
            for d in range(4):
                for p in range(3):
                    row = pl.multiple_of(base + (d * 3 + p) * 16, 16)
                    wqkv_ref[d * 256 + yx * 16 : d * 256 + yx * 16 + 16, p * 256 : (p + 1) * 256] = (
                        buf_ref[b, pl.ds(row, 16), :]
                    )
            for cg in range(4):
                row = pl.multiple_of(base + 192 + cg * 16, 16)
                wd_ref[yx * 16 : yx * 16 + 16, cg * 256 : (cg + 1) * 256] = buf_ref[
                    b, pl.ds(row, 16), :
                ]


def read_vectors(me, buf_ref, vec_ref, qb_ref, ub_ref):
    image = sum([buf_ref[b, 1024 : 1024 + IMAGE, :].astype(f32) for b in range(4)])

    def long(start):
        return jnp.concatenate([image[start + i : start + i + 1, :] for i in range(4)], axis=1)

    vec_ref[...] = jnp.zeros_like(vec_ref)
    for i in range(4):
        vec_ref[i : i + 1, :] = long(4 * i)
    vec_ref[4:5, :] = long(28) + long(48)
    own = [jnp.where(me == d, 1.0, 0.0) for d in range(4)]
    rows = [sum([image[16 + p * 4 + d : 17 + p * 4 + d] * own[d] for d in range(4)]) for p in range(3)]
    qb_ref[...] = jnp.concatenate(rows, axis=1)
    ub_ref[...] = sum([long(32 + 4 * d) * own[d] for d in range(4)])


def assemble_b(me, buf_ref, wup_ref, wdown_ref):
    c = me % 2
    for y in range(4):
        for x in range(4):
            b, a = swapped(y, x, c)
            yx = y * 4 + x
            base = a * 512
            for d in range(4):
                for cg in range(4):
                    row = pl.multiple_of(base + (d * 4 + cg) * 16, 16)
                    wup_ref[d * 256 + yx * 16 : d * 256 + yx * 16 + 16, cg * 256 : (cg + 1) * 256] = (
                        buf_ref[b, pl.ds(row, 16), :]
                    )
            for cg in range(4):
                row = pl.multiple_of(base + 256 + cg * 64, 16)
                wdown_ref[yx * 64 : yx * 64 + 64, cg * 256 : (cg + 1) * 256] = buf_ref[
                    b, pl.ds(row, 64), :
                ]


def turn(u, cosine, sin_left, sin_right):
    return (
        u * cosine
        + pltpu.roll(u, u.shape[1] - ROT // 2, 1) * sin_left
        + pltpu.roll(u, ROT // 2, 1) * sin_right
    )


def rotary_tables():
    places = np.arange(ROW, dtype=np.float32)
    freqs = (10000.0 ** (-(np.arange(ROT // 2, dtype=np.float32) * 2.0) / ROT)).astype(np.float32)
    angle = (places[:, None] * freqs[None, :]).astype(np.float32)
    cosine, sine = np.cos(angle), np.sin(angle)
    zeros = np.zeros_like(sine)
    rest = np.zeros((ROW, HEAD_DIM - ROT), np.float32)
    parts = [[cosine, cosine, rest + 1.0], [-sine, zeros, rest], [zeros, sine, rest]]
    columns = []
    for part in parts:
        whole = np.tile(np.concatenate(part, axis=1), (1, 2)).astype(np.float32)
        high = whole.astype(ml_dtypes.bfloat16)
        columns += [high, (whole - high.astype(np.float32)).astype(ml_dtypes.bfloat16)]
    return np.concatenate(columns, axis=1)


def row_sums(values):
    total = jnp.sum(values, axis=1, keepdims=True)
    return jnp.transpose(jnp.broadcast_to(total, (256, 128)))[0:1, :]


def through(sums, matrix):
    high = sums.astype(bf16)
    low = (sums - high.astype(f32)).astype(bf16)
    both = jnp.concatenate([high.astype(f32), low.astype(f32)] + [jnp.zeros_like(sums)] * 6, axis=0)
    out = dot_nt(both.astype(bf16), matrix)
    return out[0:1] + out[1:2]


def attention_kernel(
    info_ref,
    x0,
    x1,
    x2,
    x3,
    c0,
    c1,
    c2,
    c3,
    w0,
    w1,
    w2,
    w3,
    rot_in,
    sent_out,
    gb_out,
    ctx_out,
    dqkv_out,
    xhat_out,
    vec_ref,
    ub_ref,
    sums_ref,
    x_ref,
    cot_ref,
    wqkv_ref,
    wd_ref,
    qb_ref,
    gb_ref,
    ctx_ref,
    dqkv_ref,
    xhat_ref,
    sent_ref,
    in_sem,
    out_sem,
    sent_sem,
    vec_col_ref,
    buf_ref,
    buf_sem,
    rot_ref,
    rot_sem,
):
    me = info_ref[64]
    place = info_ref[66]
    parts = []
    for n, (src, step) in enumerate(zip((w0, w1, w2, w3), STEPS)):
        b = (place + 4 - step) % 4
        parts.append(pltpu.make_async_copy(src, buf_ref.at[b], buf_sem.at[n]))
    for copy in parts:
        copy.start()
    loads = []
    for i, (one, other) in enumerate(zip((x0, x1, x2, x3), (c0, c1, c2, c3))):
        loads.append(pltpu.make_async_copy(one, x_ref.at[i], in_sem.at[i, 0]))
        loads.append(pltpu.make_async_copy(other, cot_ref.at[i], in_sem.at[i, 1]))
    for load in loads[:2]:
        load.start()
    for copy in parts:
        copy.wait()
    assemble_a(me, buf_ref, wqkv_ref, wd_ref)
    rotary = pltpu.make_async_copy(rot_in, rot_ref, rot_sem)
    rotary.start()
    for load in loads[2:]:
        load.start()
    read_vectors(me, buf_ref, vec_ref, qb_ref, ub_ref)
    rotary.wait()
    stores = (
        (gb_ref, gb_out),
        (ctx_ref, ctx_out),
        (xhat_ref, xhat_out),
        (dqkv_ref, dqkv_out),
    )

    def store(n, r):
        rows = pl.ds(pl.multiple_of(r * ROW, ROW), ROW)
        src, dst = stores[n]
        return pltpu.make_async_copy(src.at[rows, :], dst.at[rows, :], out_sem.at[n, r])

    sums_ref[...] = jnp.zeros_like(sums_ref)

    @pl.loop(0, TP)
    def _(r):
        pltpu.make_async_copy(x0, x_ref.at[r], in_sem.at[r, 0]).wait()
        pltpu.make_async_copy(c0, cot_ref.at[r], in_sem.at[r, 1]).wait()
        here = pl.ds(pl.multiple_of(r * ROW, ROW), ROW)
        xhat, _ = normalize(x_ref[r].astype(f32))
        xhat_ref[here, :] = xhat.astype(bf16)
        attn_in = (xhat * vec_ref[0:1] + vec_ref[1:2]).astype(bf16)
        qkv = dot(attn_in, wqkv_ref[...]) + qb_ref[...]
        d = me ^ ((r & 1) * 2 + r // 2)
        base = (d * 2 + info_ref[65]) * SEGS
        ends, end = [], 0
        for j in range(SEGS - 1):
            end = end + info_ref[base + j]
            ends.append(end)
        rows = lax.broadcasted_iota(jnp.int32, (ROW, 1), 0)
        cols = lax.broadcasted_iota(jnp.int32, (1, ROW), 1)
        row_doc = sum([(rows >= e).astype(jnp.int32) for e in ends])
        col_doc = sum([(cols >= e).astype(jnp.int32) for e in ends])
        allowed = (row_doc == col_doc) & (rows <= cols)
        start = jnp.zeros_like(rows)
        for e in ends:
            start = jnp.maximum(start, jnp.where(rows >= e, e, 0))
        kept = jnp.where(rows < ends[-1], cot_ref[r].astype(f32), 0.0)
        gb = kept.astype(bf16)
        gb_ref[here, :] = gb
        dctx = dot_nt(gb, wd_ref[...]).astype(bf16)
        chosen = ((rows - start) == cols).astype(f32).astype(bf16)
        table = dot(chosen, rot_ref[...])
        pair = lambda n: table[:, n * 256 : n * 256 + 128] + table[:, n * 256 + 128 : n * 256 + 256]
        cosine, left, right = [jnp.concatenate([pair(n)] * 2, axis=1) for n in range(3)]
        scale = HEAD_DIM**-0.5
        q = (turn(qkv[:, 0:256], cosine, left, right).astype(bf16).astype(f32) * scale).astype(bf16)
        k = turn(qkv[:, 256:512], cosine, left, right).astype(bf16)
        v = qkv[:, 512:768].astype(bf16)
        lanes = lax.broadcasted_iota(jnp.int32, (1, 256), 1) // HEAD_DIM
        ctx, dq, dk, dv = [jnp.zeros((ROW, 256), f32)] * 4
        heads = range(LOCAL_HEADS)
        only = [(lanes == h).astype(f32).astype(bf16) for h in heads]
        qs, dcs = [q * m for m in only], [dctx * m for m in only]
        s_all = dot_nt(k, jnp.concatenate(qs, axis=0))
        dp_all = dot_nt(v, jnp.concatenate(dcs, axis=0))
        cut = [slice(h * ROW, (h + 1) * ROW) for h in heads]
        scores = [jnp.where(allowed, s_all[:, c], -1000000000.0) for c in cut]
        dprobs = [dp_all[:, c] for c in cut]
        probs = []
        for h in heads:
            shifted = jnp.exp(scores[h] - jnp.max(scores[h], axis=0, keepdims=True))
            probs.append(shifted * (1.0 / jnp.sum(shifted, axis=0, keepdims=True)))
        lows = [p.astype(bf16) for p in probs]
        ds = []
        for h in heads:
            inner = jnp.sum(dprobs[h] * probs[h], axis=0, keepdims=True)
            ds.append((probs[h] * (dprobs[h] - inner)).astype(bf16))
        p_all = jnp.concatenate(lows, axis=0)
        ds_all = jnp.concatenate(ds, axis=0)
        ctx = dot_tn(p_all, jnp.concatenate([v * m for m in only], axis=0))
        dq = dot_tn(ds_all, jnp.concatenate([k * m for m in only], axis=0))
        dv = dot(jnp.concatenate(lows, axis=1), jnp.concatenate(dcs, axis=0))
        dk = dot(jnp.concatenate(ds, axis=1), jnp.concatenate(qs, axis=0))
        ctx_ref[here, :] = ctx.astype(bf16)
        dqs = turn(dq * scale, cosine, -left, -right)
        dks = turn(dk, cosine, -left, -right)
        dqkv = jnp.concatenate([dqs, dks, dv], axis=1).astype(bf16)
        dqkv_ref[here, :] = dqkv

        @pl.when(r == 0)
        def _():
            sums_ref[0:1, :] = jnp.sum(kept, axis=0, keepdims=True)

        sums_ref[1:2, 0:QC] += jnp.sum(dqkv.astype(f32), axis=0, keepdims=True)
        for n in range(4):
            store(n, r).start()

    c = me % 2
    sums_ref[3:4, :] = through(sums_ref[1:2, 0:QC], wqkv_ref[...])
    columns = jnp.transpose(vec_ref[...])
    vec_col_ref[...] = columns

    def sent(d, n):
        rows = pl.ds(pl.multiple_of(d * 48, 16), 48)
        if n == 1:
            rows = pl.ds(pl.multiple_of(192 + d * 16, 16), 16)
        return pltpu.make_async_copy(
            sent_ref.at[:, :, rows, :], sent_out.at[:, :, rows, :], sent_sem.at[d, n]
        )

    @pl.loop(0, 4)
    def _(d):
        raw = dot_tn(xhat_ref[:, tile(d)], dqkv_ref[...])
        gain, bias = vec_col_ref[tile(d), 0:1], vec_col_ref[tile(d), 1:2]
        qkv_grad = (raw * gain + bias * sums_ref[1:2, 0:QC]).astype(bf16)
        sums_ref[2:3, tile(d)] = row_sums(raw * wqkv_ref[tile(d), :].astype(f32))
        dense_grad = dot_tn(ctx_ref[...], gb_ref[:, tile(d)]).astype(bf16)
        base = pl.multiple_of(d * 48, 16)
        dense_base = pl.multiple_of(192 + d * 16, 16)
        for y in range(4):
            for x in range(4):
                b, a = swapped(y, x, c)
                at = slice((y * 4 + x) * 16, (y * 4 + x + 1) * 16)
                for p in range(3):
                    sent_ref[b, a, pl.ds(base + p * 16, 16), :] = qkv_grad[
                        at, p * 256 : (p + 1) * 256
                    ]
                sent_ref[b, a, pl.ds(dense_base, 16), :] = dense_grad[at]
        sent(d, 0).start()
        sent(d, 1).start()

    @pl.loop(0, 4)
    def _(i):
        for n in range(4):
            store(n, i).wait()
        sent(i, 0).wait()
        sent(i, 1).wait()


def attention(info, xs, cots, blocks):
    tokens = TP * ROW
    dma = pltpu.SemaphoreType.DMA
    return call(
        attention_kernel,
        [
            shaped(4, 4, 256, 256),
            shaped(tokens, D),
            shaped(tokens, 256),
            shaped(tokens, QC),
            shaped(tokens, D),
            shaped(8, D, dtype=f32),
            shaped(1, HC, dtype=f32),
            shaped(8, D, dtype=f32),
        ],
        info,
        *xs,
        *cots,
        *blocks,
        jnp.asarray(rotary_tables()),
        places="s" + "a" * 12 + "h",
        outs="h" * 5 + "vvv",
        scratch=[
            pltpu.VMEM((TP, ROW, D), bf16),
            pltpu.VMEM((TP, ROW, D), bf16),
            pltpu.VMEM((D, QC), bf16),
            pltpu.VMEM((D // TP, D), bf16),
            pltpu.VMEM((1, QC), f32),
            pltpu.VMEM((tokens, D), bf16),
            pltpu.VMEM((tokens, 256), bf16),
            pltpu.VMEM((tokens, QC), bf16),
            pltpu.VMEM((tokens, D), bf16),
            pltpu.VMEM((4, 4, 256, 256), bf16),
            dma((4, 2)),
            dma((4, 4)),
            dma((4, 2)),
            pltpu.VMEM((D, 8), f32),
            pltpu.VMEM((4, 1024 + IMAGE, 256), bf16),
            dma((4,)),
            pltpu.VMEM((ROW, 768), bf16),
            dma,
        ],
        flops=6e9,
        nbytes=2e7,
        trans=1e6,
    )


def mlp_kernel(
    info_ref,
    w0,
    w1,
    w2,
    w3,
    gb_in,
    xhat_in,
    ub_ref,
    vec_ref,
    sums_a_ref,
    sent_out,
    hidden_out,
    dpre_out,
    buf_ref,
    gb_ref,
    wup_ref,
    wdown_ref,
    hidden_ref,
    dpre_ref,
    sent_ref,
    xhat_ref,
    sums_ref,
    image_ref,
    vec_col_ref,
    min_ref,
    rows_ref,
    turned_ref,
    buf_sem,
    in_sem,
    out_sem,
    sent_sem,
    image_sem,
):
    me, place = info_ref[64], info_ref[66]
    c = me % 2
    parts = []
    for n, (src, step) in enumerate(zip((w0, w1, w2, w3), STEPS)):
        b = (place + 4 - step) % 4
        parts.append(pltpu.make_async_copy(src, buf_ref.at[b], buf_sem.at[n]))

    def load(t, n):
        src, dst = ((gb_in, gb_ref), (xhat_in, xhat_ref))[n]
        return pltpu.make_async_copy(src.at[tile(t), :], dst.at[tile(t), :], in_sem.at[t, n])

    for part in parts:
        part.start()
    for t in range(4):
        for n in range(2):
            load(t, n).start()
    for part in parts:
        part.wait()
    assemble_b(me, buf_ref, wup_ref, wdown_ref)
    sums_ref[...] = jnp.zeros_like(sums_ref)

    vec_col_ref[...] = jnp.transpose(vec_ref[...])
    rows_ref[...] = jnp.zeros_like(rows_ref)

    def store(j, n):
        src, dst = ((hidden_ref, hidden_out), (dpre_ref, dpre_out))[n]
        return pltpu.make_async_copy(src.at[:, tile(j)], dst.at[:, tile(j)], out_sem.at[j, n])

    def sent_up(j):
        rows = pl.ds(pl.multiple_of(j * 64, 64), 64)
        return pltpu.make_async_copy(
            sent_ref.at[:, :, rows, :], sent_out.at[:, :, rows, :], sent_sem.at[j, 4]
        )

    def sent_down(j, x):
        b, a = swapped(j, x, c)
        rows = pl.ds(256, 256)
        return pltpu.make_async_copy(
            sent_ref.at[b, a, rows, :], sent_out.at[b, a, rows, :], sent_sem.at[j, x]
        )

    def hidden_tile(j, t):
        at = pl.ds(t * ROW, ROW)
        pre = dot(min_ref[at, :], wup_ref[:, tile(j)]) + ub_ref[:, tile(j)]
        return pre, dot_nt(gb_ref[at, :], wdown_ref[tile(j), :])

    def activate(j, t, pre, back):
        total = jnp.zeros((8, 256), f32)
        for i in range(0, ROW, STRIP):
            at = pl.ds(t * ROW + i, STRIP)
            a, b = pre[i : i + STRIP], back[i : i + STRIP]
            size = jnp.abs(a) * 0.7071067811865476
            bell = jnp.exp(-0.5 * a * a)
            s = 1.0 / (1.0 + 0.3275911 * size)
            poly = s * (
                0.127414796
                + s * (-0.142248368 + s * (0.7107068705 + s * (-0.7265760135 + s * 0.5307027145)))
            )
            tail = poly * bell
            cumul = jnp.where(a >= 0.0, 1.0 - tail, tail)
            hidden_ref[at, tile(j)] = (a * cumul).astype(bf16)
            dpre = (b * (cumul + a * (bell * 0.3989422804014327))).astype(bf16)
            dpre_ref[at, tile(j)] = dpre
            total += jnp.sum(dpre.astype(f32).reshape(STRIP // 8, 8, 256), axis=0)
        return jnp.sum(total, axis=0, keepdims=True)

    def put_down(j):
        down = dot_tn(hidden_ref[:, tile(j)], gb_ref[...]).astype(bf16)
        for x in range(4):
            b, a = swapped(j, x, c)
            for cg in range(4):
                sent_ref[b, a, 256 + cg * 64 : 256 + (cg + 1) * 64, :] = down[
                    x * 64 : (x + 1) * 64, cg * 256 : (cg + 1) * 256
                ]

    def put_up(j, t, raw):
        row = pl.multiple_of(j * 64 + t * 16, 16)
        sums = sums_ref[0:1, tile(j)]
        for y in range(4):
            for x in range(4):
                b, a = swapped(y, x, c)
                i = (y * 4 + x) * 16
                at = slice(t * 256 + i, t * 256 + i + 16)
                part = raw[i : i + 16]
                product = part * wup_ref[at, tile(j)].astype(f32)
                rows_ref[at, :] += product[:, :128] + product[:, 128:]
                gain, bias = vec_col_ref[at, 2:3], vec_col_ref[at, 3:4]
                sent_ref[b, a, pl.ds(row, 16), :] = (part * gain + bias * sums).astype(bf16)

    def step(j, last=False, first=False):
        if not last:
            total = jnp.zeros((1, 256), f32)
        for t in range(TP):
            if first:
                at = pl.ds(t * ROW, ROW)
                load(t, 0).wait()
                load(t, 1).wait()
                for i in range(0, ROW, 16):
                    strip = pl.ds(t * ROW + i, 16)
                    values = xhat_ref[strip, :].astype(f32)
                    min_ref[strip, :] = (values * vec_ref[2:3] + vec_ref[3:4]).astype(bf16)
                turned_ref[:, at] = jnp.transpose(xhat_ref[at, :])
            if not last:
                pre, back = hidden_tile(j, t)
            if not first:
                if t == 0:
                    put_down(j - 1)
                raw = dot(turned_ref[t * 256 : (t + 1) * 256, :], dpre_ref[:, tile(j - 1)])
            if not last:
                total += activate(j, t, pre, back)
            if not first:
                put_up(j - 1, t, raw)
        if not last:
            sums_ref[0:1, tile(j)] = total
            store(j, 0).start()
            store(j, 1).start()
        if not first:
            sent_up(j - 1).start()
            for x in range(4):
                sent_down(j - 1, x).start()

    step(0, first=True)

    @pl.loop(1, 4)
    def _(j):
        step(j)

    step(4, last=True)
    total = jnp.sum(rows_ref[...], axis=1, keepdims=True)
    sums_ref[1:2, :] = jnp.transpose(jnp.broadcast_to(total, (D, 128)))[0:1, :]
    sums_ref[2:3, :] = through(sums_ref[0:1, :], wup_ref[...])

    image_ref[...] = jnp.zeros_like(image_ref)

    def put(row, ref, line, count):
        for i in range(count):
            image_ref[pl.ds(row + i, 1), :] = ref[line : line + 1, i * 256 : (i + 1) * 256]

    put(0, sums_a_ref, 2, 4)
    put(4, sums_a_ref, 3, 4)
    put(8, sums_ref, 1, 4)
    put(12, sums_ref, 2, 4)
    for p in range(3):
        image_ref[pl.ds(16 + p * 4 + me, 1), :] = sums_a_ref[1:2, p * 256 : (p + 1) * 256]
    put(28, sums_a_ref, 0, 4)
    put(32 + 4 * me, sums_ref, 0, 4)
    put(48, sums_a_ref, 0, 4)
    image = image_ref[...]
    high = image.astype(bf16)
    low = (image - high.astype(f32)).astype(bf16)
    for b in range(4):
        for a in range(4):
            half = (high, low)[a // 2]
            sent_ref[b, a, 512 : 512 + IMAGE // 2, :] = half[a % 2 * 32 : a % 2 * 32 + 32]
    rows = pl.ds(512, IMAGE // 2)
    images = pltpu.make_async_copy(
        sent_ref.at[:, :, rows, :], sent_out.at[:, :, rows, :], image_sem
    )
    images.start()
    for i in range(TP):
        store(i, 0).wait()
        store(i, 1).wait()
        sent_up(i).wait()
        for x in range(4):
            sent_down(i, x).wait()
    images.wait()


def mlp(info, blocks, gb, xhat, ub, vec, sums):
    tokens = TP * ROW
    dma = pltpu.SemaphoreType.DMA
    return call(
        mlp_kernel,
        [
            shaped(4, 4, 512 + IMAGE // 2, 256),
            shaped(tokens, HC),
            shaped(tokens, HC),
        ],
        info,
        *blocks,
        gb,
        xhat,
        ub,
        vec,
        sums,
        places="s" + "a" * 4 + "hhvvv",
        outs="hhh",
        scratch=[
            pltpu.VMEM((4, 2048, 256), bf16),
            pltpu.VMEM((tokens, D), bf16),
            pltpu.VMEM((D, HC), bf16),
            pltpu.VMEM((HC, D), bf16),
            pltpu.VMEM((tokens, HC), bf16),
            pltpu.VMEM((tokens, HC), bf16),
            pltpu.VMEM((4, 4, 512 + IMAGE // 2, 256), bf16),
            pltpu.VMEM((tokens, D), bf16),
            pltpu.VMEM((8, D), f32),
            pltpu.VMEM((IMAGE, 256), f32),
            pltpu.VMEM((D, 8), f32),
            pltpu.VMEM((tokens, D), bf16),
            pltpu.VMEM((D, 128), f32),
            pltpu.VMEM((D, tokens), bf16),
            dma((4,)),
            dma((4, 2)),
            dma((4, 2)),
            dma((4, 5)),
            dma,
        ],
        flops=9e9,
        nbytes=2e7,
        trans=2e6,
    )


def outputs_kernel(
    info_ref,
    ctx_in,
    hidden_in,
    dqkv_in,
    dpre_in,
    a0,
    a1,
    a2,
    a3,
    b0,
    b1,
    b2,
    b3,
    vec_ref,
    theirs_out,
    mine_out,
    ctx_ref,
    hidden_ref,
    dqkv_ref,
    dpre_ref,
    wd_ref,
    wdown_ref,
    wqkv_ref,
    wup_ref,
    both_ref,
    buf_a_ref,
    buf_b_ref,
    weight_sem,
    in_sem,
    out_sem,
):
    me, place = info_ref[64], info_ref[66]
    weights = []
    for n, step in enumerate(STEPS):
        b = (place + 4 - step) % 4
        pairs = (((a0, a1, a2, a3)[n], buf_a_ref), ((b0, b1, b2, b3)[n], buf_b_ref))
        for i, (src, dst) in enumerate(pairs):
            weights.append(pltpu.make_async_copy(src, dst.at[b], weight_sem.at[n, i]))
    inputs = (
        (dqkv_in, dqkv_ref),
        (dpre_in, dpre_ref),
        (ctx_in, ctx_ref),
        (hidden_in, hidden_ref),
    )

    def load(t, n):
        src, dst = inputs[n]
        return pltpu.make_async_copy(src.at[tile(t), :], dst.at[tile(t), :], in_sem.at[t, n])

    def finished(i, n):
        dst = (theirs_out, mine_out)[n]
        return pltpu.make_async_copy(both_ref.at[i], dst.at[i - 2 * n], out_sem.at[i])

    for weight in weights:
        weight.start()
    for i in range(TP):
        for n in range(4):
            load((i + 2) % 4, n).start()
    for weight in weights:
        weight.wait()
    assemble_a(me, buf_a_ref, wqkv_ref, wd_ref)
    assemble_b(me, buf_b_ref, wup_ref, wdown_ref)

    @pl.loop(0, TP)
    def _(i):
        t = (i + 2) % 4
        for n in range(4):
            load(t, n).wait()
        here = tile(t)
        dattn = dot_nt(dqkv_ref[here, :], wqkv_ref[...])
        dmlp = dot_nt(dpre_ref[here, :], wup_ref[...])
        both_ref[i, 1] = (dattn * vec_ref[0:1] + dmlp * vec_ref[2:3]).astype(bf16)
        forward = dot(ctx_ref[here, :], wd_ref[...]) + dot(hidden_ref[here, :], wdown_ref[...])
        both_ref[i, 0] = forward.astype(bf16)

        @pl.when(i < 2)
        def _():
            finished(i, 0).start()

        @pl.when(i >= 2)
        def _():
            finished(i, 1).start()

    for i in range(TP):
        finished(i, i // 2).wait()


def outputs(info, ctx, hidden, dqkv, dpre, blocks_a, blocks_b, vec):
    tokens = TP * ROW
    dma = pltpu.SemaphoreType.DMA
    return call(
        outputs_kernel,
        [shaped(2, 2, ROW, D), shaped(2, 2, ROW, D)],
        info,
        ctx,
        hidden,
        dqkv,
        dpre,
        *blocks_a,
        *blocks_b,
        vec,
        places="s" + "a" * 12 + "v",
        outs="hh",
        scratch=[
            pltpu.VMEM((tokens, 256), bf16),
            pltpu.VMEM((tokens, HC), bf16),
            pltpu.VMEM((tokens, QC), bf16),
            pltpu.VMEM((tokens, HC), bf16),
            pltpu.VMEM((D // TP, D), bf16),
            pltpu.VMEM((HC, D), bf16),
            pltpu.VMEM((D, QC), bf16),
            pltpu.VMEM((D, HC), bf16),
            pltpu.VMEM((TP, 2, ROW, D), bf16),
            pltpu.VMEM((4, 1024 + IMAGE, 256), bf16),
            pltpu.VMEM((4, 2048, 256), bf16),
            dma((4, 2)),
            dma((4, 4)),
            dma((4,)),
        ],
        flops=6.5e9,
        nbytes=1.6e7,
    )


def half_kernel(mine_in, got_in, kept_out, send_out, mine_ref, got_ref, kept_ref, send_ref, in_sem, out_sem):
    loads = []
    for i in (1, 0):
        for n in range(2):
            pair = (
                pltpu.make_async_copy(mine_in.at[i, n], mine_ref.at[i, n], in_sem.at[i, n, 0]),
                pltpu.make_async_copy(got_in.at[i, n], got_ref.at[i, n], in_sem.at[i, n, 1]),
            )
            loads.append((i, n, pair))
            for copy in pair:
                copy.start()
    stores = []
    for i, n, pair in loads:
        for copy in pair:
            copy.wait()
        total = mine_ref[i, n].astype(f32) + got_ref[i, n].astype(f32)
        ref, out = ((kept_ref, kept_out), (send_ref, send_out))[i]
        ref[n] = total.astype(ref.dtype)
        stores.append(pltpu.make_async_copy(ref.at[n], out.at[0, n], out_sem.at[i, n]))
        stores[-1].start()
    for store in stores:
        store.wait()


def half_sum(mine, got):
    dma = pltpu.SemaphoreType.DMA
    return call(
        half_kernel,
        [shaped(1, 2, ROW, D, dtype=f32), shaped(1, 2, ROW, D)],
        mine,
        got,
        places="ha",
        outs="hh",
        scratch=[
            pltpu.VMEM((2, 2, ROW, D), bf16),
            pltpu.VMEM((2, 2, ROW, D), bf16),
            pltpu.VMEM((2, ROW, D), f32),
            pltpu.VMEM((2, ROW, D), bf16),
            dma((2, 2, 2)),
            dma((2, 2)),
        ],
        nbytes=8e6,
    )


def close_kernel(len_ref, x_ref, cot_ref, kept_ref, got_ref, vec_ref, out_ref, grad_ref):
    x = x_ref[...].astype(f32)
    out_ref[...] = (x + kept_ref[0, 0] + got_ref[0, 0].astype(f32) + vec_ref[4:5]).astype(bf16)
    e = kept_ref[0, 1] + got_ref[0, 1].astype(f32)
    xhat, inv_std = normalize(x)
    mean_e = jnp.mean(e, axis=-1, keepdims=True)
    mean_ex = jnp.mean(e * xhat, axis=-1, keepdims=True)
    used = sum([len_ref[0, j] for j in range(SEGS - 1)])
    rows = pl.program_id(0) * x.shape[0] + lax.broadcasted_iota(jnp.int32, (x.shape[0], 1), 0)
    kept = jnp.where(rows < used, cot_ref[...].astype(f32), 0.0)
    grad_ref[...] = kept + inv_std * (e - mean_e - xhat * mean_ex)


def close(lengths, x, cot, kept, got, vec):
    row = pl.BlockSpec((ROW // 4, D), lambda k: (k, 0))
    both = pl.BlockSpec((1, 2, ROW // 4, D), lambda k: (0, 0, k, 0))
    return pl.pallas_call(
        close_kernel,
        grid=(4,),
        in_specs=[SMEM_SPEC, row, row, both, both, pl.BlockSpec((8, D), lambda k: (0, 0))],
        out_specs=[row, row],
        out_shape=[pltpu.HBM((ROW, D), bf16), pltpu.HBM((ROW, D), f32)],
        compiler_params=pltpu.CompilerParams(vmem_limit_bytes=VMEM),
        cost_estimate=pl.CostEstimate(flops=0, bytes_accessed=6000000, transcendentals=0),
    )(lengths, *[in_hbm(v) for v in (x, cot, kept, got)], vec)


def add_early_kernel(a_ref, out_ref):
    out_ref[0] = sum([a_ref[i, 0].astype(f32) for i in range(4)]).astype(bf16)


def add_early(sent_a):
    return pl.pallas_call(
        add_early_kernel,
        grid=(4,),
        in_specs=[pl.BlockSpec((4, 1, 256, 256), lambda a: (0, a, 0, 0))],
        out_specs=pl.BlockSpec((1, 256, 256), lambda a: (a, 0, 0)),
        out_shape=pltpu.HBM((4, 256, 256), bf16),
        compiler_params=pltpu.CompilerParams(vmem_limit_bytes=VMEM),
        cost_estimate=pl.CostEstimate(flops=0, bytes_accessed=3000000, transcendentals=0),
    )(sent_a)


def add_kernel(
    place_ref, early_in, b_in, o0, o1, o2, o3, early_ref, b_ref, image_ref, both_ref, early_sem, b_sem, image_sem, sem
):
    place = place_ref[0]

    def load(n, i):
        a = (place + STEPS[n]) % 4
        return pltpu.make_async_copy(
            b_in.at[i, a, pl.ds(0, 512), :], b_ref.at[n, i], b_sem.at[n, i]
        )

    images = [
        pltpu.make_async_copy(
            b_in.at[i, :, pl.ds(512, IMAGE // 2), :], image_ref.at[i], image_sem.at[i]
        )
        for i in range(4)
    ]
    early = [
        pltpu.make_async_copy(
            early_in.at[(place + step) % 4], early_ref.at[n], early_sem.at[n]
        )
        for n, step in enumerate(STEPS)
    ]
    for copy in images:
        copy.start()
    for n in range(4):
        early[n].start()
        for i in range(4):
            load(n, i).start()
    for copy in images:
        copy.wait()
    image = sum([image_ref[i].astype(f32) for i in range(4)]).reshape(2, IMAGE, 256)
    image = image[0] + image[1]
    high = image.astype(bf16)
    low = (image - high.astype(f32)).astype(bf16)
    stores = [
        pltpu.make_async_copy(both_ref.at[n], out, sem.at[n]) for n, out in enumerate((o0, o1, o2, o3))
    ]
    for n in range(4):
        both_ref[n, 768 : 768 + IMAGE, :] = high
        both_ref[n, 768 + IMAGE : 768 + 2 * IMAGE, :] = low
        early[n].wait()
        both_ref[n, 0:256, :] = early_ref[n]
        for i in range(4):
            load(n, i).wait()
        total = sum([b_ref[n, i].astype(f32) for i in range(4)])
        both_ref[n, 256:768, :] = total.astype(bf16)
        stores[n].start()
    for store in stores:
        store.wait()


def add(place, early, sent_b):
    rows = 768 + 2 * IMAGE
    dma = pltpu.SemaphoreType.DMA
    return call(
        add_kernel,
        [shaped(rows, 256)] * 4,
        place,
        early,
        sent_b,
        places="shh",
        outs="hhhh",
        scratch=[
            pltpu.VMEM((4, 256, 256), bf16),
            pltpu.VMEM((4, 4, 512, 256), bf16),
            pltpu.VMEM((4, 4, IMAGE // 2, 256), bf16),
            pltpu.VMEM((4, rows, 256), bf16),
            dma((4,)),
            dma((4, 4)),
            dma((4,)),
            dma((4,)),
        ],
        nbytes=6e6,
    )


LAST = QC + HC + 4 * 256


def image_rows(d):
    return [start + d for start in STARTS[:4]] + [28 + d, 48 + d] + [
        32 + 4 * d + i for i in range(4)
    ] + [16 + 3 * d + i for i in range(3)]


def part_kernel(far_ref, r0, r1, r2, r3, slots_ref, keep_ref, send_ref, total_ref, rows_ref):
    far = far_ref[0]
    total_ref[...] = sum([ref[...].astype(f32) for ref in (r0, r1, r2, r3)])
    rows_ref[...] = jnp.zeros_like(rows_ref)
    for d in range(4):
        for i, row in enumerate(image_rows(d)):
            high = total_ref[768 + row : 769 + row, :]
            low = total_ref[768 + IMAGE + row : 769 + IMAGE + row, :]
            rows_ref[d, i : i + 1, :] = high + low
        image = rows_ref[d]
        high = image.astype(bf16)
        low = (image - high.astype(f32)).astype(bf16)
        for zh in range(2):
            s = d * 2 + zh
            for p in range(3):
                row = (d * 3 + p) * 16 + zh * 8
                slots_ref[s, :, p * 256 : (p + 1) * 256] = total_ref[row : row + 8, :].astype(bf16)
            for cg in range(4):
                row = 256 + (cg * 4 + d) * 16 + zh * 8
                at = QC + cg * 256
                slots_ref[s, :, at : at + 256] = total_ref[row : row + 8, :].astype(bf16)
            for n, block in enumerate((high[:8], high[8:], low[:8], low[8:])):
                at = QC + HC + n * 256
                slots_ref[s, :, at : at + 256] = block
    for ref, half in ((keep_ref, far), (send_ref, 1 - far)):
        for cg in range(4):
            at = slice(cg * 256, (cg + 1) * 256)
            row = pl.multiple_of(192 + cg * 16 + half * 8, 8)
            ref[32:40, at] = total_ref[pl.ds(row, 8), :].astype(ref.dtype)
            row = pl.multiple_of(512 + cg * 64 + half * 32, 8)
            ref[0:32, at] = total_ref[pl.ds(row, 32), :].astype(ref.dtype)


def part(far, received):
    return call(
        part_kernel,
        [shaped(8, 8, LAST), shaped(40, D, dtype=f32), shaped(40, D)],
        far,
        *received,
        outs="uuu",
        scratch=[pltpu.VMEM((768 + 2 * IMAGE, 256), f32), pltpu.VMEM((4, 16, 256), f32)],
        nbytes=4e6,
    )


def finish_kernel(
    place_ref, slots_ref, keep_ref, got_ref, qkv_out, up_out, dense_out, down_out, *rest
):
    tiny_refs = rest[:8]
    image_ref, qkv_ref, up_ref, dense_ref, down_ref, sem = rest[8:]
    image = [jnp.zeros((8, 256), f32)] * 2
    for s in range(8):
        for n in range(4):
            at = QC + HC + n * 256
            image[n % 2] = image[n % 2] + slots_ref[s, :, at : at + 256].astype(f32)
    image_ref[0:8, :] = image[0]
    image_ref[8:16, :] = image[1]
    def rows_out(ref, out, first):
        width = ref.shape[2]
        copies = [
            pltpu.make_async_copy(
                ref.at[r, 0], out.at[pl.ds(r * width, width)], sem.at[first + r]
            )
            for r in range(ref.shape[0])
        ]
        for copy in copies:
            copy.start()
        return copies

    total = keep_ref[...] + got_ref[...].astype(f32)
    dense_ref[:, 0, :] = total[32:40]
    down_ref[:, 0, :] = total[0:32]
    copies = rows_out(dense_ref, dense_out, 0) + rows_out(down_ref, down_out, 8)
    for d in range(4):
        both = slots_ref[2 * d, :, 0 : QC + HC].astype(f32) + slots_ref[
            2 * d + 1, :, 0 : QC + HC
        ].astype(f32)
        for p in range(3):
            at = p * D + d * 256
            qkv_ref[:, 0, at : at + 256] = both[:, p * 256 : (p + 1) * 256]
        up_ref[:, 0, d * HC : (d + 1) * HC] = both[:, QC:]
    copies += rows_out(qkv_ref, qkv_out, 40) + rows_out(up_ref, up_out, 48)
    p = place_ref[0]
    f = p % 32
    lines = (0, 1, 2, 3, 10 + f * 24 // 256, 4, 6 + f // 8, 5)
    for line, size, ref in zip(lines, SIZES, tiny_refs):
        lane = (p * size) % 256
        values = image_ref[pl.ds(line, 1), :]
        if size == 24:
            values = jnp.concatenate([values, image_ref[pl.ds(line + 1, 1), :]], axis=1)
        ref[...] = pltpu.roll(values, values.shape[1] - lane, 1)[:, :size]
    for copy in copies:
        copy.wait()


def finish(place, slots, keep, got):
    return call(
        finish_kernel,
        [
            shaped(8 * 3 * D, dtype=f32),
            shaped(8 * FF, dtype=f32),
            shaped(8 * D, dtype=f32),
            shaped(32 * D, dtype=f32),
        ]
        + [shaped(1, size, dtype=f32) for size in SIZES],
        place,
        slots,
        keep,
        got,
        outs="hhhh" + "v" * 8,
        scratch=[
            pltpu.VMEM((16, 256), f32),
            pltpu.VMEM((8, 1, 3 * D), f32),
            pltpu.VMEM((8, 1, FF), f32),
            pltpu.VMEM((8, 1, D), f32),
            pltpu.VMEM((32, 1, D), f32),
            pltpu.SemaphoreType.DMA((56,)),
        ],
        nbytes=2e6,
    )


def body(
    inputs,
    cotangent,
    lengths,
    norm1_gain,
    norm1_bias,
    norm2_gain,
    norm2_bias,
    qkv_weight,
    qkv_bias,
    dense_weight,
    dense_bias,
    up_weight,
    up_bias,
    down_weight,
    down_bias,
):
    me = lax.axis_index("dp").astype(jnp.int32)
    index = lax.axis_index("fsdp").astype(jnp.int32)
    far = (index % 2)[None]
    me1 = me[None]
    outer, inner = outer_groups(), inner_groups()

    vectors = (
        norm1_gain,
        norm1_bias,
        norm2_gain,
        norm2_bias,
        qkv_bias,
        dense_bias,
        up_bias,
        down_bias,
    )
    x2, c2 = flip_core(inputs), flip_core(cotangent)
    slots, pieces = prepare(
        qkv_weight.reshape(8, 3 * D),
        up_weight.reshape(8, FF),
        dense_weight.reshape(8, D),
        down_weight.reshape(32, D),
        lengths,
        vectors,
    )
    slots, x2, c2 = lax.optimization_barrier((slots, x2, c2))
    far_pieces = flip_far(pieces)
    first = a2a(slots, stack_groups())
    block, lens = spread(index[None], first.reshape(4, 16, SLOT), pieces, far_pieces)
    along_x, along_y = index // 2 % 4, index // 8
    core = me % 2 == 1
    near = jnp.where(core, along_x, along_y)[None]
    deep = jnp.where(core, along_y, along_x)[None]
    info = jnp.concatenate([lens[0], me1, far, near])

    block, x0, c0 = lax.optimization_barrier((block, inputs, cotangent))
    x1, c1 = flip_chip(x0), flip_chip(c0)
    second = gather(block, inner)
    second, x1 = lax.optimization_barrier((second, x1))
    third_a = gather(merge_a(deep, second), outer)
    x3, c3 = flip_core(x1), flip_core(c1)
    xs, cots = (x0, x1, x2, x3), (c0, c1, c2, c3)
    wide_b, xs, cots = lax.optimization_barrier((merge_b(deep, second), xs, cots))
    third_b = gather(wide_b, outer)

    sent_a, gb, ctx, dqkv, xhat, vec, up_b, sums = attention(info, xs, cots, third_a)
    sent_a = a2a(sent_a, outer)
    sent_b, hidden, dpre = mlp(info, third_b, gb, xhat, up_b, vec, sums)
    sent_b = a2a(sent_b, outer)

    theirs, mine = outputs(info, ctx, hidden, dqkv, dpre, third_a, third_b, vec)
    kept, send = half_sum(mine, flip_core(theirs))

    got = flip_chip(send)
    early, send = lax.optimization_barrier((add_early(sent_a), send))
    fourth = scatter(add(deep, early, sent_b), inner)
    slots, keep, rest = part(far, fourth)
    block_output, input_grad = close(lengths, inputs, cotangent, kept, got, vec)
    place = (me * 32 + index)[None]
    slots, rest, block_output, input_grad = lax.optimization_barrier(
        (a2a(slots, stack_groups()), flip_far(rest), block_output, input_grad)
    )
    results = finish(place, slots, keep, rest)
    flat = [r.reshape(-1) for r in results]
    return (
        block_output,
        input_grad,
        flat[4],
        flat[5],
        flat[6],
        flat[7],
        flat[0],
        flat[8],
        flat[2],
        flat[9],
        flat[1],
        flat[10],
        flat[3],
        flat[11],
    )


def solution(mesh):
    flat = P(("dp", "fsdp"))
    rows = P(("dp", "fsdp"), None)
    return jax.shard_map(
        body,
        mesh=mesh,
        in_specs=(rows,) * 3 + (flat,) * 12,
        out_specs=(rows,) * 2 + (flat,) * 12,
        check_vma=False,
    )
```

```python
import jax
import jax.numpy as jnp
import ml_dtypes
import numpy as np
from jax import lax
from jax.experimental import pallas as pl
from jax.experimental.pallas import tpu as pltpu
from jax.sharding import PartitionSpec as P

D = 1024
HEADS = 16
HEAD_DIM = 64
ROT = 16
FF = 4096
ROW = 256
SEGS = 8
TP = 4
QC = 3 * D // TP
HC = FF // TP
LOCAL_HEADS = HEADS // TP
STRIP = 32
AXES = ("dp", "fsdp")
VMEM = 44 * 1024 * 1024

f32 = jnp.float32
bf16 = jnp.bfloat16


def dev(d, y, x, zh):
    return d * 32 + y * 8 + x * 2 + zh


def outer_groups(flip=0):
    groups = []
    for d in range(4):
        for k in range(4):
            for zh in range(2):
                if d % 2 == flip:
                    groups.append([dev(d, i, k, zh) for i in range(4)])
                else:
                    groups.append([dev(d, k, i, zh) for i in range(4)])
    return groups


def inner_groups():
    return outer_groups(flip=1)


def stack_groups():
    return [
        [dev(d, y, x, zh) for d in range(4) for zh in range(2)] for y in range(4) for x in range(4)
    ]


def plane_groups():
    return [
        [dev(d, y, x, zh) for y in range(4) for x in range(4)] for d in range(4) for zh in range(2)
    ]


def ring(values, groups, step):
    pairs = [(g[i], g[(i + step) % 4]) for g in groups for i in range(4)]
    return lax.ppermute(values, AXES, pairs)


STEPS = (0, 1, 3, 2)


def gather(values, groups):
    return [values] + [ring(values, groups, k) for k in STEPS[1:]]


def scatter(values, groups):
    return [values[0]] + [ring(v, groups, k) for v, k in zip(values[1:], STEPS[1:])]


def a2a(values, groups):
    return lax.all_to_all(values, AXES, 0, 0, tiled=True, axis_index_groups=groups)


def flip_core(values):
    return lax.ppermute(values, "dp", [(0, 1), (1, 0), (2, 3), (3, 2)])


def flip_chip(values):
    return lax.ppermute(values, "dp", [(0, 2), (2, 0), (1, 3), (3, 1)])


def flip_far(values):
    return lax.ppermute(values, "fsdp", [(i, i ^ 1) for i in range(32)])


def dot(left, right):
    return jnp.dot(left, right, preferred_element_type=f32)


def dot_nt(left, right):
    return lax.dot_general(left, right, (((1,), (1,)), ((), ())), preferred_element_type=f32)


def dot_tn(left, right):
    return lax.dot_general(left, right, (((0,), (0,)), ((), ())), preferred_element_type=f32)


def in_hbm(values):
    return pltpu.with_memory_space_constraint(values, pltpu.HBM)


VMEM_SPEC = pl.BlockSpec(memory_space=pltpu.VMEM)
SMEM_SPEC = pl.BlockSpec(memory_space=pltpu.SMEM)
HBM_SPEC = pl.BlockSpec(memory_space=pltpu.HBM)
SPECS = {"a": pl.BlockSpec(memory_space=pl.ANY), "s": SMEM_SPEC, "v": VMEM_SPEC, "u": VMEM_SPEC, "h": HBM_SPEC}


def call(kernel, out_shape, *args, places=None, outs=None, scratch=(), flops=0, nbytes=0, trans=0):
    places = places or "s" + "v" * (len(args) - 1)
    out_specs = jax.tree.map(lambda _: VMEM_SPEC, out_shape)
    if outs is not None:
        out_specs = [SPECS[o] for o in outs]
        out_shape = [
            v if o == "v" else pltpu.HBM(v.shape, v.dtype) for o, v in zip(outs, out_shape)
        ]
    args = [in_hbm(v) if p == "h" else v for p, v in zip(places, args)]
    return pl.pallas_call(
        kernel,
        in_specs=[SPECS[p] for p in places],
        out_specs=out_specs,
        out_shape=out_shape,
        scratch_shapes=list(scratch),
        compiler_params=pltpu.CompilerParams(vmem_limit_bytes=VMEM),
        cost_estimate=pl.CostEstimate(
            flops=int(flops), bytes_accessed=int(nbytes), transcendentals=int(trans)
        ),
    )(*args)


def shaped(*shape, dtype=bf16):
    return jax.ShapeDtypeStruct(shape, dtype)


def normalize(x):
    average = jnp.mean(x, axis=-1, keepdims=True)
    centred = x - average
    inv_std = lax.rsqrt(jnp.mean(centred * centred, axis=-1, keepdims=True) + 1e-05)
    return centred * inv_std, inv_std


STARTS = (0, 4, 8, 12, 16, 28, 32, 48)
SIZES = (8, 8, 8, 8, 24, 8, 32, 8)
IMAGE = 64
LENS = 64
SLOT = QC + HC + 128


def tile(n):
    return pl.ds(pl.multiple_of(n * 256, 256), 256)


def swapped(y, x, c):
    return y + c * (x - y), x + c * (y - x)


def prepare_kernel(
    qkv_ref, up_ref, dense_in, down_in, len_in, n1g, n1b, n2g, n2b, qb, db, ub, dnb,
    out_ref, pieces_ref, tile_ref, *rest
):
    sources = (len_in, n1g, n1b, n2g, n2b, qb, db, ub, dnb)
    holders, sem = rest[:9], rest[9]
    copies = [
        pltpu.make_async_copy(src, dst, sem.at[i])
        for i, (src, dst) in enumerate(zip(sources, holders))
    ]
    for copy in copies:
        copy.start()
    for d in range(4):
        for zh in range(2):
            s = d * 2 + zh
            for p in range(3):
                at = p * D + d * 256
                out_ref[s, :, p * 256 : (p + 1) * 256] = qkv_ref[:, at : at + 256]
            out_ref[s, :, QC : QC + HC] = up_ref[:, d * HC : (d + 1) * HC]
    pieces_ref[0:32, :] = down_in[...]
    pieces_ref[32:40, :] = dense_in[...]
    tile_ref[...] = jnp.zeros_like(tile_ref)
    for copy in copies:
        copy.wait()
    for i, (size, ref) in enumerate(zip(SIZES, holders[1:])):
        tile_ref[i : i + 1, 0:size] = ref[...].astype(f32)
    tile_ref[0:1, LENS : LENS + SEGS] = holders[0][...].astype(f32)
    block = tile_ref[...].astype(bf16)
    for s in range(8):
        out_ref[s, :, QC + HC : SLOT] = block


def prepare(qkv, up, dense, down, lengths, vectors):
    vectors = [v[None, :] for v in vectors]
    return call(
        prepare_kernel,
        [shaped(8, 8, SLOT), shaped(40, D)],
        qkv,
        up,
        dense,
        down,
        lengths,
        *vectors,
        places="vvvv" + "h" * 9,
        scratch=[pltpu.VMEM((8, 128), f32), pltpu.VMEM((1, SEGS), jnp.int32)]
        + [pltpu.VMEM(v.shape, bf16) for v in vectors]
        + [pltpu.SemaphoreType.DMA((9,))],
        nbytes=1e6,
    )


def locate(p, start, size):
    first = p * size
    return start + first // 256, first % 256


def spread_kernel(index_ref, first_ref, mine_ref, theirs_ref, out_ref, lens_ref, image_ref):
    index = index_ref[0]
    far = index % 2 == 1
    mine, theirs = mine_ref[...].astype(f32), theirs_ref[...].astype(f32)
    low, high = jnp.where(far, theirs, mine), jnp.where(far, mine, theirs)
    down = jnp.concatenate([low[:32], high[:32]], axis=0).astype(bf16)
    dense = jnp.concatenate([low[32:], high[32:]], axis=0).astype(bf16)
    image_ref[...] = jnp.zeros_like(image_ref)
    lens = []
    for d in range(4):
        both = first_ref[d, :, QC + HC : SLOT].astype(f32)
        for zh in range(2):
            p = d * 32 + index // 2 * 2 + zh
            tile = both[zh * 8 : zh * 8 + 8]
            lens.append(tile[0:1, LENS : LENS + SEGS])
            for i, (start, size) in enumerate(zip(STARTS, SIZES)):
                row, lane = locate(p, start, size)
                wide = 512 if size == 24 else 256
                blank = jnp.zeros((1, wide - size), f32)
                values = jnp.concatenate([tile[i : i + 1, :size], blank], axis=1)
                values = pltpu.roll(values, lane, 1)
                image_ref[pl.ds(row, 1), :] += values[:, :256]
                if wide == 512:
                    image_ref[pl.ds(row + 1, 1), :] += values[:, 256:]
    lens_ref[...] = jnp.concatenate(lens, axis=1).astype(jnp.int32)
    image = image_ref[...].astype(bf16)
    for d in range(4):
        for p in range(3):
            row = (d * 3 + p) * 16
            out_ref[row : row + 16, :] = first_ref[d, :, p * 256 : (p + 1) * 256]
        for cg in range(4):
            row = 256 + (d * 4 + cg) * 16
            at = QC + cg * 256
            out_ref[row : row + 16, :] = first_ref[d, :, at : at + 256]
    for cg in range(4):
        at = slice(cg * 256, (cg + 1) * 256)
        out_ref[192 + cg * 16 : 208 + cg * 16, :] = dense[:, at]
        out_ref[512 + cg * 64 : 576 + cg * 64, :] = down[:, at]
    out_ref[768 : 768 + IMAGE, :] = image


def spread(index, first, mine, theirs):
    return call(
        spread_kernel,
        [shaped(768 + IMAGE, 256), shaped(1, 64, dtype=jnp.int32)],
        index,
        first,
        mine,
        theirs,
        scratch=[pltpu.VMEM((IMAGE, 256), f32)],
        nbytes=2e6,
    )


def merge_a_kernel(place_ref, b0, b1, b2, b3, out_ref):
    blocks = (b0, b1, b2, b3)
    for block, step in zip(blocks, STEPS):
        a = (place_ref[0] + 4 - step) % 4
        out_ref[tile(a), :] = block[0:256, :]
    total = sum([block[768 : 768 + IMAGE, :].astype(f32) for block in blocks])
    out_ref[1024 : 1024 + IMAGE, :] = total.astype(bf16)


def merge_a(place, blocks):
    return call(
        merge_a_kernel, [shaped(1024 + IMAGE, 256)], place, *blocks, outs="u", nbytes=1e6
    )[0]


def merge_b_kernel(place_ref, b0, b1, b2, b3, out_ref):
    for block, step in zip((b0, b1, b2, b3), STEPS):
        a = (place_ref[0] + 4 - step) % 4
        out_ref[pl.ds(pl.multiple_of(a * 512, 512), 512), :] = block[256:768, :]


def merge_b(place, blocks):
    return call(merge_b_kernel, [shaped(2048, 256)], place, *blocks, outs="u", nbytes=2e6)[0]


def assemble_a(me, buf_ref, wqkv_ref, wd_ref):
    c = me % 2
    for y in range(4):
        for x in range(4):
            b, a = swapped(y, x, c)
            yx = y * 4 + x
            base = a * 256
            for d in range(4):
                for p in range(3):
                    row = pl.multiple_of(base + (d * 3 + p) * 16, 16)
                    wqkv_ref[d * 256 + yx * 16 : d * 256 + yx * 16 + 16, p * 256 : (p + 1) * 256] = (
                        buf_ref[b, pl.ds(row, 16), :]
                    )
            for cg in range(4):
                row = pl.multiple_of(base + 192 + cg * 16, 16)
                wd_ref[yx * 16 : yx * 16 + 16, cg * 256 : (cg + 1) * 256] = buf_ref[
                    b, pl.ds(row, 16), :
                ]


def read_vectors(me, buf_ref, vec_ref, qb_ref, ub_ref):
    image = sum([buf_ref[b, 1024 : 1024 + IMAGE, :].astype(f32) for b in range(4)])

    def long(start):
        return jnp.concatenate([image[start + i : start + i + 1, :] for i in range(4)], axis=1)

    vec_ref[...] = jnp.zeros_like(vec_ref)
    for i in range(4):
        vec_ref[i : i + 1, :] = long(4 * i)
    vec_ref[4:5, :] = long(28) + long(48)
    own = [jnp.where(me == d, 1.0, 0.0) for d in range(4)]
    rows = [sum([image[16 + p * 4 + d : 17 + p * 4 + d] * own[d] for d in range(4)]) for p in range(3)]
    qb_ref[...] = jnp.concatenate(rows, axis=1)
    ub_ref[...] = sum([long(32 + 4 * d) * own[d] for d in range(4)])


def assemble_b(me, buf_ref, wup_ref, wdown_ref):
    c = me % 2
    for y in range(4):
        for x in range(4):
            b, a = swapped(y, x, c)
            yx = y * 4 + x
            base = a * 512
            for d in range(4):
                for cg in range(4):
                    row = pl.multiple_of(base + (d * 4 + cg) * 16, 16)
                    wup_ref[d * 256 + yx * 16 : d * 256 + yx * 16 + 16, cg * 256 : (cg + 1) * 256] = (
                        buf_ref[b, pl.ds(row, 16), :]
                    )
            for cg in range(4):
                row = pl.multiple_of(base + 256 + cg * 64, 16)
                wdown_ref[yx * 64 : yx * 64 + 64, cg * 256 : (cg + 1) * 256] = buf_ref[
                    b, pl.ds(row, 64), :
                ]


def turn(u, cosine, sin_left, sin_right):
    return (
        u * cosine
        + pltpu.roll(u, u.shape[1] - ROT // 2, 1) * sin_left
        + pltpu.roll(u, ROT // 2, 1) * sin_right
    )


def rotary_tables():
    places = np.arange(ROW, dtype=np.float32)
    freqs = (10000.0 ** (-(np.arange(ROT // 2, dtype=np.float32) * 2.0) / ROT)).astype(np.float32)
    angle = (places[:, None] * freqs[None, :]).astype(np.float32)
    cosine, sine = np.cos(angle), np.sin(angle)
    zeros = np.zeros_like(sine)
    rest = np.zeros((ROW, HEAD_DIM - ROT), np.float32)
    parts = [[cosine, cosine, rest + 1.0], [-sine, zeros, rest], [zeros, sine, rest]]
    columns = []
    for part in parts:
        whole = np.tile(np.concatenate(part, axis=1), (1, 2)).astype(np.float32)
        high = whole.astype(ml_dtypes.bfloat16)
        columns += [high, (whole - high.astype(np.float32)).astype(ml_dtypes.bfloat16)]
    return np.concatenate(columns, axis=1)


def row_sums(values):
    total = jnp.sum(values, axis=1, keepdims=True)
    return jnp.transpose(jnp.broadcast_to(total, (256, 128)))[0:1, :]


def through(sums, matrix):
    high = sums.astype(bf16)
    low = (sums - high.astype(f32)).astype(bf16)
    both = jnp.concatenate([high.astype(f32), low.astype(f32)] + [jnp.zeros_like(sums)] * 6, axis=0)
    out = dot_nt(both.astype(bf16), matrix)
    return out[0:1] + out[1:2]


def in_turn(rows):
    while rows:
        rows = [row for row in rows if next(row, "end") != "end"]


def attention_kernel(
    info_ref,
    x0,
    x1,
    x2,
    x3,
    c0,
    c1,
    c2,
    c3,
    w0,
    w1,
    w2,
    w3,
    rot_in,
    sent_out,
    gb_out,
    ctx_out,
    dqkv_out,
    xhat_out,
    vec_ref,
    ub_ref,
    sums_ref,
    x_ref,
    cot_ref,
    wqkv_ref,
    wd_ref,
    qb_ref,
    gb_ref,
    ctx_ref,
    dqkv_ref,
    xhat_ref,
    sent_ref,
    in_sem,
    out_sem,
    sent_sem,
    vec_col_ref,
    buf_ref,
    buf_sem,
    rot_ref,
    rot_sem,
):
    me = info_ref[64]
    place = info_ref[66]
    parts = []
    for n, (src, step) in enumerate(zip((w0, w1, w2, w3), STEPS)):
        b = (place + 4 - step) % 4
        parts.append(pltpu.make_async_copy(src, buf_ref.at[b], buf_sem.at[n]))
    for copy in parts:
        copy.start()
    loads = []
    for i, (one, other) in enumerate(zip((x0, x1, x2, x3), (c0, c1, c2, c3))):
        loads.append(pltpu.make_async_copy(one, x_ref.at[i], in_sem.at[i, 0]))
        loads.append(pltpu.make_async_copy(other, cot_ref.at[i], in_sem.at[i, 1]))
    for load in loads[:2]:
        load.start()
    for copy in parts:
        copy.wait()
    assemble_a(me, buf_ref, wqkv_ref, wd_ref)
    rotary = pltpu.make_async_copy(rot_in, rot_ref, rot_sem)
    rotary.start()
    for load in loads[2:]:
        load.start()
    read_vectors(me, buf_ref, vec_ref, qb_ref, ub_ref)
    rotary.wait()
    stores = (
        (gb_ref, gb_out),
        (ctx_ref, ctx_out),
        (xhat_ref, xhat_out),
        (dqkv_ref, dqkv_out),
    )

    def store(n, r):
        rows = pl.ds(pl.multiple_of(r * ROW, ROW), ROW)
        src, dst = stores[n]
        return pltpu.make_async_copy(src.at[rows, :], dst.at[rows, :], out_sem.at[n, r])

    sums_ref[...] = jnp.zeros_like(sums_ref)

    def one_row(r):
        pltpu.make_async_copy(x0, x_ref.at[r], in_sem.at[r, 0]).wait()
        pltpu.make_async_copy(c0, cot_ref.at[r], in_sem.at[r, 1]).wait()
        here = pl.ds(pl.multiple_of(r * ROW, ROW), ROW)
        xhat, _ = normalize(x_ref[r].astype(f32))
        xhat_ref[here, :] = xhat.astype(bf16)
        attn_in = (xhat * vec_ref[0:1] + vec_ref[1:2]).astype(bf16)
        yield
        qkv = dot(attn_in, wqkv_ref[...]) + qb_ref[...]
        d = me ^ ((r & 1) * 2 + r // 2)
        base = (d * 2 + info_ref[65]) * SEGS
        ends, end = [], 0
        for j in range(SEGS - 1):
            end = end + info_ref[base + j]
            ends.append(end)
        rows = lax.broadcasted_iota(jnp.int32, (ROW, 1), 0)
        cols = lax.broadcasted_iota(jnp.int32, (1, ROW), 1)
        row_doc = sum([(rows >= e).astype(jnp.int32) for e in ends])
        col_doc = sum([(cols >= e).astype(jnp.int32) for e in ends])
        allowed = (row_doc == col_doc) & (rows <= cols)
        start = jnp.zeros_like(rows)
        for e in ends:
            start = jnp.maximum(start, jnp.where(rows >= e, e, 0))
        kept = jnp.where(rows < ends[-1], cot_ref[r].astype(f32), 0.0)
        gb = kept.astype(bf16)
        gb_ref[here, :] = gb
        yield
        dctx = dot_nt(gb, wd_ref[...]).astype(bf16)
        chosen = ((rows - start) == cols).astype(f32).astype(bf16)
        yield
        table = dot(chosen, rot_ref[...])
        pair = lambda n: table[:, n * 256 : n * 256 + 128] + table[:, n * 256 + 128 : n * 256 + 256]
        cosine, left, right = [jnp.concatenate([pair(n)] * 2, axis=1) for n in range(3)]
        scale = HEAD_DIM**-0.5
        q = (turn(qkv[:, 0:256], cosine, left, right).astype(bf16).astype(f32) * scale).astype(bf16)
        k = turn(qkv[:, 256:512], cosine, left, right).astype(bf16)
        v = qkv[:, 512:768].astype(bf16)
        yield
        lanes = lax.broadcasted_iota(jnp.int32, (1, 256), 1) // HEAD_DIM
        ctx, dq, dk, dv = [jnp.zeros((ROW, 256), f32)] * 4
        heads = range(LOCAL_HEADS)
        only = [(lanes == h).astype(f32).astype(bf16) for h in heads]
        qs, dcs = [q * m for m in only], [dctx * m for m in only]
        s_all = dot_nt(k, jnp.concatenate(qs, axis=0))
        dp_all = dot_nt(v, jnp.concatenate(dcs, axis=0))
        yield
        cut = [slice(h * ROW, (h + 1) * ROW) for h in heads]
        scores = [jnp.where(allowed, s_all[:, c], -1000000000.0) for c in cut]
        dprobs = [dp_all[:, c] for c in cut]
        probs = []
        for h in heads:
            yield
            shifted = jnp.exp(scores[h] - jnp.max(scores[h], axis=0, keepdims=True))
            probs.append(shifted * (1.0 / jnp.sum(shifted, axis=0, keepdims=True)))
        yield
        lows = [p.astype(bf16) for p in probs]
        ds = []
        for h in heads:
            yield
            inner = jnp.sum(dprobs[h] * probs[h], axis=0, keepdims=True)
            ds.append((probs[h] * (dprobs[h] - inner)).astype(bf16))
        yield
        p_all = jnp.concatenate(lows, axis=0)
        ds_all = jnp.concatenate(ds, axis=0)
        ctx = dot_tn(p_all, jnp.concatenate([v * m for m in only], axis=0))
        dq = dot_tn(ds_all, jnp.concatenate([k * m for m in only], axis=0))
        dv = dot(jnp.concatenate(lows, axis=1), jnp.concatenate(dcs, axis=0))
        dk = dot(jnp.concatenate(ds, axis=1), jnp.concatenate(qs, axis=0))
        yield
        ctx_ref[here, :] = ctx.astype(bf16)
        dqs = turn(dq * scale, cosine, -left, -right)
        dks = turn(dk, cosine, -left, -right)
        dqkv = jnp.concatenate([dqs, dks, dv], axis=1).astype(bf16)
        dqkv_ref[here, :] = dqkv

        first = jnp.where(r == 0, 1.0, 0.0)
        sums_ref[0:1, :] += first * jnp.sum(kept, axis=0, keepdims=True)
        sums_ref[1:2, 0:QC] += jnp.sum(dqkv.astype(f32), axis=0, keepdims=True)
        for n in range(4):
            store(n, r).start()

    in_turn([one_row(r) for r in range(TP)])

    c = me % 2
    sums_ref[3:4, :] = through(sums_ref[1:2, 0:QC], wqkv_ref[...])
    columns = jnp.transpose(vec_ref[...])
    vec_col_ref[...] = columns

    def sent(d, n):
        rows = pl.ds(pl.multiple_of(d * 48, 16), 48)
        if n == 1:
            rows = pl.ds(pl.multiple_of(192 + d * 16, 16), 16)
        return pltpu.make_async_copy(
            sent_ref.at[:, :, rows, :], sent_out.at[:, :, rows, :], sent_sem.at[d, n]
        )

    @pl.loop(0, 4)
    def _(d):
        raw = dot_tn(xhat_ref[:, tile(d)], dqkv_ref[...])
        gain, bias = vec_col_ref[tile(d), 0:1], vec_col_ref[tile(d), 1:2]
        qkv_grad = (raw * gain + bias * sums_ref[1:2, 0:QC]).astype(bf16)
        sums_ref[2:3, tile(d)] = row_sums(raw * wqkv_ref[tile(d), :].astype(f32))
        dense_grad = dot_tn(ctx_ref[...], gb_ref[:, tile(d)]).astype(bf16)
        base = pl.multiple_of(d * 48, 16)
        dense_base = pl.multiple_of(192 + d * 16, 16)
        for y in range(4):
            for x in range(4):
                b, a = swapped(y, x, c)
                at = slice((y * 4 + x) * 16, (y * 4 + x + 1) * 16)
                for p in range(3):
                    sent_ref[b, a, pl.ds(base + p * 16, 16), :] = qkv_grad[
                        at, p * 256 : (p + 1) * 256
                    ]
                sent_ref[b, a, pl.ds(dense_base, 16), :] = dense_grad[at]
        sent(d, 0).start()
        sent(d, 1).start()

    @pl.loop(0, 4)
    def _(i):
        for n in range(4):
            store(n, i).wait()
        sent(i, 0).wait()
        sent(i, 1).wait()


def attention(info, xs, cots, blocks):
    tokens = TP * ROW
    dma = pltpu.SemaphoreType.DMA
    return call(
        attention_kernel,
        [
            shaped(4, 4, 256, 256),
            shaped(tokens, D),
            shaped(tokens, 256),
            shaped(tokens, QC),
            shaped(tokens, D),
            shaped(8, D, dtype=f32),
            shaped(1, HC, dtype=f32),
            shaped(8, D, dtype=f32),
        ],
        info,
        *xs,
        *cots,
        *blocks,
        jnp.asarray(rotary_tables()),
        places="s" + "a" * 12 + "h",
        outs="h" * 5 + "vvv",
        scratch=[
            pltpu.VMEM((TP, ROW, D), bf16),
            pltpu.VMEM((TP, ROW, D), bf16),
            pltpu.VMEM((D, QC), bf16),
            pltpu.VMEM((D // TP, D), bf16),
            pltpu.VMEM((1, QC), f32),
            pltpu.VMEM((tokens, D), bf16),
            pltpu.VMEM((tokens, 256), bf16),
            pltpu.VMEM((tokens, QC), bf16),
            pltpu.VMEM((tokens, D), bf16),
            pltpu.VMEM((4, 4, 256, 256), bf16),
            dma((4, 2)),
            dma((4, 4)),
            dma((4, 2)),
            pltpu.VMEM((D, 8), f32),
            pltpu.VMEM((4, 1024 + IMAGE, 256), bf16),
            dma((4,)),
            pltpu.VMEM((ROW, 768), bf16),
            dma,
        ],
        flops=6e9,
        nbytes=2e7,
        trans=1e6,
    )


def mlp_kernel(
    info_ref,
    w0,
    w1,
    w2,
    w3,
    gb_in,
    xhat_in,
    ub_ref,
    vec_ref,
    sums_a_ref,
    sent_out,
    hidden_out,
    dpre_out,
    buf_ref,
    gb_ref,
    wup_ref,
    wdown_ref,
    hidden_ref,
    dpre_ref,
    sent_ref,
    xhat_ref,
    sums_ref,
    image_ref,
    vec_col_ref,
    min_ref,
    rows_ref,
    turned_ref,
    buf_sem,
    in_sem,
    out_sem,
    sent_sem,
    image_sem,
):
    me, place = info_ref[64], info_ref[66]
    c = me % 2
    parts = []
    for n, (src, step) in enumerate(zip((w0, w1, w2, w3), STEPS)):
        b = (place + 4 - step) % 4
        parts.append(pltpu.make_async_copy(src, buf_ref.at[b], buf_sem.at[n]))

    def load(t, n):
        src, dst = ((gb_in, gb_ref), (xhat_in, xhat_ref))[n]
        return pltpu.make_async_copy(src.at[tile(t), :], dst.at[tile(t), :], in_sem.at[t, n])

    for part in parts:
        part.start()
    for t in range(4):
        for n in range(2):
            load(t, n).start()
    for part in parts:
        part.wait()
    assemble_b(me, buf_ref, wup_ref, wdown_ref)
    sums_ref[...] = jnp.zeros_like(sums_ref)

    vec_col_ref[...] = jnp.transpose(vec_ref[...])
    rows_ref[...] = jnp.zeros_like(rows_ref)

    def store(j, n):
        src, dst = ((hidden_ref, hidden_out), (dpre_ref, dpre_out))[n]
        return pltpu.make_async_copy(src.at[:, tile(j)], dst.at[:, tile(j)], out_sem.at[j, n])

    def sent_up(j):
        rows = pl.ds(pl.multiple_of(j * 64, 64), 64)
        return pltpu.make_async_copy(
            sent_ref.at[:, :, rows, :], sent_out.at[:, :, rows, :], sent_sem.at[j, 4]
        )

    def sent_down(j, x):
        b, a = swapped(j, x, c)
        rows = pl.ds(256, 256)
        return pltpu.make_async_copy(
            sent_ref.at[b, a, rows, :], sent_out.at[b, a, rows, :], sent_sem.at[j, x]
        )

    def hidden_tile(j, t):
        at = pl.ds(t * ROW, ROW)
        pre = dot(min_ref[at, :], wup_ref[:, tile(j)]) + ub_ref[:, tile(j)]
        return pre, dot_nt(gb_ref[at, :], wdown_ref[tile(j), :])

    def activate(j, t, pre, back):
        total = jnp.zeros((8, 256), f32)
        for i in range(0, ROW, STRIP):
            at = pl.ds(t * ROW + i, STRIP)
            a, b = pre[i : i + STRIP], back[i : i + STRIP]
            size = jnp.abs(a) * 0.7071067811865476
            bell = jnp.exp(-0.5 * a * a)
            s = 1.0 / (1.0 + 0.3275911 * size)
            poly = s * (
                0.127414796
                + s * (-0.142248368 + s * (0.7107068705 + s * (-0.7265760135 + s * 0.5307027145)))
            )
            tail = poly * bell
            cumul = jnp.where(a >= 0.0, 1.0 - tail, tail)
            hidden_ref[at, tile(j)] = (a * cumul).astype(bf16)
            dpre = (b * (cumul + a * (bell * 0.3989422804014327))).astype(bf16)
            dpre_ref[at, tile(j)] = dpre
            total += jnp.sum(dpre.astype(f32).reshape(STRIP // 8, 8, 256), axis=0)
        return jnp.sum(total, axis=0, keepdims=True)

    def put_down(j):
        down = dot_tn(hidden_ref[:, tile(j)], gb_ref[...]).astype(bf16)
        for x in range(4):
            b, a = swapped(j, x, c)
            for cg in range(4):
                sent_ref[b, a, 256 + cg * 64 : 256 + (cg + 1) * 64, :] = down[
                    x * 64 : (x + 1) * 64, cg * 256 : (cg + 1) * 256
                ]

    def put_up(j, t, raw):
        row = pl.multiple_of(j * 64 + t * 16, 16)
        sums = sums_ref[0:1, tile(j)]
        for y in range(4):
            for x in range(4):
                b, a = swapped(y, x, c)
                i = (y * 4 + x) * 16
                at = slice(t * 256 + i, t * 256 + i + 16)
                part = raw[i : i + 16]
                product = part * wup_ref[at, tile(j)].astype(f32)
                rows_ref[at, :] += product[:, :128] + product[:, 128:]
                gain, bias = vec_col_ref[at, 2:3], vec_col_ref[at, 3:4]
                sent_ref[b, a, pl.ds(row, 16), :] = (part * gain + bias * sums).astype(bf16)

    def step(j, last=False, first=False):
        if not last:
            total = jnp.zeros((1, 256), f32)
        for t in range(TP):
            if first:
                at = pl.ds(t * ROW, ROW)
                load(t, 0).wait()
                load(t, 1).wait()
                for i in range(0, ROW, 16):
                    strip = pl.ds(t * ROW + i, 16)
                    values = xhat_ref[strip, :].astype(f32)
                    min_ref[strip, :] = (values * vec_ref[2:3] + vec_ref[3:4]).astype(bf16)
                turned_ref[:, at] = jnp.transpose(xhat_ref[at, :])
            if not last:
                pre, back = hidden_tile(j, t)
            if not first:
                if t == 0:
                    put_down(j - 1)
                raw = dot(turned_ref[t * 256 : (t + 1) * 256, :], dpre_ref[:, tile(j - 1)])
            if not last:
                total += activate(j, t, pre, back)
            if not first:
                put_up(j - 1, t, raw)
        if not last:
            sums_ref[0:1, tile(j)] = total
            store(j, 0).start()
            store(j, 1).start()
        if not first:
            sent_up(j - 1).start()
            for x in range(4):
                sent_down(j - 1, x).start()

    step(0, first=True)

    @pl.loop(1, 4)
    def _(j):
        step(j)

    step(4, last=True)
    total = jnp.sum(rows_ref[...], axis=1, keepdims=True)
    sums_ref[1:2, :] = jnp.transpose(jnp.broadcast_to(total, (D, 128)))[0:1, :]
    sums_ref[2:3, :] = through(sums_ref[0:1, :], wup_ref[...])

    image_ref[...] = jnp.zeros_like(image_ref)

    def put(row, ref, line, count):
        for i in range(count):
            image_ref[pl.ds(row + i, 1), :] = ref[line : line + 1, i * 256 : (i + 1) * 256]

    put(0, sums_a_ref, 2, 4)
    put(4, sums_a_ref, 3, 4)
    put(8, sums_ref, 1, 4)
    put(12, sums_ref, 2, 4)
    for p in range(3):
        image_ref[pl.ds(16 + p * 4 + me, 1), :] = sums_a_ref[1:2, p * 256 : (p + 1) * 256]
    put(28, sums_a_ref, 0, 4)
    put(32 + 4 * me, sums_ref, 0, 4)
    put(48, sums_a_ref, 0, 4)
    image = image_ref[...]
    high = image.astype(bf16)
    low = (image - high.astype(f32)).astype(bf16)
    for b in range(4):
        for a in range(4):
            half = (high, low)[a // 2]
            sent_ref[b, a, 512 : 512 + IMAGE // 2, :] = half[a % 2 * 32 : a % 2 * 32 + 32]
    rows = pl.ds(512, IMAGE // 2)
    images = pltpu.make_async_copy(
        sent_ref.at[:, :, rows, :], sent_out.at[:, :, rows, :], image_sem
    )
    images.start()
    for i in range(TP):
        store(i, 0).wait()
        store(i, 1).wait()
        sent_up(i).wait()
        for x in range(4):
            sent_down(i, x).wait()
    images.wait()


def mlp(info, blocks, gb, xhat, ub, vec, sums):
    tokens = TP * ROW
    dma = pltpu.SemaphoreType.DMA
    return call(
        mlp_kernel,
        [
            shaped(4, 4, 512 + IMAGE // 2, 256),
            shaped(tokens, HC),
            shaped(tokens, HC),
        ],
        info,
        *blocks,
        gb,
        xhat,
        ub,
        vec,
        sums,
        places="s" + "a" * 4 + "hhvvv",
        outs="hhh",
        scratch=[
            pltpu.VMEM((4, 2048, 256), bf16),
            pltpu.VMEM((tokens, D), bf16),
            pltpu.VMEM((D, HC), bf16),
            pltpu.VMEM((HC, D), bf16),
            pltpu.VMEM((tokens, HC), bf16),
            pltpu.VMEM((tokens, HC), bf16),
            pltpu.VMEM((4, 4, 512 + IMAGE // 2, 256), bf16),
            pltpu.VMEM((tokens, D), bf16),
            pltpu.VMEM((8, D), f32),
            pltpu.VMEM((IMAGE, 256), f32),
            pltpu.VMEM((D, 8), f32),
            pltpu.VMEM((tokens, D), bf16),
            pltpu.VMEM((D, 128), f32),
            pltpu.VMEM((D, tokens), bf16),
            dma((4,)),
            dma((4, 2)),
            dma((4, 2)),
            dma((4, 5)),
            dma,
        ],
        flops=9e9,
        nbytes=2e7,
        trans=2e6,
    )


def outputs_kernel(
    info_ref,
    ctx_in,
    hidden_in,
    dqkv_in,
    dpre_in,
    a0,
    a1,
    a2,
    a3,
    b0,
    b1,
    b2,
    b3,
    vec_ref,
    theirs_out,
    mine_out,
    ctx_ref,
    hidden_ref,
    dqkv_ref,
    dpre_ref,
    wd_ref,
    wdown_ref,
    wqkv_ref,
    wup_ref,
    both_ref,
    buf_a_ref,
    buf_b_ref,
    weight_sem,
    in_sem,
    out_sem,
):
    me, place = info_ref[64], info_ref[66]
    weights = []
    for n, step in enumerate(STEPS):
        b = (place + 4 - step) % 4
        pairs = (((a0, a1, a2, a3)[n], buf_a_ref), ((b0, b1, b2, b3)[n], buf_b_ref))
        for i, (src, dst) in enumerate(pairs):
            weights.append(pltpu.make_async_copy(src, dst.at[b], weight_sem.at[n, i]))
    inputs = (
        (dqkv_in, dqkv_ref),
        (dpre_in, dpre_ref),
        (ctx_in, ctx_ref),
        (hidden_in, hidden_ref),
    )

    def load(t, n):
        src, dst = inputs[n]
        return pltpu.make_async_copy(src.at[tile(t), :], dst.at[tile(t), :], in_sem.at[t, n])

    def finished(i, n):
        dst = (theirs_out, mine_out)[n]
        return pltpu.make_async_copy(both_ref.at[i], dst.at[i - 2 * n], out_sem.at[i])

    for weight in weights:
        weight.start()
    for i in range(TP):
        for n in range(4):
            load((i + 2) % 4, n).start()
    for weight in weights:
        weight.wait()
    assemble_a(me, buf_a_ref, wqkv_ref, wd_ref)
    assemble_b(me, buf_b_ref, wup_ref, wdown_ref)

    @pl.loop(0, TP)
    def _(i):
        t = (i + 2) % 4
        for n in range(4):
            load(t, n).wait()
        here = tile(t)
        dattn = dot_nt(dqkv_ref[here, :], wqkv_ref[...])
        dmlp = dot_nt(dpre_ref[here, :], wup_ref[...])
        both_ref[i, 1] = (dattn * vec_ref[0:1] + dmlp * vec_ref[2:3]).astype(bf16)
        forward = dot(ctx_ref[here, :], wd_ref[...]) + dot(hidden_ref[here, :], wdown_ref[...])
        both_ref[i, 0] = forward.astype(bf16)

        @pl.when(i < 2)
        def _():
            finished(i, 0).start()

        @pl.when(i >= 2)
        def _():
            finished(i, 1).start()

    for i in range(TP):
        finished(i, i // 2).wait()


def outputs(info, ctx, hidden, dqkv, dpre, blocks_a, blocks_b, vec):
    tokens = TP * ROW
    dma = pltpu.SemaphoreType.DMA
    return call(
        outputs_kernel,
        [shaped(2, 2, ROW, D), shaped(2, 2, ROW, D)],
        info,
        ctx,
        hidden,
        dqkv,
        dpre,
        *blocks_a,
        *blocks_b,
        vec,
        places="s" + "a" * 12 + "v",
        outs="hh",
        scratch=[
            pltpu.VMEM((tokens, 256), bf16),
            pltpu.VMEM((tokens, HC), bf16),
            pltpu.VMEM((tokens, QC), bf16),
            pltpu.VMEM((tokens, HC), bf16),
            pltpu.VMEM((D // TP, D), bf16),
            pltpu.VMEM((HC, D), bf16),
            pltpu.VMEM((D, QC), bf16),
            pltpu.VMEM((D, HC), bf16),
            pltpu.VMEM((TP, 2, ROW, D), bf16),
            pltpu.VMEM((4, 1024 + IMAGE, 256), bf16),
            pltpu.VMEM((4, 2048, 256), bf16),
            dma((4, 2)),
            dma((4, 4)),
            dma((4,)),
        ],
        flops=6.5e9,
        nbytes=1.6e7,
    )


def half_kernel(mine_in, got_in, kept_out, send_out, mine_ref, got_ref, kept_ref, send_ref, in_sem, out_sem):
    loads = []
    for i in (1, 0):
        for n in range(2):
            pair = (
                pltpu.make_async_copy(mine_in.at[i, n], mine_ref.at[i, n], in_sem.at[i, n, 0]),
                pltpu.make_async_copy(got_in.at[i, n], got_ref.at[i, n], in_sem.at[i, n, 1]),
            )
            loads.append((i, n, pair))
            for copy in pair:
                copy.start()
    stores = []
    for i, n, pair in loads:
        for copy in pair:
            copy.wait()
        total = mine_ref[i, n].astype(f32) + got_ref[i, n].astype(f32)
        ref, out = ((kept_ref, kept_out), (send_ref, send_out))[i]
        ref[n] = total.astype(ref.dtype)
        stores.append(pltpu.make_async_copy(ref.at[n], out.at[0, n], out_sem.at[i, n]))
        stores[-1].start()
    for store in stores:
        store.wait()


def half_sum(mine, got):
    dma = pltpu.SemaphoreType.DMA
    return call(
        half_kernel,
        [shaped(1, 2, ROW, D, dtype=f32), shaped(1, 2, ROW, D)],
        mine,
        got,
        places="ha",
        outs="hh",
        scratch=[
            pltpu.VMEM((2, 2, ROW, D), bf16),
            pltpu.VMEM((2, 2, ROW, D), bf16),
            pltpu.VMEM((2, ROW, D), f32),
            pltpu.VMEM((2, ROW, D), bf16),
            dma((2, 2, 2)),
            dma((2, 2)),
        ],
        nbytes=8e6,
    )


def close_kernel(len_ref, x_ref, cot_ref, kept_ref, got_ref, vec_ref, out_ref, grad_ref):
    x = x_ref[...].astype(f32)
    out_ref[...] = (x + kept_ref[0, 0] + got_ref[0, 0].astype(f32) + vec_ref[4:5]).astype(bf16)
    e = kept_ref[0, 1] + got_ref[0, 1].astype(f32)
    xhat, inv_std = normalize(x)
    mean_e = jnp.mean(e, axis=-1, keepdims=True)
    mean_ex = jnp.mean(e * xhat, axis=-1, keepdims=True)
    used = sum([len_ref[0, j] for j in range(SEGS - 1)])
    rows = pl.program_id(0) * x.shape[0] + lax.broadcasted_iota(jnp.int32, (x.shape[0], 1), 0)
    kept = jnp.where(rows < used, cot_ref[...].astype(f32), 0.0)
    grad_ref[...] = kept + inv_std * (e - mean_e - xhat * mean_ex)


def close(lengths, x, cot, kept, got, vec):
    row = pl.BlockSpec((ROW // 4, D), lambda k: (k, 0))
    both = pl.BlockSpec((1, 2, ROW // 4, D), lambda k: (0, 0, k, 0))
    return pl.pallas_call(
        close_kernel,
        grid=(4,),
        in_specs=[SMEM_SPEC, row, row, both, both, pl.BlockSpec((8, D), lambda k: (0, 0))],
        out_specs=[row, row],
        out_shape=[pltpu.HBM((ROW, D), bf16), pltpu.HBM((ROW, D), f32)],
        compiler_params=pltpu.CompilerParams(vmem_limit_bytes=VMEM),
        cost_estimate=pl.CostEstimate(flops=0, bytes_accessed=6000000, transcendentals=0),
    )(lengths, *[in_hbm(v) for v in (x, cot, kept, got)], vec)


def add_early_kernel(a_ref, out_ref):
    out_ref[0] = sum([a_ref[i, 0].astype(f32) for i in range(4)]).astype(bf16)


def add_early(sent_a):
    return pl.pallas_call(
        add_early_kernel,
        grid=(4,),
        in_specs=[pl.BlockSpec((4, 1, 256, 256), lambda a: (0, a, 0, 0))],
        out_specs=pl.BlockSpec((1, 256, 256), lambda a: (a, 0, 0)),
        out_shape=pltpu.HBM((4, 256, 256), bf16),
        compiler_params=pltpu.CompilerParams(vmem_limit_bytes=VMEM),
        cost_estimate=pl.CostEstimate(flops=0, bytes_accessed=3000000, transcendentals=0),
    )(sent_a)


def add_kernel(
    place_ref, early_in, b_in, o0, o1, o2, o3, early_ref, b_ref, image_ref, both_ref, early_sem, b_sem, image_sem, sem
):
    place = place_ref[0]

    def load(n, i):
        a = (place + STEPS[n]) % 4
        return pltpu.make_async_copy(
            b_in.at[i, a, pl.ds(0, 512), :], b_ref.at[n, i], b_sem.at[n, i]
        )

    images = [
        pltpu.make_async_copy(
            b_in.at[i, :, pl.ds(512, IMAGE // 2), :], image_ref.at[i], image_sem.at[i]
        )
        for i in range(4)
    ]
    early = [
        pltpu.make_async_copy(
            early_in.at[(place + step) % 4], early_ref.at[n], early_sem.at[n]
        )
        for n, step in enumerate(STEPS)
    ]
    for copy in images:
        copy.start()
    for n in range(4):
        early[n].start()
        for i in range(4):
            load(n, i).start()
    for copy in images:
        copy.wait()
    image = sum([image_ref[i].astype(f32) for i in range(4)]).reshape(2, IMAGE, 256)
    image = image[0] + image[1]
    high = image.astype(bf16)
    low = (image - high.astype(f32)).astype(bf16)
    stores = [
        pltpu.make_async_copy(both_ref.at[n], out, sem.at[n]) for n, out in enumerate((o0, o1, o2, o3))
    ]
    for n in range(4):
        both_ref[n, 768 : 768 + IMAGE, :] = high
        both_ref[n, 768 + IMAGE : 768 + 2 * IMAGE, :] = low
        early[n].wait()
        both_ref[n, 0:256, :] = early_ref[n]
        for i in range(4):
            load(n, i).wait()
        total = sum([b_ref[n, i].astype(f32) for i in range(4)])
        both_ref[n, 256:768, :] = total.astype(bf16)
        stores[n].start()
    for store in stores:
        store.wait()


def add(place, early, sent_b):
    rows = 768 + 2 * IMAGE
    dma = pltpu.SemaphoreType.DMA
    return call(
        add_kernel,
        [shaped(rows, 256)] * 4,
        place,
        early,
        sent_b,
        places="shh",
        outs="hhhh",
        scratch=[
            pltpu.VMEM((4, 256, 256), bf16),
            pltpu.VMEM((4, 4, 512, 256), bf16),
            pltpu.VMEM((4, 4, IMAGE // 2, 256), bf16),
            pltpu.VMEM((4, rows, 256), bf16),
            dma((4,)),
            dma((4, 4)),
            dma((4,)),
            dma((4,)),
        ],
        nbytes=6e6,
    )


LAST = QC + HC + 4 * 256


def image_rows(d):
    return [start + d for start in STARTS[:4]] + [28 + d, 48 + d] + [
        32 + 4 * d + i for i in range(4)
    ] + [16 + 3 * d + i for i in range(3)]


def part_kernel(far_ref, r0, r1, r2, r3, slots_ref, keep_ref, send_ref, total_ref, rows_ref):
    far = far_ref[0]
    total_ref[...] = sum([ref[...].astype(f32) for ref in (r0, r1, r2, r3)])
    rows_ref[...] = jnp.zeros_like(rows_ref)
    for d in range(4):
        for i, row in enumerate(image_rows(d)):
            high = total_ref[768 + row : 769 + row, :]
            low = total_ref[768 + IMAGE + row : 769 + IMAGE + row, :]
            rows_ref[d, i : i + 1, :] = high + low
        image = rows_ref[d]
        high = image.astype(bf16)
        low = (image - high.astype(f32)).astype(bf16)
        for zh in range(2):
            s = d * 2 + zh
            for p in range(3):
                row = (d * 3 + p) * 16 + zh * 8
                slots_ref[s, :, p * 256 : (p + 1) * 256] = total_ref[row : row + 8, :].astype(bf16)
            for cg in range(4):
                row = 256 + (cg * 4 + d) * 16 + zh * 8
                at = QC + cg * 256
                slots_ref[s, :, at : at + 256] = total_ref[row : row + 8, :].astype(bf16)
            for n, block in enumerate((high[:8], high[8:], low[:8], low[8:])):
                at = QC + HC + n * 256
                slots_ref[s, :, at : at + 256] = block
    for ref, half in ((keep_ref, far), (send_ref, 1 - far)):
        for cg in range(4):
            at = slice(cg * 256, (cg + 1) * 256)
            row = pl.multiple_of(192 + cg * 16 + half * 8, 8)
            ref[32:40, at] = total_ref[pl.ds(row, 8), :].astype(ref.dtype)
            row = pl.multiple_of(512 + cg * 64 + half * 32, 8)
            ref[0:32, at] = total_ref[pl.ds(row, 32), :].astype(ref.dtype)


def part(far, received):
    return call(
        part_kernel,
        [shaped(8, 8, LAST), shaped(40, D, dtype=f32), shaped(40, D)],
        far,
        *received,
        outs="uuu",
        scratch=[pltpu.VMEM((768 + 2 * IMAGE, 256), f32), pltpu.VMEM((4, 16, 256), f32)],
        nbytes=4e6,
    )


def finish_kernel(
    place_ref, slots_ref, keep_ref, got_ref, qkv_out, up_out, dense_out, down_out, *rest
):
    tiny_refs = rest[:8]
    image_ref, qkv_ref, up_ref, dense_ref, down_ref, sem = rest[8:]
    image = [jnp.zeros((8, 256), f32)] * 2
    for s in range(8):
        for n in range(4):
            at = QC + HC + n * 256
            image[n % 2] = image[n % 2] + slots_ref[s, :, at : at + 256].astype(f32)
    image_ref[0:8, :] = image[0]
    image_ref[8:16, :] = image[1]
    def rows_out(ref, out, first):
        width = ref.shape[2]
        copies = [
            pltpu.make_async_copy(
                ref.at[r, 0], out.at[pl.ds(r * width, width)], sem.at[first + r]
            )
            for r in range(ref.shape[0])
        ]
        for copy in copies:
            copy.start()
        return copies

    total = keep_ref[...] + got_ref[...].astype(f32)
    dense_ref[:, 0, :] = total[32:40]
    down_ref[:, 0, :] = total[0:32]
    copies = rows_out(dense_ref, dense_out, 0) + rows_out(down_ref, down_out, 8)
    for d in range(4):
        both = slots_ref[2 * d, :, 0 : QC + HC].astype(f32) + slots_ref[
            2 * d + 1, :, 0 : QC + HC
        ].astype(f32)
        for p in range(3):
            at = p * D + d * 256
            qkv_ref[:, 0, at : at + 256] = both[:, p * 256 : (p + 1) * 256]
        up_ref[:, 0, d * HC : (d + 1) * HC] = both[:, QC:]
    copies += rows_out(qkv_ref, qkv_out, 40) + rows_out(up_ref, up_out, 48)
    p = place_ref[0]
    f = p % 32
    lines = (0, 1, 2, 3, 10 + f * 24 // 256, 4, 6 + f // 8, 5)
    for line, size, ref in zip(lines, SIZES, tiny_refs):
        lane = (p * size) % 256
        values = image_ref[pl.ds(line, 1), :]
        if size == 24:
            values = jnp.concatenate([values, image_ref[pl.ds(line + 1, 1), :]], axis=1)
        width = values.shape[1]
        ref[...] = pltpu.roll(values, (width - lane) % width, 1)[:, :size]
    for copy in copies:
        copy.wait()


def finish(place, slots, keep, got):
    return call(
        finish_kernel,
        [
            shaped(8 * 3 * D, dtype=f32),
            shaped(8 * FF, dtype=f32),
            shaped(8 * D, dtype=f32),
            shaped(32 * D, dtype=f32),
        ]
        + [shaped(1, size, dtype=f32) for size in SIZES],
        place,
        slots,
        keep,
        got,
        outs="hhhh" + "v" * 8,
        scratch=[
            pltpu.VMEM((16, 256), f32),
            pltpu.VMEM((8, 1, 3 * D), f32),
            pltpu.VMEM((8, 1, FF), f32),
            pltpu.VMEM((8, 1, D), f32),
            pltpu.VMEM((32, 1, D), f32),
            pltpu.SemaphoreType.DMA((56,)),
        ],
        nbytes=2e6,
    )


def body(
    inputs,
    cotangent,
    lengths,
    norm1_gain,
    norm1_bias,
    norm2_gain,
    norm2_bias,
    qkv_weight,
    qkv_bias,
    dense_weight,
    dense_bias,
    up_weight,
    up_bias,
    down_weight,
    down_bias,
):
    me = lax.axis_index("dp").astype(jnp.int32)
    index = lax.axis_index("fsdp").astype(jnp.int32)
    far = (index % 2)[None]
    me1 = me[None]
    outer, inner = outer_groups(), inner_groups()

    vectors = (
        norm1_gain,
        norm1_bias,
        norm2_gain,
        norm2_bias,
        qkv_bias,
        dense_bias,
        up_bias,
        down_bias,
    )
    x2, c2 = flip_core(inputs), flip_core(cotangent)
    slots, pieces = prepare(
        qkv_weight.reshape(8, 3 * D),
        up_weight.reshape(8, FF),
        dense_weight.reshape(8, D),
        down_weight.reshape(32, D),
        lengths,
        vectors,
    )
    far_pieces = flip_far(pieces)
    first = a2a(slots, stack_groups())
    first, x2, c2 = lax.optimization_barrier((first, x2, c2))
    block, lens = spread(index[None], first.reshape(4, 16, SLOT), pieces, far_pieces)
    along_x, along_y = index // 2 % 4, index // 8
    core = me % 2 == 1
    near = jnp.where(core, along_x, along_y)[None]
    deep = jnp.where(core, along_y, along_x)[None]
    info = jnp.concatenate([lens[0], me1, far, near])

    block, x0, c0 = lax.optimization_barrier((block, inputs, cotangent))
    x1, c1 = flip_chip(x0), flip_chip(c0)
    second = gather(block, inner)
    second, x1 = lax.optimization_barrier((second, x1))
    third_a = gather(merge_a(deep, second), outer)
    x3, c3 = flip_core(x1), flip_core(c1)
    xs, cots = (x0, x1, x2, x3), (c0, c1, c2, c3)
    wide_b, xs = lax.optimization_barrier((merge_b(deep, second), xs))
    third_b = gather(wide_b, outer)

    sent_a, gb, ctx, dqkv, xhat, vec, up_b, sums = attention(info, xs, cots, third_a)
    sent_a = a2a(sent_a, outer)
    sent_b, hidden, dpre = mlp(info, third_b, gb, xhat, up_b, vec, sums)
    sent_b = a2a(sent_b, outer)

    theirs, mine = outputs(info, ctx, hidden, dqkv, dpre, third_a, third_b, vec)
    kept, send = half_sum(mine, flip_core(theirs))

    got = flip_chip(send)
    early, send = lax.optimization_barrier((add_early(sent_a), send))
    fourth = scatter(add(deep, early, sent_b), inner)
    slots, keep, rest = part(far, fourth)
    block_output, input_grad = close(lengths, inputs, cotangent, kept, got, vec)
    place = (me * 32 + index)[None]
    slots, rest, block_output, input_grad = lax.optimization_barrier(
        (a2a(slots, stack_groups()), flip_far(rest), block_output, input_grad)
    )
    results = finish(place, slots, keep, rest)
    flat = [r.reshape(-1) for r in results]
    return (
        block_output,
        input_grad,
        flat[4],
        flat[5],
        flat[6],
        flat[7],
        flat[0],
        flat[8],
        flat[2],
        flat[9],
        flat[1],
        flat[10],
        flat[3],
        flat[11],
    )


def solution(mesh):
    flat = P(("dp", "fsdp"))
    rows = P(("dp", "fsdp"), None)
    return jax.shard_map(
        body,
        mesh=mesh,
        in_specs=(rows,) * 3 + (flat,) * 12,
        out_specs=(rows,) * 2 + (flat,) * 12,
        check_vma=False,
    )
```

```python
import jax
import jax.numpy as jnp
import ml_dtypes
import numpy as np
from jax import lax
from jax.experimental import pallas as pl
from jax.experimental.pallas import tpu as pltpu
from jax.sharding import PartitionSpec as P

D = 1024
HEADS = 16
HEAD_DIM = 64
ROT = 16
FF = 4096
ROW = 256
SEGS = 8
TP = 4
QC = 3 * D // TP
HC = FF // TP
LOCAL_HEADS = HEADS // TP
STRIP = 32
AXES = ("dp", "fsdp")
VMEM = 44 * 1024 * 1024

f32 = jnp.float32
bf16 = jnp.bfloat16


def dev(d, y, x, zh):
    return d * 32 + y * 8 + x * 2 + zh


def outer_groups(flip=0):
    groups = []
    for d in range(4):
        for k in range(4):
            for zh in range(2):
                if d % 2 == flip:
                    groups.append([dev(d, i, k, zh) for i in range(4)])
                else:
                    groups.append([dev(d, k, i, zh) for i in range(4)])
    return groups


def inner_groups():
    return outer_groups(flip=1)


def stack_groups():
    return [
        [dev(d, y, x, zh) for d in range(4) for zh in range(2)] for y in range(4) for x in range(4)
    ]


def plane_groups():
    return [
        [dev(d, y, x, zh) for y in range(4) for x in range(4)] for d in range(4) for zh in range(2)
    ]


def ring(values, groups, step):
    pairs = [(g[i], g[(i + step) % 4]) for g in groups for i in range(4)]
    return lax.ppermute(values, AXES, pairs)


STEPS = (0, 1, 3, 2)


def gather(values, groups):
    return [values] + [ring(values, groups, k) for k in STEPS[1:]]


def scatter(values, groups):
    return [values[0]] + [ring(v, groups, k) for v, k in zip(values[1:], STEPS[1:])]


def a2a(values, groups):
    return lax.all_to_all(values, AXES, 0, 0, tiled=True, axis_index_groups=groups)


def flip_core(values):
    return lax.ppermute(values, "dp", [(0, 1), (1, 0), (2, 3), (3, 2)])


def flip_chip(values):
    return lax.ppermute(values, "dp", [(0, 2), (2, 0), (1, 3), (3, 1)])


def flip_far(values):
    return lax.ppermute(values, "fsdp", [(i, i ^ 1) for i in range(32)])


def dot(left, right):
    return jnp.dot(left, right, preferred_element_type=f32)


def dot_nt(left, right):
    return lax.dot_general(left, right, (((1,), (1,)), ((), ())), preferred_element_type=f32)


def dot_tn(left, right):
    return lax.dot_general(left, right, (((0,), (0,)), ((), ())), preferred_element_type=f32)


def in_hbm(values):
    return pltpu.with_memory_space_constraint(values, pltpu.HBM)


VMEM_SPEC = pl.BlockSpec(memory_space=pltpu.VMEM)
SMEM_SPEC = pl.BlockSpec(memory_space=pltpu.SMEM)
HBM_SPEC = pl.BlockSpec(memory_space=pltpu.HBM)
SPECS = {"a": pl.BlockSpec(memory_space=pl.ANY), "s": SMEM_SPEC, "v": VMEM_SPEC, "u": VMEM_SPEC, "h": HBM_SPEC}


def call(kernel, out_shape, *args, places=None, outs=None, scratch=(), flops=0, nbytes=0, trans=0):
    places = places or "s" + "v" * (len(args) - 1)
    out_specs = jax.tree.map(lambda _: VMEM_SPEC, out_shape)
    if outs is not None:
        out_specs = [SPECS[o] for o in outs]
        out_shape = [
            v if o == "v" else pltpu.HBM(v.shape, v.dtype) for o, v in zip(outs, out_shape)
        ]
    args = [in_hbm(v) if p == "h" else v for p, v in zip(places, args)]
    return pl.pallas_call(
        kernel,
        in_specs=[SPECS[p] for p in places],
        out_specs=out_specs,
        out_shape=out_shape,
        scratch_shapes=list(scratch),
        compiler_params=pltpu.CompilerParams(vmem_limit_bytes=VMEM),
        cost_estimate=pl.CostEstimate(
            flops=int(flops), bytes_accessed=int(nbytes), transcendentals=int(trans)
        ),
    )(*args)


def shaped(*shape, dtype=bf16):
    return jax.ShapeDtypeStruct(shape, dtype)


def normalize(x):
    average = jnp.mean(x, axis=-1, keepdims=True)
    centred = x - average
    inv_std = lax.rsqrt(jnp.mean(centred * centred, axis=-1, keepdims=True) + 1e-05)
    return centred * inv_std, inv_std


STARTS = (0, 4, 8, 12, 16, 28, 32, 48)
SIZES = (8, 8, 8, 8, 24, 8, 32, 8)
IMAGE = 64
LENS = 64
SLOT = QC + HC + 128


def tile(n):
    return pl.ds(pl.multiple_of(n * 256, 256), 256)


def swapped(y, x, c):
    return y + c * (x - y), x + c * (y - x)


def prepare_kernel(
    qkv_ref, up_ref, dense_in, down_in, len_in, n1g, n1b, n2g, n2b, qb, db, ub, dnb,
    out_ref, pieces_ref, tile_ref, *rest
):
    sources = (len_in, n1g, n1b, n2g, n2b, qb, db, ub, dnb)
    holders, sem = rest[:9], rest[9]
    copies = [
        pltpu.make_async_copy(src, dst, sem.at[i])
        for i, (src, dst) in enumerate(zip(sources, holders))
    ]
    for copy in copies:
        copy.start()
    for d in range(4):
        for zh in range(2):
            s = d * 2 + zh
            for p in range(3):
                at = p * D + d * 256
                out_ref[s, :, p * 256 : (p + 1) * 256] = qkv_ref[:, at : at + 256]
            out_ref[s, :, QC : QC + HC] = up_ref[:, d * HC : (d + 1) * HC]
    pieces_ref[0:32, :] = down_in[...]
    pieces_ref[32:40, :] = dense_in[...]
    tile_ref[...] = jnp.zeros_like(tile_ref)
    for copy in copies:
        copy.wait()
    for i, (size, ref) in enumerate(zip(SIZES, holders[1:])):
        tile_ref[i : i + 1, 0:size] = ref[...].astype(f32)
    tile_ref[0:1, LENS : LENS + SEGS] = holders[0][...].astype(f32)
    block = tile_ref[...].astype(bf16)
    for s in range(8):
        out_ref[s, :, QC + HC : SLOT] = block


def prepare(qkv, up, dense, down, lengths, vectors):
    vectors = [v[None, :] for v in vectors]
    return call(
        prepare_kernel,
        [shaped(8, 8, SLOT), shaped(40, D)],
        qkv,
        up,
        dense,
        down,
        lengths,
        *vectors,
        places="vvvv" + "h" * 9,
        scratch=[pltpu.VMEM((8, 128), f32), pltpu.VMEM((1, SEGS), jnp.int32)]
        + [pltpu.VMEM(v.shape, bf16) for v in vectors]
        + [pltpu.SemaphoreType.DMA((9,))],
        nbytes=1e6,
    )


def locate(p, start, size):
    first = p * size
    return start + first // 256, first % 256


def spread_kernel(index_ref, first_ref, mine_ref, theirs_ref, out_ref, lens_ref, image_ref):
    index = index_ref[0]
    far = index % 2 == 1
    mine, theirs = mine_ref[...].astype(f32), theirs_ref[...].astype(f32)
    low, high = jnp.where(far, theirs, mine), jnp.where(far, mine, theirs)
    down = jnp.concatenate([low[:32], high[:32]], axis=0).astype(bf16)
    dense = jnp.concatenate([low[32:], high[32:]], axis=0).astype(bf16)
    image_ref[...] = jnp.zeros_like(image_ref)
    lens = []
    for d in range(4):
        both = first_ref[d, :, QC + HC : SLOT].astype(f32)
        for zh in range(2):
            p = d * 32 + index // 2 * 2 + zh
            tile = both[zh * 8 : zh * 8 + 8]
            lens.append(tile[0:1, LENS : LENS + SEGS])
            for i, (start, size) in enumerate(zip(STARTS, SIZES)):
                row, lane = locate(p, start, size)
                wide = 512 if size == 24 else 256
                blank = jnp.zeros((1, wide - size), f32)
                values = jnp.concatenate([tile[i : i + 1, :size], blank], axis=1)
                values = pltpu.roll(values, lane, 1)
                image_ref[pl.ds(row, 1), :] += values[:, :256]
                if wide == 512:
                    image_ref[pl.ds(row + 1, 1), :] += values[:, 256:]
    lens_ref[...] = jnp.concatenate(lens, axis=1).astype(jnp.int32)
    image = image_ref[...].astype(bf16)
    for d in range(4):
        for p in range(3):
            row = (d * 3 + p) * 16
            out_ref[row : row + 16, :] = first_ref[d, :, p * 256 : (p + 1) * 256]
        for cg in range(4):
            row = 256 + (d * 4 + cg) * 16
            at = QC + cg * 256
            out_ref[row : row + 16, :] = first_ref[d, :, at : at + 256]
    for cg in range(4):
        at = slice(cg * 256, (cg + 1) * 256)
        out_ref[192 + cg * 16 : 208 + cg * 16, :] = dense[:, at]
        out_ref[512 + cg * 64 : 576 + cg * 64, :] = down[:, at]
    out_ref[768 : 768 + IMAGE, :] = image


def spread(index, first, mine, theirs):
    return call(
        spread_kernel,
        [shaped(768 + IMAGE, 256), shaped(1, 64, dtype=jnp.int32)],
        index,
        first,
        mine,
        theirs,
        scratch=[pltpu.VMEM((IMAGE, 256), f32)],
        nbytes=2e6,
    )


def merge_a_kernel(place_ref, b0, b1, b2, b3, out_ref):
    blocks = (b0, b1, b2, b3)
    for block, step in zip(blocks, STEPS):
        a = (place_ref[0] + 4 - step) % 4
        out_ref[tile(a), :] = block[0:256, :]
    total = sum([block[768 : 768 + IMAGE, :].astype(f32) for block in blocks])
    out_ref[1024 : 1024 + IMAGE, :] = total.astype(bf16)


def merge_a(place, blocks):
    return call(
        merge_a_kernel, [shaped(1024 + IMAGE, 256)], place, *blocks, outs="u", nbytes=1e6
    )[0]


def merge_b_kernel(place_ref, b0, b1, b2, b3, out_ref):
    for block, step in zip((b0, b1, b2, b3), STEPS):
        a = (place_ref[0] + 4 - step) % 4
        out_ref[pl.ds(pl.multiple_of(a * 512, 512), 512), :] = block[256:768, :]


def merge_b(place, blocks):
    return call(merge_b_kernel, [shaped(2048, 256)], place, *blocks, outs="u", nbytes=2e6)[0]


def assemble_a(me, buf_ref, wqkv_ref, wd_ref):
    c = me % 2
    for y in range(4):
        for x in range(4):
            b, a = swapped(y, x, c)
            yx = y * 4 + x
            base = a * 256
            for d in range(4):
                for p in range(3):
                    row = pl.multiple_of(base + (d * 3 + p) * 16, 16)
                    wqkv_ref[d * 256 + yx * 16 : d * 256 + yx * 16 + 16, p * 256 : (p + 1) * 256] = (
                        buf_ref[b, pl.ds(row, 16), :]
                    )
            for cg in range(4):
                row = pl.multiple_of(base + 192 + cg * 16, 16)
                wd_ref[yx * 16 : yx * 16 + 16, cg * 256 : (cg + 1) * 256] = buf_ref[
                    b, pl.ds(row, 16), :
                ]


def read_vectors(me, buf_ref, vec_ref, qb_ref, ub_ref):
    image = sum([buf_ref[b, 1024 : 1024 + IMAGE, :].astype(f32) for b in range(4)])

    def long(start):
        return jnp.concatenate([image[start + i : start + i + 1, :] for i in range(4)], axis=1)

    vec_ref[...] = jnp.zeros_like(vec_ref)
    for i in range(4):
        vec_ref[i : i + 1, :] = long(4 * i)
    vec_ref[4:5, :] = long(28) + long(48)
    own = [jnp.where(me == d, 1.0, 0.0) for d in range(4)]
    rows = [sum([image[16 + p * 4 + d : 17 + p * 4 + d] * own[d] for d in range(4)]) for p in range(3)]
    qb_ref[...] = jnp.concatenate(rows, axis=1)
    ub_ref[...] = sum([long(32 + 4 * d) * own[d] for d in range(4)])


def assemble_b(me, buf_ref, wup_ref, wdown_ref):
    c = me % 2
    for y in range(4):
        for x in range(4):
            b, a = swapped(y, x, c)
            yx = y * 4 + x
            base = a * 512
            for d in range(4):
                for cg in range(4):
                    row = pl.multiple_of(base + (d * 4 + cg) * 16, 16)
                    wup_ref[d * 256 + yx * 16 : d * 256 + yx * 16 + 16, cg * 256 : (cg + 1) * 256] = (
                        buf_ref[b, pl.ds(row, 16), :]
                    )
            for cg in range(4):
                row = pl.multiple_of(base + 256 + cg * 64, 16)
                wdown_ref[yx * 64 : yx * 64 + 64, cg * 256 : (cg + 1) * 256] = buf_ref[
                    b, pl.ds(row, 64), :
                ]


def turn(u, cosine, sin_left, sin_right):
    return (
        u * cosine
        + pltpu.roll(u, u.shape[1] - ROT // 2, 1) * sin_left
        + pltpu.roll(u, ROT // 2, 1) * sin_right
    )


def rotary_tables():
    places = np.arange(ROW, dtype=np.float32)
    freqs = (10000.0 ** (-(np.arange(ROT // 2, dtype=np.float32) * 2.0) / ROT)).astype(np.float32)
    angle = (places[:, None] * freqs[None, :]).astype(np.float32)
    cosine, sine = np.cos(angle), np.sin(angle)
    zeros = np.zeros_like(sine)
    rest = np.zeros((ROW, HEAD_DIM - ROT), np.float32)
    parts = [[cosine, cosine, rest + 1.0], [-sine, zeros, rest], [zeros, sine, rest]]
    columns = []
    for part in parts:
        whole = np.tile(np.concatenate(part, axis=1), (1, 2)).astype(np.float32)
        high = whole.astype(ml_dtypes.bfloat16)
        columns += [high, (whole - high.astype(np.float32)).astype(ml_dtypes.bfloat16)]
    return np.concatenate(columns, axis=1)


def row_sums(values):
    total = jnp.sum(values, axis=1, keepdims=True)
    return jnp.transpose(jnp.broadcast_to(total, (256, 128)))[0:1, :]


def through(sums, matrix):
    high = sums.astype(bf16)
    low = (sums - high.astype(f32)).astype(bf16)
    both = jnp.concatenate([high.astype(f32), low.astype(f32)] + [jnp.zeros_like(sums)] * 6, axis=0)
    out = dot_nt(both.astype(bf16), matrix)
    return out[0:1] + out[1:2]


def in_turn(rows):
    while rows:
        rows = [row for row in rows if next(row, "end") != "end"]


def attention_kernel(
    info_ref,
    x0,
    x1,
    x2,
    x3,
    c0,
    c1,
    c2,
    c3,
    w0,
    w1,
    w2,
    w3,
    rot_in,
    sent_out,
    gb_out,
    ctx_out,
    dqkv_out,
    xhat_out,
    vec_ref,
    ub_ref,
    sums_ref,
    x_ref,
    cot_ref,
    wqkv_ref,
    wd_ref,
    qb_ref,
    gb_ref,
    ctx_ref,
    dqkv_ref,
    xhat_ref,
    sent_ref,
    in_sem,
    out_sem,
    sent_sem,
    vec_col_ref,
    buf_ref,
    buf_sem,
    rot_ref,
    rot_sem,
):
    me = info_ref[64]
    place = info_ref[66]
    parts = []
    for n, (src, step) in enumerate(zip((w0, w1, w2, w3), STEPS)):
        b = (place + 4 - step) % 4
        parts.append(pltpu.make_async_copy(src, buf_ref.at[b], buf_sem.at[n]))
    for copy in parts:
        copy.start()
    loads = []
    for i, (one, other) in enumerate(zip((x0, x1, x2, x3), (c0, c1, c2, c3))):
        loads.append(pltpu.make_async_copy(one, x_ref.at[i], in_sem.at[i, 0]))
        loads.append(pltpu.make_async_copy(other, cot_ref.at[i], in_sem.at[i, 1]))
    for load in loads[:2]:
        load.start()
    for copy in parts:
        copy.wait()
    assemble_a(me, buf_ref, wqkv_ref, wd_ref)
    rotary = pltpu.make_async_copy(rot_in, rot_ref, rot_sem)
    rotary.start()
    for load in loads[2:]:
        load.start()
    read_vectors(me, buf_ref, vec_ref, qb_ref, ub_ref)
    rotary.wait()
    stores = (
        (gb_ref, gb_out),
        (ctx_ref, ctx_out),
        (xhat_ref, xhat_out),
        (dqkv_ref, dqkv_out),
    )

    def store(n, r):
        rows = pl.ds(pl.multiple_of(r * ROW, ROW), ROW)
        src, dst = stores[n]
        return pltpu.make_async_copy(src.at[rows, :], dst.at[rows, :], out_sem.at[n, r])

    sums_ref[...] = jnp.zeros_like(sums_ref)

    def one_row(r):
        pltpu.make_async_copy(x0, x_ref.at[r], in_sem.at[r, 0]).wait()
        pltpu.make_async_copy(c0, cot_ref.at[r], in_sem.at[r, 1]).wait()
        here = pl.ds(pl.multiple_of(r * ROW, ROW), ROW)
        xhat, _ = normalize(x_ref[r].astype(f32))
        xhat_ref[here, :] = xhat.astype(bf16)
        attn_in = (xhat * vec_ref[0:1] + vec_ref[1:2]).astype(bf16)
        yield
        qkv = dot(attn_in, wqkv_ref[...]) + qb_ref[...]
        d = me ^ ((r & 1) * 2 + r // 2)
        base = (d * 2 + info_ref[65]) * SEGS
        ends, end = [], 0
        for j in range(SEGS - 1):
            end = end + info_ref[base + j]
            ends.append(end)
        rows = lax.broadcasted_iota(jnp.int32, (ROW, 1), 0)
        cols = lax.broadcasted_iota(jnp.int32, (1, ROW), 1)
        row_doc = sum([(rows >= e).astype(jnp.int32) for e in ends])
        col_doc = sum([(cols >= e).astype(jnp.int32) for e in ends])
        allowed = (row_doc == col_doc) & (rows <= cols)
        start = jnp.zeros_like(rows)
        for e in ends:
            start = jnp.maximum(start, jnp.where(rows >= e, e, 0))
        kept = jnp.where(rows < ends[-1], cot_ref[r].astype(f32), 0.0)
        gb = kept.astype(bf16)
        gb_ref[here, :] = gb
        yield
        dctx = dot_nt(gb, wd_ref[...]).astype(bf16)
        chosen = ((rows - start) == cols).astype(f32).astype(bf16)
        yield
        table = dot(chosen, rot_ref[...])
        pair = lambda n: table[:, n * 256 : n * 256 + 128] + table[:, n * 256 + 128 : n * 256 + 256]
        cosine, left, right = [jnp.concatenate([pair(n)] * 2, axis=1) for n in range(3)]
        scale = HEAD_DIM**-0.5
        q = (turn(qkv[:, 0:256], cosine, left, right).astype(bf16).astype(f32) * scale).astype(bf16)
        k = turn(qkv[:, 256:512], cosine, left, right).astype(bf16)
        v = qkv[:, 512:768].astype(bf16)
        yield
        lanes = lax.broadcasted_iota(jnp.int32, (1, 256), 1) // HEAD_DIM
        ctx, dq, dk, dv = [jnp.zeros((ROW, 256), f32)] * 4
        heads = range(LOCAL_HEADS)
        only = [(lanes == h).astype(f32).astype(bf16) for h in heads]
        qs, dcs = [q * m for m in only], [dctx * m for m in only]
        s_all = dot_nt(k, jnp.concatenate(qs, axis=0))
        dp_all = dot_nt(v, jnp.concatenate(dcs, axis=0))
        yield
        cut = [slice(h * ROW, (h + 1) * ROW) for h in heads]
        scores = [jnp.where(allowed, s_all[:, c], -1000000000.0) for c in cut]
        dprobs = [dp_all[:, c] for c in cut]
        probs = []
        for h in heads:
            yield
            shifted = jnp.exp(scores[h] - jnp.max(scores[h], axis=0, keepdims=True))
            probs.append(shifted * (1.0 / jnp.sum(shifted, axis=0, keepdims=True)))
        yield
        lows = [p.astype(bf16) for p in probs]
        ds = []
        for h in heads:
            yield
            inner = jnp.sum(dprobs[h] * probs[h], axis=0, keepdims=True)
            ds.append((probs[h] * (dprobs[h] - inner)).astype(bf16))
        yield
        p_all = jnp.concatenate(lows, axis=0)
        ds_all = jnp.concatenate(ds, axis=0)
        ctx = dot_tn(p_all, jnp.concatenate([v * m for m in only], axis=0))
        dq = dot_tn(ds_all, jnp.concatenate([k * m for m in only], axis=0))
        dv = dot(jnp.concatenate(lows, axis=1), jnp.concatenate(dcs, axis=0))
        dk = dot(jnp.concatenate(ds, axis=1), jnp.concatenate(qs, axis=0))
        yield
        ctx_ref[here, :] = ctx.astype(bf16)
        dqs = turn(dq * scale, cosine, -left, -right)
        dks = turn(dk, cosine, -left, -right)
        dqkv = jnp.concatenate([dqs, dks, dv], axis=1).astype(bf16)
        dqkv_ref[here, :] = dqkv

        first = jnp.where(r == 0, 1.0, 0.0)
        sums_ref[0:1, :] += first * jnp.sum(kept, axis=0, keepdims=True)
        sums_ref[1:2, 0:QC] += jnp.sum(dqkv.astype(f32), axis=0, keepdims=True)
        for n in range(4):
            store(n, r).start()

    in_turn([one_row(r) for r in range(TP)])

    c = me % 2
    sums_ref[3:4, :] = through(sums_ref[1:2, 0:QC], wqkv_ref[...])
    columns = jnp.transpose(vec_ref[...])
    vec_col_ref[...] = columns

    def sent(d, n):
        rows = pl.ds(pl.multiple_of(d * 48, 16), 48)
        if n == 1:
            rows = pl.ds(pl.multiple_of(192 + d * 16, 16), 16)
        return pltpu.make_async_copy(
            sent_ref.at[:, :, rows, :], sent_out.at[:, :, rows, :], sent_sem.at[d, n]
        )

    @pl.loop(0, 4)
    def _(d):
        raw = dot_tn(xhat_ref[:, tile(d)], dqkv_ref[...])
        gain, bias = vec_col_ref[tile(d), 0:1], vec_col_ref[tile(d), 1:2]
        qkv_grad = (raw * gain + bias * sums_ref[1:2, 0:QC]).astype(bf16)
        sums_ref[2:3, tile(d)] = row_sums(raw * wqkv_ref[tile(d), :].astype(f32))
        dense_grad = dot_tn(ctx_ref[...], gb_ref[:, tile(d)]).astype(bf16)
        base = pl.multiple_of(d * 48, 16)
        dense_base = pl.multiple_of(192 + d * 16, 16)
        for y in range(4):
            for x in range(4):
                b, a = swapped(y, x, c)
                at = slice((y * 4 + x) * 16, (y * 4 + x + 1) * 16)
                for p in range(3):
                    sent_ref[b, a, pl.ds(base + p * 16, 16), :] = qkv_grad[
                        at, p * 256 : (p + 1) * 256
                    ]
                sent_ref[b, a, pl.ds(dense_base, 16), :] = dense_grad[at]
        sent(d, 0).start()
        sent(d, 1).start()

    @pl.loop(0, 4)
    def _(i):
        for n in range(4):
            store(n, i).wait()
        sent(i, 0).wait()
        sent(i, 1).wait()


def attention(info, xs, cots, blocks):
    tokens = TP * ROW
    dma = pltpu.SemaphoreType.DMA
    return call(
        attention_kernel,
        [
            shaped(4, 4, 256, 256),
            shaped(tokens, D),
            shaped(tokens, 256),
            shaped(tokens, QC),
            shaped(tokens, D),
            shaped(8, D, dtype=f32),
            shaped(1, HC, dtype=f32),
            shaped(8, D, dtype=f32),
        ],
        info,
        *xs,
        *cots,
        *blocks,
        jnp.asarray(rotary_tables()),
        places="s" + "a" * 12 + "h",
        outs="h" * 5 + "vvv",
        scratch=[
            pltpu.VMEM((TP, ROW, D), bf16),
            pltpu.VMEM((TP, ROW, D), bf16),
            pltpu.VMEM((D, QC), bf16),
            pltpu.VMEM((D // TP, D), bf16),
            pltpu.VMEM((1, QC), f32),
            pltpu.VMEM((tokens, D), bf16),
            pltpu.VMEM((tokens, 256), bf16),
            pltpu.VMEM((tokens, QC), bf16),
            pltpu.VMEM((tokens, D), bf16),
            pltpu.VMEM((4, 4, 256, 256), bf16),
            dma((4, 2)),
            dma((4, 4)),
            dma((4, 2)),
            pltpu.VMEM((D, 8), f32),
            pltpu.VMEM((4, 1024 + IMAGE, 256), bf16),
            dma((4,)),
            pltpu.VMEM((ROW, 768), bf16),
            dma,
        ],
        flops=6e9,
        nbytes=2e7,
        trans=1e6,
    )


def mlp_kernel(
    info_ref,
    w0,
    w1,
    w2,
    w3,
    gb_in,
    xhat_in,
    ub_ref,
    vec_ref,
    sums_a_ref,
    sent_out,
    hidden_out,
    dpre_out,
    buf_ref,
    gb_ref,
    wup_ref,
    wdown_ref,
    hidden_ref,
    dpre_ref,
    sent_ref,
    xhat_ref,
    sums_ref,
    image_ref,
    vec_col_ref,
    min_ref,
    rows_ref,
    turned_ref,
    buf_sem,
    in_sem,
    out_sem,
    sent_sem,
    image_sem,
):
    me, place = info_ref[64], info_ref[66]
    c = me % 2
    parts = []
    for n, (src, step) in enumerate(zip((w0, w1, w2, w3), STEPS)):
        b = (place + 4 - step) % 4
        parts.append(pltpu.make_async_copy(src, buf_ref.at[b], buf_sem.at[n]))

    def load(t, n):
        src, dst = ((gb_in, gb_ref), (xhat_in, xhat_ref))[n]
        return pltpu.make_async_copy(src.at[tile(t), :], dst.at[tile(t), :], in_sem.at[t, n])

    for part in parts:
        part.start()
    for t in range(4):
        for n in range(2):
            load(t, n).start()
    for part in parts:
        part.wait()
    assemble_b(me, buf_ref, wup_ref, wdown_ref)
    sums_ref[...] = jnp.zeros_like(sums_ref)

    vec_col_ref[...] = jnp.transpose(vec_ref[...])
    rows_ref[...] = jnp.zeros_like(rows_ref)

    def store(j, n):
        src, dst = ((hidden_ref, hidden_out), (dpre_ref, dpre_out))[n]
        return pltpu.make_async_copy(src.at[:, tile(j)], dst.at[:, tile(j)], out_sem.at[j, n])

    def sent_up(j):
        rows = pl.ds(pl.multiple_of(j * 64, 64), 64)
        return pltpu.make_async_copy(
            sent_ref.at[:, :, rows, :], sent_out.at[:, :, rows, :], sent_sem.at[j, 4]
        )

    def sent_down(j, x):
        b, a = swapped(j, x, c)
        rows = pl.ds(256, 256)
        return pltpu.make_async_copy(
            sent_ref.at[b, a, rows, :], sent_out.at[b, a, rows, :], sent_sem.at[j, x]
        )

    def hidden_tile(j, t):
        at = pl.ds(t * ROW, ROW)
        pre = dot(min_ref[at, :], wup_ref[:, tile(j)]) + ub_ref[:, tile(j)]
        return pre, dot_nt(gb_ref[at, :], wdown_ref[tile(j), :])

    def activate(j, t, pre, back):
        total = jnp.zeros((8, 256), f32)
        for i in range(0, ROW, STRIP):
            at = pl.ds(t * ROW + i, STRIP)
            a, b = pre[i : i + STRIP], back[i : i + STRIP]
            size = jnp.abs(a) * 0.7071067811865476
            bell = jnp.exp(-0.5 * a * a)
            s = 1.0 / (1.0 + 0.3275911 * size)
            poly = s * (
                0.127414796
                + s * (-0.142248368 + s * (0.7107068705 + s * (-0.7265760135 + s * 0.5307027145)))
            )
            tail = poly * bell
            cumul = jnp.where(a >= 0.0, 1.0 - tail, tail)
            hidden_ref[at, tile(j)] = (a * cumul).astype(bf16)
            dpre = (b * (cumul + a * (bell * 0.3989422804014327))).astype(bf16)
            dpre_ref[at, tile(j)] = dpre
            total += jnp.sum(dpre.astype(f32).reshape(STRIP // 8, 8, 256), axis=0)
        return jnp.sum(total, axis=0, keepdims=True)

    def put_down(j):
        down = dot_tn(hidden_ref[:, tile(j)], gb_ref[...]).astype(bf16)
        for x in range(4):
            b, a = swapped(j, x, c)
            for cg in range(4):
                sent_ref[b, a, 256 + cg * 64 : 256 + (cg + 1) * 64, :] = down[
                    x * 64 : (x + 1) * 64, cg * 256 : (cg + 1) * 256
                ]

    def put_up(j, t, raw):
        row = pl.multiple_of(j * 64 + t * 16, 16)
        sums = sums_ref[0:1, tile(j)]
        for y in range(4):
            for x in range(4):
                b, a = swapped(y, x, c)
                i = (y * 4 + x) * 16
                at = slice(t * 256 + i, t * 256 + i + 16)
                part = raw[i : i + 16]
                product = part * wup_ref[at, tile(j)].astype(f32)
                rows_ref[at, :] += product[:, :128] + product[:, 128:]
                gain, bias = vec_col_ref[at, 2:3], vec_col_ref[at, 3:4]
                sent_ref[b, a, pl.ds(row, 16), :] = (part * gain + bias * sums).astype(bf16)

    def step(j, last=False, first=False):
        if not last:
            total = jnp.zeros((1, 256), f32)
        for t in range(TP):
            if first:
                at = pl.ds(t * ROW, ROW)
                load(t, 0).wait()
                load(t, 1).wait()
                for i in range(0, ROW, 16):
                    strip = pl.ds(t * ROW + i, 16)
                    values = xhat_ref[strip, :].astype(f32)
                    min_ref[strip, :] = (values * vec_ref[2:3] + vec_ref[3:4]).astype(bf16)
                turned_ref[:, at] = jnp.transpose(xhat_ref[at, :])
            if not last:
                pre, back = hidden_tile(j, t)
            if not first:
                if t == 0:
                    put_down(j - 1)
                raw = dot(turned_ref[t * 256 : (t + 1) * 256, :], dpre_ref[:, tile(j - 1)])
            if not last:
                total += activate(j, t, pre, back)
            if not first:
                put_up(j - 1, t, raw)
        if not last:
            sums_ref[0:1, tile(j)] = total
            store(j, 0).start()
            store(j, 1).start()
        if not first:
            sent_up(j - 1).start()
            for x in range(4):
                sent_down(j - 1, x).start()

    step(0, first=True)

    @pl.loop(1, 4)
    def _(j):
        step(j)

    step(4, last=True)
    total = jnp.sum(rows_ref[...], axis=1, keepdims=True)
    sums_ref[1:2, :] = jnp.transpose(jnp.broadcast_to(total, (D, 128)))[0:1, :]
    sums_ref[2:3, :] = through(sums_ref[0:1, :], wup_ref[...])

    image_ref[...] = jnp.zeros_like(image_ref)

    def put(row, ref, line, count):
        for i in range(count):
            image_ref[pl.ds(row + i, 1), :] = ref[line : line + 1, i * 256 : (i + 1) * 256]

    put(0, sums_a_ref, 2, 4)
    put(4, sums_a_ref, 3, 4)
    put(8, sums_ref, 1, 4)
    put(12, sums_ref, 2, 4)
    for p in range(3):
        image_ref[pl.ds(16 + p * 4 + me, 1), :] = sums_a_ref[1:2, p * 256 : (p + 1) * 256]
    put(28, sums_a_ref, 0, 4)
    put(32 + 4 * me, sums_ref, 0, 4)
    put(48, sums_a_ref, 0, 4)
    image = image_ref[...]
    high = image.astype(bf16)
    low = (image - high.astype(f32)).astype(bf16)
    for b in range(4):
        for a in range(4):
            half = (high, low)[a // 2]
            sent_ref[b, a, 512 : 512 + IMAGE // 2, :] = half[a % 2 * 32 : a % 2 * 32 + 32]
    rows = pl.ds(512, IMAGE // 2)
    images = pltpu.make_async_copy(
        sent_ref.at[:, :, rows, :], sent_out.at[:, :, rows, :], image_sem
    )
    images.start()
    for i in range(TP):
        store(i, 0).wait()
        store(i, 1).wait()
        sent_up(i).wait()
        for x in range(4):
            sent_down(i, x).wait()
    images.wait()


def mlp(info, blocks, gb, xhat, ub, vec, sums):
    tokens = TP * ROW
    dma = pltpu.SemaphoreType.DMA
    return call(
        mlp_kernel,
        [
            shaped(4, 4, 512 + IMAGE // 2, 256),
            shaped(tokens, HC),
            shaped(tokens, HC),
        ],
        info,
        *blocks,
        gb,
        xhat,
        ub,
        vec,
        sums,
        places="s" + "a" * 4 + "hhvvv",
        outs="hhh",
        scratch=[
            pltpu.VMEM((4, 2048, 256), bf16),
            pltpu.VMEM((tokens, D), bf16),
            pltpu.VMEM((D, HC), bf16),
            pltpu.VMEM((HC, D), bf16),
            pltpu.VMEM((tokens, HC), bf16),
            pltpu.VMEM((tokens, HC), bf16),
            pltpu.VMEM((4, 4, 512 + IMAGE // 2, 256), bf16),
            pltpu.VMEM((tokens, D), bf16),
            pltpu.VMEM((8, D), f32),
            pltpu.VMEM((IMAGE, 256), f32),
            pltpu.VMEM((D, 8), f32),
            pltpu.VMEM((tokens, D), bf16),
            pltpu.VMEM((D, 128), f32),
            pltpu.VMEM((D, tokens), bf16),
            dma((4,)),
            dma((4, 2)),
            dma((4, 2)),
            dma((4, 5)),
            dma,
        ],
        flops=9e9,
        nbytes=2e7,
        trans=2e6,
    )


def outputs_kernel(
    info_ref,
    ctx_in,
    hidden_in,
    dqkv_in,
    dpre_in,
    a0,
    a1,
    a2,
    a3,
    b0,
    b1,
    b2,
    b3,
    vec_ref,
    theirs_out,
    mine_out,
    ctx_ref,
    hidden_ref,
    dqkv_ref,
    dpre_ref,
    wd_ref,
    wdown_ref,
    wqkv_ref,
    wup_ref,
    both_ref,
    buf_a_ref,
    buf_b_ref,
    weight_sem,
    in_sem,
    out_sem,
):
    me, place = info_ref[64], info_ref[66]
    weights = []
    for n, step in enumerate(STEPS):
        b = (place + 4 - step) % 4
        pairs = (((a0, a1, a2, a3)[n], buf_a_ref), ((b0, b1, b2, b3)[n], buf_b_ref))
        for i, (src, dst) in enumerate(pairs):
            weights.append(pltpu.make_async_copy(src, dst.at[b], weight_sem.at[n, i]))
    inputs = (
        (dqkv_in, dqkv_ref),
        (dpre_in, dpre_ref),
        (ctx_in, ctx_ref),
        (hidden_in, hidden_ref),
    )

    def load(t, n):
        src, dst = inputs[n]
        return pltpu.make_async_copy(src.at[tile(t), :], dst.at[tile(t), :], in_sem.at[t, n])

    def finished(i, n):
        dst = (theirs_out, mine_out)[n]
        return pltpu.make_async_copy(both_ref.at[i], dst.at[i - 2 * n], out_sem.at[i])

    for weight in weights:
        weight.start()
    for i in range(TP):
        for n in range(4):
            load((i + 2) % 4, n).start()
    for weight in weights:
        weight.wait()
    assemble_a(me, buf_a_ref, wqkv_ref, wd_ref)
    assemble_b(me, buf_b_ref, wup_ref, wdown_ref)

    @pl.loop(0, TP)
    def _(i):
        t = (i + 2) % 4
        for n in range(4):
            load(t, n).wait()
        here = tile(t)
        dattn = dot_nt(dqkv_ref[here, :], wqkv_ref[...])
        dmlp = dot_nt(dpre_ref[here, :], wup_ref[...])
        both_ref[i, 1] = (dattn * vec_ref[0:1] + dmlp * vec_ref[2:3]).astype(bf16)
        forward = dot(ctx_ref[here, :], wd_ref[...]) + dot(hidden_ref[here, :], wdown_ref[...])
        both_ref[i, 0] = forward.astype(bf16)

        @pl.when(i < 2)
        def _():
            finished(i, 0).start()

        @pl.when(i >= 2)
        def _():
            finished(i, 1).start()

    for i in range(TP):
        finished(i, i // 2).wait()


def outputs(info, ctx, hidden, dqkv, dpre, blocks_a, blocks_b, vec):
    tokens = TP * ROW
    dma = pltpu.SemaphoreType.DMA
    return call(
        outputs_kernel,
        [shaped(2, 2, ROW, D), shaped(2, 2, ROW, D)],
        info,
        ctx,
        hidden,
        dqkv,
        dpre,
        *blocks_a,
        *blocks_b,
        vec,
        places="s" + "a" * 12 + "v",
        outs="hh",
        scratch=[
            pltpu.VMEM((tokens, 256), bf16),
            pltpu.VMEM((tokens, HC), bf16),
            pltpu.VMEM((tokens, QC), bf16),
            pltpu.VMEM((tokens, HC), bf16),
            pltpu.VMEM((D // TP, D), bf16),
            pltpu.VMEM((HC, D), bf16),
            pltpu.VMEM((D, QC), bf16),
            pltpu.VMEM((D, HC), bf16),
            pltpu.VMEM((TP, 2, ROW, D), bf16),
            pltpu.VMEM((4, 1024 + IMAGE, 256), bf16),
            pltpu.VMEM((4, 2048, 256), bf16),
            dma((4, 2)),
            dma((4, 4)),
            dma((4,)),
        ],
        flops=6.5e9,
        nbytes=1.6e7,
    )


def half_kernel(mine_in, got_in, kept_out, send_out, mine_ref, got_ref, kept_ref, send_ref, in_sem, out_sem):
    loads = []
    for i in (1, 0):
        for n in range(2):
            pair = (
                pltpu.make_async_copy(mine_in.at[i, n], mine_ref.at[i, n], in_sem.at[i, n, 0]),
                pltpu.make_async_copy(got_in.at[i, n], got_ref.at[i, n], in_sem.at[i, n, 1]),
            )
            loads.append((i, n, pair))
            for copy in pair:
                copy.start()
    stores = []
    for i, n, pair in loads:
        for copy in pair:
            copy.wait()
        total = mine_ref[i, n].astype(f32) + got_ref[i, n].astype(f32)
        ref, out = ((kept_ref, kept_out), (send_ref, send_out))[i]
        ref[n] = total.astype(ref.dtype)
        stores.append(pltpu.make_async_copy(ref.at[n], out.at[0, n], out_sem.at[i, n]))
        stores[-1].start()
    for store in stores:
        store.wait()


def half_sum(mine, got):
    dma = pltpu.SemaphoreType.DMA
    return call(
        half_kernel,
        [shaped(1, 2, ROW, D, dtype=f32), shaped(1, 2, ROW, D)],
        mine,
        got,
        places="ha",
        outs="hh",
        scratch=[
            pltpu.VMEM((2, 2, ROW, D), bf16),
            pltpu.VMEM((2, 2, ROW, D), bf16),
            pltpu.VMEM((2, ROW, D), f32),
            pltpu.VMEM((2, ROW, D), bf16),
            dma((2, 2, 2)),
            dma((2, 2)),
        ],
        nbytes=8e6,
    )


def close_kernel(len_ref, x_ref, cot_ref, kept_ref, got_ref, vec_ref, out_ref, grad_ref):
    x = x_ref[...].astype(f32)
    out_ref[...] = (x + kept_ref[0, 0] + got_ref[0, 0].astype(f32) + vec_ref[4:5]).astype(bf16)
    e = kept_ref[0, 1] + got_ref[0, 1].astype(f32)
    xhat, inv_std = normalize(x)
    mean_e = jnp.mean(e, axis=-1, keepdims=True)
    mean_ex = jnp.mean(e * xhat, axis=-1, keepdims=True)
    used = sum([len_ref[0, j] for j in range(SEGS - 1)])
    rows = pl.program_id(0) * x.shape[0] + lax.broadcasted_iota(jnp.int32, (x.shape[0], 1), 0)
    kept = jnp.where(rows < used, cot_ref[...].astype(f32), 0.0)
    grad_ref[...] = kept + inv_std * (e - mean_e - xhat * mean_ex)


def close(lengths, x, cot, kept, got, vec):
    row = pl.BlockSpec((ROW // 4, D), lambda k: (k, 0))
    both = pl.BlockSpec((1, 2, ROW // 4, D), lambda k: (0, 0, k, 0))
    return pl.pallas_call(
        close_kernel,
        grid=(4,),
        in_specs=[SMEM_SPEC, row, row, both, both, pl.BlockSpec((8, D), lambda k: (0, 0))],
        out_specs=[row, row],
        out_shape=[pltpu.HBM((ROW, D), bf16), pltpu.HBM((ROW, D), f32)],
        compiler_params=pltpu.CompilerParams(vmem_limit_bytes=VMEM),
        cost_estimate=pl.CostEstimate(flops=0, bytes_accessed=6000000, transcendentals=0),
    )(lengths, *[in_hbm(v) for v in (x, cot, kept, got)], vec)


def add_early_kernel(a_ref, out_ref):
    out_ref[0] = sum([a_ref[i, 0].astype(f32) for i in range(4)]).astype(bf16)


def add_early(sent_a):
    return pl.pallas_call(
        add_early_kernel,
        grid=(4,),
        in_specs=[pl.BlockSpec((4, 1, 256, 256), lambda a: (0, a, 0, 0))],
        out_specs=pl.BlockSpec((1, 256, 256), lambda a: (a, 0, 0)),
        out_shape=pltpu.HBM((4, 256, 256), bf16),
        compiler_params=pltpu.CompilerParams(vmem_limit_bytes=VMEM),
        cost_estimate=pl.CostEstimate(flops=0, bytes_accessed=3000000, transcendentals=0),
    )(sent_a)


def add_kernel(
    place_ref, early_in, b_in, o0, o1, o2, o3, early_ref, b_ref, image_ref, both_ref, early_sem, b_sem, image_sem, sem
):
    place = place_ref[0]

    def load(n, i):
        a = (place + STEPS[n]) % 4
        return pltpu.make_async_copy(
            b_in.at[i, a, pl.ds(0, 512), :], b_ref.at[n, i], b_sem.at[n, i]
        )

    images = [
        pltpu.make_async_copy(
            b_in.at[i, :, pl.ds(512, IMAGE // 2), :], image_ref.at[i], image_sem.at[i]
        )
        for i in range(4)
    ]
    early = [
        pltpu.make_async_copy(
            early_in.at[(place + step) % 4], early_ref.at[n], early_sem.at[n]
        )
        for n, step in enumerate(STEPS)
    ]
    for copy in images:
        copy.start()
    for n in range(4):
        early[n].start()
        for i in range(4):
            load(n, i).start()
    for copy in images:
        copy.wait()
    image = sum([image_ref[i].astype(f32) for i in range(4)]).reshape(2, IMAGE, 256)
    image = image[0] + image[1]
    high = image.astype(bf16)
    low = (image - high.astype(f32)).astype(bf16)
    stores = [
        pltpu.make_async_copy(both_ref.at[n], out, sem.at[n]) for n, out in enumerate((o0, o1, o2, o3))
    ]
    for n in range(4):
        both_ref[n, 768 : 768 + IMAGE, :] = high
        both_ref[n, 768 + IMAGE : 768 + 2 * IMAGE, :] = low
        early[n].wait()
        both_ref[n, 0:256, :] = early_ref[n]
        for i in range(4):
            load(n, i).wait()
        total = sum([b_ref[n, i].astype(f32) for i in range(4)])
        both_ref[n, 256:768, :] = total.astype(bf16)
        stores[n].start()
    for store in stores:
        store.wait()


def add(place, early, sent_b):
    rows = 768 + 2 * IMAGE
    dma = pltpu.SemaphoreType.DMA
    return call(
        add_kernel,
        [shaped(rows, 256)] * 4,
        place,
        early,
        sent_b,
        places="shh",
        outs="hhhh",
        scratch=[
            pltpu.VMEM((4, 256, 256), bf16),
            pltpu.VMEM((4, 4, 512, 256), bf16),
            pltpu.VMEM((4, 4, IMAGE // 2, 256), bf16),
            pltpu.VMEM((4, rows, 256), bf16),
            dma((4,)),
            dma((4, 4)),
            dma((4,)),
            dma((4,)),
        ],
        nbytes=6e6,
    )


LAST = QC + HC + 4 * 256


def image_rows(d):
    return [start + d for start in STARTS[:4]] + [28 + d, 48 + d] + [
        32 + 4 * d + i for i in range(4)
    ] + [16 + 3 * d + i for i in range(3)]


def part_kernel(far_ref, r0, r1, r2, r3, slots_ref, keep_ref, send_ref, total_ref, rows_ref):
    far = far_ref[0]
    total_ref[...] = sum([ref[...].astype(f32) for ref in (r0, r1, r2, r3)])
    rows_ref[...] = jnp.zeros_like(rows_ref)
    for d in range(4):
        for i, row in enumerate(image_rows(d)):
            high = total_ref[768 + row : 769 + row, :]
            low = total_ref[768 + IMAGE + row : 769 + IMAGE + row, :]
            rows_ref[d, i : i + 1, :] = high + low
        image = rows_ref[d]
        high = image.astype(bf16)
        low = (image - high.astype(f32)).astype(bf16)
        for zh in range(2):
            s = d * 2 + zh
            for p in range(3):
                row = (d * 3 + p) * 16 + zh * 8
                slots_ref[s, :, p * 256 : (p + 1) * 256] = total_ref[row : row + 8, :].astype(bf16)
            for cg in range(4):
                row = 256 + (cg * 4 + d) * 16 + zh * 8
                at = QC + cg * 256
                slots_ref[s, :, at : at + 256] = total_ref[row : row + 8, :].astype(bf16)
            for n, block in enumerate((high[:8], high[8:], low[:8], low[8:])):
                at = QC + HC + n * 256
                slots_ref[s, :, at : at + 256] = block
    for ref, half in ((keep_ref, far), (send_ref, 1 - far)):
        for cg in range(4):
            at = slice(cg * 256, (cg + 1) * 256)
            row = pl.multiple_of(192 + cg * 16 + half * 8, 8)
            ref[32:40, at] = total_ref[pl.ds(row, 8), :].astype(ref.dtype)
            row = pl.multiple_of(512 + cg * 64 + half * 32, 8)
            ref[0:32, at] = total_ref[pl.ds(row, 32), :].astype(ref.dtype)


def part(far, received):
    return call(
        part_kernel,
        [shaped(8, 8, LAST), shaped(40, D, dtype=f32), shaped(40, D)],
        far,
        *received,
        outs="uuu",
        scratch=[pltpu.VMEM((768 + 2 * IMAGE, 256), f32), pltpu.VMEM((4, 16, 256), f32)],
        nbytes=4e6,
    )


def finish_kernel(
    place_ref, slots_ref, keep_ref, got_ref, qkv_out, up_out, dense_out, down_out, *rest
):
    tiny_refs = rest[:8]
    image_ref, qkv_ref, up_ref, dense_ref, down_ref, sem = rest[8:]
    image = [jnp.zeros((8, 256), f32)] * 2
    for s in range(8):
        for n in range(4):
            at = QC + HC + n * 256
            image[n % 2] = image[n % 2] + slots_ref[s, :, at : at + 256].astype(f32)
    image_ref[0:8, :] = image[0]
    image_ref[8:16, :] = image[1]
    def rows_out(ref, out, first):
        width = ref.shape[2]
        copies = [
            pltpu.make_async_copy(
                ref.at[r, 0], out.at[pl.ds(r * width, width)], sem.at[first + r]
            )
            for r in range(ref.shape[0])
        ]
        for copy in copies:
            copy.start()
        return copies

    total = keep_ref[...] + got_ref[...].astype(f32)
    dense_ref[:, 0, :] = total[32:40]
    down_ref[:, 0, :] = total[0:32]
    copies = rows_out(dense_ref, dense_out, 0) + rows_out(down_ref, down_out, 8)
    for d in range(4):
        both = slots_ref[2 * d, :, 0 : QC + HC].astype(f32) + slots_ref[
            2 * d + 1, :, 0 : QC + HC
        ].astype(f32)
        for p in range(3):
            at = p * D + d * 256
            qkv_ref[:, 0, at : at + 256] = both[:, p * 256 : (p + 1) * 256]
        up_ref[:, 0, d * HC : (d + 1) * HC] = both[:, QC:]
    copies += rows_out(qkv_ref, qkv_out, 40) + rows_out(up_ref, up_out, 48)
    p = place_ref[0]
    f = p % 32
    lines = (0, 1, 2, 3, 10 + f * 24 // 256, 4, 6 + f // 8, 5)
    for line, size, ref in zip(lines, SIZES, tiny_refs):
        lane = (p * size) % 256
        values = image_ref[pl.ds(line, 1), :]
        if size == 24:
            values = jnp.concatenate([values, image_ref[pl.ds(line + 1, 1), :]], axis=1)
        width = values.shape[1]
        ref[...] = pltpu.roll(values, (width - lane) % width, 1)[:, :size]
    for copy in copies:
        copy.wait()


def finish(place, slots, keep, got):
    return call(
        finish_kernel,
        [
            shaped(8 * 3 * D, dtype=f32),
            shaped(8 * FF, dtype=f32),
            shaped(8 * D, dtype=f32),
            shaped(32 * D, dtype=f32),
        ]
        + [shaped(1, size, dtype=f32) for size in SIZES],
        place,
        slots,
        keep,
        got,
        outs="hhhh" + "v" * 8,
        scratch=[
            pltpu.VMEM((16, 256), f32),
            pltpu.VMEM((8, 1, 3 * D), f32),
            pltpu.VMEM((8, 1, FF), f32),
            pltpu.VMEM((8, 1, D), f32),
            pltpu.VMEM((32, 1, D), f32),
            pltpu.SemaphoreType.DMA((56,)),
        ],
        nbytes=2e6,
    )


def body(
    inputs,
    cotangent,
    lengths,
    norm1_gain,
    norm1_bias,
    norm2_gain,
    norm2_bias,
    qkv_weight,
    qkv_bias,
    dense_weight,
    dense_bias,
    up_weight,
    up_bias,
    down_weight,
    down_bias,
):
    me = lax.axis_index("dp").astype(jnp.int32)
    index = lax.axis_index("fsdp").astype(jnp.int32)
    far = (index % 2)[None]
    me1 = me[None]
    outer, inner = outer_groups(), inner_groups()

    vectors = (
        norm1_gain,
        norm1_bias,
        norm2_gain,
        norm2_bias,
        qkv_bias,
        dense_bias,
        up_bias,
        down_bias,
    )
    x2, c2 = flip_core(inputs), flip_core(cotangent)
    slots, pieces = prepare(
        qkv_weight.reshape(8, 3 * D),
        up_weight.reshape(8, FF),
        dense_weight.reshape(8, D),
        down_weight.reshape(32, D),
        lengths,
        vectors,
    )
    far_pieces = flip_far(pieces)
    first = a2a(slots, stack_groups())
    first, x2, c2 = lax.optimization_barrier((first, x2, c2))
    block, lens = spread(index[None], first.reshape(4, 16, SLOT), pieces, far_pieces)
    along_x, along_y = index // 2 % 4, index // 8
    core = me % 2 == 1
    near = jnp.where(core, along_x, along_y)[None]
    deep = jnp.where(core, along_y, along_x)[None]
    info = jnp.concatenate([lens[0], me1, far, near])

    info, x0, c0 = lax.optimization_barrier((info, inputs, cotangent))
    x1, c1 = flip_chip(x0), flip_chip(c0)
    second = gather(block, inner)
    second, x1 = lax.optimization_barrier((second, x1))
    third_a = gather(merge_a(deep, second), outer)
    x3, c3 = flip_core(x1), flip_core(c1)
    xs, cots = (x0, x1, x2, x3), (c0, c1, c2, c3)
    wide_b, xs = lax.optimization_barrier((merge_b(deep, second), xs))
    third_b = gather(wide_b, outer)

    sent_a, gb, ctx, dqkv, xhat, vec, up_b, sums = attention(info, xs, cots, third_a)
    sent_a = a2a(sent_a, outer)
    sent_b, hidden, dpre = mlp(info, third_b, gb, xhat, up_b, vec, sums)
    sent_b = a2a(sent_b, outer)

    theirs, mine = outputs(info, ctx, hidden, dqkv, dpre, third_a, third_b, vec)
    kept, send = half_sum(mine, flip_core(theirs))

    got = flip_chip(send)
    early, send = lax.optimization_barrier((add_early(sent_a), send))
    fourth = scatter(add(deep, early, sent_b), inner)
    slots, keep, rest = part(far, fourth)
    block_output, input_grad = close(lengths, inputs, cotangent, kept, got, vec)
    place = (me * 32 + index)[None]
    slots, rest, block_output, input_grad = lax.optimization_barrier(
        (a2a(slots, stack_groups()), flip_far(rest), block_output, input_grad)
    )
    results = finish(place, slots, keep, rest)
    flat = [r.reshape(-1) for r in results]
    return (
        block_output,
        input_grad,
        flat[4],
        flat[5],
        flat[6],
        flat[7],
        flat[0],
        flat[8],
        flat[2],
        flat[9],
        flat[1],
        flat[10],
        flat[3],
        flat[11],
    )


def solution(mesh):
    flat = P(("dp", "fsdp"))
    rows = P(("dp", "fsdp"), None)
    return jax.shard_map(
        body,
        mesh=mesh,
        in_specs=(rows,) * 3 + (flat,) * 12,
        out_specs=(rows,) * 2 + (flat,) * 12,
        check_vma=False,
    )
```
